32 devices in a mesh: dp: 8 (over z, y), tensor: 4 (over x, core).
Axes of the slice: x: 2, y: 2, z: 4, core: 2. Of those that a mesh axis runs over, the one named last changes fastest.
Arguments:
- token_ids: int32 [1024], P('dp'), may hold values from 0 to 31999
- targets: int32 [1024], P('dp'), may hold values from 0 to 31999
- loss_offsets: int32 [128], P('dp'), may hold values from 0 to 127, as said below
- routes: int32 [1024, 2], P('dp'), may hold values from 0 to 3, all different within a row; in each aligned block of 128 rows (0 to 127, 128 to 255, ...) at most 128 rows name the same one
- picture_start: int32 [1, 1], replicated, may hold values from 0 to 768, as said below
- buckets: int32 [2047], replicated, may hold values from 0 to 31
- embedding: float32 [32000, 768], P('tensor', 'dp')
- embedding_first: float32 [32000, 768], P('tensor', 'dp'), may hold values from -4.5776367e-05 to 4.5776367e-05
- embedding_second: float32 [32000, 768], P('tensor', 'dp'), may hold values from 2.837829e-10 to 1.1569611e-09
- attn_proj: float32 [3, 768, 768], P(None, 'dp', 'tensor'), may hold values from -0.109375 to 0.109375
- attn_proj_first: float32 [3, 768, 768], P(None, 'dp', 'tensor'), may hold values from -9.1552734e-05 to 9.1552734e-05
- attn_proj_second: float32 [3, 768, 768], P(None, 'dp', 'tensor'), may hold values from 1.1569611e-09 to 4.5841855e-09
- out_proj: float32 [768, 768], P('tensor', 'dp'), may hold values from -1.75 to 1.75
- out_proj_first: float32 [768, 768], P('tensor', 'dp'), may hold values from -9.1552734e-05 to 9.1552734e-05
- out_proj_second: float32 [768, 768], P('tensor', 'dp'), may hold values from 1.1569611e-09 to 4.5841855e-09
- router: float32 [4, 768], P(None, 'dp'), may hold values from -0.078125 to 0.078125
- router_first: float32 [4, 768], P(None, 'dp'), may hold values from -0.00030517578 to 0.00030517578
- router_second: float32 [4, 768], P(None, 'dp'), may hold values from 1.0259844e-08 to 4.1475964e-08
- expert_in: float32 [768, 12288], P(None, ('dp', 'tensor')), may hold values from -0.21875 to 0.21875
- expert_in_first: float32 [768, 12288], P(None, ('dp', 'tensor')), may hold values from -9.1552734e-05 to 9.1552734e-05
- expert_in_second: float32 [768, 12288], P(None, ('dp', 'tensor')), may hold values from 1.1569611e-09 to 4.5841855e-09
- expert_out: float32 [12288, 768], P(('dp', 'tensor')), may hold values from -0.109375 to 0.109375
- expert_out_first: float32 [12288, 768], P(('dp', 'tensor')), may hold values from -9.1552734e-05 to 9.1552734e-05
- expert_out_second: float32 [12288, 768], P(('dp', 'tensor')), may hold values from 1.1569611e-09 to 4.5841855e-09
- norm_gains: float32 [3, 768], P(None, 'dp')
- norm_gains_first: float32 [3, 768], P(None, 'dp'), may hold values from -0.00036621094 to 0.00036621094
- norm_gains_second: float32 [3, 768], P(None, 'dp'), may hold values from 3.2744183e-09 to 1.3097673e-08
- position_bias: float32 [12, 32], P('tensor'), may hold values from -6 to 6
- position_bias_first: float32 [12, 32], P('tensor'), may hold values from -0.0009765625 to 0.0009765625
- position_bias_second: float32 [12, 32], P('tensor'), may hold values from 1.1569611e-07 to 4.5841855e-07
Outputs:
- new_embedding: float32 [32000, 768], P('tensor', 'dp')
- new_embedding_first: float32 [32000, 768], P('tensor', 'dp')
- new_embedding_second: float32 [32000, 768], P('tensor', 'dp')
- new_attn_proj: float32 [3, 768, 768], P(None, 'dp', 'tensor')
- new_attn_proj_first: float32 [3, 768, 768], P(None, 'dp', 'tensor')
- new_attn_proj_second: float32 [3, 768, 768], P(None, 'dp', 'tensor')
- new_out_proj: float32 [768, 768], P('tensor', 'dp')
- new_out_proj_first: float32 [768, 768], P('tensor', 'dp')
- new_out_proj_second: float32 [768, 768], P('tensor', 'dp')
- new_router: float32 [4, 768], P(None, 'dp')
- new_router_first: float32 [4, 768], P(None, 'dp')
- new_router_second: float32 [4, 768], P(None, 'dp')
- new_expert_in: float32 [768, 12288], P(None, ('dp', 'tensor'))
- new_expert_in_first: float32 [768, 12288], P(None, ('dp', 'tensor'))
- new_expert_in_second: float32 [768, 12288], P(None, ('dp', 'tensor'))
- new_expert_out: float32 [12288, 768], P(('dp', 'tensor'))
- new_expert_out_first: float32 [12288, 768], P(('dp', 'tensor'))
- new_expert_out_second: float32 [12288, 768], P(('dp', 'tensor'))
- new_norm_gains: float32 [3, 768], P(None, 'dp')
- new_norm_gains_first: float32 [3, 768], P(None, 'dp')
- new_norm_gains_second: float32 [3, 768], P(None, 'dp')
- new_position_bias: float32 [12, 32], P('tensor')
- new_position_bias_first: float32 [12, 32], P('tensor')
- new_position_bias_second: float32 [12, 32], P('tensor')
- grad_norm: float32 [], replicated
- loss_sum: float32 [], replicated
- loss_count: float32 [], replicated
The draws below stay inside these ranges and needn't reach their ends.
Inputs may be any that keep to these rules, and one draw needn't show every extreme that they name: `loss_offsets`: in each aligned block of 16 entries the offsets are distinct. `picture_start`: increasing along each row; the pieces of 256 positions do not intersect and end inside their sequence. The two routes of a token differ; among the rows of one device no expert is named more than 128 times, a bound that some block reaches.
All inputs are finite; a program needn't handle non-finite values.
Results may differ from the reference program's by a relative error of at most 0.02.
The reference program's roundings to bfloat16 on the way count: a program that leaves them out, or rounds other values in their place, can miss the bound.
Values may be sent and summed in bfloat16 or wider, within the bound.
A program may use at most 256 MiB of HBM per device.

```python
import math
import jax
import jax.numpy as jnp
import numpy as np
from jax import lax

D = 768
HEADS = 12
HD = 64
FF = 3072
VOCAB = 32000
BUCKETS = 32
TOP = 2
PIECE = 256
LPOS = 16
STEP = 10
TOK_DEV = 128
TOKENS = 1024
LENGTH = 1024
SEQS = 1
SUB = 128
EXPERTS = 4
CAP = 128
PICS = 1
N_TENSOR = 4


def draw_picture_start(key, part):
    key = jax.random.fold_in(key, 11)
    number = jnp.arange(PICS, dtype=jnp.int32)
    spread = 2 * (LENGTH - PICS * PIECE) // (PICS * PICS)
    lower = number * spread // 2
    upper = number * spread + spread // 2 + 1
    gaps = jax.random.randint(key, (SEQS, PICS), lower[None, :], upper[None, :], dtype=jnp.int32)
    drawn = number[None, :] * PIECE + jnp.cumsum(gaps, 1).astype(jnp.int32)
    last = jnp.full((SEQS, PICS), LENGTH - PIECE, jnp.int32)
    return jnp.where(number[None, :] == PICS - 1, last, drawn).astype(jnp.int32)


def draw_loss_offsets(key, part):
    key = jax.random.fold_in(key, 12)
    blocks = TOKENS // TOK_DEV
    keys = jax.random.split(key, blocks)
    chosen = jax.vmap(lambda k: jax.random.permutation(k, TOK_DEV)[:LPOS])(keys)
    return chosen.reshape(blocks * LPOS).astype(jnp.int32)


def draw_embedding(key, part):
    key = jax.random.fold_in(key, 13)
    rise = jnp.arange(VOCAB, dtype=jnp.float32)[:, None] / VOCAB
    noise = jax.random.normal(key, (VOCAB, D), jnp.float32)
    scale = 1.0 + 2.0 * rise
    return noise * scale * (0.48 / math.sqrt(D))


def draw_norm_gains(key, part):
    key = jax.random.fold_in(key, 14)
    rise = jnp.arange(D, dtype=jnp.float32)[None, :] / D
    jitter = jax.random.uniform(key, (3, D), jnp.float32, 0.8, 1.25)
    growth = 1.0 + 2.0 * rise
    return growth * jitter


def touch_ends(array, key, smallest, high):
    spot = [jax.random.randint(jax.random.fold_in(key, axis), (), 0, length) for axis, length in enumerate(array.shape)]
    widest = array.shape.index(max(array.shape))
    beside = spot[:widest] + [(spot[widest] + 1) % array.shape[widest]] + spot[widest + 1:]
    return array.at[tuple(spot)].set(smallest).at[tuple(beside)].set(high)


def levels(stream_key, dims, shards, least, high):
    def one(position, blocks):
        steps = jax.random.uniform(jax.random.fold_in(jax.random.fold_in(stream_key, 6), position), (blocks,), jnp.float32, least / len(shards), high / len(shards))
        return jnp.repeat(jnp.exp(steps), dims[position] // blocks).reshape((-1,) + (1,) * (len(dims) - position - 1))

    loudness = one(*shards[0])
    for cut in shards[1:]:
        loudness = loudness * one(*cut)
    return loudness


def rank_bounds(amount, slope):
    loads = [(1 << 20) // math.isqrt(rank ** slope) + 1 for rank in range(1, amount + 1)]
    deviation = 1 + sum(loads) // (1 << 30)
    return np.cumsum(np.array([max(1, weight // deviation) for weight in loads]))


def skewed_ids(key, dims, count, lean):
    table = rank_bounds(count, lean)
    pick = jax.random.randint(jax.random.fold_in(key, 1), dims, 0, int(table[count - 1]))
    rank = jnp.searchsorted(jnp.asarray(table, jnp.int32), pick, side="right")
    return jax.random.permutation(jax.random.fold_in(key, 2), count)[rank].astype(jnp.int32)


def routed_block(rng, own, number, rows, count, top, limit, slope):
    ranking = jax.random.permutation(rng, count)
    crowded, common = shares(count, rows * top, limit, slope, True), shares(count, rows * top, limit, slope, False)
    places = jnp.arange(count)

    def named(lengths, rotation):
        used = int((lengths > 0).sum())
        fixed = max(1, used // 4)
        moved = fixed + (places - fixed + rotation * (used - fixed)) % max(1, count - fixed)
        return jnp.zeros((count,), jnp.int32).at[ranking[jnp.where(places < fixed, places, moved)]].set(jnp.asarray(lengths, jnp.int32))

    lengths = jnp.where(number % 4 == 0, named(crowded, number // 4), named(common, number - number // 4 - 1))
    mixed = jax.random.permutation(jax.random.fold_in(own, 3), count)
    giver, receiver = mixed[0:count // 2 * 2:2], mixed[1:count // 2 * 2:2]
    room = jnp.minimum(lengths[giver] - 1, limit - lengths[receiver]) // 2
    room = jnp.where((giver == ranking[0]) | (receiver == ranking[0]) | (lengths[receiver] == 0), 0, jnp.maximum(room, 0))
    moved = jax.random.randint(jax.random.fold_in(own, 4), (count // 2,), 0, 1 << 20) % (room + 1)
    lengths = lengths.at[giver].add(-moved).at[receiver].add(moved)
    members = jnp.searchsorted(jnp.cumsum(lengths), jnp.arange(rows * top), side="right").astype(jnp.int32)
    grid = members.reshape(top, rows).T
    grid = grid[jax.random.permutation(jax.random.fold_in(own, 1), rows)]
    rotation = jax.random.randint(jax.random.fold_in(own, 2), (rows, 1), 0, top)
    return jnp.take_along_axis(grid, (jnp.arange(top)[None, :] + rotation) % top, axis=1)


def shares(number_of, total, bound, slope, full):
    portions = [(1 << 20) // math.isqrt(rank ** slope) + 1 for rank in range(1, number_of + 1)]
    largest = bound if full else min(bound, max(-(-total // number_of), total * portions[0] // sum(portions)))
    least = 1 if total - largest >= number_of - 1 else 0
    counts, surplus = [largest] + [least] * (number_of - 1), total - largest - least * (number_of - 1)
    while surplus > 0:
        candidates = [i for i in range(1, number_of) if counts[i] < largest] or [i for i in range(1, number_of) if counts[i] < bound]
        pool, budget = sum([portions[i] for i in candidates]), surplus
        for i in candidates:
            addition = min(bound - counts[i], max(1, budget * portions[i] // pool), surplus)
            counts[i] = counts[i] + addition
            surplus = surplus - addition
    return np.array(counts)


def centred(key, extent, width, limit, cuts=(), kind=jnp.bfloat16):
    level = levels(key, extent, cuts, -0.22, 0.18) if cuts else 1.0
    array = jax.random.normal(key, extent, jnp.float32) * width * level
    return jnp.minimum(jnp.maximum(array, -limit), limit).astype(kind)


def setup_inputs(seed: int = 0) -> dict:
    seeds = jax.random.split(jax.random.key(seed), 31)
    token_ids = touch_ends(skewed_ids(seeds[0], (TOKENS,), VOCAB, 2), jax.random.fold_in(seeds[0], 3), 0, VOCAB - 1).astype(jnp.int32)
    targets = touch_ends(skewed_ids(seeds[1], (TOKENS,), VOCAB, 2), jax.random.fold_in(seeds[1], 3), 0, VOCAB - 1).astype(jnp.int32)
    loss_offsets = draw_loss_offsets(jax.random.fold_in(seeds[30], 71), 0)
    routes_keys = jax.random.split(jax.random.fold_in(seeds[3], 1), TOKENS // TOK_DEV)
    routes_turns = jax.random.permutation(jax.random.fold_in(seeds[3], 3), TOKENS // TOK_DEV)
    routes = jax.vmap(lambda own, number: routed_block(jax.random.fold_in(seeds[3], 2), own, number, TOK_DEV, EXPERTS, TOP, CAP, 1))(routes_keys, routes_turns).reshape((TOKENS, TOP))
    picture_start = draw_picture_start(jax.random.fold_in(seeds[30], 71), 0)
    buckets = touch_ends(jax.random.randint(seeds[5], (2 * LENGTH - 1,), 0, BUCKETS), jax.random.fold_in(seeds[5], 1), 0, BUCKETS - 1).astype(jnp.int32)
    embedding = draw_embedding(jax.random.fold_in(seeds[30], 71), 0)
    embedding_first = centred(seeds[7], (VOCAB, D), (0.055 / (VOCAB * D + 4 * D * D + 2 * EXPERTS * D * FF) ** 0.5), 4.57763671875e-05, ((0, 4), (1, 8)), jnp.float32)
    embedding_second = jnp.clip(jnp.exp(math.log(1.156961082493524e-09) - 1.40534253 * jax.random.uniform(seeds[8], (VOCAB, D), jnp.float32) ** levels(seeds[8], (VOCAB, D), ((0, 4), (1, 8)), -0.2, 0.2)), 2.837829138346848e-10, 1.156961082493524e-09)
    attn_proj = centred(seeds[9], (3, D, D), (4 * D) ** -0.5, 0.109375, ((1, 8), (2, 4)), jnp.float32)
    attn_proj_first = centred(seeds[10], (3, D, D), (0.11 / (VOCAB * D + 4 * D * D + 2 * EXPERTS * D * FF) ** 0.5), 9.1552734375e-05, ((1, 8), (2, 4)), jnp.float32)
    attn_proj_second = jnp.clip(jnp.exp(math.log(4.584185475664526e-09) - 1.37681563 * jax.random.uniform(seeds[11], (3, D, D), jnp.float32) ** levels(seeds[11], (3, D, D), ((1, 8), (2, 4)), -0.2, 0.2)), 1.156961082493524e-09, 4.584185475664526e-09)
    out_proj = centred(seeds[12], (D, D), (max(1, D * 16 // LENGTH)) ** -0.5, 1.75, ((0, 4), (1, 8)), jnp.float32)
    out_proj_first = centred(seeds[13], (D, D), (0.11 / (VOCAB * D + 4 * D * D + 2 * EXPERTS * D * FF) ** 0.5), 9.1552734375e-05, ((0, 4), (1, 8)), jnp.float32)
    out_proj_second = jnp.clip(jnp.exp(math.log(4.584185475664526e-09) - 1.37681563 * jax.random.uniform(seeds[14], (D, D), jnp.float32) ** levels(seeds[14], (D, D), ((0, 4), (1, 8)), -0.2, 0.2)), 1.156961082493524e-09, 4.584185475664526e-09)
    router = centred(seeds[15], (EXPERTS, D), (8 * D) ** -0.5, 0.078125, ((1, 8),), jnp.float32)
    router_first = centred(seeds[16], (EXPERTS, D), (0.33 / (VOCAB * D + 4 * D * D + 2 * EXPERTS * D * FF) ** 0.5), 0.00030517578, ((1, 8),), jnp.float32)
    router_second = jnp.clip(jnp.exp(math.log(4.147596399661779e-08) - 1.3968765 * jax.random.uniform(seeds[17], (EXPERTS, D), jnp.float32) ** levels(seeds[17], (EXPERTS, D), ((1, 8),), -0.2, 0.2)), 1.025984364133592e-08, 4.147596399661779e-08)
    expert_in = centred(seeds[18], (D, EXPERTS * FF), D ** -0.5, 0.21875, ((1, 32),), jnp.float32)
    expert_in_first = centred(seeds[19], (D, EXPERTS * FF), (0.11 / (VOCAB * D + 4 * D * D + 2 * EXPERTS * D * FF) ** 0.5), 9.1552734375e-05, ((1, 32),), jnp.float32)
    expert_in_second = jnp.clip(jnp.exp(math.log(4.584185475664526e-09) - 1.37681563 * jax.random.uniform(seeds[20], (D, EXPERTS * FF), jnp.float32) ** levels(seeds[20], (D, EXPERTS * FF), ((1, 32),), -0.2, 0.2)), 1.156961082493524e-09, 4.584185475664526e-09)
    expert_out = centred(seeds[21], (EXPERTS * FF, D), FF ** -0.5, 0.109375, ((0, 32),), jnp.float32)
    expert_out_first = centred(seeds[22], (EXPERTS * FF, D), (0.11 / (VOCAB * D + 4 * D * D + 2 * EXPERTS * D * FF) ** 0.5), 9.1552734375e-05, ((0, 32),), jnp.float32)
    expert_out_second = jnp.clip(jnp.exp(math.log(4.584185475664526e-09) - 1.37681563 * jax.random.uniform(seeds[23], (EXPERTS * FF, D), jnp.float32) ** levels(seeds[23], (EXPERTS * FF, D), ((0, 32),), -0.2, 0.2)), 1.156961082493524e-09, 4.584185475664526e-09)
    norm_gains = draw_norm_gains(jax.random.fold_in(seeds[30], 71), 0)
    norm_gains_first = centred(seeds[25], (3, D), (0.4 / (VOCAB * D + 4 * D * D + 2 * EXPERTS * D * FF) ** 0.5), 0.00036621094, ((1, 8),), jnp.float32)
    norm_gains_second = jnp.clip(jnp.exp(math.log(1.3097673168260826e-08) - 1.3862944 * jax.random.uniform(seeds[26], (3, D), jnp.float32) ** levels(seeds[26], (3, D), ((1, 8),), -0.2, 0.2)), 3.2744182920652065e-09, 1.3097673168260826e-08)
    position_bias = centred(seeds[27], (HEADS, BUCKETS), 1.0, 6.0, ((0, 4),), jnp.float32)
    position_bias_first = centred(seeds[28], (HEADS, BUCKETS), (1.1 / (VOCAB * D + 4 * D * D + 2 * EXPERTS * D * FF) ** 0.5), 0.0009765625, ((0, 4),), jnp.float32)
    position_bias_second = jnp.clip(jnp.exp(math.log(4.5841855467188e-07) - 1.37681563 * jax.random.uniform(seeds[29], (HEADS, BUCKETS), jnp.float32) ** levels(seeds[29], (HEADS, BUCKETS), ((0, 4),), -0.2, 0.2)), 1.1569611046979844e-07, 4.5841855467188e-07)
    return dict(token_ids=token_ids, targets=targets, loss_offsets=loss_offsets, routes=routes, picture_start=picture_start, buckets=buckets, embedding=embedding, embedding_first=embedding_first, embedding_second=embedding_second, attn_proj=attn_proj, attn_proj_first=attn_proj_first, attn_proj_second=attn_proj_second, out_proj=out_proj, out_proj_first=out_proj_first, out_proj_second=out_proj_second, router=router, router_first=router_first, router_second=router_second, expert_in=expert_in, expert_in_first=expert_in_first, expert_in_second=expert_in_second, expert_out=expert_out, expert_out_first=expert_out_first, expert_out_second=expert_out_second, norm_gains=norm_gains, norm_gains_first=norm_gains_first, norm_gains_second=norm_gains_second, position_bias=position_bias, position_bias_first=position_bias_first, position_bias_second=position_bias_second)


@jax.custom_vjp
def low(v):
    return lax.optimization_barrier(v.astype(jnp.bfloat16)).astype(jnp.float32)

@jax.custom_vjp
def low_back(v):
    return v

def low_keep(v):
    return (low(v), None)

def low_pass(kept, grad):
    return (grad,)

def back_keep(v):
    return (v, None)

def back_low(kept, grad):
    return (low(grad),)
low.defvjp(low_keep, low_pass)
low_back.defvjp(back_keep, back_low)
HIGH = lax.Precision.HIGHEST
SMOOTH = 0.1
ZLOSS = 0.0001
NORM_EPS = 1e-06
MAX_NORM = 1.0
BETA1 = 0.9
BETA2 = 0.95
ADAM_EPS = 1e-08
RATES = (0.04, 0.04, 1.0, 0.03, 0.07, 0.035, 1.0, 0.7)
DECAYS = (0.1, 0.1, 0.1, 0.1, 0.1, 0.1, 0.0, 0.0)
NEGATIVE = -1e+30

def normed(v, g):
    return v * lax.rsqrt(lax.optimization_barrier(jnp.mean(v * v, -1, keepdims=True)) + NORM_EPS) * g

def picture_of(positions, starts):
    inside = (positions[:, None] >= starts[None, :]) & (positions[:, None] < starts[None, :] + PIECE)
    number = jnp.arange(starts.shape[0], dtype=jnp.int32) + 1
    return lax.optimization_barrier(jnp.sum(inside.astype(jnp.int32) * number[None, :], 1)) - 1

def attend(query_block, key_prefix, value_prefix, position_bias, bucket_index, allowed):
    scores = jnp.einsum('qhd,khd->hqk', query_block, key_prefix, precision=HIGH) * (1.0 / math.sqrt(HD))
    scores = low_back(scores + position_bias[:, bucket_index])
    probs = jax.nn.softmax(jnp.where(allowed[None], scores, NEGATIVE), -1)
    return jnp.einsum('hqk,khd->qhd', low(probs), value_prefix, precision=HIGH)

def attend_sequence(item, position_bias, buckets):
    queries, keys, values, picture = item
    block = min(512, LENGTH)
    results = []
    for index in range(LENGTH // block):
        reach = min(LENGTH, (index + 1) * block + PIECE)
        query_pos = index * block + jnp.arange(block, dtype=jnp.int32)
        key_pos = jnp.arange(reach, dtype=jnp.int32)
        bucket_index = buckets[query_pos[:, None] - key_pos[None, :] + LENGTH - 1]
        query_pic = picture[query_pos][:, None]
        allowed = (key_pos[None, :] <= query_pos[:, None]) | (picture[key_pos][None, :] == query_pic) & (query_pic >= 0)
        results.append(jax.checkpoint(attend)(queries[index * block:(index + 1) * block], keys[:reach], values[:reach], position_bias, bucket_index, allowed))
    return jnp.concatenate(results, 0)

def forward(embedding, attn_proj, out_proj, router, expert_in, expert_out, norm_gains, position_bias, token_ids, targets, lpos, weight, routes, picture_seq, buckets, perm, inverse):
    table = low(embedding)
    projection = low(attn_proj)
    output_map = low(out_proj)
    router_full = low(router)
    gain = low(norm_gains)
    stream_in = table[token_ids]
    normed_in = low(normed(stream_in, gain[0]))
    fresh = low_back(low(jnp.einsum('td,sde->ste', normed_in, projection, precision=HIGH)))
    seq_view = fresh[:, perm].reshape(3, SEQS, LENGTH, HEADS, HD)
    attended_seq = lax.map(lambda item: attend_sequence(item, position_bias, buckets), (seq_view[0], seq_view[1], seq_view[2], picture_seq))
    attended = attended_seq.reshape(SEQS * LENGTH, D)[inverse]
    attended_low = low_back(low(attended))
    stream_mid = stream_in + low_back(jnp.dot(attended_low, output_map, precision=HIGH))
    normed_mid = low(normed(stream_mid, gain[1]))
    router_logits = low_back(jnp.dot(normed_mid, router_full.T, precision=HIGH))
    gates = jax.nn.softmax(jnp.take_along_axis(router_logits, routes, 1), -1)
    slivers = 2 * N_TENSOR
    sliver_width = FF // slivers
    flat = routes.reshape(-1)
    order = jnp.argsort(flat, stable=True)
    owner = (jnp.arange(TOKENS * TOP, dtype=jnp.int32) // TOP)[order]
    sizes = lax.optimization_barrier(jnp.sum((flat[:, None] == jnp.arange(EXPERTS, dtype=jnp.int32)[None, :]).astype(jnp.int32), 0))
    rows_in = normed_mid[owner]
    weights_in = low(expert_in).reshape(D, EXPERTS, slivers, sliver_width)
    weights_out = low(expert_out).reshape(EXPERTS, slivers, sliver_width, D)
    produced = jnp.zeros((TOKENS * TOP, D), jnp.float32)
    for sliver in range(slivers):
        sliver_in = jnp.transpose(weights_in[:, :, sliver], (1, 0, 2))
        inner = low_back(lax.ragged_dot(low_back(rows_in), sliver_in, sizes, precision=HIGH))
        active = low(jax.nn.gelu(inner))
        produced = produced + low_back(low(lax.ragged_dot(active, weights_out[:, sliver], sizes, precision=HIGH)))
    routed = jnp.zeros_like(produced).at[order].set(produced)
    mixed = lax.optimization_barrier(jnp.sum(gates[..., None] * routed.reshape(TOKENS, TOP, D), 1))
    stream_out = stream_mid + mixed
    normed_out = low(normed(stream_out, gain[2]))
    logits = low_back(jnp.dot(normed_out[lpos], table.T, precision=HIGH))
    log_total = jax.nn.logsumexp(logits, -1)
    target_logit = jnp.take_along_axis(logits, targets[lpos][:, None], 1)[:, 0]
    per_row = log_total - (1 - SMOOTH) * target_logit - SMOOTH * lax.optimization_barrier(jnp.mean(logits, -1)) + ZLOSS * log_total * log_total
    return jnp.sum(weight * per_row)

def adam_update(weight, first, second, grad, rate, decay):
    first = BETA1 * first + (1 - BETA1) * grad
    second = BETA2 * second + (1 - BETA2) * grad * grad
    fixed_first = first / (1 - BETA1 ** STEP)
    fixed_second = second / (1 - BETA2 ** STEP)
    weight = weight - rate * (fixed_first / (jnp.sqrt(fixed_second) + ADAM_EPS) + decay * weight)
    return (weight, first, second)

def reference(token_ids, targets, loss_offsets, routes, picture_start, buckets, embedding, embedding_first, embedding_second, attn_proj, attn_proj_first, attn_proj_second, out_proj, out_proj_first, out_proj_second, router, router_first, router_second, expert_in, expert_in_first, expert_in_second, expert_out, expert_out_first, expert_out_second, norm_gains, norm_gains_first, norm_gains_second, position_bias, position_bias_first, position_bias_second):
    positions = jnp.arange(LENGTH, dtype=jnp.int32)
    picture_seq = jax.vmap(lambda starts: picture_of(positions, starts))(picture_start)
    place = jnp.arange(TOKENS, dtype=jnp.int32)
    block_of = place // TOK_DEV
    local = place % TOK_DEV
    inverse = (local // SUB * LENGTH + block_of * SUB + local % SUB).astype(jnp.int32)
    perm = jnp.zeros((TOKENS,), jnp.int32).at[inverse].set(place).reshape(SEQS, LENGTH)
    lpos = loss_offsets + jnp.arange(loss_offsets.shape[0], dtype=jnp.int32) // LPOS * TOK_DEV
    weight = (picture_seq.reshape(-1)[inverse[lpos]] < 0).astype(jnp.float32)
    params = (embedding, attn_proj, out_proj, router, expert_in, expert_out, norm_gains, position_bias)
    firsts = (embedding_first, attn_proj_first, out_proj_first, router_first, expert_in_first, expert_out_first, norm_gains_first, position_bias_first)
    seconds = (embedding_second, attn_proj_second, out_proj_second, router_second, expert_in_second, expert_out_second, norm_gains_second, position_bias_second)

    def loss_of(*weights):
        return forward(*weights, token_ids, targets, lpos, weight, routes, picture_seq, buckets, perm, inverse)
    loss_sum, pull = jax.vjp(loss_of, *params)
    grads = pull(jnp.ones_like(loss_sum))
    squares = jnp.sum(jnp.stack([jnp.sum(g * g) for g in grads]))
    grad_norm = jnp.sqrt(squares)
    clip = MAX_NORM / jnp.maximum(grad_norm, MAX_NORM)
    results = []
    for index in range(8):
        results.extend(adam_update(params[index], firsts[index], seconds[index], clip * grads[index], RATES[index], DECAYS[index]))
    return (results[0], results[1], results[2], results[3], results[4], results[5], results[6], results[7], results[8], results[9], results[10], results[11], results[12], results[13], results[14], results[15], results[16], results[17], results[18], results[19], results[20], results[21], results[22], results[23], grad_norm, loss_sum, jnp.sum(weight))
```

```python
import math

import jax
import jax.numpy as jnp
from jax import lax
from jax.sharding import PartitionSpec as P

HD = 64
VOCAB = 32000
PIECE = 256
SEQ = 4096
STEP = 10


SMOOTH = 0.1
ZLOSS = 0.0001
NORM_EPS = 1e-06
MAX_NORM = 1.0
BETA1 = 0.9
BETA2 = 0.95
ADAM_EPS = 1e-08
RATES = (0.04, 0.04, 1.0, 0.03, 0.07, 0.035, 1.0, 0.7)
DECAYS = (0.1, 0.1, 0.1, 0.1, 0.1, 0.1, 0.0, 0.0)
NEGATIVE = -1e30
HIGH = lax.Precision.HIGHEST


def merged(shard, axis, combine):
    everything = jax.tree.map(lambda part: lax.all_gather(part, axis), shard)
    initial = jax.tree.map(lambda part: part[0], everything)

    def lap(k, so_far):
        return combine(so_far, jax.tree.map(lambda part: part[k], everything))

    return lax.fori_loop(1, lax.axis_size(axis), lap, initial)


def normed(v, g):
    return v * lax.rsqrt(jnp.mean(v * v, -1, keepdims=True) + NORM_EPS) * g


def norm_back(v, g, upstream):
    unused, pull = jax.vjp(normed, v, g)
    return pull(upstream)


def picture_of(positions, starts, width):
    inside = (positions[:, None] >= starts[None, :]) & (
        positions[:, None] < starts[None, :] + width
    )
    number = jnp.arange(starts.shape[0], dtype=jnp.int32) + 1
    return jnp.sum(inside.astype(jnp.int32) * number[None, :], 1) - 1


def rel_window(relative, query_start, query_count, key_start, key_count, length):
    centre = query_start - key_start + length - 1
    window = lax.dynamic_slice_in_dim(
        relative, centre - key_count + 1, query_count + key_count - 1, 1
    )
    span = query_count + key_count
    wrapped = jnp.concatenate(
        [
            jnp.flip(window[:, :key_count], 1),
            jnp.zeros((window.shape[0], 1), window.dtype),
            jnp.flip(window[:, key_count:], 1),
        ],
        1,
    )
    tiled = jnp.tile(wrapped, (1, query_count))[:, : query_count * (span - 1)]
    return tiled.reshape(window.shape[0], query_count, span - 1)[:, :, :key_count]


def tensor_total(value):
    return lax.psum(value, "tensor")


def route_exchange(value):
    return lax.all_to_all(value, "dp", split_axis=0, concat_axis=0, tiled=True)


def combine_stats(left, right):
    peak = jnp.maximum(left[0], right[0])
    total = left[1] * jnp.exp(left[0] - peak) + right[1] * jnp.exp(right[0] - peak)
    return (peak, total, left[2] + right[2], left[3] + right[3])


def adam_update(weight, first, second, grad, rate, decay):
    first = BETA1 * first + (1 - BETA1) * grad
    second = BETA2 * second + (1 - BETA2) * grad * grad
    fixed_first = first / (1 - BETA1**STEP)
    fixed_second = second / (1 - BETA2**STEP)
    weight = weight - rate * (fixed_first / (jnp.sqrt(fixed_second) + ADAM_EPS) + decay * weight)
    return (weight, first, second)


def wide_norm_back(v, g, upstream):
    size = v.shape[-1]
    root = lax.rsqrt(jnp.mean(v * v, -1, keepdims=True) + NORM_EPS)
    scaled = g * upstream
    inner = jnp.sum(scaled * v, -1, keepdims=True)
    return (root * scaled - v * (root * root * root * inner / size), jnp.sum(upstream * v * root, 0))


def fast_local(
    token_ids,
    targets,
    loss_offsets,
    routes,
    picture_start,
    buckets,
    embedding,
    embedding_first,
    embedding_second,
    attn_proj,
    attn_proj_first,
    attn_proj_second,
    out_proj,
    out_proj_first,
    out_proj_second,
    router,
    router_first,
    router_second,
    expert_in,
    expert_in_first,
    expert_in_second,
    expert_out,
    expert_out_first,
    expert_out_second,
    norm_gains,
    norm_gains_first,
    norm_gains_second,
    position_bias,
    position_bias_first,
    position_bias_second,
):
    f32 = jnp.float32
    bf16 = jnp.bfloat16
    dp_count = lax.axis_size("dp")
    tensor_count = lax.axis_size("tensor")
    dp_place = lax.axis_index("dp")
    tensor_place = lax.axis_index("tensor")
    rows = token_ids.shape[0]
    every = rows * dp_count
    picks = loss_offsets.shape[0]
    all_picks = picks * dp_count
    scale = 1.0 / math.sqrt(HD)
    vocab_rows, columns = embedding.shape
    features = columns * dp_count
    width = attn_proj.shape[2]
    heads = width // HD
    experts = router.shape[0]
    both = ("dp", "tensor")
    loss_hot = loss_offsets[:, None] == jnp.arange(rows, dtype=jnp.int32)[None, :]

    def at_loss(values):
        return jnp.sum(jnp.where(loss_hot, values[None, :], 0), 1)

    packed = jnp.concatenate(
        [token_ids, loss_offsets, at_loss(targets), at_loss(routes[:, 0]), at_loss(routes[:, 1])]
    )
    known = lax.all_gather(packed, "dp")
    ids = known[:, :rows].reshape(every)
    offsets, wanted, route_a, route_b = (
        known[:, rows + k * picks : rows + (k + 1) * picks].reshape(all_picks) for k in range(4)
    )
    pick_block = jnp.arange(all_picks, dtype=jnp.int32) // picks
    loss_rows = offsets + pick_block * rows
    projection = lax.all_gather(attn_proj.astype(bf16), "dp", axis=1, tiled=True)
    output_map = lax.all_gather(
        lax.all_gather(out_proj.astype(bf16), "dp", axis=1, tiled=True),
        "tensor",
        axis=0,
        tiled=True,
    )
    router_full = lax.all_gather(router.astype(bf16), "dp", axis=1, tiled=True)
    gain = lax.all_gather(norm_gains.astype(bf16), "dp", axis=1, tiled=True).astype(f32)
    own_gain = norm_gains.astype(bf16).astype(f32)
    table_rows = lax.all_to_all(
        embedding.astype(bf16), "dp", split_axis=0, concat_axis=1, tiled=True
    )
    place = ids - tensor_place * vocab_rows
    owned = (place >= 0) & (place < vocab_rows)
    looked = jnp.take(embedding, jnp.clip(place, 0, vocab_rows - 1), axis=0)
    looked = jnp.where(owned[:, None], looked, 0.0).astype(bf16)
    stream_in = lax.psum(
        lax.all_to_all(looked, "dp", split_axis=0, concat_axis=1, tiled=True).astype(f32), "tensor"
    )
    in_columns = lax.psum(looked.astype(f32), "tensor")
    root_in = lax.rsqrt(jnp.mean(stream_in * stream_in, -1, keepdims=True) + NORM_EPS)
    normed_in = (stream_in * root_in * gain[0]).astype(bf16)
    fresh = jnp.einsum("td,sde->ste", normed_in, projection, preferred_element_type=f32).astype(
        bf16
    )
    loss_one = loss_hot.astype(bf16)
    own_query = jnp.dot(loss_one, fresh[0], preferred_element_type=f32).astype(bf16)
    own_stream = jnp.dot(
        loss_one, stream_in.astype(bf16), preferred_element_type=f32
    ).astype(bf16)
    keys, values, query, stream_picked, root_all = (
        lax.all_gather(part, "dp", axis=0, tiled=True)
        for part in (fresh[1], fresh[2], own_query, own_stream, root_in)
    )
    stream_picked = stream_picked.astype(f32)
    in_columns_normed = (in_columns * root_all * own_gain[0]).astype(bf16)
    flipped = jnp.pad(jnp.flip(buckets), (0, 1)).astype(bf16)
    period = 2 * every
    shifted = jnp.tile(flipped, rows + 1)[: rows * (period + 1)].reshape(rows, period + 1)
    shifted = shifted[:, : period - rows]
    turn = (rows - 1 - offsets)[:, None] == jnp.arange(rows, dtype=jnp.int32)[None, :]
    shifted = jnp.dot(turn.astype(bf16), shifted, preferred_element_type=f32)
    bucket = jnp.concatenate(
        [
            shifted[
                picks * k : picks * (k + 1),
                rows * (dp_count - 1 - k) : rows * (dp_count - 1 - k) + every,
            ]
            for k in range(dp_count)
        ]
    ).astype(jnp.int32)
    position = jnp.arange(every, dtype=jnp.int32)
    key_picture = picture_of(position, picture_start[0], PIECE)
    query_picture = picture_of(loss_rows, picture_start[0], PIECE)
    allowed = (position[None, :] <= loss_rows[:, None]) | (
        (key_picture[None, :] == query_picture[:, None]) & (query_picture[:, None] >= 0)
    )
    bucket_count = position_bias.shape[1]

    def head(value, h):
        return value[:, h * HD : (h + 1) * HD]

    def scores_of(h):
        raw = lax.dot_general(
            head(query, h), head(keys, h), (((1,), (1,)), ((), ())), preferred_element_type=f32
        )
        bias = jnp.zeros(bucket.shape, f32)
        for b in range(bucket_count):
            bias = jnp.where(bucket == b, position_bias[h, b], bias)
        return jnp.where(allowed, raw * scale + bias, NEGATIVE)

    probs = []
    for h in range(heads):
        raw = scores_of(h)
        terms = jnp.exp(raw - jnp.max(raw, -1, keepdims=True))
        probs.append(terms / jnp.sum(terms, -1, keepdims=True))
    attended = jnp.concatenate(
        [
            jnp.dot(probs[h].astype(bf16), head(values, h), preferred_element_type=f32)
            for h in range(heads)
        ],
        1,
    )
    attended_low = attended.astype(bf16)
    attended_all = lax.all_gather(attended_low, "tensor", axis=1, tiled=True)
    stream_mid = stream_picked + jnp.dot(attended_all, output_map, preferred_element_type=f32)
    normed_mid = normed(stream_mid, gain[1]).astype(bf16)
    router_logits = jnp.dot(normed_mid, router_full.T, preferred_element_type=f32)
    expert_ids = jnp.arange(experts, dtype=jnp.int32)[None, :]
    hot_a = route_a[:, None] == expert_ids
    hot_b = route_b[:, None] == expert_ids
    logit_a = jnp.sum(jnp.where(hot_a, router_logits, 0.0), 1)
    logit_b = jnp.sum(jnp.where(hot_b, router_logits, 0.0), 1)
    logit_top = jnp.maximum(logit_a, logit_b)
    gate_a, gate_b = jnp.exp(logit_a - logit_top), jnp.exp(logit_b - logit_top)
    gate_a, gate_b = gate_a / (gate_a + gate_b), gate_b / (gate_a + gate_b)
    spread = dp_count * tensor_count // experts
    expert = (dp_place * tensor_count + tensor_place) // spread
    gate = jnp.where(route_a == expert, gate_a, 0.0) + jnp.where(route_b == expert, gate_b, 0.0)
    in_low = expert_in.astype(bf16)
    out_low = expert_out.astype(bf16)
    inner = jnp.dot(normed_mid, in_low, preferred_element_type=f32)
    active = jax.nn.gelu(inner).astype(bf16)
    piece = jnp.dot(active, out_low, preferred_element_type=f32).astype(bf16).astype(f32)
    mixed = lax.psum(gate[:, None] * piece, both)
    stream_out = stream_mid + mixed
    normed_out = normed(stream_out, gain[2]).astype(bf16)
    logits = lax.dot_general(
        normed_out, table_rows, (((1,), (1,)), ((), ())), preferred_element_type=f32
    )
    share = table_rows.shape[0]
    first_id = tensor_place * vocab_rows + dp_place * share
    hit = jnp.arange(share, dtype=jnp.int32)[None, :] == (wanted - first_id)[:, None]
    local_top = jnp.max(logits, -1)
    stats = jnp.stack(
        [
            local_top,
            jnp.sum(jnp.exp(logits - local_top[:, None]), -1),
            jnp.sum(jnp.where(hit, logits, 0.0), -1),
            jnp.sum(logits, -1),
        ]
    )
    stats = lax.all_gather(stats, both)
    peak = jnp.max(stats[:, 0], 0)
    vocab_total = jnp.sum(stats[:, 1] * jnp.exp(stats[:, 0] - peak), 0)
    target_logit = jnp.sum(stats[:, 2], 0)
    logit_sum = jnp.sum(stats[:, 3], 0)
    loss_total = peak + jnp.log(vocab_total)
    weight = (query_picture < 0).astype(f32)
    per_row = (
        loss_total
        - (1 - SMOOTH) * target_logit
        - SMOOTH * logit_sum / VOCAB
        + ZLOSS * loss_total * loss_total
    )
    loss_sum = jnp.sum(weight * per_row)
    loss_count = jnp.sum(weight)
    soft = jnp.exp(logits - loss_total[:, None])
    d_logits = (
        weight[:, None]
        * (
            (1 + 2 * ZLOSS * loss_total)[:, None] * soft
            - (1 - SMOOTH) * hit.astype(f32)
            - SMOOTH / VOCAB
        )
    ).astype(bf16)
    d_logits_all = lax.all_gather(d_logits, "dp", axis=1, tiled=True)
    d_normed_out = lax.psum(jnp.dot(d_logits, table_rows, preferred_element_type=f32), both)
    d_stream_out, grad_final = wide_norm_back(stream_out, gain[2], d_normed_out)
    d_piece = (gate[:, None] * d_stream_out).astype(bf16)
    d_active = lax.dot_general(
        d_piece, out_low, (((1,), (1,)), ((), ())), preferred_element_type=f32
    )
    unused, gelu_pull = jax.vjp(jax.nn.gelu, inner)
    d_inner = gelu_pull(d_active)[0].astype(bf16)
    grad_out = jnp.dot(active.T, d_piece, preferred_element_type=f32)
    grad_in = jnp.dot(normed_mid.T, d_inner, preferred_element_type=f32)
    sent_back = lax.dot_general(
        d_inner, in_low, (((1,), (1,)), ((), ())), preferred_element_type=f32
    ).astype(bf16)
    gate_part = jnp.sum(d_stream_out * piece, -1)
    gate_part = jnp.where(expert_ids == expert, gate_part[:, None], 0.0)
    d_from_experts, d_gates = lax.psum((sent_back.astype(f32), gate_part), both)
    d_gate_a = jnp.sum(jnp.where(hot_a, d_gates, 0.0), 1)
    d_gate_b = jnp.sum(jnp.where(hot_b, d_gates, 0.0), 1)
    d_mean = gate_a * d_gate_a + gate_b * d_gate_b
    d_router_logits = (
        jnp.where(hot_a, (gate_a * (d_gate_a - d_mean))[:, None], 0.0)
        + jnp.where(hot_b, (gate_b * (d_gate_b - d_mean))[:, None], 0.0)
    ).astype(bf16)

    def own_columns(value):
        return lax.dynamic_slice_in_dim(value, dp_place * columns, columns, value.ndim - 1)

    grad_router = own_columns(
        jnp.dot(d_router_logits.T, normed_mid, preferred_element_type=f32)
    )
    d_normed_mid = d_from_experts + jnp.dot(
        d_router_logits, router_full, preferred_element_type=f32
    )
    d_from_mid, grad_middle = wide_norm_back(stream_mid, gain[1], d_normed_mid)
    d_stream_mid = d_stream_out + d_from_mid
    d_attn_low = d_stream_mid.astype(bf16)
    grad_output_map = jnp.dot(
        attended_low.T, own_columns(d_attn_low), preferred_element_type=f32
    )
    own_map = lax.dynamic_slice_in_dim(output_map, tensor_place * width, width, 0)
    d_attended = lax.dot_general(
        d_attn_low, own_map, (((1,), (1,)), ((), ())), preferred_element_type=f32
    ).astype(bf16)
    d_queries, d_keys, d_values, bias_terms = [], [], [], []
    for h in range(heads):
        d_head = head(d_attended, h)
        d_probs = lax.dot_general(
            d_head, head(values, h), (((1,), (1,)), ((), ())), preferred_element_type=f32
        )
        d_scores = probs[h] * (d_probs - jnp.sum(probs[h] * d_probs, -1, keepdims=True))
        d_scores = d_scores.astype(bf16)
        d_queries.append(
            jnp.dot(d_scores, head(keys, h), preferred_element_type=f32) * scale
        )
        d_keys.append(
            jnp.dot(d_scores.T, head(query, h), preferred_element_type=f32) * scale
        )
        d_values.append(
            jnp.dot(probs[h].astype(bf16).T, d_head, preferred_element_type=f32)
        )
        wide = d_scores.astype(f32)
        bias_terms.append(
            jnp.stack([jnp.sum(jnp.where(bucket == b, wide, 0.0)) for b in range(bucket_count)])
        )
    sum_bias = jnp.stack(bias_terms)
    d_query = jnp.concatenate(d_queries, 1).astype(bf16)
    d_key = jnp.concatenate(d_keys, 1).astype(bf16)
    d_value = jnp.concatenate(d_values, 1).astype(bf16)
    back_hot = (loss_rows[None, :] == position[:, None]).astype(bf16)
    in_picked = jnp.dot(
        back_hot.T, in_columns_normed, preferred_element_type=f32
    ).astype(bf16)
    sum_proj = jnp.stack(
        [
            jnp.dot(in_picked.T, d_query, preferred_element_type=f32),
            jnp.dot(in_columns_normed.T, d_key, preferred_element_type=f32),
            jnp.dot(in_columns_normed.T, d_value, preferred_element_type=f32),
        ]
    )
    d_query_all = jnp.dot(back_hot, d_query, preferred_element_type=f32).astype(bf16)
    query_all = jnp.dot(back_hot, query, preferred_element_type=f32)
    own_proj = attn_proj.astype(bf16)
    d_columns = sum(
        lax.dot_general(part, own_proj[s], (((1,), (1,)), ((), ())), preferred_element_type=f32)
        for s, part in enumerate((d_query_all, d_key, d_value))
    )
    d_inner_in = jnp.sum(
        d_query_all.astype(f32) * query_all
        + d_key.astype(f32) * keys.astype(f32)
        + d_value.astype(f32) * values.astype(f32),
        -1,
        keepdims=True,
    )
    d_columns, d_inner_in = lax.psum((d_columns, d_inner_in), "tensor")
    grad_first = jnp.sum(d_columns * in_columns * root_all, 0)
    own_stream_mid = own_columns(d_stream_mid)
    stream_high = own_stream_mid.astype(bf16)
    stream_low = (own_stream_mid - stream_high.astype(f32)).astype(bf16)
    d_stream_in = (
        root_all * own_gain[0] * d_columns
        - in_columns * (root_all * root_all * d_inner_in / features)
        + jnp.dot(back_hot, stream_high, preferred_element_type=f32)
        + jnp.dot(back_hot, stream_low, preferred_element_type=f32)
    )
    sum_table = lax.dot_general(
        d_logits_all, own_columns(normed_out), (((0,), (0,)), ((), ())), preferred_element_type=f32
    )
    d_high = d_stream_in.astype(bf16)
    d_low = (d_stream_in - d_high.astype(f32)).astype(bf16)
    id_hot = (jnp.arange(vocab_rows, dtype=jnp.int32)[:, None] == place[None, :]).astype(bf16)
    scattered = jnp.dot(
        id_hot, jnp.concatenate([d_high, d_low], 1), preferred_element_type=f32
    )
    sum_table = sum_table + scattered[:, :columns] + scattered[:, columns:]
    sum_router = grad_router
    sum_gains = jnp.stack([grad_first, own_columns(grad_middle), own_columns(grad_final)])
    squares = (
        jnp.sum(sum_table * sum_table)
        + jnp.sum(sum_proj * sum_proj)
        + jnp.sum(grad_output_map * grad_output_map)
        + jnp.sum(grad_in * grad_in)
        + jnp.sum(grad_out * grad_out)
        + (jnp.sum(sum_router * sum_router) + jnp.sum(sum_gains * sum_gains)) / tensor_count
        + jnp.sum(sum_bias * sum_bias) / dp_count
    )
    grad_norm = jnp.sqrt(lax.psum(squares, both))
    clip = MAX_NORM / jnp.maximum(grad_norm, MAX_NORM)
    params = (
        embedding,
        attn_proj,
        out_proj,
        router,
        expert_in,
        expert_out,
        norm_gains,
        position_bias,
    )
    firsts = (
        embedding_first,
        attn_proj_first,
        out_proj_first,
        router_first,
        expert_in_first,
        expert_out_first,
        norm_gains_first,
        position_bias_first,
    )
    seconds = (
        embedding_second,
        attn_proj_second,
        out_proj_second,
        router_second,
        expert_in_second,
        expert_out_second,
        norm_gains_second,
        position_bias_second,
    )
    grads = (
        sum_table,
        sum_proj,
        grad_output_map,
        sum_router,
        grad_in,
        grad_out,
        sum_gains,
        sum_bias,
    )
    results = []
    for index in range(8):
        results.extend(
            adam_update(
                params[index],
                firsts[index],
                seconds[index],
                clip * grads[index],
                RATES[index],
                DECAYS[index],
            )
        )
    return (
        results[0],
        results[1],
        results[2],
        results[3],
        results[4],
        results[5],
        results[6],
        results[7],
        results[8],
        results[9],
        results[10],
        results[11],
        results[12],
        results[13],
        results[14],
        results[15],
        results[16],
        results[17],
        results[18],
        results[19],
        results[20],
        results[21],
        results[22],
        results[23],
        grad_norm,
        loss_sum,
        loss_count,
    )


def local(
    token_ids,
    targets,
    loss_offsets,
    routes,
    picture_start,
    buckets,
    embedding,
    embedding_first,
    embedding_second,
    attn_proj,
    attn_proj_first,
    attn_proj_second,
    out_proj,
    out_proj_first,
    out_proj_second,
    router,
    router_first,
    router_second,
    expert_in,
    expert_in_first,
    expert_in_second,
    expert_out,
    expert_out_first,
    expert_out_second,
    norm_gains,
    norm_gains_first,
    norm_gains_second,
    position_bias,
    position_bias_first,
    position_bias_second,
):
    f32 = jnp.float32
    bf16 = jnp.bfloat16
    dp_count = lax.axis_size("dp")
    tensor_count = lax.axis_size("tensor")
    dp_place = lax.axis_index("dp")
    tensor_place = lax.axis_index("tensor")
    rows = token_ids.shape[0]
    every = rows * dp_count
    length = min(SEQ, every)
    seqs = every // length
    sub = rows // seqs
    scale = 1.0 / math.sqrt(HD)
    vocab_rows = embedding.shape[0]
    table, projection, output_map, router_full, gain_full = (
        lax.all_gather(embedding.astype(bf16), "dp", axis=1, tiled=True),
        lax.all_gather(attn_proj.astype(bf16), "dp", axis=1, tiled=True),
        lax.all_gather(out_proj.astype(bf16), "dp", axis=1, tiled=True),
        lax.all_gather(router.astype(bf16), "dp", axis=1, tiled=True),
        lax.all_gather(norm_gains.astype(bf16), "dp", axis=1, tiled=True),
    )
    gain = gain_full.astype(f32)
    features = table.shape[1]
    offset = token_ids - tensor_place * vocab_rows
    owned = (offset >= 0) & (offset < vocab_rows)
    offset = jnp.clip(offset, 0, vocab_rows - 1)
    looked = jnp.take(table, offset, axis=0).astype(f32)
    stream_in = tensor_total(jnp.where(owned[:, None], looked, 0.0))
    pos_here = dp_place * sub + jnp.arange(sub, dtype=jnp.int32)
    seq_positions = jnp.arange(length, dtype=jnp.int32)
    picture_all = jax.vmap(lambda starts: picture_of(seq_positions, starts, PIECE))(picture_start)
    picture_here = lax.dynamic_slice_in_dim(picture_all, dp_place * sub, sub, 1)
    bucket_ids = jnp.arange(position_bias.shape[1], dtype=jnp.int32)
    bucket_hot = (bucket_ids[:, None] == buckets[None, :]).astype(f32)
    relative = jnp.dot(position_bias, bucket_hot, precision=HIGH)
    normed_in = normed(stream_in, gain[0]).astype(bf16)
    fresh = jnp.einsum("td,sde->ste", normed_in, projection, preferred_element_type=f32).astype(
        bf16
    )
    width = fresh.shape[2]
    heads = width // HD
    keys_local = fresh[1].reshape(seqs, sub, width)
    values_local = fresh[2].reshape(seqs, sub, width)
    query_heads = fresh[0].reshape(seqs, sub, heads, HD)
    keys_all, values_all = (
        lax.all_gather(keys_local, "dp", axis=1, tiled=True),
        lax.all_gather(values_local, "dp", axis=1, tiled=True),
    )
    block = min(512, length)
    blocks = length // block
    block_ids = jnp.arange(blocks, dtype=jnp.int32)

    def pair_scores(q_heads, q_pos, q_pic, k_heads, k_pos, k_pic, bias):
        raw = (
            jnp.einsum("sqhd,skhd->shqk", q_heads, k_heads, preferred_element_type=f32) * scale
            + bias[None]
        )
        allowed = (k_pos[None, :] <= q_pos[:, None])[None] | (
            k_pic[:, None, :] == q_pic[:, :, None]
        ) & (q_pic[:, :, None] >= 0)
        return jnp.where(allowed[:, None], raw, NEGATIVE)

    def key_slice(source, start):
        return lax.dynamic_slice_in_dim(source, start, block, 1).reshape(seqs, block, heads, HD)

    def own_bias(start):
        return rel_window(relative, dp_place * sub, sub, start, block, length)

    def fwd_scores(index, key_source):
        start = index * block
        key_pos = start + jnp.arange(block, dtype=jnp.int32)
        return pair_scores(
            query_heads,
            pos_here,
            picture_here,
            key_slice(key_source, start),
            key_pos,
            lax.dynamic_slice_in_dim(picture_all, start, block, 1),
            own_bias(start),
        )

    def max_step(carry, index):
        top, total = carry
        s = fwd_scores(index, keys_all)
        new_top = jnp.maximum(top, jnp.max(s, -1))
        terms = jnp.where(s > 0.5 * NEGATIVE, jnp.exp(s - new_top[..., None]), 0.0)
        total = total * jnp.exp(top - new_top) + jnp.sum(terms, -1)
        return ((new_top, total), None)

    start_top = jnp.full((seqs, heads, sub), NEGATIVE, f32)
    (top, total), unused = lax.scan(
        max_step, (start_top, jnp.zeros((seqs, heads, sub), f32)), block_ids
    )
    log_total = top + jnp.log(total)

    def out_step(accum, index):
        s = fwd_scores(index, keys_all)
        probs = jnp.exp(s - log_total[..., None]).astype(bf16)
        value_heads = key_slice(values_all, index * block)
        return (
            accum + jnp.einsum("shqk,skhd->sqhd", probs, value_heads, preferred_element_type=f32),
            None,
        )

    attended, unused = lax.scan(out_step, jnp.zeros((seqs, sub, heads, HD), f32), block_ids)
    attended_low = attended.reshape(rows, width).astype(bf16)
    stream_mid = stream_in + tensor_total(
        jnp.dot(attended_low, output_map, preferred_element_type=f32)
    )
    normed_mid = normed(stream_mid, gain[1]).astype(bf16)
    router_logits = jnp.dot(normed_mid, router_full.T, preferred_element_type=f32)
    gates = jax.nn.softmax(jnp.take_along_axis(router_logits, routes, 1), -1)
    experts = router_full.shape[0]
    top_k = routes.shape[1]
    capacity = 2 * rows * top_k // experts
    flat = routes.reshape(-1)
    owner = jnp.arange(rows * top_k, dtype=jnp.int32) // top_k
    hits = (flat[:, None] == jnp.arange(experts, dtype=jnp.int32)[None, :]).astype(jnp.int32)
    slot = jnp.sum(jnp.cumsum(hits, 0) * hits, 1) - 1
    first_row = 2 * flat * capacity + slot

    def pack(values):
        buffer = jnp.zeros((experts, capacity, features), bf16).at[flat, slot].set(values)
        return jnp.repeat(buffer, 2, axis=0).reshape(2 * experts * capacity, features)

    def unpack(values):
        return values[first_row].astype(f32) + values[first_row + capacity].astype(f32)

    in_low = expert_in.astype(bf16)
    out_low = expert_out.astype(bf16)
    arrived = route_exchange(pack(normed_mid[owner]))
    inner = jnp.dot(arrived, in_low, preferred_element_type=f32)
    active = jax.nn.gelu(inner).astype(bf16)
    produced = jnp.dot(active, out_low, preferred_element_type=f32).astype(bf16)
    returned = unpack(route_exchange(produced))
    mixed = jnp.sum((gates.reshape(-1)[:, None] * returned).reshape(rows, top_k, features), 1)
    stream_out = stream_mid + tensor_total(mixed)
    normed_out = normed(stream_out, gain[2]).astype(bf16)
    picked = normed_out[loss_offsets]
    logits = jnp.dot(picked, table.T, preferred_element_type=f32)
    wanted = targets[loss_offsets] - tensor_place * vocab_rows
    hit = jnp.arange(vocab_rows, dtype=jnp.int32)[None, :] == wanted[:, None]
    local_top = jnp.max(logits, -1)
    stats = (
        local_top,
        jnp.sum(jnp.exp(logits - local_top[:, None]), -1),
        jnp.sum(jnp.where(hit, logits, 0.0), -1),
        jnp.sum(logits, -1),
    )
    peak, vocab_total, target_logit, logit_sum = merged(stats, "tensor", combine_stats)
    loss_total = peak + jnp.log(vocab_total)
    weight = (picture_here.reshape(rows)[loss_offsets] < 0).astype(f32)
    per_row = (
        loss_total
        - (1 - SMOOTH) * target_logit
        - SMOOTH * logit_sum / VOCAB
        + ZLOSS * loss_total * loss_total
    )
    loss_local = jnp.sum(weight * per_row)
    soft = jnp.exp(logits - loss_total[:, None])
    d_logits = (
        weight[:, None]
        * (
            (1 + 2 * ZLOSS * loss_total)[:, None] * soft
            - (1 - SMOOTH) * hit.astype(f32)
            - SMOOTH / VOCAB
        )
    ).astype(bf16)
    d_picked = jnp.dot(d_logits, table, preferred_element_type=f32)
    grad_table = jnp.dot(d_logits.T, picked, preferred_element_type=f32)
    d_normed_out = tensor_total(jnp.zeros((rows, features), f32).at[loss_offsets].add(d_picked))
    d_stream_out, grad_final = norm_back(stream_out, gain[2], d_normed_out)
    d_piece = (gates.reshape(-1)[:, None] * d_stream_out[owner]).astype(bf16)
    d_arrived = route_exchange(pack(d_piece))
    d_active = jnp.dot(d_arrived, out_low.T, preferred_element_type=f32)
    unused, gelu_pull = jax.vjp(jax.nn.gelu, inner)
    d_inner = gelu_pull(d_active)[0].astype(bf16)
    grad_out = jnp.dot(active.T, d_arrived, preferred_element_type=f32)
    grad_in = jnp.dot(arrived.T, d_inner, preferred_element_type=f32)
    sent_back = jnp.dot(d_inner, in_low.T, preferred_element_type=f32).astype(bf16)
    d_routes = unpack(route_exchange(sent_back))
    gate_part = jnp.sum(d_stream_out[owner] * returned, -1).reshape(rows, top_k)
    route_part = jnp.sum(d_routes.reshape(rows, top_k, features), 1)
    d_from_experts, d_gates = tensor_total((route_part, gate_part))
    d_chosen = gates * (d_gates - jnp.sum(gates * d_gates, -1, keepdims=True))
    expert_hot = (routes[..., None] == jnp.arange(experts, dtype=jnp.int32)).astype(f32)
    d_router_logits = jnp.sum(expert_hot * d_chosen[..., None], 1).astype(bf16)
    grad_router = jnp.dot(d_router_logits.T, normed_mid, preferred_element_type=f32)
    d_normed_mid = d_from_experts + jnp.dot(
        d_router_logits, router_full, preferred_element_type=f32
    )
    d_from_mid, grad_middle = norm_back(stream_mid, gain[1], d_normed_mid)
    d_stream_mid = d_stream_out + d_from_mid
    d_attn_low = d_stream_mid.astype(bf16)
    grad_output_map = jnp.dot(attended_low.T, d_attn_low, preferred_element_type=f32)
    d_attended = jnp.dot(d_attn_low, output_map.T, preferred_element_type=f32).astype(bf16)
    d_heads = d_attended.reshape(seqs, sub, heads, HD)
    delta = jnp.moveaxis(jnp.sum(d_heads.astype(f32) * attended, -1), 2, 1)
    key_source, value_source = (
        lax.all_gather(keys_local, "dp", axis=1, tiled=True),
        lax.all_gather(values_local, "dp", axis=1, tiled=True),
    )

    def score_grads(
        q_heads, q_pos, q_pic, k_heads, k_pos, k_pic, bias, totals, deltas, dq_heads, v_heads
    ):
        s = pair_scores(q_heads, q_pos, q_pic, k_heads, k_pos, k_pic, bias)
        probs = jnp.exp(s - totals[..., None])
        d_probs = jnp.einsum("sqhd,skhd->shqk", dq_heads, v_heads, preferred_element_type=f32)
        d_scores = (probs * (d_probs - deltas[..., None])).astype(bf16)
        return (probs, d_scores)

    def key_step(carry, index):
        d_query, d_rel = carry
        start = index * block
        key_pos = start + jnp.arange(block, dtype=jnp.int32)
        key_heads = key_slice(key_source, start)
        value_heads = key_slice(value_source, start)
        bias, bias_pull = jax.vjp(
            lambda table_rel: rel_window(table_rel, dp_place * sub, sub, start, block, length),
            relative,
        )
        probs, d_scores = score_grads(
            query_heads,
            pos_here,
            picture_here,
            key_heads,
            key_pos,
            lax.dynamic_slice_in_dim(picture_all, start, block, 1),
            bias,
            log_total,
            delta,
            d_heads,
            value_heads,
        )
        d_query = (
            d_query
            + jnp.einsum("shqk,skhd->sqhd", d_scores, key_heads, preferred_element_type=f32) * scale
        )
        d_rel = d_rel + bias_pull(jnp.sum(d_scores.astype(f32), 0))[0]
        d_key = (
            jnp.einsum("shqk,sqhd->skhd", d_scores, query_heads, preferred_element_type=f32) * scale
        )
        d_value = jnp.einsum(
            "shqk,sqhd->skhd", probs.astype(bf16), d_heads, preferred_element_type=f32
        )
        joined = jnp.concatenate(
            [d_key.reshape(seqs, block, width), d_value.reshape(seqs, block, width)], 2
        )
        return ((d_query, d_rel), joined)

    start_carry = (jnp.zeros((seqs, sub, heads, HD), f32), jnp.zeros(relative.shape, f32))
    (d_query, d_rel), key_terms = lax.scan(key_step, start_carry, block_ids)
    d_bias = jnp.dot(d_rel, bucket_hot.T, precision=HIGH)
    ordered = jnp.moveaxis(key_terms, 0, 1).reshape(seqs, length, 2 * width)
    key_grads = lax.psum_scatter(ordered, "dp", scatter_dimension=1, tiled=True).reshape(
        rows, 2 * width
    )
    d_fresh = jnp.stack(
        [d_query.reshape(rows, width), key_grads[:, :width], key_grads[:, width:]]
    ).astype(bf16)
    grad_proj = jnp.einsum("td,ste->sde", normed_in, d_fresh, preferred_element_type=f32)
    d_normed_in = tensor_total(
        jnp.einsum("ste,sde->td", d_fresh, projection, preferred_element_type=f32)
    )
    d_from_in, grad_first = norm_back(stream_in, gain[0], d_normed_in)
    d_stream_in = d_stream_mid + d_from_in
    grad_table = grad_table + jnp.zeros((vocab_rows, features), f32).at[offset].add(
        jnp.where(owned[:, None], d_stream_in, 0.0)
    )
    sum_table, sum_proj, sum_output, sum_router, sum_gains = (
        lax.psum_scatter(grad_table, "dp", scatter_dimension=1, tiled=True),
        lax.psum_scatter(grad_proj, "dp", scatter_dimension=1, tiled=True),
        lax.psum_scatter(grad_output_map, "dp", scatter_dimension=1, tiled=True),
        lax.psum_scatter(grad_router, "dp", scatter_dimension=1, tiled=True),
        lax.psum_scatter(
            jnp.stack([grad_first, grad_middle, grad_final]), "dp", scatter_dimension=1, tiled=True
        ),
    )
    sum_bias = lax.psum(d_bias, "dp")
    squares = (
        jnp.sum(sum_table * sum_table)
        + jnp.sum(sum_proj * sum_proj)
        + jnp.sum(sum_output * sum_output)
        + jnp.sum(grad_in * grad_in)
        + jnp.sum(grad_out * grad_out)
        + (jnp.sum(sum_router * sum_router) + jnp.sum(sum_gains * sum_gains)) / tensor_count
        + jnp.sum(sum_bias * sum_bias) / dp_count
    )
    total_squares, loss_sum, loss_count = lax.psum(
        (squares, loss_local / tensor_count, jnp.sum(weight) / tensor_count), ("dp", "tensor")
    )
    grad_norm = jnp.sqrt(total_squares)
    clip = MAX_NORM / jnp.maximum(grad_norm, MAX_NORM)
    params = (
        embedding,
        attn_proj,
        out_proj,
        router,
        expert_in,
        expert_out,
        norm_gains,
        position_bias,
    )
    firsts = (
        embedding_first,
        attn_proj_first,
        out_proj_first,
        router_first,
        expert_in_first,
        expert_out_first,
        norm_gains_first,
        position_bias_first,
    )
    seconds = (
        embedding_second,
        attn_proj_second,
        out_proj_second,
        router_second,
        expert_in_second,
        expert_out_second,
        norm_gains_second,
        position_bias_second,
    )
    grads = (sum_table, sum_proj, sum_output, sum_router, grad_in, grad_out, sum_gains, sum_bias)
    results = []
    for index in range(8):
        results.extend(
            adam_update(
                params[index],
                firsts[index],
                seconds[index],
                clip * grads[index],
                RATES[index],
                DECAYS[index],
            )
        )
    return (
        results[0],
        results[1],
        results[2],
        results[3],
        results[4],
        results[5],
        results[6],
        results[7],
        results[8],
        results[9],
        results[10],
        results[11],
        results[12],
        results[13],
        results[14],
        results[15],
        results[16],
        results[17],
        results[18],
        results[19],
        results[20],
        results[21],
        results[22],
        results[23],
        grad_norm,
        loss_sum,
        loss_count,
    )


def solution(mesh):
    in_specs = (
        P("dp"),
        P("dp"),
        P("dp"),
        P("dp", None),
        P(),
        P(),
        P("tensor", "dp"),
        P("tensor", "dp"),
        P("tensor", "dp"),
        P(None, "dp", "tensor"),
        P(None, "dp", "tensor"),
        P(None, "dp", "tensor"),
        P("tensor", "dp"),
        P("tensor", "dp"),
        P("tensor", "dp"),
        P(None, "dp"),
        P(None, "dp"),
        P(None, "dp"),
        P(None, ("dp", "tensor")),
        P(None, ("dp", "tensor")),
        P(None, ("dp", "tensor")),
        P(("dp", "tensor"), None),
        P(("dp", "tensor"), None),
        P(("dp", "tensor"), None),
        P(None, "dp"),
        P(None, "dp"),
        P(None, "dp"),
        P("tensor", None),
        P("tensor", None),
        P("tensor", None),
    )
    out_specs = (
        P("tensor", "dp"),
        P("tensor", "dp"),
        P("tensor", "dp"),
        P(None, "dp", "tensor"),
        P(None, "dp", "tensor"),
        P(None, "dp", "tensor"),
        P("tensor", "dp"),
        P("tensor", "dp"),
        P("tensor", "dp"),
        P(None, "dp"),
        P(None, "dp"),
        P(None, "dp"),
        P(None, ("dp", "tensor")),
        P(None, ("dp", "tensor")),
        P(None, ("dp", "tensor")),
        P(("dp", "tensor"), None),
        P(("dp", "tensor"), None),
        P(("dp", "tensor"), None),
        P(None, "dp"),
        P(None, "dp"),
        P(None, "dp"),
        P("tensor", None),
        P("tensor", None),
        P("tensor", None),
        P(),
        P(),
        P(),
    )

    def chosen(*arrays):
        token_ids, routes, embedding, router = arrays[0], arrays[3], arrays[6], arrays[9 + 6]
        rows = token_ids.shape[0]
        dp_count, tensor_count = lax.axis_size("dp"), lax.axis_size("tensor")
        single = rows * dp_count <= SEQ and arrays[4].shape[0] == 1
        even = embedding.shape[0] % dp_count == 0
        whole = dp_count * tensor_count % router.shape[0] == 0 and routes.shape[1] == 2
        return (fast_local if single and even and whole else local)(*arrays)

    return jax.shard_map(chosen, mesh=mesh, in_specs=in_specs, out_specs=out_specs, check_vma=False)
```

```python
import functools
import math

import jax
import jax.numpy as jnp
from jax.experimental import pallas as pl
from jax.experimental.pallas import tpu as pltpu
from jax import lax
from jax.sharding import PartitionSpec as P

HD = 64
VOCAB = 32000
PIECE = 256
SEQ = 4096
STEP = 10


SMOOTH = 0.1
ZLOSS = 0.0001
NORM_EPS = 1e-06
MAX_NORM = 1.0
BETA1 = 0.9
BETA2 = 0.95
ADAM_EPS = 1e-08
RATES = (0.04, 0.04, 1.0, 0.03, 0.07, 0.035, 1.0, 0.7)
DECAYS = (0.1, 0.1, 0.1, 0.1, 0.1, 0.1, 0.0, 0.0)
NEGATIVE = -1e30
HIGH = lax.Precision.HIGHEST


def merged(shard, axis, combine):
    everything = jax.tree.map(lambda part: lax.all_gather(part, axis), shard)
    initial = jax.tree.map(lambda part: part[0], everything)

    def lap(k, so_far):
        return combine(so_far, jax.tree.map(lambda part: part[k], everything))

    return lax.fori_loop(1, lax.axis_size(axis), lap, initial)


def normed(v, g):
    return v * lax.rsqrt(jnp.mean(v * v, -1, keepdims=True) + NORM_EPS) * g


def norm_back(v, g, upstream):
    unused, pull = jax.vjp(normed, v, g)
    return pull(upstream)


def picture_of(positions, starts, width):
    inside = (positions[:, None] >= starts[None, :]) & (
        positions[:, None] < starts[None, :] + width
    )
    number = jnp.arange(starts.shape[0], dtype=jnp.int32) + 1
    return jnp.sum(inside.astype(jnp.int32) * number[None, :], 1) - 1


def rel_window(relative, query_start, query_count, key_start, key_count, length):
    centre = query_start - key_start + length - 1
    window = lax.dynamic_slice_in_dim(
        relative, centre - key_count + 1, query_count + key_count - 1, 1
    )
    span = query_count + key_count
    wrapped = jnp.concatenate(
        [
            jnp.flip(window[:, :key_count], 1),
            jnp.zeros((window.shape[0], 1), window.dtype),
            jnp.flip(window[:, key_count:], 1),
        ],
        1,
    )
    tiled = jnp.tile(wrapped, (1, query_count))[:, : query_count * (span - 1)]
    return tiled.reshape(window.shape[0], query_count, span - 1)[:, :, :key_count]


def tensor_total(value):
    return lax.psum(value, "tensor")


def route_exchange(value):
    return lax.all_to_all(value, "dp", split_axis=0, concat_axis=0, tiled=True)


def combine_stats(left, right):
    peak = jnp.maximum(left[0], right[0])
    total = left[1] * jnp.exp(left[0] - peak) + right[1] * jnp.exp(right[0] - peak)
    return (peak, total, left[2] + right[2], left[3] + right[3])


def adam_update(weight, first, second, grad, rate, decay):
    first = BETA1 * first + (1 - BETA1) * grad
    second = BETA2 * second + (1 - BETA2) * grad * grad
    fixed_first = first / (1 - BETA1**STEP)
    fixed_second = second / (1 - BETA2**STEP)
    weight = weight - rate * (fixed_first / (jnp.sqrt(fixed_second) + ADAM_EPS) + decay * weight)
    return (weight, first, second)


MESH = pl.DeviceIdType.MESH
VMEM_BYTES = 48 * 1024 * 1024
WHOLE = pl.BlockSpec(memory_space=pltpu.VMEM)
DMA = pltpu.SemaphoreType.DMA
F32 = jnp.float32
BF16 = jnp.bfloat16


def greet(axes):
    barrier = pltpu.get_barrier_semaphore()
    total = 0
    for axis in axes:
        count, here = lax.axis_size(axis), lax.axis_index(axis)
        for step in range(1, count):
            pl.semaphore_signal(
                barrier, inc=1, device_id={axis: lax.rem(here + step, count)}, device_id_type=MESH
            )
        total += count - 1
    return barrier, total


def met(greeting):
    pl.semaphore_wait(*greeting)


class Exchange:
    def __init__(self, axis, source, dest, sems):
        self.axis, self.count, self.here = axis, lax.axis_size(axis), lax.axis_index(axis)
        self.source, self.dest, self.sems = source, dest, sems

    def copy(self, step):
        target = lax.rem(self.here + step, self.count)
        return pltpu.make_async_remote_copy(
            src_ref=self.source(target),
            dst_ref=self.dest.at[self.here],
            send_sem=self.sems.at[0, step],
            recv_sem=self.sems.at[1, step],
            device_id={self.axis: target},
            device_id_type=MESH,
        )

    def start(self):
        for step in range(1, self.count):
            self.copy(step).start()
        return self

    def arrive(self):
        for step in range(1, self.count):
            self.copy(step).wait_recv()

    def finish(self):
        for step in range(1, self.count):
            self.copy(step).wait_send()


def scatter_rows(axis, source, dest, sems):
    count = dest.shape[0]
    height = dest.shape[1]
    return Exchange(
        axis,
        lambda target: source.at[pl.ds(pl.multiple_of(target * height, height), height)],
        dest,
        sems,
    ).start()


def share_block(axis, dest, sems):
    here = lax.axis_index(axis)
    return Exchange(axis, lambda target: dest.at[here], dest, sems).start()


def sems_of(axis_size):
    return DMA((2, axis_size))


def gather_kernel(axis, count, *refs):
    parts, outs, own, sems = refs[:count], refs[count : 2 * count], refs[-2], refs[-1]
    greeting = greet((axis,))
    here = lax.axis_index(axis)
    mine = [
        pltpu.make_async_copy(part, out.at[here], own.at[k])
        for k, (part, out) in enumerate(zip(parts, outs))
    ]
    for copy in mine:
        copy.start()
    met(greeting)
    moves = [
        Exchange(axis, lambda target, part=part: part, out, sems.at[k]).start()
        for k, (part, out) in enumerate(zip(parts, outs))
    ]
    for move in moves:
        move.arrive()
    for copy in mine:
        copy.wait()
    for move in moves:
        move.finish()


def gather_blocks(parts, axis, number, name):
    size = lax.axis_size(axis)
    count = len(parts)
    return pl.pallas_call(
        functools.partial(gather_kernel, axis, count),
        out_shape=[jax.ShapeDtypeStruct((size,) + p.shape, p.dtype) for p in parts],
        in_specs=[WHOLE] * count,
        out_specs=[WHOLE] * count,
        scratch_shapes=[DMA((count,)), DMA((count, 2, size))],
        compiler_params=pltpu.CompilerParams(
            collective_id=number, has_side_effects=True, vmem_limit_bytes=VMEM_BYTES
        ),
        name=name,
    )(*parts)


def lookup_kernel(looked, rows_out, columns_out, first, second, sems_a, sems_b, sems_c, sems_d):
    greeting = greet(("tensor", "dp"))
    here, block = lax.axis_index("tensor"), lax.axis_index("dp")
    met(greeting)
    split = Exchange("tensor", lambda target: looked.at[target], first, sems_a).start()
    first[here] = looked[here]
    split.arrive()
    total = first[0].astype(F32)
    for k in range(1, first.shape[0]):
        total = total + first[k].astype(F32)
    columns_out[here] = total.astype(BF16)
    to_rows = Exchange("dp", lambda target: columns_out.at[here, target], second, sems_b).start()
    to_columns = share_block("tensor", columns_out, sems_c)
    second[block] = columns_out[here, block]
    to_rows.arrive()
    rows_out[here] = second[...]
    to_all = share_block("tensor", rows_out, sems_d)
    to_all.arrive()
    to_columns.arrive()
    for move in (split, to_rows, to_columns, to_all):
        move.finish()


def exchange_lookups(looked):
    tensor, blocks, part, columns = looked.shape
    shape = jax.ShapeDtypeStruct(looked.shape, BF16)
    return pl.pallas_call(
        lookup_kernel,
        out_shape=[shape, shape],
        in_specs=[WHOLE],
        out_specs=[WHOLE] * 2,
        scratch_shapes=[
            pltpu.VMEM((tensor, blocks, part, columns), BF16),
            pltpu.VMEM((blocks, part, columns), BF16),
            sems_of(tensor),
            sems_of(blocks),
            sems_of(tensor),
            sems_of(tensor),
        ],
        compiler_params=pltpu.CompilerParams(
            collective_id=2, has_side_effects=True, vmem_limit_bytes=VMEM_BYTES
        ),
        name="exchange_lookups",
    )(looked)


def dot_nt(a, b):
    return lax.dot_general(a, b, (((1,), (1,)), ((), ())), preferred_element_type=F32)


def dot_nn(a, b):
    return jnp.dot(a, b, preferred_element_type=F32)


def root_of(v):
    return lax.rsqrt(jnp.mean(v * v, -1, keepdims=True) + NORM_EPS)


def gelu_parts(x):
    slope = math.sqrt(2.0 / math.pi)
    t = jnp.tanh(slope * (x + 0.044715 * (x * x * x)))
    value = 0.5 * x * (1.0 + t)
    grad = 0.5 * (1.0 + t) + 0.5 * x * (1.0 - t * t) * (slope * (1.0 + 3 * 0.044715 * x * x))
    return value, grad


def lanes(shape):
    return lax.broadcasted_iota(jnp.int32, shape, len(shape) - 1)


def own_rows(count):
    here = lax.axis_index("dp")
    return pl.ds(pl.multiple_of(here * count, count), count)


def tensor_sum(total, buffer, sems):
    here = lax.axis_index("tensor")
    buffer[here] = total
    move = share_block("tensor", buffer, sems)
    move.arrive()
    total = buffer[0]
    for k in range(1, buffer.shape[0]):
        total = total + buffer[k]
    return total, move


def experts_kernel(
    experts,
    attended,
    stream,
    output_map,
    router,
    gains,
    routes,
    expert_in,
    expert_out,
    normed_out,
    normed_mid_out,
    stream_mid_own,
    stream_out_own,
    gates_out,
    inner_out,
    active_out,
    piece_out,
    heads,
    stream_mid,
    arrived,
    summed,
    sems_a,
    sems_b,
    sems_c,
    sems_d,
):
    greeting = greet(("tensor", "dp"))
    block, here = lax.axis_index("dp"), lax.axis_index("tensor")
    blocks, picks = arrived.shape[0], arrived.shape[1]
    width = attended.shape[1]
    heads[here] = attended[...]
    met(greeting)
    to_heads = share_block("tensor", heads, sems_a)
    to_heads.arrive()
    middle = stream[...].astype(F32)
    for k in range(heads.shape[0]):
        middle = middle + dot_nn(heads[k], output_map[pl.ds(k * width, width), :])
    stream_mid[...] = middle
    stream_mid_own[...] = stream_mid[own_rows(picks), :]
    normed_mid = (middle * root_of(middle) * gains[1:2, :]).astype(BF16)
    normed_mid_out[...] = normed_mid
    inner = dot_nn(normed_mid, expert_in[...].astype(BF16))
    active = gelu_parts(inner)[0].astype(BF16)
    piece_out[...] = dot_nn(active, expert_out[...].astype(BF16)).astype(BF16)
    to_owner = scatter_rows("dp", piece_out, arrived, sems_b)
    inner_out[...] = inner
    active_out[...] = active
    router_logits = dot_nt(normed_mid, router[...])
    lane = lanes(router_logits.shape)
    hot_a = lane == routes[:, 0:1]
    hot_b = lane == routes[:, 1:2]
    logit_a = jnp.sum(jnp.where(hot_a, router_logits, 0.0), 1, keepdims=True)
    logit_b = jnp.sum(jnp.where(hot_b, router_logits, 0.0), 1, keepdims=True)
    logit_top = jnp.maximum(logit_a, logit_b)
    gate_a, gate_b = jnp.exp(logit_a - logit_top), jnp.exp(logit_b - logit_top)
    both = gate_a + gate_b
    gates_out[...] = jnp.where(hot_a, gate_a / both, 0.0) + jnp.where(hot_b, gate_b / both, 0.0)
    arrived[block] = piece_out[own_rows(picks), :]
    own_gates = gates_out[own_rows(picks), :]
    to_owner.arrive()
    spread = blocks // experts
    mixed = jnp.zeros(stream_out_own.shape, F32)
    for e in range(experts):
        part = arrived[e * spread].astype(F32)
        for k in range(1, spread):
            part = part + arrived[e * spread + k].astype(F32)
        mixed = mixed + own_gates[:, e : e + 1] * part
    mixed, to_sum = tensor_sum(mixed, summed, sems_c)
    final = stream_mid_own[...] + mixed
    stream_out_own[...] = final
    normed_out[block] = (final * root_of(final) * gains[2:3, :]).astype(BF16)
    to_all = share_block("dp", normed_out, sems_d)
    to_all.arrive()
    for move in (to_heads, to_owner, to_sum, to_all):
        move.finish()


def run_experts(experts, blocks, tensor, attended, stream, output_map, router, gains, routes, expert_in, expert_out):
    count, features = stream.shape
    picks = count // blocks
    hidden = expert_in.shape[1]
    out = jax.ShapeDtypeStruct
    return pl.pallas_call(
        functools.partial(experts_kernel, experts),
        out_shape=[
            out((blocks, picks, features), BF16),
            out((count, features), BF16),
            out((picks, features), F32),
            out((picks, features), F32),
            out((count, router.shape[0]), F32),
            out((count, hidden), F32),
            out((count, hidden), BF16),
            out((count, features), BF16),
        ],
        in_specs=[WHOLE] * 8,
        out_specs=[WHOLE] * 8,
        scratch_shapes=[
            pltpu.VMEM((tensor,) + attended.shape, BF16),
            pltpu.VMEM((count, features), F32),
            pltpu.VMEM((blocks, picks, features), BF16),
            pltpu.VMEM((tensor, picks, features), F32),
            sems_of(tensor),
            sems_of(blocks),
            sems_of(tensor),
            sems_of(blocks),
        ],
        compiler_params=pltpu.CompilerParams(
            collective_id=3, has_side_effects=True, vmem_limit_bytes=VMEM_BYTES
        ),
        name="experts_forward",
    )(attended, stream, output_map, router, gains, routes, expert_in, expert_out)


def norm_back_rows(v, g, upstream):
    root = root_of(v)
    scaled = g * upstream
    inner = jnp.sum(scaled * v, -1, keepdims=True)
    back = root * scaled - v * (root * root * root * inner / v.shape[-1])
    return back, jnp.sum(upstream * v * root, 0, keepdims=True)


def merge_stats(parts):
    peak = parts[0][0:1]
    for part in parts[1:]:
        peak = jnp.maximum(peak, part[0:1])
    total = sum(part[1:2] * jnp.exp(part[0:1] - peak) for part in parts)
    target = sum(part[2:3] for part in parts)
    plain = sum(part[3:4] for part in parts)
    return jnp.concatenate([peak, total, target, plain, parts[0][4:8]], 0)


def backward_kernel(
    experts,
    normed_out,
    table,
    wanted,
    weight,
    gates,
    routes,
    router,
    gains,
    stream_out_own,
    stream_mid_own,
    normed_mid,
    inner,
    active,
    piece,
    expert_in,
    expert_out,
    d_logits_all,
    d_middle,
    gain_parts,
    grad_in,
    grad_out,
    losses,
    stats_a,
    stats_b,
    sent,
    arrived,
    summed,
    d_final,
    sent_wide,
    arrived_wide,
    summed_wide,
    sems_a,
    sems_b,
    sems_c,
    sems_d,
    sems_e,
    sems_f,
    sems_g,
    sems_h,
    sems_i,
    sems_j,
):
    greeting = greet(("tensor", "dp"))
    block, here = lax.axis_index("dp"), lax.axis_index("tensor")
    blocks, picks, features = arrived.shape
    count = blocks * picks
    out = jnp.concatenate([normed_out[k] for k in range(blocks)], 0)
    logits = dot_nn(out, table[...])
    share = logits.shape[1]
    hit = lanes(logits.shape) == wanted[...]
    local_top = jnp.max(logits, -1, keepdims=True)
    local = (
        local_top,
        jnp.sum(jnp.exp(logits - local_top), -1, keepdims=True),
        jnp.sum(jnp.where(hit, logits, 0.0), -1, keepdims=True),
        jnp.sum(logits, -1, keepdims=True),
    )
    lane = lanes((count, 128))
    packed = jnp.zeros((count, 128), F32)
    for k, column in enumerate(local):
        packed = jnp.where(lane == k, column, packed)
    stats_a[here] = packed.T[0:8, :]
    met(greeting)
    moves = [share_block("tensor", stats_a, sems_a)]
    moves[-1].arrive()
    stats_b[block] = merge_stats([stats_a[k] for k in range(stats_a.shape[0])])
    moves.append(share_block("dp", stats_b, sems_b))
    moves[-1].arrive()
    merged_rows = merge_stats([stats_b[k] for k in range(blocks)])
    loss_total = merged_rows[0:1] + jnp.log(merged_rows[1:2])
    row_weight = weight[...]
    per_row = (
        loss_total
        - (1 - SMOOTH) * merged_rows[2:3]
        - SMOOTH * merged_rows[3:4] / VOCAB
        + ZLOSS * loss_total * loss_total
    )
    losses[0:1, :] = row_weight * per_row
    losses[1:2, :] = row_weight
    sublane = lax.broadcasted_iota(jnp.int32, (128, count), 0)
    columns = jnp.where(sublane == 0, loss_total, jnp.where(sublane == 1, row_weight, 0.0)).T
    total_column, weight_column = columns[:, 0:1], columns[:, 1:2]
    d_logits = (
        weight_column
        * (
            (1 + 2 * ZLOSS * total_column) * jnp.exp(logits - total_column)
            - jnp.where(hit, 1 - SMOOTH, 0.0)
            - SMOOTH / VOCAB
        )
    ).astype(BF16)
    d_logits_all[block] = d_logits
    sent[...] = dot_nt(d_logits, table[...]).astype(BF16)
    moves.append(scatter_rows("dp", sent, arrived, sems_c))
    arrived[block] = sent[own_rows(picks), :]
    moves[-1].arrive()
    total = arrived[0].astype(F32)
    for k in range(1, blocks):
        total = total + arrived[k].astype(F32)
    d_normed, to_sum = tensor_sum(total, summed, sems_d)
    moves.append(to_sum)
    d_stream_out, grad_final = norm_back_rows(stream_out_own[...], gains[2:3, :], d_normed)
    d_final[block] = d_stream_out.astype(BF16)
    moves.append(share_block("dp", d_final, sems_e))
    moves[-1].arrive()
    moves.append(share_block("dp", d_logits_all, sems_f))
    upstream = jnp.concatenate([d_final[k] for k in range(blocks)], 0).astype(F32)
    expert = block // (blocks // experts)
    gate = jnp.sum(jnp.where(lane == expert, gates[...], 0.0), 1, keepdims=True)
    d_piece = (gate * upstream).astype(BF16)
    d_active = dot_nt(d_piece, expert_out[...].astype(BF16))
    d_inner = (d_active * gelu_parts(inner[...])[1]).astype(BF16)
    sent_wide[:, 0:features] = dot_nt(d_inner, expert_in[...].astype(BF16)).astype(BF16)
    gate_part = jnp.sum(upstream * piece[...].astype(F32), 1, keepdims=True)
    high = gate_part.astype(BF16).astype(F32)
    sent_wide[:, features:] = jnp.where(
        lane == expert, high, jnp.where(lane == expert + 64, gate_part - high, 0.0)
    ).astype(BF16)
    moves.append(scatter_rows("dp", sent_wide, arrived_wide, sems_g))
    arrived_wide[block] = sent_wide[own_rows(picks), :]
    grad_out[...] = dot_nn(active[...].T, d_piece)
    grad_in[...] = dot_nn(normed_mid[...].T, d_inner)
    moves[-1].arrive()
    total = arrived_wide[0].astype(F32)
    for k in range(1, blocks):
        total = total + arrived_wide[k].astype(F32)
    total, to_sum = tensor_sum(total, summed_wide, sems_h)
    moves.append(to_sum)
    tail = total[:, features:]
    d_gates = tail + pltpu.roll(tail, 64, 1)
    own_routes = routes[own_rows(picks), :]
    own_gates = gates[own_rows(picks), :]
    slim = lanes(tail.shape)
    chosen = (slim == own_routes[:, 0:1]) | (slim == own_routes[:, 1:2])
    d_gates = jnp.where(chosen, d_gates, 0.0)
    mean = jnp.sum(own_gates * d_gates, 1, keepdims=True)
    d_router = jnp.where(chosen, own_gates * (d_gates - mean), 0.0).astype(BF16)
    d_normed_mid = total[:, 0:features] + dot_nn(d_router, router[...])
    d_from_mid, grad_middle = norm_back_rows(stream_mid_own[...], gains[1:2, :], d_normed_mid)
    d_middle[block, :, 0:features] = (d_stream_out + d_from_mid).astype(BF16)
    d_middle[block, :, features:] = d_router
    gain_parts[block, 0:1, :] = grad_middle
    gain_parts[block, 1:2, :] = grad_final
    moves.append(share_block("dp", d_middle, sems_i))
    moves.append(share_block("dp", gain_parts, sems_j))
    moves[-2].arrive()
    moves[-1].arrive()
    moves[5].arrive()
    for move in moves:
        move.finish()


def run_backward(experts, blocks, tensor, *operands):
    normed_out, table, expert_in = operands[0], operands[1], operands[14]
    picks, features = normed_out.shape[1:]
    count = blocks * picks
    share = table.shape[1]
    wide = features + 128
    out = jax.ShapeDtypeStruct
    return pl.pallas_call(
        functools.partial(backward_kernel, experts),
        out_shape=[
            out((blocks, count, share), BF16),
            out((blocks, picks, wide), BF16),
            out((blocks, 2, features), F32),
            out(expert_in.shape, F32),
            out(expert_in.shape[::-1], F32),
            out((2, count), F32),
        ],
        in_specs=[WHOLE] * len(operands),
        out_specs=[WHOLE] * 6,
        scratch_shapes=[
            pltpu.VMEM((tensor, 8, 128), F32),
            pltpu.VMEM((blocks, 8, 128), F32),
            pltpu.VMEM((count, features), BF16),
            pltpu.VMEM((blocks, picks, features), BF16),
            pltpu.VMEM((tensor, picks, features), F32),
            pltpu.VMEM((blocks, picks, features), BF16),
            pltpu.VMEM((count, wide), BF16),
            pltpu.VMEM((blocks, picks, wide), BF16),
            pltpu.VMEM((tensor, picks, wide), F32),
            sems_of(tensor),
            sems_of(blocks),
            sems_of(blocks),
            sems_of(tensor),
            sems_of(blocks),
            sems_of(blocks),
            sems_of(blocks),
            sems_of(tensor),
            sems_of(blocks),
            sems_of(blocks),
        ],
        compiler_params=pltpu.CompilerParams(
            collective_id=4, has_side_effects=True, vmem_limit_bytes=VMEM_BYTES
        ),
        name="loss_and_experts_backward",
    )(*operands)


def head_of(ref, h):
    return ref[:, h * HD : (h + 1) * HD]


def attention_kernel(
    query,
    keys,
    values,
    flipped,
    offsets,
    positions,
    query_picture,
    key_picture,
    table,
    attended_low,
    probs,
    bucket,
    shifted,
    bias,
):
    count, every = bucket.shape
    heads, bucket_count = table.shape
    rows = 128
    blocks = every // rows
    picks = count // blocks
    period = flipped.shape[1]
    spread = jnp.broadcast_to(flipped[...], (rows, period))
    turned = pltpu.roll(spread, period - rows + 1, 1, stride=1, stride_axis=0).astype(BF16)
    chosen = (lanes((count, rows)) == offsets[...]).astype(F32).astype(BF16)
    shifted[...] = dot_nn(chosen, turned).astype(jnp.int32)
    for k in range(blocks):
        first = rows * (blocks - 1 - k)
        bucket[k * picks : (k + 1) * picks, :] = shifted[
            k * picks : (k + 1) * picks, first : first + every
        ]

    def fill(k, carry):
        here = pl.ds(pl.multiple_of(k * picks, picks), picks)
        block = bucket[here, :]
        terms = [jnp.zeros(block.shape, F32)] * heads
        for b in range(bucket_count):
            same = block == b
            terms = [jnp.where(same, table[h, b], terms[h]) for h in range(heads)]
        for h in range(heads):
            bias[h, here, :] = terms[h]
        return carry

    lax.fori_loop(0, blocks, fill, 0)
    key_position = lanes((count, every))
    picture = query_picture[...]
    allowed = (key_position <= positions[...]) | (
        (key_picture[...] == picture) & (picture >= 0)
    )
    for h in range(heads):
        raw = dot_nt(head_of(query, h), head_of(keys, h)) * (1.0 / math.sqrt(HD)) + bias[h]
        raw = jnp.where(allowed, raw, NEGATIVE)
        terms = jnp.exp(raw - jnp.max(raw, -1, keepdims=True))
        soft = terms / jnp.sum(terms, -1, keepdims=True)
        probs[h] = soft
        attended_low[:, h * HD : (h + 1) * HD] = dot_nn(
            soft.astype(BF16), head_of(values, h)
        ).astype(BF16)


def run_attention(query, keys, values, flipped, offsets, positions, query_picture, key_picture, table):
    count, width = query.shape
    every = keys.shape[0]
    heads = table.shape[0]
    out = jax.ShapeDtypeStruct
    smem = pl.BlockSpec(memory_space=pltpu.SMEM)
    return pl.pallas_call(
        attention_kernel,
        out_shape=[
            out((count, width), BF16),
            out((heads, count, every), F32),
            out((count, every), jnp.int32),
        ],
        in_specs=[WHOLE] * 8 + [smem],
        out_specs=[WHOLE] * 3,
        scratch_shapes=[
            pltpu.VMEM((count, flipped.shape[1]), jnp.int32),
            pltpu.VMEM((heads, count, every), F32),
        ],
        compiler_params=pltpu.CompilerParams(vmem_limit_bytes=VMEM_BYTES),
        name="attention",
    )(query, keys, values, flipped, offsets, positions, query_picture, key_picture, table)


def attention_back_kernel(
    upstream, output_map, query, keys, values, probs, bucket, d_query, d_key, d_value, bias_rows, spare
):
    heads, count, every = probs.shape
    picks = 16
    scale = 1.0 / math.sqrt(HD)
    d_attended = dot_nt(upstream[...], output_map[...]).astype(BF16)
    for h in range(heads):
        span = slice(h * HD, (h + 1) * HD)
        soft = probs[h]
        d_head = d_attended[:, span]
        d_probs = dot_nt(d_head, head_of(values, h))
        d_scores = soft * (d_probs - jnp.sum(soft * d_probs, -1, keepdims=True))
        d_scores = d_scores.astype(BF16)
        spare[h] = d_scores.astype(F32)
        d_query[:, span] = (dot_nn(d_scores, head_of(keys, h)) * scale).astype(BF16)
        d_key[:, span] = (dot_nn(d_scores.T, head_of(query, h)) * scale).astype(BF16)
        d_value[:, span] = dot_nn(soft.astype(BF16).T, d_head).astype(BF16)
    bias_rows[...] = jnp.zeros(bias_rows.shape, F32)
    bucket_count = bias_rows.shape[1]

    def collect(k, carry):
        here = pl.ds(pl.multiple_of(k * picks, picks), picks)
        block = bucket[here, :]
        parts = [spare[h, here, :] for h in range(heads)]
        for b in range(bucket_count):
            same = block == b
            for h in range(heads):
                kept = jnp.where(same, parts[h], 0.0)
                kept = kept[0:8] + kept[8:16]
                slim = kept[:, 0:128]
                for c in range(1, every // 128):
                    slim = slim + kept[:, c * 128 : (c + 1) * 128]
                bias_rows[h, b] += slim
        return carry

    lax.fori_loop(0, count // picks, collect, 0)


def run_attention_back(upstream, output_map, query, keys, values, probs, bucket, bucket_count):
    heads, count, every = probs.shape
    out = jax.ShapeDtypeStruct
    return pl.pallas_call(
        attention_back_kernel,
        out_shape=[
            out(query.shape, BF16),
            out(keys.shape, BF16),
            out(keys.shape, BF16),
            out((heads, bucket_count, 8, 128), F32),
        ],
        in_specs=[WHOLE] * 7,
        out_specs=[WHOLE] * 4,
        scratch_shapes=[pltpu.VMEM((heads, count, every), F32)],
        compiler_params=pltpu.CompilerParams(vmem_limit_bytes=VMEM_BYTES),
        name="attention_backward",
    )(upstream, output_map, query, keys, values, probs, bucket)


def wide_norm_back(v, g, upstream):
    size = v.shape[-1]
    root = lax.rsqrt(jnp.mean(v * v, -1, keepdims=True) + NORM_EPS)
    scaled = g * upstream
    inner = jnp.sum(scaled * v, -1, keepdims=True)
    return (root * scaled - v * (root * root * root * inner / size), jnp.sum(upstream * v * root, 0))


def fast_local(
    token_ids,
    targets,
    loss_offsets,
    routes,
    picture_start,
    buckets,
    embedding,
    embedding_first,
    embedding_second,
    attn_proj,
    attn_proj_first,
    attn_proj_second,
    out_proj,
    out_proj_first,
    out_proj_second,
    router,
    router_first,
    router_second,
    expert_in,
    expert_in_first,
    expert_in_second,
    expert_out,
    expert_out_first,
    expert_out_second,
    norm_gains,
    norm_gains_first,
    norm_gains_second,
    position_bias,
    position_bias_first,
    position_bias_second,
):
    f32 = jnp.float32
    bf16 = jnp.bfloat16
    dp_count = lax.axis_size("dp")
    tensor_count = lax.axis_size("tensor")
    dp_place = lax.axis_index("dp")
    tensor_place = lax.axis_index("tensor")
    rows = token_ids.shape[0]
    every = rows * dp_count
    picks = loss_offsets.shape[0]
    all_picks = picks * dp_count
    scale = 1.0 / math.sqrt(HD)
    vocab_rows, columns = embedding.shape
    features = columns * dp_count
    width = attn_proj.shape[2]
    heads = width // HD
    experts = router.shape[0]
    both = ("dp", "tensor")
    loss_hot = loss_offsets[:, None] == jnp.arange(rows, dtype=jnp.int32)[None, :]

    def at_loss(values):
        return jnp.sum(jnp.where(loss_hot, values[None, :], 0), 1)

    packed = jnp.concatenate(
        [token_ids, loss_offsets, at_loss(targets), at_loss(routes[:, 0]), at_loss(routes[:, 1])]
    )
    packed = jnp.pad(packed, (0, 256 - packed.shape[0])).reshape(2, 128)
    known = gather_blocks((packed,), "dp", 1, "gather_integers")[0].reshape(dp_count, 256)
    ids = known[:, :rows].reshape(every)
    offsets, wanted, route_a, route_b = (
        known[:, rows + k * picks : rows + (k + 1) * picks].reshape(all_picks) for k in range(4)
    )
    pick_block = jnp.arange(all_picks, dtype=jnp.int32) // picks
    loss_rows = offsets + pick_block * rows
    projection = lax.all_gather(attn_proj.astype(bf16), "dp", axis=1, tiled=True)
    output_map = lax.all_gather(
        lax.all_gather(out_proj.astype(bf16), "dp", axis=1, tiled=True),
        "tensor",
        axis=0,
        tiled=True,
    )
    router_full = lax.all_gather(router.astype(bf16), "dp", axis=1, tiled=True)
    gain = lax.all_gather(norm_gains.astype(bf16), "dp", axis=1, tiled=True).astype(f32)
    own_gain = norm_gains.astype(bf16).astype(f32)
    table_rows = lax.all_to_all(
        embedding.astype(bf16), "dp", split_axis=0, concat_axis=1, tiled=True
    )
    part = rows // tensor_count
    sorted_ids = jnp.swapaxes(ids.reshape(dp_count, tensor_count, part), 0, 1).reshape(every)
    place = sorted_ids - tensor_place * vocab_rows
    owned = (place >= 0) & (place < vocab_rows)
    looked = jnp.take(embedding.astype(bf16), jnp.clip(place, 0, vocab_rows - 1), axis=0)
    looked = jnp.where(owned[:, None], looked, 0.0).astype(bf16)
    stream_parts, column_parts = exchange_lookups(
        looked.reshape(tensor_count, dp_count, part, columns)
    )
    stream_in = jnp.swapaxes(stream_parts, 1, 2).reshape(rows, features).astype(f32)
    in_columns = jnp.swapaxes(column_parts, 0, 1).reshape(every, columns).astype(f32)
    place = ids - tensor_place * vocab_rows
    root_in = lax.rsqrt(jnp.mean(stream_in * stream_in, -1, keepdims=True) + NORM_EPS)
    normed_in = (stream_in * root_in * gain[0]).astype(bf16)
    fresh = jnp.einsum("td,sde->ste", normed_in, projection, preferred_element_type=f32).astype(
        bf16
    )
    loss_one = loss_hot.astype(bf16)
    own_query = jnp.dot(loss_one, fresh[0], preferred_element_type=f32).astype(bf16)
    own_stream = jnp.dot(
        loss_one, stream_in.astype(bf16), preferred_element_type=f32
    ).astype(bf16)
    shared = jnp.concatenate([fresh[1], fresh[2]], 1)
    shared, query, stream_picked, root_all = gather_blocks(
        (shared, own_query, own_stream, root_in.reshape(1, rows)), "dp", 5, "gather_keys"
    )
    shared = shared.reshape(every, 2 * width)
    keys, values = shared[:, :width], shared[:, width:]
    query = query.reshape(all_picks, width)
    stream_picked = stream_picked.reshape(all_picks, features)
    root_all = root_all.reshape(every, 1)
    in_columns_normed = (in_columns * root_all * own_gain[0]).astype(bf16)
    flipped = jnp.pad(jnp.flip(buckets), (0, 1)).astype(f32)[None, :]
    position = jnp.arange(every, dtype=jnp.int32)
    key_picture = picture_of(position, picture_start[0], PIECE)
    query_picture = picture_of(loss_rows, picture_start[0], PIECE)
    bucket_count = position_bias.shape[1]
    attended_low, probs, bucket = run_attention(
        query,
        keys,
        values,
        flipped,
        offsets[:, None],
        loss_rows[:, None],
        query_picture[:, None],
        key_picture[None, :],
        position_bias,
    )
    route_pair = jnp.stack([route_a, route_b], 1)
    router_wide = jnp.pad(router_full, ((0, 128 - experts), (0, 0)))
    (
        normed_out,
        normed_mid,
        stream_mid_own,
        stream_out_own,
        gates,
        inner,
        active,
        piece,
    ) = run_experts(
        experts,
        dp_count,
        tensor_count,
        attended_low,
        stream_picked,
        output_map,
        router_wide,
        gain,
        route_pair,
        expert_in,
        expert_out,
    )
    share = table_rows.shape[0]
    first_id = tensor_place * vocab_rows + dp_place * share
    weight = (query_picture < 0).astype(f32)
    d_logits_all, d_middle, gain_parts, grad_in, grad_out, losses = run_backward(
        experts,
        dp_count,
        tensor_count,
        normed_out,
        table_rows.T,
        (wanted - first_id)[:, None],
        weight[None, :],
        gates,
        route_pair,
        router_wide,
        gain,
        stream_out_own,
        stream_mid_own,
        normed_mid,
        inner,
        active,
        piece,
        expert_in,
        expert_out,
    )
    loss_sum, loss_count = jnp.sum(losses[0]), jnp.sum(losses[1])
    d_middle = d_middle.reshape(all_picks, features + 128)
    d_attn_low, d_router_logits = d_middle[:, :features], d_middle[:, features:]

    def own_columns(value):
        return lax.dynamic_slice_in_dim(value, dp_place * columns, columns, value.ndim - 1)

    grad_router = jnp.dot(
        d_router_logits.T, own_columns(normed_mid), preferred_element_type=f32
    )[:experts]
    grad_middle, grad_final = jnp.sum(gain_parts[:, 0], 0), jnp.sum(gain_parts[:, 1], 0)
    grad_output_map = jnp.dot(
        attended_low.T, own_columns(d_attn_low), preferred_element_type=f32
    )
    own_map = lax.dynamic_slice_in_dim(output_map, tensor_place * width, width, 0)
    d_query, d_key, d_value, bias_rows = run_attention_back(
        d_attn_low, own_map, query, keys, values, probs, bucket, bucket_count
    )
    sum_bias = jnp.sum(bias_rows, (2, 3))
    back_hot = (loss_rows[None, :] == position[:, None]).astype(bf16)
    in_picked = jnp.dot(
        back_hot.T, in_columns_normed, preferred_element_type=f32
    ).astype(bf16)
    sum_proj = jnp.stack(
        [
            jnp.dot(in_picked.T, d_query, preferred_element_type=f32),
            jnp.dot(in_columns_normed.T, d_key, preferred_element_type=f32),
            jnp.dot(in_columns_normed.T, d_value, preferred_element_type=f32),
        ]
    )
    d_query_all = jnp.dot(back_hot, d_query, preferred_element_type=f32).astype(bf16)
    query_all = jnp.dot(back_hot, query, preferred_element_type=f32)
    own_proj = attn_proj.astype(bf16)
    d_columns = sum(
        lax.dot_general(part, own_proj[s], (((1,), (1,)), ((), ())), preferred_element_type=f32)
        for s, part in enumerate((d_query_all, d_key, d_value))
    )
    d_inner_in = jnp.sum(
        d_query_all.astype(f32) * query_all
        + d_key.astype(f32) * keys.astype(f32)
        + d_value.astype(f32) * values.astype(f32),
        -1,
        keepdims=True,
    )
    d_columns, d_inner_in = lax.psum((d_columns, d_inner_in), "tensor")
    grad_first = jnp.sum(d_columns * in_columns * root_all, 0)
    own_stream_mid = own_columns(d_attn_low)
    d_stream_in = (
        root_all * own_gain[0] * d_columns
        - in_columns * (root_all * root_all * d_inner_in / features)
        + jnp.dot(back_hot, own_stream_mid, preferred_element_type=f32)
    )
    own_out = own_columns(normed_out.reshape(all_picks, features))
    sum_table = jnp.einsum("kqv,qd->kvd", d_logits_all, own_out, preferred_element_type=f32)
    sum_table = sum_table.reshape(vocab_rows, columns)
    d_high = d_stream_in.astype(bf16)
    d_low = (d_stream_in - d_high.astype(f32)).astype(bf16)
    id_hot = (jnp.arange(vocab_rows, dtype=jnp.int32)[:, None] == place[None, :]).astype(bf16)
    scattered = jnp.dot(
        id_hot, jnp.concatenate([d_high, d_low], 1), preferred_element_type=f32
    )
    sum_table = sum_table + scattered[:, :columns] + scattered[:, columns:]
    sum_router = grad_router
    sum_gains = jnp.stack([grad_first, own_columns(grad_middle), own_columns(grad_final)])
    squares = (
        jnp.sum(sum_table * sum_table)
        + jnp.sum(sum_proj * sum_proj)
        + jnp.sum(grad_output_map * grad_output_map)
        + jnp.sum(grad_in * grad_in)
        + jnp.sum(grad_out * grad_out)
        + (jnp.sum(sum_router * sum_router) + jnp.sum(sum_gains * sum_gains)) / tensor_count
        + jnp.sum(sum_bias * sum_bias) / dp_count
    )
    grad_norm = jnp.sqrt(lax.psum(squares, both))
    clip = MAX_NORM / jnp.maximum(grad_norm, MAX_NORM)
    params = (
        embedding,
        attn_proj,
        out_proj,
        router,
        expert_in,
        expert_out,
        norm_gains,
        position_bias,
    )
    firsts = (
        embedding_first,
        attn_proj_first,
        out_proj_first,
        router_first,
        expert_in_first,
        expert_out_first,
        norm_gains_first,
        position_bias_first,
    )
    seconds = (
        embedding_second,
        attn_proj_second,
        out_proj_second,
        router_second,
        expert_in_second,
        expert_out_second,
        norm_gains_second,
        position_bias_second,
    )
    grads = (
        sum_table,
        sum_proj,
        grad_output_map,
        sum_router,
        grad_in,
        grad_out,
        sum_gains,
        sum_bias,
    )
    results = []
    for index in range(8):
        results.extend(
            adam_update(
                params[index],
                firsts[index],
                seconds[index],
                clip * grads[index],
                RATES[index],
                DECAYS[index],
            )
        )
    return (
        results[0],
        results[1],
        results[2],
        results[3],
        results[4],
        results[5],
        results[6],
        results[7],
        results[8],
        results[9],
        results[10],
        results[11],
        results[12],
        results[13],
        results[14],
        results[15],
        results[16],
        results[17],
        results[18],
        results[19],
        results[20],
        results[21],
        results[22],
        results[23],
        grad_norm,
        loss_sum,
        loss_count,
    )


def local(
    token_ids,
    targets,
    loss_offsets,
    routes,
    picture_start,
    buckets,
    embedding,
    embedding_first,
    embedding_second,
    attn_proj,
    attn_proj_first,
    attn_proj_second,
    out_proj,
    out_proj_first,
    out_proj_second,
    router,
    router_first,
    router_second,
    expert_in,
    expert_in_first,
    expert_in_second,
    expert_out,
    expert_out_first,
    expert_out_second,
    norm_gains,
    norm_gains_first,
    norm_gains_second,
    position_bias,
    position_bias_first,
    position_bias_second,
):
    f32 = jnp.float32
    bf16 = jnp.bfloat16
    dp_count = lax.axis_size("dp")
    tensor_count = lax.axis_size("tensor")
    dp_place = lax.axis_index("dp")
    tensor_place = lax.axis_index("tensor")
    rows = token_ids.shape[0]
    every = rows * dp_count
    length = min(SEQ, every)
    seqs = every // length
    sub = rows // seqs
    scale = 1.0 / math.sqrt(HD)
    vocab_rows = embedding.shape[0]
    table, projection, output_map, router_full, gain_full = (
        lax.all_gather(embedding.astype(bf16), "dp", axis=1, tiled=True),
        lax.all_gather(attn_proj.astype(bf16), "dp", axis=1, tiled=True),
        lax.all_gather(out_proj.astype(bf16), "dp", axis=1, tiled=True),
        lax.all_gather(router.astype(bf16), "dp", axis=1, tiled=True),
        lax.all_gather(norm_gains.astype(bf16), "dp", axis=1, tiled=True),
    )
    gain = gain_full.astype(f32)
    features = table.shape[1]
    offset = token_ids - tensor_place * vocab_rows
    owned = (offset >= 0) & (offset < vocab_rows)
    offset = jnp.clip(offset, 0, vocab_rows - 1)
    looked = jnp.take(table, offset, axis=0).astype(f32)
    stream_in = tensor_total(jnp.where(owned[:, None], looked, 0.0))
    pos_here = dp_place * sub + jnp.arange(sub, dtype=jnp.int32)
    seq_positions = jnp.arange(length, dtype=jnp.int32)
    picture_all = jax.vmap(lambda starts: picture_of(seq_positions, starts, PIECE))(picture_start)
    picture_here = lax.dynamic_slice_in_dim(picture_all, dp_place * sub, sub, 1)
    bucket_ids = jnp.arange(position_bias.shape[1], dtype=jnp.int32)
    bucket_hot = (bucket_ids[:, None] == buckets[None, :]).astype(f32)
    relative = jnp.dot(position_bias, bucket_hot, precision=HIGH)
    normed_in = normed(stream_in, gain[0]).astype(bf16)
    fresh = jnp.einsum("td,sde->ste", normed_in, projection, preferred_element_type=f32).astype(
        bf16
    )
    width = fresh.shape[2]
    heads = width // HD
    keys_local = fresh[1].reshape(seqs, sub, width)
    values_local = fresh[2].reshape(seqs, sub, width)
    query_heads = fresh[0].reshape(seqs, sub, heads, HD)
    keys_all, values_all = (
        lax.all_gather(keys_local, "dp", axis=1, tiled=True),
        lax.all_gather(values_local, "dp", axis=1, tiled=True),
    )
    block = min(512, length)
    blocks = length // block
    block_ids = jnp.arange(blocks, dtype=jnp.int32)

    def pair_scores(q_heads, q_pos, q_pic, k_heads, k_pos, k_pic, bias):
        raw = (
            jnp.einsum("sqhd,skhd->shqk", q_heads, k_heads, preferred_element_type=f32) * scale
            + bias[None]
        )
        allowed = (k_pos[None, :] <= q_pos[:, None])[None] | (
            k_pic[:, None, :] == q_pic[:, :, None]
        ) & (q_pic[:, :, None] >= 0)
        return jnp.where(allowed[:, None], raw, NEGATIVE)

    def key_slice(source, start):
        return lax.dynamic_slice_in_dim(source, start, block, 1).reshape(seqs, block, heads, HD)

    def own_bias(start):
        return rel_window(relative, dp_place * sub, sub, start, block, length)

    def fwd_scores(index, key_source):
        start = index * block
        key_pos = start + jnp.arange(block, dtype=jnp.int32)
        return pair_scores(
            query_heads,
            pos_here,
            picture_here,
            key_slice(key_source, start),
            key_pos,
            lax.dynamic_slice_in_dim(picture_all, start, block, 1),
            own_bias(start),
        )

    def max_step(carry, index):
        top, total = carry
        s = fwd_scores(index, keys_all)
        new_top = jnp.maximum(top, jnp.max(s, -1))
        terms = jnp.where(s > 0.5 * NEGATIVE, jnp.exp(s - new_top[..., None]), 0.0)
        total = total * jnp.exp(top - new_top) + jnp.sum(terms, -1)
        return ((new_top, total), None)

    start_top = jnp.full((seqs, heads, sub), NEGATIVE, f32)
    (top, total), unused = lax.scan(
        max_step, (start_top, jnp.zeros((seqs, heads, sub), f32)), block_ids
    )
    log_total = top + jnp.log(total)

    def out_step(accum, index):
        s = fwd_scores(index, keys_all)
        probs = jnp.exp(s - log_total[..., None]).astype(bf16)
        value_heads = key_slice(values_all, index * block)
        return (
            accum + jnp.einsum("shqk,skhd->sqhd", probs, value_heads, preferred_element_type=f32),
            None,
        )

    attended, unused = lax.scan(out_step, jnp.zeros((seqs, sub, heads, HD), f32), block_ids)
    attended_low = attended.reshape(rows, width).astype(bf16)
    stream_mid = stream_in + tensor_total(
        jnp.dot(attended_low, output_map, preferred_element_type=f32)
    )
    normed_mid = normed(stream_mid, gain[1]).astype(bf16)
    router_logits = jnp.dot(normed_mid, router_full.T, preferred_element_type=f32)
    gates = jax.nn.softmax(jnp.take_along_axis(router_logits, routes, 1), -1)
    experts = router_full.shape[0]
    top_k = routes.shape[1]
    capacity = 2 * rows * top_k // experts
    flat = routes.reshape(-1)
    owner = jnp.arange(rows * top_k, dtype=jnp.int32) // top_k
    hits = (flat[:, None] == jnp.arange(experts, dtype=jnp.int32)[None, :]).astype(jnp.int32)
    slot = jnp.sum(jnp.cumsum(hits, 0) * hits, 1) - 1
    first_row = 2 * flat * capacity + slot

    def pack(values):
        buffer = jnp.zeros((experts, capacity, features), bf16).at[flat, slot].set(values)
        return jnp.repeat(buffer, 2, axis=0).reshape(2 * experts * capacity, features)

    def unpack(values):
        return values[first_row].astype(f32) + values[first_row + capacity].astype(f32)

    in_low = expert_in.astype(bf16)
    out_low = expert_out.astype(bf16)
    arrived = route_exchange(pack(normed_mid[owner]))
    inner = jnp.dot(arrived, in_low, preferred_element_type=f32)
    active = jax.nn.gelu(inner).astype(bf16)
    produced = jnp.dot(active, out_low, preferred_element_type=f32).astype(bf16)
    returned = unpack(route_exchange(produced))
    mixed = jnp.sum((gates.reshape(-1)[:, None] * returned).reshape(rows, top_k, features), 1)
    stream_out = stream_mid + tensor_total(mixed)
    normed_out = normed(stream_out, gain[2]).astype(bf16)
    picked = normed_out[loss_offsets]
    logits = jnp.dot(picked, table.T, preferred_element_type=f32)
    wanted = targets[loss_offsets] - tensor_place * vocab_rows
    hit = jnp.arange(vocab_rows, dtype=jnp.int32)[None, :] == wanted[:, None]
    local_top = jnp.max(logits, -1)
    stats = (
        local_top,
        jnp.sum(jnp.exp(logits - local_top[:, None]), -1),
        jnp.sum(jnp.where(hit, logits, 0.0), -1),
        jnp.sum(logits, -1),
    )
    peak, vocab_total, target_logit, logit_sum = merged(stats, "tensor", combine_stats)
    loss_total = peak + jnp.log(vocab_total)
    weight = (picture_here.reshape(rows)[loss_offsets] < 0).astype(f32)
    per_row = (
        loss_total
        - (1 - SMOOTH) * target_logit
        - SMOOTH * logit_sum / VOCAB
        + ZLOSS * loss_total * loss_total
    )
    loss_local = jnp.sum(weight * per_row)
    soft = jnp.exp(logits - loss_total[:, None])
    d_logits = (
        weight[:, None]
        * (
            (1 + 2 * ZLOSS * loss_total)[:, None] * soft
            - (1 - SMOOTH) * hit.astype(f32)
            - SMOOTH / VOCAB
        )
    ).astype(bf16)
    d_picked = jnp.dot(d_logits, table, preferred_element_type=f32)
    grad_table = jnp.dot(d_logits.T, picked, preferred_element_type=f32)
    d_normed_out = tensor_total(jnp.zeros((rows, features), f32).at[loss_offsets].add(d_picked))
    d_stream_out, grad_final = norm_back(stream_out, gain[2], d_normed_out)
    d_piece = (gates.reshape(-1)[:, None] * d_stream_out[owner]).astype(bf16)
    d_arrived = route_exchange(pack(d_piece))
    d_active = jnp.dot(d_arrived, out_low.T, preferred_element_type=f32)
    unused, gelu_pull = jax.vjp(jax.nn.gelu, inner)
    d_inner = gelu_pull(d_active)[0].astype(bf16)
    grad_out = jnp.dot(active.T, d_arrived, preferred_element_type=f32)
    grad_in = jnp.dot(arrived.T, d_inner, preferred_element_type=f32)
    sent_back = jnp.dot(d_inner, in_low.T, preferred_element_type=f32).astype(bf16)
    d_routes = unpack(route_exchange(sent_back))
    gate_part = jnp.sum(d_stream_out[owner] * returned, -1).reshape(rows, top_k)
    route_part = jnp.sum(d_routes.reshape(rows, top_k, features), 1)
    d_from_experts, d_gates = tensor_total((route_part, gate_part))
    d_chosen = gates * (d_gates - jnp.sum(gates * d_gates, -1, keepdims=True))
    expert_hot = (routes[..., None] == jnp.arange(experts, dtype=jnp.int32)).astype(f32)
    d_router_logits = jnp.sum(expert_hot * d_chosen[..., None], 1).astype(bf16)
    grad_router = jnp.dot(d_router_logits.T, normed_mid, preferred_element_type=f32)
    d_normed_mid = d_from_experts + jnp.dot(
        d_router_logits, router_full, preferred_element_type=f32
    )
    d_from_mid, grad_middle = norm_back(stream_mid, gain[1], d_normed_mid)
    d_stream_mid = d_stream_out + d_from_mid
    d_attn_low = d_stream_mid.astype(bf16)
    grad_output_map = jnp.dot(attended_low.T, d_attn_low, preferred_element_type=f32)
    d_attended = jnp.dot(d_attn_low, output_map.T, preferred_element_type=f32).astype(bf16)
    d_heads = d_attended.reshape(seqs, sub, heads, HD)
    delta = jnp.moveaxis(jnp.sum(d_heads.astype(f32) * attended, -1), 2, 1)
    key_source, value_source = (
        lax.all_gather(keys_local, "dp", axis=1, tiled=True),
        lax.all_gather(values_local, "dp", axis=1, tiled=True),
    )

    def score_grads(
        q_heads, q_pos, q_pic, k_heads, k_pos, k_pic, bias, totals, deltas, dq_heads, v_heads
    ):
        s = pair_scores(q_heads, q_pos, q_pic, k_heads, k_pos, k_pic, bias)
        probs = jnp.exp(s - totals[..., None])
        d_probs = jnp.einsum("sqhd,skhd->shqk", dq_heads, v_heads, preferred_element_type=f32)
        d_scores = (probs * (d_probs - deltas[..., None])).astype(bf16)
        return (probs, d_scores)

    def key_step(carry, index):
        d_query, d_rel = carry
        start = index * block
        key_pos = start + jnp.arange(block, dtype=jnp.int32)
        key_heads = key_slice(key_source, start)
        value_heads = key_slice(value_source, start)
        bias, bias_pull = jax.vjp(
            lambda table_rel: rel_window(table_rel, dp_place * sub, sub, start, block, length),
            relative,
        )
        probs, d_scores = score_grads(
            query_heads,
            pos_here,
            picture_here,
            key_heads,
            key_pos,
            lax.dynamic_slice_in_dim(picture_all, start, block, 1),
            bias,
            log_total,
            delta,
            d_heads,
            value_heads,
        )
        d_query = (
            d_query
            + jnp.einsum("shqk,skhd->sqhd", d_scores, key_heads, preferred_element_type=f32) * scale
        )
        d_rel = d_rel + bias_pull(jnp.sum(d_scores.astype(f32), 0))[0]
        d_key = (
            jnp.einsum("shqk,sqhd->skhd", d_scores, query_heads, preferred_element_type=f32) * scale
        )
        d_value = jnp.einsum(
            "shqk,sqhd->skhd", probs.astype(bf16), d_heads, preferred_element_type=f32
        )
        joined = jnp.concatenate(
            [d_key.reshape(seqs, block, width), d_value.reshape(seqs, block, width)], 2
        )
        return ((d_query, d_rel), joined)

    start_carry = (jnp.zeros((seqs, sub, heads, HD), f32), jnp.zeros(relative.shape, f32))
    (d_query, d_rel), key_terms = lax.scan(key_step, start_carry, block_ids)
    d_bias = jnp.dot(d_rel, bucket_hot.T, precision=HIGH)
    ordered = jnp.moveaxis(key_terms, 0, 1).reshape(seqs, length, 2 * width)
    key_grads = lax.psum_scatter(ordered, "dp", scatter_dimension=1, tiled=True).reshape(
        rows, 2 * width
    )
    d_fresh = jnp.stack(
        [d_query.reshape(rows, width), key_grads[:, :width], key_grads[:, width:]]
    ).astype(bf16)
    grad_proj = jnp.einsum("td,ste->sde", normed_in, d_fresh, preferred_element_type=f32)
    d_normed_in = tensor_total(
        jnp.einsum("ste,sde->td", d_fresh, projection, preferred_element_type=f32)
    )
    d_from_in, grad_first = norm_back(stream_in, gain[0], d_normed_in)
    d_stream_in = d_stream_mid + d_from_in
    grad_table = grad_table + jnp.zeros((vocab_rows, features), f32).at[offset].add(
        jnp.where(owned[:, None], d_stream_in, 0.0)
    )
    sum_table, sum_proj, sum_output, sum_router, sum_gains = (
        lax.psum_scatter(grad_table, "dp", scatter_dimension=1, tiled=True),
        lax.psum_scatter(grad_proj, "dp", scatter_dimension=1, tiled=True),
        lax.psum_scatter(grad_output_map, "dp", scatter_dimension=1, tiled=True),
        lax.psum_scatter(grad_router, "dp", scatter_dimension=1, tiled=True),
        lax.psum_scatter(
            jnp.stack([grad_first, grad_middle, grad_final]), "dp", scatter_dimension=1, tiled=True
        ),
    )
    sum_bias = lax.psum(d_bias, "dp")
    squares = (
        jnp.sum(sum_table * sum_table)
        + jnp.sum(sum_proj * sum_proj)
        + jnp.sum(sum_output * sum_output)
        + jnp.sum(grad_in * grad_in)
        + jnp.sum(grad_out * grad_out)
        + (jnp.sum(sum_router * sum_router) + jnp.sum(sum_gains * sum_gains)) / tensor_count
        + jnp.sum(sum_bias * sum_bias) / dp_count
    )
    total_squares, loss_sum, loss_count = lax.psum(
        (squares, loss_local / tensor_count, jnp.sum(weight) / tensor_count), ("dp", "tensor")
    )
    grad_norm = jnp.sqrt(total_squares)
    clip = MAX_NORM / jnp.maximum(grad_norm, MAX_NORM)
    params = (
        embedding,
        attn_proj,
        out_proj,
        router,
        expert_in,
        expert_out,
        norm_gains,
        position_bias,
    )
    firsts = (
        embedding_first,
        attn_proj_first,
        out_proj_first,
        router_first,
        expert_in_first,
        expert_out_first,
        norm_gains_first,
        position_bias_first,
    )
    seconds = (
        embedding_second,
        attn_proj_second,
        out_proj_second,
        router_second,
        expert_in_second,
        expert_out_second,
        norm_gains_second,
        position_bias_second,
    )
    grads = (sum_table, sum_proj, sum_output, sum_router, grad_in, grad_out, sum_gains, sum_bias)
    results = []
    for index in range(8):
        results.extend(
            adam_update(
                params[index],
                firsts[index],
                seconds[index],
                clip * grads[index],
                RATES[index],
                DECAYS[index],
            )
        )
    return (
        results[0],
        results[1],
        results[2],
        results[3],
        results[4],
        results[5],
        results[6],
        results[7],
        results[8],
        results[9],
        results[10],
        results[11],
        results[12],
        results[13],
        results[14],
        results[15],
        results[16],
        results[17],
        results[18],
        results[19],
        results[20],
        results[21],
        results[22],
        results[23],
        grad_norm,
        loss_sum,
        loss_count,
    )


def solution(mesh):
    in_specs = (
        P("dp"),
        P("dp"),
        P("dp"),
        P("dp", None),
        P(),
        P(),
        P("tensor", "dp"),
        P("tensor", "dp"),
        P("tensor", "dp"),
        P(None, "dp", "tensor"),
        P(None, "dp", "tensor"),
        P(None, "dp", "tensor"),
        P("tensor", "dp"),
        P("tensor", "dp"),
        P("tensor", "dp"),
        P(None, "dp"),
        P(None, "dp"),
        P(None, "dp"),
        P(None, ("dp", "tensor")),
        P(None, ("dp", "tensor")),
        P(None, ("dp", "tensor")),
        P(("dp", "tensor"), None),
        P(("dp", "tensor"), None),
        P(("dp", "tensor"), None),
        P(None, "dp"),
        P(None, "dp"),
        P(None, "dp"),
        P("tensor", None),
        P("tensor", None),
        P("tensor", None),
    )
    out_specs = (
        P("tensor", "dp"),
        P("tensor", "dp"),
        P("tensor", "dp"),
        P(None, "dp", "tensor"),
        P(None, "dp", "tensor"),
        P(None, "dp", "tensor"),
        P("tensor", "dp"),
        P("tensor", "dp"),
        P("tensor", "dp"),
        P(None, "dp"),
        P(None, "dp"),
        P(None, "dp"),
        P(None, ("dp", "tensor")),
        P(None, ("dp", "tensor")),
        P(None, ("dp", "tensor")),
        P(("dp", "tensor"), None),
        P(("dp", "tensor"), None),
        P(("dp", "tensor"), None),
        P(None, "dp"),
        P(None, "dp"),
        P(None, "dp"),
        P("tensor", None),
        P("tensor", None),
        P("tensor", None),
        P(),
        P(),
        P(),
    )

    def chosen(*arrays):
        token_ids, routes, embedding, router = arrays[0], arrays[3], arrays[6], arrays[9 + 6]
        rows = token_ids.shape[0]
        dp_count, tensor_count = lax.axis_size("dp"), lax.axis_size("tensor")
        single = rows * dp_count <= SEQ and arrays[4].shape[0] == 1
        even = embedding.shape[0] % dp_count == 0
        whole = dp_count * tensor_count % router.shape[0] == 0 and routes.shape[1] == 2
        whole = whole and dp_count % router.shape[0] == 0
        tiles = rows == 128 and arrays[2].shape[0] * dp_count == 128
        return (fast_local if single and even and whole and tiles else local)(*arrays)

    return jax.shard_map(chosen, mesh=mesh, in_specs=in_specs, out_specs=out_specs, check_vma=False)
```

```python
import functools
import math
import types

import jax
import jax.numpy as jnp
from jax.experimental import pallas as pl
from jax.experimental.pallas import tpu as pltpu
from jax import lax
from jax.sharding import PartitionSpec as P

HD = 64
VOCAB = 32000
PIECE = 256
SEQ = 4096
STEP = 10


SMOOTH = 0.1
ZLOSS = 0.0001
NORM_EPS = 1e-06
MAX_NORM = 1.0
BETA1 = 0.9
BETA2 = 0.95
ADAM_EPS = 1e-08
RATES = (0.04, 0.04, 1.0, 0.03, 0.07, 0.035, 1.0, 0.7)
DECAYS = (0.1, 0.1, 0.1, 0.1, 0.1, 0.1, 0.0, 0.0)
NEGATIVE = -1e30
HIGH = lax.Precision.HIGHEST


def merged(shard, axis, combine):
    everything = jax.tree.map(lambda part: lax.all_gather(part, axis), shard)
    initial = jax.tree.map(lambda part: part[0], everything)

    def lap(k, so_far):
        return combine(so_far, jax.tree.map(lambda part: part[k], everything))

    return lax.fori_loop(1, lax.axis_size(axis), lap, initial)


def normed(v, g):
    return v * lax.rsqrt(jnp.mean(v * v, -1, keepdims=True) + NORM_EPS) * g


def norm_back(v, g, upstream):
    unused, pull = jax.vjp(normed, v, g)
    return pull(upstream)


def picture_of(positions, starts, width):
    inside = (positions[:, None] >= starts[None, :]) & (
        positions[:, None] < starts[None, :] + width
    )
    number = jnp.arange(starts.shape[0], dtype=jnp.int32) + 1
    return jnp.sum(inside.astype(jnp.int32) * number[None, :], 1) - 1


def rel_window(relative, query_start, query_count, key_start, key_count, length):
    centre = query_start - key_start + length - 1
    window = lax.dynamic_slice_in_dim(
        relative, centre - key_count + 1, query_count + key_count - 1, 1
    )
    span = query_count + key_count
    wrapped = jnp.concatenate(
        [
            jnp.flip(window[:, :key_count], 1),
            jnp.zeros((window.shape[0], 1), window.dtype),
            jnp.flip(window[:, key_count:], 1),
        ],
        1,
    )
    tiled = jnp.tile(wrapped, (1, query_count))[:, : query_count * (span - 1)]
    return tiled.reshape(window.shape[0], query_count, span - 1)[:, :, :key_count]


def tensor_total(value):
    return lax.psum(value, "tensor")


def route_exchange(value):
    return lax.all_to_all(value, "dp", split_axis=0, concat_axis=0, tiled=True)


def combine_stats(left, right):
    peak = jnp.maximum(left[0], right[0])
    total = left[1] * jnp.exp(left[0] - peak) + right[1] * jnp.exp(right[0] - peak)
    return (peak, total, left[2] + right[2], left[3] + right[3])


def adam_update(weight, first, second, grad, rate, decay):
    first = BETA1 * first + (1 - BETA1) * grad
    second = BETA2 * second + (1 - BETA2) * grad * grad
    fixed_first = first / (1 - BETA1**STEP)
    fixed_second = second / (1 - BETA2**STEP)
    weight = weight - rate * (fixed_first / (jnp.sqrt(fixed_second) + ADAM_EPS) + decay * weight)
    return (weight, first, second)


MESH = pl.DeviceIdType.MESH
DP = "dp"
OUTSIDE = "_hbm"
TENSOR = "tensor"
UPDATE_BYTES = 20 * 1024 * 1024
VMEM_BYTES = 33 * 1024 * 1024
WHOLE = pl.BlockSpec(memory_space=pltpu.VMEM)
DMA = pltpu.SemaphoreType.DMA
F32 = jnp.float32
BF16 = jnp.bfloat16
STRIP = 256


def greet_everyone():
    barrier = pltpu.get_barrier_semaphore()
    tensor = lax.axis_size(TENSOR)
    total = lax.axis_size(DP) * tensor
    here = lax.axis_index(DP) * tensor + lax.axis_index(TENSOR)

    def signal(step, carry):
        other = lax.rem(here + step, total)
        pl.semaphore_signal(
            barrier,
            inc=1,
            device_id={DP: other // tensor, TENSOR: lax.rem(other, tensor)},
            device_id_type=MESH,
        )
        return carry

    lax.fori_loop(1, total, signal, 0)
    return barrier, total - 1


class Move:
    def __init__(self, axis, source, dest, sems, steps=None):
        self.axis, self.count, self.here = axis, lax.axis_size(axis), lax.axis_index(axis)
        self.source, self.dest, self.sems = source, dest, sems
        self.steps = range(1, self.count) if steps is None else steps

    def copy(self, step):
        target = lax.rem(self.here + step, self.count)
        return pltpu.make_async_remote_copy(
            src_ref=self.source(target),
            dst_ref=self.dest.at[self.here],
            send_sem=self.sems.at[0, step],
            recv_sem=self.sems.at[1, step],
            device_id={self.axis: target},
            device_id_type=MESH,
        )

    def start(self):
        for step in self.steps:
            self.copy(step).start()
        return self

    def arrive(self):
        for step in self.steps:
            self.copy(step).wait_recv()

    def finish(self):
        for step in self.steps:
            self.copy(step).wait_send()


def scatter_rows(axis, source, dest, sems):
    height = dest.shape[1]
    return Move(
        axis,
        lambda target: source.at[pl.ds(pl.multiple_of(target * height, height), height)],
        dest,
        sems,
    ).start()


def share_block(axis, dest, sems):
    here = lax.axis_index(axis)
    return Move(axis, lambda target: dest.at[here], dest, sems).start()


class PairGather:
    def __init__(self, buffer, sems):
        self.buffer, self.sems = buffer, sems
        self.count, self.here = lax.axis_size(DP), lax.axis_index(DP)
        self.partner = self.here + 1 - 2 * lax.rem(self.here, 2)
        self.half = self.count // 2

    def copy(self, block, target, slot):
        return pltpu.make_async_remote_copy(
            src_ref=self.buffer.at[block],
            dst_ref=self.buffer.at[block],
            send_sem=self.sems.at[0, slot],
            recv_sem=self.sems.at[1, slot],
            device_id={DP: target},
            device_id_type=MESH,
        )

    def direct(self, step):
        return self.copy(self.here, lax.rem(self.here + 2 * step, self.count), step)

    def onward(self, step):
        block = lax.rem(self.here + self.count - 2 * step, self.count)
        return self.copy(block, self.partner, self.half + step)

    def start(self):
        for step in range(1, self.half):
            self.direct(step).start()
        self.onward(0).start()
        return self

    def forward_one(self, step):
        self.direct(step).wait_recv()
        self.onward(step).start()

    def forward(self):
        for step in range(1, self.half):
            self.forward_one(step)

    def arrive(self):
        for step in range(self.half):
            self.onward(step).wait_recv()

    def finish(self):
        for step in range(1, self.half):
            self.direct(step).wait_send()
        for step in range(self.half):
            self.onward(step).wait_send()


class Relay:
    def __init__(self, buffer, dp_sems, sems):
        self.buffer, self.sems = buffer, sems
        self.here = lax.axis_index(TENSOR)
        self.gather = PairGather(buffer.at[self.here], dp_sems)
        self.far = lax.rem(self.here + 2, 4)
        self.near = self.here + 1 - 2 * lax.rem(self.here, 2)
        self.blocks, self.block = lax.axis_size(DP), lax.axis_index(DP)
        self.half = self.blocks // 2
        partner = self.gather.partner
        own = [lax.rem(self.block + self.blocks - 2 * k, self.blocks) for k in range(self.half)]
        other = [lax.rem(partner + self.blocks - 2 * k, self.blocks) for k in range(self.half)]
        self.order = own + other

    def copy(self, kind, index):
        source = self.far if kind == 2 else self.here
        block = self.order[index]
        return pltpu.make_async_remote_copy(
            src_ref=self.buffer.at[source, block],
            dst_ref=self.buffer.at[source, block],
            send_sem=self.sems.at[0, kind, index],
            recv_sem=self.sems.at[1, kind, index],
            device_id={TENSOR: self.far if kind == 0 else self.near},
            device_id_type=MESH,
        )

    def send(self, index):
        self.copy(0, index).start()
        self.copy(1, index).start()

    def start(self):
        self.gather.start()
        self.send(0)
        return self

    def pass_on(self):
        for step in range(1, self.half):
            self.gather.forward_one(step)
            self.send(step)
        for step in range(self.half):
            self.gather.onward(step).wait_recv()
            self.send(self.half + step)

    def spread(self):
        for index in range(self.blocks):
            self.copy(0, index).wait_recv()
            self.copy(2, index).start()

    def arrive(self):
        for index in range(self.blocks):
            self.copy(1, index).wait_recv()
            self.copy(2, index).wait_recv()

    def finish(self):
        self.gather.finish()
        for index in range(self.blocks):
            for kind in range(3):
                self.copy(kind, index).wait_send()


class Everyone:
    def __init__(self, buffer, sems):
        self.buffer, self.sems = buffer, sems
        self.tensor = lax.axis_size(TENSOR)
        self.total = lax.axis_size(DP) * self.tensor
        self.here = lax.axis_index(DP) * self.tensor + lax.axis_index(TENSOR)

    def copy(self, step):
        other = lax.rem(self.here + step, self.total)
        return pltpu.make_async_remote_copy(
            src_ref=self.buffer.at[self.here],
            dst_ref=self.buffer.at[self.here],
            send_sem=self.sems.at[0, step],
            recv_sem=self.sems.at[1, step],
            device_id={DP: other // self.tensor, TENSOR: lax.rem(other, self.tensor)},
            device_id_type=MESH,
        )

    def each(self, act):
        def one(step, carry):
            act(self.copy(step))
            return carry

        lax.fori_loop(1, self.total, one, 0)

    def start(self):
        self.each(lambda copy: copy.start())
        return self

    def arrive(self):
        self.each(lambda copy: copy.wait_recv())

    def finish(self):
        self.each(lambda copy: copy.wait_send())


def dot_nt(a, b):
    return lax.dot_general(a, b, (((1,), (1,)), ((), ())), preferred_element_type=F32)


def dot_nn(a, b):
    return jnp.dot(a, b, preferred_element_type=F32)


def root_of(v):
    return lax.rsqrt(jnp.mean(v * v, -1, keepdims=True) + NORM_EPS)


def low(v):
    return v.astype(BF16).astype(F32)


def gelu_value(x):
    slope = math.sqrt(2.0 / math.pi)
    return 0.5 * x * (1.0 + jnp.tanh(slope * (x + 0.044715 * (x * x * x))))


def gelu_slope(x):
    slope = math.sqrt(2.0 / math.pi)
    t = jnp.tanh(slope * (x + 0.044715 * (x * x * x)))
    return 0.5 * (1.0 + t) + 0.5 * x * (1.0 - t * t) * (slope * (1.0 + 3 * 0.044715 * x * x))


def lanes(shape):
    return lax.broadcasted_iota(jnp.int32, shape, len(shape) - 1)


def sublanes(shape):
    return lax.broadcasted_iota(jnp.int32, shape, len(shape) - 2)


def tensor_sum(total, buffer, sems):
    here = lax.axis_index(TENSOR)
    buffer[here] = total
    move = share_block(TENSOR, buffer, sems)
    move.arrive()
    total = buffer[0]
    for k in range(1, buffer.shape[0]):
        total = total + buffer[k]
    return total, move


def norm_back_rows(v, g, upstream):
    root = root_of(v)
    scaled = g * upstream
    inner = jnp.sum(scaled * v, -1, keepdims=True)
    back = root * scaled - v * (root * root * root * inner / v.shape[-1])
    return back, jnp.sum(upstream * v * root, 0, keepdims=True)


def merge_stats(parts):
    peak = parts[0][0:1]
    for part in parts[1:]:
        peak = jnp.maximum(peak, part[0:1])
    total = sum(part[1:2] * jnp.exp(part[0:1] - peak) for part in parts)
    target = sum(part[2:3] for part in parts)
    plain = sum(part[3:4] for part in parts)
    return jnp.concatenate([peak, total, target, plain, parts[0][4:8]], 0)


def sum_blocks(ref):
    total = ref[0].astype(F32)
    for k in range(1, ref.shape[0]):
        total = total + ref[k].astype(F32)
    return total


def across(ref, axis):
    return jnp.concatenate([ref[k] for k in range(ref.shape[0])], axis)


def squared(value):
    return jnp.sum(value * value, keepdims=True)


def step_kernel(names, small, weights, experts, vocab_rows, starts, *refs):
    r = types.SimpleNamespace(**dict(zip(names, refs, strict=True)))
    block, here = lax.axis_index(DP), lax.axis_index(TENSOR)
    blocks, tensor = lax.axis_size(DP), lax.axis_size(TENSOR)
    rows = r.own_ids.shape[1]
    every = rows * blocks
    picks = r.own_offsets.shape[1]
    count = picks * blocks
    columns, width = r.proj_weight.shape[1:]
    features = columns * blocks
    heads = width // HD
    share = r.pages.shape[2]
    group = blocks // tensor
    scale = 1.0 / math.sqrt(HD)
    own_rows = pl.ds(pl.multiple_of(block * picks, picks), picks)
    moves = []

    def keep(move):
        moves.append(move)
        return move

    def load(name, sems, k):
        copy = pltpu.make_async_copy(getattr(r, name + OUTSIDE), getattr(r, name), sems.at[k])
        copy.start()
        return copy

    loads = [load(name, r.load_sems, k) for k, name in enumerate(small)]
    greeting = greet_everyone()
    held = [load(name, r.held_sems, k) for k, name in enumerate(weights)]
    proj_load, map_load, table_load, in_load, out_load = held[:5]
    for copy in loads:
        copy.wait()

    ids = r.own_ids[...].astype(F32)
    offset_row = jnp.concatenate(
        [r.own_offsets[...].astype(F32), jnp.zeros((1, rows - picks), F32)], 1
    )
    slot = lanes((rows, rows))
    loss_hot = (sublanes((rows, rows)).astype(F32) == offset_row) & (slot < picks)
    targets = r.own_targets[...]
    upper = targets // 256
    facts = jnp.concatenate(
        [
            upper.astype(F32),
            (targets - upper * 256).astype(F32),
            r.own_routes[...].astype(F32),
            jnp.zeros((4, rows), F32),
        ],
        0,
    )
    facts = dot_nn(facts.astype(BF16), loss_hot.astype(F32).astype(BF16))
    known = jnp.concatenate(
        [
            offset_row,
            facts[0:1] * 256.0 + facts[1:2],
            facts[2:4],
            ids,
            jnp.zeros((3, rows), F32),
        ],
        0,
    )
    r.known[block] = known
    own_router = r.own_router[...]
    own_small = jnp.concatenate(
        [own_router, jnp.zeros((4 - experts, columns), F32), r.own_gains[...], jnp.zeros((1, columns), F32)]
        if experts < 4
        else [own_router, r.own_gains[...], jnp.zeros((1, columns), F32)],
        0,
    )
    r.small[block] = jnp.concatenate([own_small, jnp.zeros((8, 128 - columns), F32)], 1)
    map_load.wait()
    r.maps[here, block] = r.map_weight[...].T.astype(BF16)
    proj_load.wait()
    for s in range(3):
        r.proj[block, :, s * width : (s + 1) * width] = r.proj_weight[s].astype(BF16)
    pl.semaphore_wait(*greeting)
    to_known = keep(share_block(DP, r.known, r.sem_known))
    to_small = keep(share_block(DP, r.small, r.sem_small))
    to_proj = keep(PairGather(r.proj, r.sem_proj).start())

    table_load.wait()
    for k in range(blocks):
        stop = min(vocab_rows, (k + 1) * share)
        span = max(0, stop - k * share)
        if span > 0:
            r.pages[k, :, 0:span] = r.table_weight[:, k * share : stop].astype(BF16)
        if span < share:
            r.pages[k, :, span:share] = jnp.zeros((columns, share - span), BF16)
    r.table[block] = r.pages[block]

    def pages_move(steps):
        return keep(
            Move(DP, lambda target: r.pages.at[target], r.table, r.sem_pages, steps).start()
        )

    to_known.arrive()
    base = (here * vocab_rows).astype(F32)
    for k in range(blocks):
        r.id_row[:, k * rows : (k + 1) * rows] = r.known[k][4:5, :] - base
    chunk = group * rows
    id_high = jnp.floor(r.id_row[...] * (1.0 / STRIP))
    r.id_high[...] = id_high
    r.id_place[...] = r.id_row[...] - id_high * STRIP
    strips_of_page = share // STRIP
    for step in range(1, tensor + 1):
        target = lax.rem(here + step, tensor)
        at = pl.ds(pl.multiple_of(target * chunk, chunk), chunk)
        hot = sublanes((STRIP, chunk)).astype(F32) == r.id_place[:, at]
        hot = hot.astype(F32).astype(BF16)
        number = r.id_high[:, at]

        def look(k, total, hot=hot, number=number):
            strips = jnp.concatenate(
                [r.pages[k, :, n * STRIP : (n + 1) * STRIP] for n in range(strips_of_page)], 0
            )
            found = dot_nn(strips, hot)
            for n in range(strips_of_page):
                mine = number == (k * strips_of_page + n).astype(F32)
                total = total + jnp.where(mine, found[n * columns : (n + 1) * columns], 0.0)
            return total

        found = lax.fori_loop(0, blocks, look, jnp.zeros((columns, chunk), F32))
        for b in range(group):
            r.looked[target, b] = found[:, b * rows : (b + 1) * rows].astype(BF16)
        if step == tensor - 1:
            to_total = keep(
                Move(TENSOR, lambda target: r.looked.at[target], r.first, r.sem_first).start()
            )
    to_proj.forward()
    r.first[here] = r.looked[here]
    to_total.arrive()
    for b in range(group):
        r.streams[here, block, :, b * rows : (b + 1) * rows] = sum_blocks(r.first.at[:, b]).astype(
            BF16
        )
    to_streams = keep(Relay(r.streams, r.sem_stream, r.sem_streams).start())
    to_maps = keep(Relay(r.maps, r.sem_map, r.sem_maps).start())
    to_streams.pass_on()
    to_maps.pass_on()
    pages_now = [pages_move((1, 7, 2, 6) if blocks == 8 else None)]
    to_small.arrive()
    gain_columns = [low(r.small[k].T[0:columns, 4:5]) for k in range(blocks)]
    small_rows = jnp.concatenate([r.small[k][:, 0:columns] for k in range(blocks)], 1)
    gains = low(small_rows)
    r.router[...] = jnp.concatenate(
        [
            jnp.where(sublanes(gains.shape) < experts, gains, 0.0),
            jnp.zeros((128 - gains.shape[0], features), F32),
        ],
        0,
    ).astype(BF16)
    r.gains[...] = gains
    r.id_low[...] = (
        (sublanes((STRIP, every)).astype(F32) == r.id_place[...]).astype(F32).astype(BF16).T
    )

    def column_of(field):
        table = jnp.concatenate(
            [r.known[k][field : field + 1, :] for k in range(blocks)]
            + ([jnp.zeros((8 - blocks, rows), F32)] if blocks < 8 else []),
            0,
        ).T
        return jnp.concatenate([table[0:picks, k : k + 1] for k in range(blocks)], 0)

    offsets, wanted, route_a, route_b = (
        column_of(field).astype(jnp.int32) for field in range(4)
    )
    positions = offsets + sublanes((count, 1)) // picks * rows
    period = 2 * every
    bucket_row = jnp.concatenate(
        [r.own_buckets[...].astype(F32), jnp.zeros((1, 1), F32)], 1
    )
    strips = [bucket_row[:, k * rows : (k + 1) * rows] for k in range(period // rows)]
    mirror = (lanes((rows, rows)) + sublanes((rows, rows)) == rows - 1).astype(F32).astype(BF16)
    strips = dot_nn(jnp.concatenate(strips, 0).astype(BF16), mirror)
    flipped = jnp.concatenate(
        [strips[k : k + 1, :] for k in reversed(range(period // rows))], 1
    )
    spread = jnp.broadcast_to(flipped, (rows, period))
    turned = pltpu.roll(spread, period - rows, 1, stride=1, stride_axis=0).astype(BF16)
    chosen = (lanes((count, rows)) == offsets).astype(F32).astype(BF16)
    r.shifted[...] = dot_nn(chosen, turned).astype(jnp.int32)
    for k in range(blocks):
        begin = rows * (blocks - 1 - k)
        r.bucket[k * picks : (k + 1) * picks, :] = r.shifted[
            k * picks : (k + 1) * picks, begin : begin + every
        ]
    bucket_count = r.position_bias.shape[1]

    def fill(k, carry):
        at = pl.ds(pl.multiple_of(k * picks, picks), picks)
        numbers = r.bucket[at, :]
        terms = [jnp.zeros(numbers.shape, F32)] * heads
        for b in range(bucket_count):
            same = numbers == b
            terms = [jnp.where(same, r.position_bias[h, b], terms[h]) for h in range(heads)]
        for h in range(heads):
            r.bias[h, at, :] = terms[h]
        return carry

    lax.fori_loop(0, blocks, fill, 0)

    def picture_at(place):
        inside = jnp.full(place.shape, -1, jnp.int32)
        for n in range(starts):
            begin = r.picture_start[0, n]
            inside = jnp.where((place >= begin) & (place < begin + PIECE), n, inside)
        return inside

    key_position = lanes((count, every))
    query_picture = picture_at(positions)
    allowed = (key_position <= positions) | (
        (picture_at(lanes((1, every))) == query_picture) & (query_picture >= 0)
    )
    to_streams.spread()
    to_proj.arrive()
    all_proj = across(r.proj, 0)
    key_proj, value_proj = (
        all_proj[:, k * width : (k + 1) * width].astype(F32).T.astype(BF16) for k in (1, 2)
    )
    gain_column = jnp.concatenate(gain_columns, 0)
    back_hot = (key_position == positions).astype(F32).astype(BF16)
    stream = jnp.zeros((count, features), F32)
    normed_loss = jnp.zeros((count, features), F32)
    to_streams.arrive()
    for k in range(tensor):
        part = slice(k * chunk, (k + 1) * chunk)
        low_part = across(r.streams.at[k], 0)
        wide_part = low_part.astype(F32)
        root = lax.rsqrt(jnp.mean(wide_part * wide_part, 0, keepdims=True) + NORM_EPS)
        r.roots[:, part] = root
        normed_in = (wide_part * root * gain_column).astype(BF16)
        r.keys[:, part] = dot_nn(key_proj, normed_in).astype(BF16)
        r.values[:, part] = dot_nn(value_proj, normed_in).astype(BF16)
        stream = stream + dot_nt(back_hot[:, part], low_part)
        normed_loss = normed_loss + dot_nt(back_hot[:, part], normed_in)
    query = dot_nn(normed_loss.astype(BF16), all_proj[:, 0:width]).astype(BF16)
    to_maps.spread()

    def head(value, h):
        return value[:, h * HD : (h + 1) * HD]

    def tall(ref, h):
        return ref[h * HD : (h + 1) * HD, :]

    for h in range(heads):
        raw = dot_nn(head(query, h), tall(r.keys, h)) * scale + r.bias[h]
        raw = jnp.where(allowed, raw, NEGATIVE)
        terms = jnp.exp(raw - jnp.max(raw, -1, keepdims=True))
        r.probs[h] = terms / jnp.sum(terms, -1, keepdims=True)
    attended = jnp.concatenate(
        [dot_nt(r.probs[h].astype(BF16), tall(r.values, h)).astype(BF16) for h in range(heads)],
        1,
    )
    r.heads[here] = attended
    to_heads = keep(share_block(TENSOR, r.heads, r.sem_heads))
    in_load.wait()
    out_load.wait()
    in_low, out_low = r.in_weight[...].astype(BF16), r.out_weight[...].astype(BF16)
    to_maps.arrive()
    to_heads.arrive()

    middle = stream
    for k in range(tensor):
        full = jnp.concatenate([r.maps[k, i] for i in range(blocks)], 0)
        middle = middle + dot_nt(r.heads[k], full)
    r.middle[...] = middle
    gain_middle, gain_final = r.gains[5:6, :], r.gains[6:7, :]
    normed_mid = (middle * root_of(middle) * gain_middle).astype(BF16)
    inner = dot_nn(normed_mid, in_low)
    active = gelu_value(inner).astype(BF16)
    r.piece[...] = dot_nn(active, out_low).astype(BF16)
    to_rows = keep(scatter_rows(DP, r.piece, r.arrived, r.sem_piece))
    router_logits = dot_nt(normed_mid, r.router[...])
    lane = lanes(router_logits.shape)
    hot_a, hot_b = lane == route_a, lane == route_b
    logit_a = jnp.sum(jnp.where(hot_a, router_logits, 0.0), 1, keepdims=True)
    logit_b = jnp.sum(jnp.where(hot_b, router_logits, 0.0), 1, keepdims=True)
    logit_top = jnp.maximum(logit_a, logit_b)
    gate_a, gate_b = jnp.exp(logit_a - logit_top), jnp.exp(logit_b - logit_top)
    both = gate_a + gate_b
    r.gates[...] = jnp.where(hot_a, gate_a / both, 0.0) + jnp.where(hot_b, gate_b / both, 0.0)
    own_gates = r.gates[own_rows, :]
    own_middle = r.middle[own_rows, :]
    if blocks == 8:
        pages_now.append(pages_move((3,)))
    r.arrived[block] = r.piece[own_rows, :]
    to_rows.arrive()
    depth = blocks // experts
    mixed = jnp.zeros((picks, features), F32)
    for e in range(experts):
        part = r.arrived[e * depth].astype(F32)
        for k in range(1, depth):
            part = part + r.arrived[e * depth + k].astype(F32)
        mixed = mixed + own_gates[:, e : e + 1] * part
    mixed, to_sum = tensor_sum(mixed, r.summed, r.sem_summed)
    keep(to_sum)
    own_final = own_middle + mixed
    r.final[block] = (own_final * root_of(own_final) * gain_final).astype(BF16)
    to_final = keep(share_block(DP, r.final, r.sem_final))
    if blocks == 8:
        pages_now.append(pages_move((5, 4)))
    to_final.arrive()
    for move in pages_now:
        move.arrive()

    out = across(r.final, 0)
    table = across(r.table, 0)
    logits = dot_nn(out, table)
    slot = lanes(logits.shape) + block * share
    logits = jnp.where(slot < vocab_rows, logits, NEGATIVE)
    hit = slot == wanted - here * vocab_rows
    local_top = jnp.max(logits, -1, keepdims=True)
    local_stats = (
        local_top,
        jnp.sum(jnp.exp(logits - local_top), -1, keepdims=True),
        jnp.sum(jnp.where(hit & (slot < vocab_rows), logits, 0.0), -1, keepdims=True),
        jnp.sum(jnp.where(slot < vocab_rows, logits, 0.0), -1, keepdims=True),
    )
    packed = jnp.zeros((count, 128), F32)
    for k, column in enumerate(local_stats):
        packed = jnp.where(lane == k, column, packed)
    r.stats_a[here] = packed.T[0:8, :]
    to_stats = keep(share_block(TENSOR, r.stats_a, r.sem_stats_a))
    to_stats.arrive()
    r.stats_b[block] = merge_stats([r.stats_a[k] for k in range(tensor)])
    to_stats = keep(share_block(DP, r.stats_b, r.sem_stats_b))
    weight = (query_picture < 0).astype(F32)
    weight_row = jnp.where(lane == 0, weight, 0.0).T[0:1, :]
    to_stats.arrive()
    stats = merge_stats([r.stats_b[k] for k in range(blocks)])
    log_total = stats[0:1] + jnp.log(stats[1:2])
    per_row = (
        log_total
        - (1 - SMOOTH) * stats[2:3]
        - SMOOTH * stats[3:4] / VOCAB
        + ZLOSS * log_total * log_total
    )
    loss_sum = jnp.sum(weight_row * per_row, keepdims=True)
    loss_count = jnp.sum(weight_row, keepdims=True)
    total_column = jnp.where(sublanes((128, count)) == 0, log_total, 0.0).T[:, 0:1]
    d_logits = weight * (
        (1 + 2 * ZLOSS * total_column) * jnp.exp(logits - total_column)
        - jnp.where(hit, 1 - SMOOTH, 0.0)
        - SMOOTH / VOCAB
    )
    d_logits = jnp.where(slot < vocab_rows, d_logits, 0.0).astype(BF16)
    r.d_logits_parts = [r.d_logits.at[k] for k in range(r.d_logits.shape[0])]
    piece_rows = r.d_logits.shape[2]
    for k, part in enumerate(r.d_logits_parts):
        part[block] = d_logits[k * piece_rows : (k + 1) * piece_rows]
    logit_moves = [
        keep(PairGather(part, r.sem_logits.at[k])) for k, part in enumerate(r.d_logits_parts)
    ]
    r.sent[...] = dot_nt(d_logits, table).astype(BF16)
    to_rows = keep(scatter_rows(DP, r.sent, r.arrived_b, r.sem_sent))
    r.arrived_b[block] = r.sent[own_rows, :]
    to_rows.arrive()
    logit_moves[0].start()
    d_normed, to_sum = tensor_sum(sum_blocks(r.arrived_b), r.summed_b, r.sem_summed_b)
    keep(to_sum)
    d_final, grad_final = norm_back_rows(own_final, gain_final, d_normed)
    r.d_final[block] = d_final.astype(BF16)
    to_final = keep(share_block(DP, r.d_final, r.sem_d_final))
    to_final.arrive()
    logit_moves[0].forward()
    logit_moves[1].start()
    upstream = across(r.d_final, 0).astype(F32)
    expert = block // depth
    gate = jnp.sum(jnp.where(lane == expert, r.gates[...], 0.0), 1, keepdims=True)
    d_piece = (gate * upstream).astype(BF16)
    d_inner = (dot_nt(d_piece, out_low) * gelu_slope(inner)).astype(BF16)
    r.wide[:, 0:features] = dot_nt(d_inner, in_low).astype(BF16)
    gate_part = jnp.sum(upstream * r.piece[...].astype(F32), 1, keepdims=True)
    high = low(gate_part)
    r.wide[:, features:] = jnp.where(
        lane == expert, high, jnp.where(lane == expert + 64, gate_part - high, 0.0)
    ).astype(BF16)
    to_rows = keep(scatter_rows(DP, r.wide, r.arrived_c, r.sem_wide))
    r.arrived_c[block] = r.wide[own_rows, :]
    grad_out = dot_nn(active.T, d_piece)
    grad_in = dot_nn(normed_mid.T, d_inner)
    r.grad_out[...] = grad_out
    r.grad_in[...] = grad_in
    squares = squared(grad_out) + squared(grad_in)
    to_rows.arrive()
    logit_moves[1].forward()
    logit_moves[2].start()
    total, to_sum = tensor_sum(sum_blocks(r.arrived_c), r.summed_c, r.sem_summed_c)
    keep(to_sum)
    tail = total[:, features:]
    d_gates = tail + pltpu.roll(tail, 64, 1)
    own_known = known.T[0:picks].astype(jnp.int32)
    slim = lanes(tail.shape)
    named = (slim == own_known[:, 2:3]) | (slim == own_known[:, 3:4])
    d_gates = jnp.where(named, d_gates, 0.0)
    mean = jnp.sum(own_gates * d_gates, 1, keepdims=True)
    d_router = jnp.where(named, own_gates * (d_gates - mean), 0.0).astype(BF16)
    d_normed_mid = total[:, 0:features] + dot_nn(d_router, r.router[...])
    d_from_mid, grad_middle = norm_back_rows(own_middle, gain_middle, d_normed_mid)
    r.d_middle[block, :, 0:features] = (d_final + d_from_mid).astype(BF16)
    r.d_middle[block, :, features:] = d_router
    r.gain_parts[block, 0:1, :] = grad_middle
    r.gain_parts[block, 1:2, :] = grad_final
    to_middle = keep(share_block(DP, r.d_middle, r.sem_d_middle))
    to_gains = keep(share_block(DP, r.gain_parts, r.sem_gains))
    logit_moves[2].forward()
    logit_moves[3].start()
    stream_c = jnp.concatenate([r.streams[k, block] for k in range(tensor)], 1).astype(F32)
    roots = r.roots[...]
    gain_column = low(r.small[block].T[0:columns, 4:5])
    normed_c = (stream_c * roots * gain_column).astype(BF16)
    normed_loss = dot_nt(normed_c, back_hot).astype(BF16)
    query_wide = dot_nn(query.T, back_hot)
    to_middle.arrive()

    d_middle = across(r.d_middle, 0)
    d_attn = d_middle[:, 0:features]
    own_map = jnp.concatenate([r.maps[here, i] for i in range(blocks)], 0)
    d_attended = dot_nn(d_attn, own_map).astype(BF16)
    d_query = []
    for h in range(heads):
        soft = r.probs[h]
        d_head = head(d_attended, h)
        d_probs = dot_nn(d_head, tall(r.values, h))
        d_scores = soft * (d_probs - jnp.sum(soft * d_probs, -1, keepdims=True))
        d_scores = d_scores.astype(BF16)
        r.bias[h] = d_scores.astype(F32)
        d_query.append((dot_nt(d_scores, tall(r.keys, h)) * scale).astype(BF16))
        r.d_keys[h * HD : (h + 1) * HD, :] = (
            dot_nn(head(query, h).T, d_scores) * scale
        ).astype(BF16)
        r.d_values[h * HD : (h + 1) * HD, :] = dot_nn(d_head.T, soft.astype(BF16)).astype(BF16)
    d_query = jnp.concatenate(d_query, 1)
    d_query_wide = dot_nn(d_query.T, back_hot).astype(BF16)
    own_proj = r.proj[block]
    d_columns = (
        dot_nn(own_proj[:, 0:width], d_query_wide)
        + dot_nn(own_proj[:, width : 2 * width], r.d_keys[...])
        + dot_nn(own_proj[:, 2 * width :], r.d_values[...])
    )
    inner_row = jnp.sum(
        d_query_wide.astype(F32) * query_wide
        + r.d_keys[...].astype(F32) * r.keys[...].astype(F32)
        + r.d_values[...].astype(F32) * r.values[...].astype(F32),
        0,
        keepdims=True,
    )
    inner_high = low(inner_row)
    extra = sublanes((16, every))
    r.part[0:columns, :] = d_columns.astype(BF16)
    r.part[columns:, :] = jnp.where(
        extra == 0, inner_high, jnp.where(extra == 1, inner_row - inner_high, 0.0)
    ).astype(BF16)
    to_part = keep(
        Move(
            TENSOR,
            lambda target: r.part.at[:, pl.ds(pl.multiple_of(target * chunk, chunk), chunk)],
            r.part_in,
            r.sem_part,
        ).start()
    )
    r.part_in[here] = r.part[:, pl.ds(pl.multiple_of(here * chunk, chunk), chunk)]
    grad_proj = (
        dot_nn(normed_loss, d_query),
        dot_nt(normed_c, r.d_keys[...]),
        dot_nt(normed_c, r.d_values[...]),
    )
    for s in range(3):
        r.grad_proj[s] = grad_proj[s]
        squares = squares + squared(grad_proj[s])
    to_part.arrive()
    r.part_all[here] = sum_blocks(r.part_in).astype(BF16)
    to_parts = keep(share_block(TENSOR, r.part_all, r.sem_part_all))
    r.bias_rows[...] = jnp.zeros(r.bias_rows.shape, F32)

    def collect(k, carry):
        at = pl.ds(pl.multiple_of(k * picks, picks), picks)
        numbers = r.bucket[at, :]
        parts = [r.bias[h, at, :] for h in range(heads)]
        for b in range(bucket_count):
            same = numbers == b
            for h in range(heads):
                kept = jnp.where(same, parts[h], 0.0)
                kept = kept[0:8] + kept[8:16]
                narrow = kept[:, 0:128]
                for c in range(1, every // 128):
                    narrow = narrow + kept[:, c * 128 : (c + 1) * 128]
                r.bias_rows[h, b] += narrow
        return carry

    lax.fori_loop(0, count // picks, collect, 0)
    grad_bias = jnp.sum(r.bias_rows[...], 2)
    r.grad_bias[...] = grad_bias
    grad_bias = jnp.sum(grad_bias, -1, keepdims=True)
    squares = squares + jnp.sum(grad_bias * grad_bias, keepdims=True)[0] / blocks
    pick_own = lanes((columns, features)) == sublanes((columns, features)) + block * columns
    pick_own = pick_own.astype(F32).astype(BF16)
    d_attn_t = dot_nt(pick_own, d_attn).astype(BF16)
    out_t = dot_nt(pick_own, out).astype(BF16)
    middle_t = dot_nt(pick_own, normed_mid).astype(BF16)
    grad_map = dot_nt(attended.T, d_attn_t)
    r.grad_map[...] = grad_map
    squares = squares + squared(grad_map)
    grad_router = dot_nt(d_middle[:, features:].T, middle_t)[0:8]
    residual = dot_nn(d_attn_t, back_hot)
    logit_moves[3].forward()
    to_gains.arrive()
    gain_sum = r.gain_parts[0]
    for k in range(1, blocks):
        gain_sum = gain_sum + r.gain_parts[k]
    gain_sum = jnp.concatenate([gain_sum, jnp.zeros((6, features), F32)], 0)
    gain_sum = pltpu.roll(gain_sum, lax.rem(features - block * columns, features), 1)
    to_parts.arrive()
    parts = across(r.part_all, 1).astype(F32)
    d_columns = parts[0:columns]
    inner_row = parts[columns : columns + 1] + parts[columns + 1 : columns + 2]
    grad_first = jnp.sum(d_columns * stream_c * roots, 1, keepdims=True)
    grad_first = jnp.broadcast_to(grad_first, (columns, 128)).T[0:1, :]
    small = jnp.concatenate(
        [
            grad_router[0:4],
            grad_first,
            gain_sum[0:2, 0:columns],
            jnp.zeros((1, columns), F32),
        ],
        0,
    )
    r.grad_small[:, 0:columns] = small
    r.grad_small[:, columns:] = jnp.zeros((8, 128 - columns), F32)
    squares = squares + squared(small) / tensor
    d_stream = (
        roots * gain_column * d_columns
        - stream_c * (roots * roots * inner_row / features)
        + residual
    )
    d_high = d_stream.astype(BF16)
    d_low = (d_stream - d_high.astype(F32)).astype(BF16)
    low_half = d_stream.astype(BF16)
    full = vocab_rows // STRIP
    ends = [(k, min(STRIP, vocab_rows - k * STRIP)) for k in range(full - full % 4, -(-vocab_rows // STRIP))]

    def strip_mask(number):
        return (r.id_high[...] == number).astype(F32).astype(BF16)

    def scatter_four(k, carry):
        masked = [low_half * strip_mask((k * 4 + n).astype(F32)) for n in range(4)]
        found = dot_nn(jnp.concatenate(masked, 0), r.id_low[...])
        begin = pl.multiple_of(k * 4 * STRIP, STRIP)
        for n in range(4):
            r.grad_table[:, pl.ds(begin + n * STRIP, STRIP)] = found[
                n * columns : (n + 1) * columns
            ]
        return carry

    lax.fori_loop(0, full // 4, scatter_four, 0)
    masked = jnp.concatenate([low_half * strip_mask(float(k)) for k, size in ends], 0)
    found = dot_nn(masked, r.id_low[...])
    for n, (k, size) in enumerate(ends):
        r.grad_table[:, k * STRIP : k * STRIP + size] = found[
            n * columns : (n + 1) * columns, 0:size
        ]
    for move in logit_moves:
        move.arrive()

    def page_strips(k, total):
        begin = pl.multiple_of(k * share, share)
        return total + add_page(k, pl.ds(begin, share))

    def add_page(k, where, size=share):
        page = jnp.concatenate([part[k] for part in r.d_logits_parts], 0)
        value = r.grad_table[:, where] + dot_nn(out_t, page)[:, 0:size]
        r.grad_table[:, where] = value
        return squared(value)

    whole = vocab_rows // share
    squares = squares + lax.fori_loop(0, whole, page_strips, jnp.zeros((1, 1), F32))
    if vocab_rows > whole * share:
        squares = squares + add_page(
            whole, slice(whole * share, vocab_rows), vocab_rows - whole * share
        )
    r.squares[block * tensor + here] = jnp.broadcast_to(squares, (1, 128))
    to_squares = keep(Everyone(r.squares, r.sem_squares).start())
    to_squares.arrive()
    norm = jnp.sqrt(sum_blocks(r.squares))
    r.norm[...] = norm[:, 0:1]
    r.clip[...] = (MAX_NORM / jnp.maximum(norm, MAX_NORM))[:, 0:1]
    r.loss_sum[...] = loss_sum
    r.loss_count[...] = loss_count
    for copy in held[5:]:
        copy.wait()
    for move in moves:
        move.finish()


def run_step(blocks, tensor, experts, small, held, scalars):
    rows = small["own_ids"].shape[1]
    every = rows * blocks
    picks = small["own_offsets"].shape[1]
    count = picks * blocks
    columns, width = held["proj_weight"].shape[1:]
    features = columns * blocks
    hidden = held["in_weight"].shape[1]
    vocab_rows = held["table_weight"].shape[1]
    heads, bucket_count = scalars["position_bias"].shape
    share = -(-vocab_rows // (blocks * STRIP)) * STRIP
    group = blocks // tensor
    chunk = group * rows
    wide = features + 128
    outputs = dict(
        grad_table=(columns, vocab_rows),
        grad_proj=(3, columns, width),
        grad_map=(width, columns),
        grad_small=(8, 128),
        grad_in=(features, hidden),
        grad_out=(hidden, features),
        grad_bias=(heads, bucket_count, 128),
        norm=(1, 1),
        clip=(1, 1),
        loss_sum=(1, 1),
        loss_count=(1, 1),
    )
    scratch = dict(
        known=((blocks, 8, rows), F32),
        small=((blocks, 8, 128), F32),
        proj=((blocks, columns, 3 * width), BF16),
        maps=((tensor, blocks, columns, width), BF16),
        pages=((blocks, columns, share), BF16),
        table=((blocks, columns, share), BF16),
        id_row=((1, every), F32),
        id_high=((1, every), F32),
        id_place=((1, every), F32),
        id_low=((every, STRIP), BF16),
        looked=((tensor, group, columns, rows), BF16),
        first=((tensor, group, columns, rows), BF16),
        router=((128, features), BF16),
        gains=((8, features), F32),
        roots=((1, every), F32),
        streams=((tensor, blocks, columns, chunk), BF16),
        shifted=((count, 2 * every), jnp.int32),
        bucket=((count, every), jnp.int32),
        bias=((heads, count, every), F32),
        keys=((width, every), BF16),
        values=((width, every), BF16),
        probs=((heads, count, every), F32),
        heads=((tensor, count, width), BF16),
        middle=((count, features), F32),
        piece=((count, features), BF16),
        gates=((count, 128), F32),
        arrived=((blocks, picks, features), BF16),
        summed=((tensor, picks, features), F32),
        final=((blocks, picks, features), BF16),
        stats_a=((tensor, 8, 128), F32),
        stats_b=((blocks, 8, 128), F32),
        d_logits=((4, blocks, count // 4, share), BF16),
        sent=((count, features), BF16),
        arrived_b=((blocks, picks, features), BF16),
        summed_b=((tensor, picks, features), F32),
        d_final=((blocks, picks, features), BF16),
        wide=((count, wide), BF16),
        arrived_c=((blocks, picks, wide), BF16),
        summed_c=((tensor, picks, wide), F32),
        d_middle=((blocks, picks, wide), BF16),
        gain_parts=((blocks, 2, features), F32),
        d_keys=((width, every), BF16),
        d_values=((width, every), BF16),
        part=((columns + 16, every), BF16),
        part_in=((tensor, columns + 16, chunk), BF16),
        part_all=((tensor, columns + 16, chunk), BF16),
        bias_rows=((heads, bucket_count, 8, 128), F32),
        squares=((blocks * tensor, 1, 128), F32),
    )
    scratch.update({name: (array.shape, array.dtype) for name, array in small.items()})
    outputs.update({name: array.shape for name, array in held.items()})
    dp, ten = (2, blocks), (2, tensor)
    sems = dict(
        load_sems=(len(small),),
        held_sems=(len(held),),
        sem_squares=(2, blocks * tensor),
        sem_logits=(4, 2, blocks),
        sem_known=dp,
        sem_small=dp,
        sem_proj=dp,
        sem_map=dp,
        sem_pages=dp,
        sem_piece=dp,
        sem_final=dp,
        sem_stats_b=dp,
        sem_sent=dp,
        sem_d_final=dp,
        sem_wide=dp,
        sem_d_middle=dp,
        sem_gains=dp,
        sem_first=ten,
        sem_stream=dp,
        sem_streams=(2, 3, blocks),
        sem_maps=(2, 3, blocks),
        sem_heads=ten,
        sem_summed=ten,
        sem_stats_a=ten,
        sem_summed_b=ten,
        sem_summed_c=ten,
        sem_part=ten,
        sem_part_all=ten,
    )
    copied = {**small, **held}
    names = tuple(name + OUTSIDE for name in copied) + tuple(scalars)
    names += tuple(outputs) + tuple(scratch) + tuple(sems)
    starts = scalars["picture_start"].shape[1]
    results = pl.pallas_call(
        functools.partial(
            step_kernel, names, tuple(small), tuple(held), experts, vocab_rows, starts
        ),
        out_shape=[
            jax.ShapeDtypeStruct(shape, F32) if shape == (1, 1) else pltpu.VMEM(shape, F32)
            for shape in outputs.values()
        ],
        in_specs=[pl.BlockSpec(memory_space=pltpu.HBM)] * len(copied)
        + [pl.BlockSpec(memory_space=pltpu.SMEM)] * len(scalars),
        out_specs=[WHOLE] * len(outputs),
        scratch_shapes=[pltpu.VMEM(*spec) for spec in scratch.values()]
        + [DMA(shape) for shape in sems.values()],
        compiler_params=pltpu.CompilerParams(
            collective_id=0, has_side_effects=True, vmem_limit_bytes=VMEM_BYTES
        ),
        name="training_step",
    )(*copied.values(), *scalars.values())
    return dict(zip(outputs, results))


def update_piece(weight, first, second, grad, rate, decay):
    first = BETA1 * first + (1 - BETA1) * grad
    second = BETA2 * second + (1 - BETA2) * (grad * grad)
    spread = second * lax.rsqrt(second) * math.sqrt(1 / (1 - BETA2**STEP)) + ADAM_EPS
    step = first / spread
    return weight * (1 - rate * decay) - (rate / (1 - BETA1**STEP)) * step, first, second


def update_kernel(jobs, clip, *refs):
    grads, refs = refs[: len(jobs)], refs[len(jobs) :]
    total = 3 * len(jobs)
    olds, outs, news, done = refs[:total], refs[total : 2 * total], refs[2 * total : -1], refs[-1]
    factor = clip[0, 0]
    copies = []
    for index, (height, rate, decay, begin, reduced) in enumerate(jobs):
        trio = slice(3 * index, 3 * index + 3)
        whole = news[3 * index].shape[0]
        for piece in range(0, whole, height):
            rows = slice(piece, piece + height)
            if reduced:
                change = jnp.sum(grads[index][...], -1)
            elif begin is not None:
                change = grads[index][begin : begin + whole, 0 : news[3 * index].shape[1]]
            else:
                change = grads[index][rows]
            values = update_piece(
                *(ref[rows] for ref in olds[trio]), factor * change, rate, decay
            )
            for which, value in enumerate(values):
                new, out = news[3 * index + which], outs[3 * index + which]
                new[rows] = value
                part = pl.ds(piece, height)
                copy = pltpu.make_async_copy(new.at[part], out.at[part], done.at[len(copies)])
                copy.start()
                copies.append(copy)
    for copy in copies:
        copy.wait()


def run_update(clip, jobs, grads, olds):
    shapes = [old.shape for old in olds]
    pieces = sum(3 * shapes[3 * k][0] // job[0] for k, job in enumerate(jobs))
    results = pl.pallas_call(
        functools.partial(update_kernel, jobs),
        out_shape=[jax.ShapeDtypeStruct(shape, F32) for shape in shapes],
        in_specs=[pl.BlockSpec(memory_space=pltpu.SMEM)] + [WHOLE] * (len(grads) + len(olds)),
        out_specs=[pl.BlockSpec(memory_space=pltpu.HBM)] * len(shapes),
        scratch_shapes=[pltpu.VMEM(shape, F32) for shape in shapes] + [DMA((pieces,))],
        compiler_params=pltpu.CompilerParams(vmem_limit_bytes=UPDATE_BYTES),
        name="update",
    )(clip, *grads, *olds)
    return [results[3 * k : 3 * k + 3] for k in range(len(jobs))]


def fast_local(
    token_ids,
    targets,
    loss_offsets,
    routes,
    picture_start,
    buckets,
    embedding,
    embedding_first,
    embedding_second,
    attn_proj,
    attn_proj_first,
    attn_proj_second,
    out_proj,
    out_proj_first,
    out_proj_second,
    router,
    router_first,
    router_second,
    expert_in,
    expert_in_first,
    expert_in_second,
    expert_out,
    expert_out_first,
    expert_out_second,
    norm_gains,
    norm_gains_first,
    norm_gains_second,
    position_bias,
    position_bias_first,
    position_bias_second,
):
    dp_count = lax.axis_size("dp")
    tensor_count = lax.axis_size("tensor")
    experts = router.shape[0]
    small = dict(
        own_ids=token_ids[None, :],
        own_targets=targets[None, :],
        own_offsets=loss_offsets[None, :],
        own_routes=routes.T,
        own_buckets=buckets[None, :],
        own_router=router,
        own_gains=norm_gains,
    )
    held = dict(
        proj_weight=attn_proj,
        map_weight=out_proj,
        table_weight=embedding.T,
        in_weight=expert_in,
        out_weight=expert_out,
        table_first=embedding_first.T,
        table_second=embedding_second.T,
        in_first=expert_in_first,
        in_second=expert_in_second,
        out_first=expert_out_first,
        out_second=expert_out_second,
        proj_first=attn_proj_first,
        proj_second=attn_proj_second,
        map_first=out_proj_first,
        map_second=out_proj_second,
    )
    scalars = dict(position_bias=position_bias, picture_start=picture_start)
    g = types.SimpleNamespace(**run_step(dp_count, tensor_count, experts, small, held, scalars))
    kinds = (
        (8, 0, None, False),
        (expert_in.shape[0] // 8, 4, None, False),
        (expert_out.shape[0] // 8, 5, None, False),
        (1, 1, None, False),
        (out_proj.shape[0], 2, None, False),
        (experts, 3, 0, False),
        (3, 6, 4, False),
        (position_bias.shape[0], 7, None, True),
    )
    jobs = tuple(
        (height, RATES[k], DECAYS[k], begin, reduced) for height, k, begin, reduced in kinds
    )
    grads = (g.grad_table, g.grad_in, g.grad_out, g.grad_proj, g.grad_map)
    grads += (g.grad_small, g.grad_small, g.grad_bias)
    olds = (g.table_weight, g.table_first, g.table_second, g.in_weight, g.in_first, g.in_second)
    olds += (g.out_weight, g.out_first, g.out_second, g.proj_weight, g.proj_first, g.proj_second)
    olds += (g.map_weight, g.map_first, g.map_second, router, router_first, router_second)
    olds += (norm_gains, norm_gains_first, norm_gains_second)
    olds += (position_bias, position_bias_first, position_bias_second)
    new = run_update(g.clip, jobs, grads, olds)
    results = [value.T for value in new[0]]
    for k in (3, 4, 5, 1, 2, 6, 7):
        results.extend(new[k])
    grad_norm, loss_sum, loss_count = (
        value.reshape(()) for value in (g.norm, g.loss_sum, g.loss_count)
    )
    return (*results, grad_norm, loss_sum, loss_count)


def local(
    token_ids,
    targets,
    loss_offsets,
    routes,
    picture_start,
    buckets,
    embedding,
    embedding_first,
    embedding_second,
    attn_proj,
    attn_proj_first,
    attn_proj_second,
    out_proj,
    out_proj_first,
    out_proj_second,
    router,
    router_first,
    router_second,
    expert_in,
    expert_in_first,
    expert_in_second,
    expert_out,
    expert_out_first,
    expert_out_second,
    norm_gains,
    norm_gains_first,
    norm_gains_second,
    position_bias,
    position_bias_first,
    position_bias_second,
):
    f32 = jnp.float32
    bf16 = jnp.bfloat16
    dp_count = lax.axis_size("dp")
    tensor_count = lax.axis_size("tensor")
    dp_place = lax.axis_index("dp")
    tensor_place = lax.axis_index("tensor")
    rows = token_ids.shape[0]
    every = rows * dp_count
    length = min(SEQ, every)
    seqs = every // length
    sub = rows // seqs
    scale = 1.0 / math.sqrt(HD)
    vocab_rows = embedding.shape[0]
    table, projection, output_map, router_full, gain_full = (
        lax.all_gather(embedding.astype(bf16), "dp", axis=1, tiled=True),
        lax.all_gather(attn_proj.astype(bf16), "dp", axis=1, tiled=True),
        lax.all_gather(out_proj.astype(bf16), "dp", axis=1, tiled=True),
        lax.all_gather(router.astype(bf16), "dp", axis=1, tiled=True),
        lax.all_gather(norm_gains.astype(bf16), "dp", axis=1, tiled=True),
    )
    gain = gain_full.astype(f32)
    features = table.shape[1]
    offset = token_ids - tensor_place * vocab_rows
    owned = (offset >= 0) & (offset < vocab_rows)
    offset = jnp.clip(offset, 0, vocab_rows - 1)
    looked = jnp.take(table, offset, axis=0).astype(f32)
    stream_in = tensor_total(jnp.where(owned[:, None], looked, 0.0))
    pos_here = dp_place * sub + jnp.arange(sub, dtype=jnp.int32)
    seq_positions = jnp.arange(length, dtype=jnp.int32)
    picture_all = jax.vmap(lambda starts: picture_of(seq_positions, starts, PIECE))(picture_start)
    picture_here = lax.dynamic_slice_in_dim(picture_all, dp_place * sub, sub, 1)
    bucket_ids = jnp.arange(position_bias.shape[1], dtype=jnp.int32)
    bucket_hot = (bucket_ids[:, None] == buckets[None, :]).astype(f32)
    relative = jnp.dot(position_bias, bucket_hot, precision=HIGH)
    normed_in = normed(stream_in, gain[0]).astype(bf16)
    fresh = jnp.einsum("td,sde->ste", normed_in, projection, preferred_element_type=f32).astype(
        bf16
    )
    width = fresh.shape[2]
    heads = width // HD
    keys_local = fresh[1].reshape(seqs, sub, width)
    values_local = fresh[2].reshape(seqs, sub, width)
    query_heads = fresh[0].reshape(seqs, sub, heads, HD)
    keys_all, values_all = (
        lax.all_gather(keys_local, "dp", axis=1, tiled=True),
        lax.all_gather(values_local, "dp", axis=1, tiled=True),
    )
    block = min(512, length)
    blocks = length // block
    block_ids = jnp.arange(blocks, dtype=jnp.int32)

    def pair_scores(q_heads, q_pos, q_pic, k_heads, k_pos, k_pic, bias):
        raw = (
            jnp.einsum("sqhd,skhd->shqk", q_heads, k_heads, preferred_element_type=f32) * scale
            + bias[None]
        )
        allowed = (k_pos[None, :] <= q_pos[:, None])[None] | (
            k_pic[:, None, :] == q_pic[:, :, None]
        ) & (q_pic[:, :, None] >= 0)
        return jnp.where(allowed[:, None], raw, NEGATIVE)

    def key_slice(source, start):
        return lax.dynamic_slice_in_dim(source, start, block, 1).reshape(seqs, block, heads, HD)

    def own_bias(start):
        return rel_window(relative, dp_place * sub, sub, start, block, length)

    def fwd_scores(index, key_source):
        start = index * block
        key_pos = start + jnp.arange(block, dtype=jnp.int32)
        return pair_scores(
            query_heads,
            pos_here,
            picture_here,
            key_slice(key_source, start),
            key_pos,
            lax.dynamic_slice_in_dim(picture_all, start, block, 1),
            own_bias(start),
        )

    def max_step(carry, index):
        top, total = carry
        s = fwd_scores(index, keys_all)
        new_top = jnp.maximum(top, jnp.max(s, -1))
        terms = jnp.where(s > 0.5 * NEGATIVE, jnp.exp(s - new_top[..., None]), 0.0)
        total = total * jnp.exp(top - new_top) + jnp.sum(terms, -1)
        return ((new_top, total), None)

    start_top = jnp.full((seqs, heads, sub), NEGATIVE, f32)
    (top, total), unused = lax.scan(
        max_step, (start_top, jnp.zeros((seqs, heads, sub), f32)), block_ids
    )
    log_total = top + jnp.log(total)

    def out_step(accum, index):
        s = fwd_scores(index, keys_all)
        probs = jnp.exp(s - log_total[..., None]).astype(bf16)
        value_heads = key_slice(values_all, index * block)
        return (
            accum + jnp.einsum("shqk,skhd->sqhd", probs, value_heads, preferred_element_type=f32),
            None,
        )

    attended, unused = lax.scan(out_step, jnp.zeros((seqs, sub, heads, HD), f32), block_ids)
    attended_low = attended.reshape(rows, width).astype(bf16)
    stream_mid = stream_in + tensor_total(
        jnp.dot(attended_low, output_map, preferred_element_type=f32)
    )
    normed_mid = normed(stream_mid, gain[1]).astype(bf16)
    router_logits = jnp.dot(normed_mid, router_full.T, preferred_element_type=f32)
    gates = jax.nn.softmax(jnp.take_along_axis(router_logits, routes, 1), -1)
    experts = router_full.shape[0]
    top_k = routes.shape[1]
    capacity = 2 * rows * top_k // experts
    flat = routes.reshape(-1)
    owner = jnp.arange(rows * top_k, dtype=jnp.int32) // top_k
    hits = (flat[:, None] == jnp.arange(experts, dtype=jnp.int32)[None, :]).astype(jnp.int32)
    slot = jnp.sum(jnp.cumsum(hits, 0) * hits, 1) - 1
    first_row = 2 * flat * capacity + slot

    def pack(values):
        buffer = jnp.zeros((experts, capacity, features), bf16).at[flat, slot].set(values)
        return jnp.repeat(buffer, 2, axis=0).reshape(2 * experts * capacity, features)

    def unpack(values):
        return values[first_row].astype(f32) + values[first_row + capacity].astype(f32)

    in_low = expert_in.astype(bf16)
    out_low = expert_out.astype(bf16)
    arrived = route_exchange(pack(normed_mid[owner]))
    inner = jnp.dot(arrived, in_low, preferred_element_type=f32)
    active = jax.nn.gelu(inner).astype(bf16)
    produced = jnp.dot(active, out_low, preferred_element_type=f32).astype(bf16)
    returned = unpack(route_exchange(produced))
    mixed = jnp.sum((gates.reshape(-1)[:, None] * returned).reshape(rows, top_k, features), 1)
    stream_out = stream_mid + tensor_total(mixed)
    normed_out = normed(stream_out, gain[2]).astype(bf16)
    picked = normed_out[loss_offsets]
    logits = jnp.dot(picked, table.T, preferred_element_type=f32)
    wanted = targets[loss_offsets] - tensor_place * vocab_rows
    hit = jnp.arange(vocab_rows, dtype=jnp.int32)[None, :] == wanted[:, None]
    local_top = jnp.max(logits, -1)
    stats = (
        local_top,
        jnp.sum(jnp.exp(logits - local_top[:, None]), -1),
        jnp.sum(jnp.where(hit, logits, 0.0), -1),
        jnp.sum(logits, -1),
    )
    peak, vocab_total, target_logit, logit_sum = merged(stats, "tensor", combine_stats)
    loss_total = peak + jnp.log(vocab_total)
    weight = (picture_here.reshape(rows)[loss_offsets] < 0).astype(f32)
    per_row = (
        loss_total
        - (1 - SMOOTH) * target_logit
        - SMOOTH * logit_sum / VOCAB
        + ZLOSS * loss_total * loss_total
    )
    loss_local = jnp.sum(weight * per_row)
    soft = jnp.exp(logits - loss_total[:, None])
    d_logits = (
        weight[:, None]
        * (
            (1 + 2 * ZLOSS * loss_total)[:, None] * soft
            - (1 - SMOOTH) * hit.astype(f32)
            - SMOOTH / VOCAB
        )
    ).astype(bf16)
    d_picked = jnp.dot(d_logits, table, preferred_element_type=f32)
    grad_table = jnp.dot(d_logits.T, picked, preferred_element_type=f32)
    d_normed_out = tensor_total(jnp.zeros((rows, features), f32).at[loss_offsets].add(d_picked))
    d_stream_out, grad_final = norm_back(stream_out, gain[2], d_normed_out)
    d_piece = (gates.reshape(-1)[:, None] * d_stream_out[owner]).astype(bf16)
    d_arrived = route_exchange(pack(d_piece))
    d_active = jnp.dot(d_arrived, out_low.T, preferred_element_type=f32)
    unused, gelu_pull = jax.vjp(jax.nn.gelu, inner)
    d_inner = gelu_pull(d_active)[0].astype(bf16)
    grad_out = jnp.dot(active.T, d_arrived, preferred_element_type=f32)
    grad_in = jnp.dot(arrived.T, d_inner, preferred_element_type=f32)
    sent_back = jnp.dot(d_inner, in_low.T, preferred_element_type=f32).astype(bf16)
    d_routes = unpack(route_exchange(sent_back))
    gate_part = jnp.sum(d_stream_out[owner] * returned, -1).reshape(rows, top_k)
    route_part = jnp.sum(d_routes.reshape(rows, top_k, features), 1)
    d_from_experts, d_gates = tensor_total((route_part, gate_part))
    d_chosen = gates * (d_gates - jnp.sum(gates * d_gates, -1, keepdims=True))
    expert_hot = (routes[..., None] == jnp.arange(experts, dtype=jnp.int32)).astype(f32)
    d_router_logits = jnp.sum(expert_hot * d_chosen[..., None], 1).astype(bf16)
    grad_router = jnp.dot(d_router_logits.T, normed_mid, preferred_element_type=f32)
    d_normed_mid = d_from_experts + jnp.dot(
        d_router_logits, router_full, preferred_element_type=f32
    )
    d_from_mid, grad_middle = norm_back(stream_mid, gain[1], d_normed_mid)
    d_stream_mid = d_stream_out + d_from_mid
    d_attn_low = d_stream_mid.astype(bf16)
    grad_output_map = jnp.dot(attended_low.T, d_attn_low, preferred_element_type=f32)
    d_attended = jnp.dot(d_attn_low, output_map.T, preferred_element_type=f32).astype(bf16)
    d_heads = d_attended.reshape(seqs, sub, heads, HD)
    delta = jnp.moveaxis(jnp.sum(d_heads.astype(f32) * attended, -1), 2, 1)
    key_source, value_source = (
        lax.all_gather(keys_local, "dp", axis=1, tiled=True),
        lax.all_gather(values_local, "dp", axis=1, tiled=True),
    )

    def score_grads(
        q_heads, q_pos, q_pic, k_heads, k_pos, k_pic, bias, totals, deltas, dq_heads, v_heads
    ):
        s = pair_scores(q_heads, q_pos, q_pic, k_heads, k_pos, k_pic, bias)
        probs = jnp.exp(s - totals[..., None])
        d_probs = jnp.einsum("sqhd,skhd->shqk", dq_heads, v_heads, preferred_element_type=f32)
        d_scores = (probs * (d_probs - deltas[..., None])).astype(bf16)
        return (probs, d_scores)

    def key_step(carry, index):
        d_query, d_rel = carry
        start = index * block
        key_pos = start + jnp.arange(block, dtype=jnp.int32)
        key_heads = key_slice(key_source, start)
        value_heads = key_slice(value_source, start)
        bias, bias_pull = jax.vjp(
            lambda table_rel: rel_window(table_rel, dp_place * sub, sub, start, block, length),
            relative,
        )
        probs, d_scores = score_grads(
            query_heads,
            pos_here,
            picture_here,
            key_heads,
            key_pos,
            lax.dynamic_slice_in_dim(picture_all, start, block, 1),
            bias,
            log_total,
            delta,
            d_heads,
            value_heads,
        )
        d_query = (
            d_query
            + jnp.einsum("shqk,skhd->sqhd", d_scores, key_heads, preferred_element_type=f32) * scale
        )
        d_rel = d_rel + bias_pull(jnp.sum(d_scores.astype(f32), 0))[0]
        d_key = (
            jnp.einsum("shqk,sqhd->skhd", d_scores, query_heads, preferred_element_type=f32) * scale
        )
        d_value = jnp.einsum(
            "shqk,sqhd->skhd", probs.astype(bf16), d_heads, preferred_element_type=f32
        )
        joined = jnp.concatenate(
            [d_key.reshape(seqs, block, width), d_value.reshape(seqs, block, width)], 2
        )
        return ((d_query, d_rel), joined)

    start_carry = (jnp.zeros((seqs, sub, heads, HD), f32), jnp.zeros(relative.shape, f32))
    (d_query, d_rel), key_terms = lax.scan(key_step, start_carry, block_ids)
    d_bias = jnp.dot(d_rel, bucket_hot.T, precision=HIGH)
    ordered = jnp.moveaxis(key_terms, 0, 1).reshape(seqs, length, 2 * width)
    key_grads = lax.psum_scatter(ordered, "dp", scatter_dimension=1, tiled=True).reshape(
        rows, 2 * width
    )
    d_fresh = jnp.stack(
        [d_query.reshape(rows, width), key_grads[:, :width], key_grads[:, width:]]
    ).astype(bf16)
    grad_proj = jnp.einsum("td,ste->sde", normed_in, d_fresh, preferred_element_type=f32)
    d_normed_in = tensor_total(
        jnp.einsum("ste,sde->td", d_fresh, projection, preferred_element_type=f32)
    )
    d_from_in, grad_first = norm_back(stream_in, gain[0], d_normed_in)
    d_stream_in = d_stream_mid + d_from_in
    grad_table = grad_table + jnp.zeros((vocab_rows, features), f32).at[offset].add(
        jnp.where(owned[:, None], d_stream_in, 0.0)
    )
    sum_table, sum_proj, sum_output, sum_router, sum_gains = (
        lax.psum_scatter(grad_table, "dp", scatter_dimension=1, tiled=True),
        lax.psum_scatter(grad_proj, "dp", scatter_dimension=1, tiled=True),
        lax.psum_scatter(grad_output_map, "dp", scatter_dimension=1, tiled=True),
        lax.psum_scatter(grad_router, "dp", scatter_dimension=1, tiled=True),
        lax.psum_scatter(
            jnp.stack([grad_first, grad_middle, grad_final]), "dp", scatter_dimension=1, tiled=True
        ),
    )
    sum_bias = lax.psum(d_bias, "dp")
    squares = (
        jnp.sum(sum_table * sum_table)
        + jnp.sum(sum_proj * sum_proj)
        + jnp.sum(sum_output * sum_output)
        + jnp.sum(grad_in * grad_in)
        + jnp.sum(grad_out * grad_out)
        + (jnp.sum(sum_router * sum_router) + jnp.sum(sum_gains * sum_gains)) / tensor_count
        + jnp.sum(sum_bias * sum_bias) / dp_count
    )
    total_squares, loss_sum, loss_count = lax.psum(
        (squares, loss_local / tensor_count, jnp.sum(weight) / tensor_count), ("dp", "tensor")
    )
    grad_norm = jnp.sqrt(total_squares)
    clip = MAX_NORM / jnp.maximum(grad_norm, MAX_NORM)
    params = (
        embedding,
        attn_proj,
        out_proj,
        router,
        expert_in,
        expert_out,
        norm_gains,
        position_bias,
    )
    firsts = (
        embedding_first,
        attn_proj_first,
        out_proj_first,
        router_first,
        expert_in_first,
        expert_out_first,
        norm_gains_first,
        position_bias_first,
    )
    seconds = (
        embedding_second,
        attn_proj_second,
        out_proj_second,
        router_second,
        expert_in_second,
        expert_out_second,
        norm_gains_second,
        position_bias_second,
    )
    grads = (sum_table, sum_proj, sum_output, sum_router, grad_in, grad_out, sum_gains, sum_bias)
    results = []
    for index in range(8):
        results.extend(
            adam_update(
                params[index],
                firsts[index],
                seconds[index],
                clip * grads[index],
                RATES[index],
                DECAYS[index],
            )
        )
    return (
        results[0],
        results[1],
        results[2],
        results[3],
        results[4],
        results[5],
        results[6],
        results[7],
        results[8],
        results[9],
        results[10],
        results[11],
        results[12],
        results[13],
        results[14],
        results[15],
        results[16],
        results[17],
        results[18],
        results[19],
        results[20],
        results[21],
        results[22],
        results[23],
        grad_norm,
        loss_sum,
        loss_count,
    )


def fits(dp_count, tensor_count, arrays):
    token_ids, loss_offsets, routes, picture_start = arrays[0], arrays[2], arrays[3], arrays[4]
    columns, router, gains = arrays[6].shape[1], arrays[15], arrays[24]
    rows, picks = token_ids.shape[0], loss_offsets.shape[0]
    return (
        rows == 128
        and rows * dp_count <= SEQ
        and picture_start.shape[0] == 1
        and picks == 16
        and picks * dp_count == 128
        and dp_count % 4 == 0
        and tensor_count == 4
        and dp_count % router.shape[0] == 0
        and dp_count % 2 == 0
        and dp_count <= 8
        and router.shape[0] <= 4
        and routes.shape[1] == 2
        and gains.shape[0] == 3
        and columns % 16 == 0
        and columns <= 128
    )


def solution(mesh):
    in_specs = (
        P("dp"),
        P("dp"),
        P("dp"),
        P("dp", None),
        P(),
        P(),
        P("tensor", "dp"),
        P("tensor", "dp"),
        P("tensor", "dp"),
        P(None, "dp", "tensor"),
        P(None, "dp", "tensor"),
        P(None, "dp", "tensor"),
        P("tensor", "dp"),
        P("tensor", "dp"),
        P("tensor", "dp"),
        P(None, "dp"),
        P(None, "dp"),
        P(None, "dp"),
        P(None, ("dp", "tensor")),
        P(None, ("dp", "tensor")),
        P(None, ("dp", "tensor")),
        P(("dp", "tensor"), None),
        P(("dp", "tensor"), None),
        P(("dp", "tensor"), None),
        P(None, "dp"),
        P(None, "dp"),
        P(None, "dp"),
        P("tensor", None),
        P("tensor", None),
        P("tensor", None),
    )
    out_specs = (
        P("tensor", "dp"),
        P("tensor", "dp"),
        P("tensor", "dp"),
        P(None, "dp", "tensor"),
        P(None, "dp", "tensor"),
        P(None, "dp", "tensor"),
        P("tensor", "dp"),
        P("tensor", "dp"),
        P("tensor", "dp"),
        P(None, "dp"),
        P(None, "dp"),
        P(None, "dp"),
        P(None, ("dp", "tensor")),
        P(None, ("dp", "tensor")),
        P(None, ("dp", "tensor")),
        P(("dp", "tensor"), None),
        P(("dp", "tensor"), None),
        P(("dp", "tensor"), None),
        P(None, "dp"),
        P(None, "dp"),
        P(None, "dp"),
        P("tensor", None),
        P("tensor", None),
        P("tensor", None),
        P(),
        P(),
        P(),
    )

    def chosen(*arrays):
        sizes = lax.axis_size("dp"), lax.axis_size("tensor")
        return (fast_local if fits(*sizes, arrays) else local)(*arrays)

    return jax.shard_map(chosen, mesh=mesh, in_specs=in_specs, out_specs=out_specs, check_vma=False)
```

```python
import functools
import math
import types

import jax
import jax.numpy as jnp
from jax.experimental import pallas as pl
from jax.experimental.pallas import tpu as pltpu
from jax import lax
from jax.sharding import PartitionSpec as P

HD = 64
VOCAB = 32000
PIECE = 256
SEQ = 4096
STEP = 10


SMOOTH = 0.1
ZLOSS = 0.0001
NORM_EPS = 1e-06
MAX_NORM = 1.0
BETA1 = 0.9
BETA2 = 0.95
ADAM_EPS = 1e-08
RATES = (0.04, 0.04, 1.0, 0.03, 0.07, 0.035, 1.0, 0.7)
DECAYS = (0.1, 0.1, 0.1, 0.1, 0.1, 0.1, 0.0, 0.0)
NEGATIVE = -1e30
HIGH = lax.Precision.HIGHEST


def merged(shard, axis, combine):
    everything = jax.tree.map(lambda part: lax.all_gather(part, axis), shard)
    initial = jax.tree.map(lambda part: part[0], everything)

    def lap(k, so_far):
        return combine(so_far, jax.tree.map(lambda part: part[k], everything))

    return lax.fori_loop(1, lax.axis_size(axis), lap, initial)


def normed(v, g):
    return v * lax.rsqrt(jnp.mean(v * v, -1, keepdims=True) + NORM_EPS) * g


def norm_back(v, g, upstream):
    unused, pull = jax.vjp(normed, v, g)
    return pull(upstream)


def picture_of(positions, starts, width):
    inside = (positions[:, None] >= starts[None, :]) & (
        positions[:, None] < starts[None, :] + width
    )
    number = jnp.arange(starts.shape[0], dtype=jnp.int32) + 1
    return jnp.sum(inside.astype(jnp.int32) * number[None, :], 1) - 1


def rel_window(relative, query_start, query_count, key_start, key_count, length):
    centre = query_start - key_start + length - 1
    window = lax.dynamic_slice_in_dim(
        relative, centre - key_count + 1, query_count + key_count - 1, 1
    )
    span = query_count + key_count
    wrapped = jnp.concatenate(
        [
            jnp.flip(window[:, :key_count], 1),
            jnp.zeros((window.shape[0], 1), window.dtype),
            jnp.flip(window[:, key_count:], 1),
        ],
        1,
    )
    tiled = jnp.tile(wrapped, (1, query_count))[:, : query_count * (span - 1)]
    return tiled.reshape(window.shape[0], query_count, span - 1)[:, :, :key_count]


def tensor_total(value):
    return lax.psum(value, "tensor")


def route_exchange(value):
    return lax.all_to_all(value, "dp", split_axis=0, concat_axis=0, tiled=True)


def combine_stats(left, right):
    peak = jnp.maximum(left[0], right[0])
    total = left[1] * jnp.exp(left[0] - peak) + right[1] * jnp.exp(right[0] - peak)
    return (peak, total, left[2] + right[2], left[3] + right[3])


def adam_update(weight, first, second, grad, rate, decay):
    first = BETA1 * first + (1 - BETA1) * grad
    second = BETA2 * second + (1 - BETA2) * grad * grad
    fixed_first = first / (1 - BETA1**STEP)
    fixed_second = second / (1 - BETA2**STEP)
    weight = weight - rate * (fixed_first / (jnp.sqrt(fixed_second) + ADAM_EPS) + decay * weight)
    return (weight, first, second)


MESH = pl.DeviceIdType.MESH
DP = "dp"
OUTSIDE = "_hbm"
TENSOR = "tensor"
UPDATE_BYTES = 20 * 1024 * 1024
VMEM_BYTES = 33 * 1024 * 1024
WHOLE = pl.BlockSpec(memory_space=pltpu.VMEM)
DMA = pltpu.SemaphoreType.DMA
F32 = jnp.float32
BF16 = jnp.bfloat16
STRIP = 256


def greet_everyone():
    barrier = pltpu.get_barrier_semaphore()
    tensor = lax.axis_size(TENSOR)
    total = lax.axis_size(DP) * tensor
    here = lax.axis_index(DP) * tensor + lax.axis_index(TENSOR)

    def signal(step, carry):
        other = lax.rem(here + step, total)
        pl.semaphore_signal(
            barrier,
            inc=1,
            device_id={DP: other // tensor, TENSOR: lax.rem(other, tensor)},
            device_id_type=MESH,
        )
        return carry

    lax.fori_loop(1, total, signal, 0)
    return barrier, total - 1


class Move:
    def __init__(self, axis, source, dest, sems, steps=None):
        self.axis, self.count, self.here = axis, lax.axis_size(axis), lax.axis_index(axis)
        self.source, self.dest, self.sems = source, dest, sems
        self.steps = range(1, self.count) if steps is None else steps

    def copy(self, step):
        target = lax.rem(self.here + step, self.count)
        return pltpu.make_async_remote_copy(
            src_ref=self.source(target),
            dst_ref=self.dest.at[self.here],
            send_sem=self.sems.at[0, step],
            recv_sem=self.sems.at[1, step],
            device_id={self.axis: target},
            device_id_type=MESH,
        )

    def start(self):
        for step in self.steps:
            self.copy(step).start()
        return self

    def arrive(self):
        for step in self.steps:
            self.copy(step).wait_recv()

    def finish(self):
        for step in self.steps:
            self.copy(step).wait_send()


def scatter_rows(axis, source, dest, sems):
    height = dest.shape[1]
    return Move(
        axis,
        lambda target: source.at[pl.ds(pl.multiple_of(target * height, height), height)],
        dest,
        sems,
    ).start()


def share_block(axis, dest, sems):
    here = lax.axis_index(axis)
    return Move(axis, lambda target: dest.at[here], dest, sems).start()


class PairGather:
    def __init__(self, buffer, sems):
        self.buffer, self.sems = buffer, sems
        self.count, self.here = lax.axis_size(DP), lax.axis_index(DP)
        self.partner = self.here + 1 - 2 * lax.rem(self.here, 2)
        self.half = self.count // 2

    def copy(self, block, target, slot):
        return pltpu.make_async_remote_copy(
            src_ref=self.buffer.at[block],
            dst_ref=self.buffer.at[block],
            send_sem=self.sems.at[0, slot],
            recv_sem=self.sems.at[1, slot],
            device_id={DP: target},
            device_id_type=MESH,
        )

    def direct(self, step):
        return self.copy(self.here, lax.rem(self.here + 2 * step, self.count), step)

    def onward(self, step):
        block = lax.rem(self.here + self.count - 2 * step, self.count)
        return self.copy(block, self.partner, self.half + step)

    def start(self):
        for step in range(1, self.half):
            self.direct(step).start()
        self.onward(0).start()
        return self

    def forward_one(self, step):
        self.direct(step).wait_recv()
        self.onward(step).start()

    def forward(self):
        for step in range(1, self.half):
            self.forward_one(step)

    def arrive(self):
        for step in range(self.half):
            self.onward(step).wait_recv()

    def finish(self):
        for step in range(1, self.half):
            self.direct(step).wait_send()
        for step in range(self.half):
            self.onward(step).wait_send()


class Relay:
    def __init__(self, buffer, dp_sems, sems):
        self.buffer, self.sems = buffer, sems
        self.here = lax.axis_index(TENSOR)
        self.gather = PairGather(buffer.at[self.here], dp_sems)
        self.far = lax.rem(self.here + 2, 4)
        self.near = self.here + 1 - 2 * lax.rem(self.here, 2)
        self.blocks, self.block = lax.axis_size(DP), lax.axis_index(DP)
        self.half = self.blocks // 2
        partner = self.gather.partner
        own = [lax.rem(self.block + self.blocks - 2 * k, self.blocks) for k in range(self.half)]
        other = [lax.rem(partner + self.blocks - 2 * k, self.blocks) for k in range(self.half)]
        self.order = own + other

    def copy(self, kind, index):
        source = self.far if kind == 2 else self.here
        block = self.order[index]
        return pltpu.make_async_remote_copy(
            src_ref=self.buffer.at[source, block],
            dst_ref=self.buffer.at[source, block],
            send_sem=self.sems.at[0, kind, index],
            recv_sem=self.sems.at[1, kind, index],
            device_id={TENSOR: self.far if kind == 0 else self.near},
            device_id_type=MESH,
        )

    def send(self, index):
        self.copy(0, index).start()
        self.copy(1, index).start()

    def start(self):
        self.gather.start()
        self.send(0)
        return self

    def pass_on(self):
        for step in range(1, self.half):
            self.gather.forward_one(step)
            self.send(step)
        for step in range(self.half):
            self.gather.onward(step).wait_recv()
            self.send(self.half + step)

    def spread(self):
        for index in range(self.blocks):
            self.copy(0, index).wait_recv()
            self.copy(2, index).start()

    def arrive(self):
        for index in range(self.blocks):
            self.copy(1, index).wait_recv()
            self.copy(2, index).wait_recv()

    def finish(self):
        self.gather.finish()
        for index in range(self.blocks):
            for kind in range(3):
                self.copy(kind, index).wait_send()


def split_again(tile):
    value = tile + pltpu.roll(tile, 64, 1)
    high = value.astype(BF16).astype(F32)
    return jnp.where(lanes(tile.shape) < 64, high, value - high)


class AllSum:
    def __init__(self, source, scratch, sems, halves):
        self.source, self.sems, self.halves = source, sems, halves
        self.parts, self.tiles, self.arrived, self.done, self.whole = scratch
        self.here, self.block = lax.axis_index(TENSOR), lax.axis_index(DP)
        self.height = self.parts.shape[1]
        self.owners = self.tiles.shape[0]
        self.own = pl.ds(pl.multiple_of(self.here * self.height, self.height), self.height)
        self.first = scatter_rows(TENSOR, source, self.parts, sems[0])
        self.parts[self.here] = source[self.own, :]

    def owned(self, act):
        pl.when(self.block < self.owners)(act)

    def to_owner(self, owner):
        return pltpu.make_async_remote_copy(
            src_ref=self.tiles.at[owner],
            dst_ref=self.arrived.at[self.block],
            send_sem=self.sems[1].at[0, owner],
            recv_sem=self.sems[1].at[1, self.block],
            device_id={DP: owner},
            device_id_type=MESH,
        )

    def from_block(self, k):
        return pltpu.make_async_remote_copy(
            src_ref=self.tiles.at[0],
            dst_ref=self.arrived.at[k],
            send_sem=self.sems[1].at[0, 0],
            recv_sem=self.sems[1].at[1, k],
            device_id={DP: k},
            device_id_type=MESH,
        )

    def others(self, limit, act):
        for k in range(limit):
            pl.when(self.block != k)(lambda k=k: act(k))

    def tile_to(self, k):
        return pltpu.make_async_remote_copy(
            src_ref=self.done.at[self.block],
            dst_ref=self.done.at[self.block],
            send_sem=self.sems[2].at[0, k],
            recv_sem=self.sems[2].at[1, self.block],
            device_id={DP: k},
            device_id_type=MESH,
        )

    def tile_from(self, k):
        return pltpu.make_async_remote_copy(
            src_ref=self.done.at[k],
            dst_ref=self.done.at[k],
            send_sem=self.sems[2].at[0, k],
            recv_sem=self.sems[2].at[1, k],
            device_id={DP: k},
            device_id_type=MESH,
        )

    def scatter(self, factor=None):
        self.first.arrive()
        total = sum_blocks(self.parts)
        if factor is not None:
            total = total * factor[self.own, :]
        for owner in range(self.owners):
            tile = total[:, owner * 128 : (owner + 1) * 128]
            if self.halves and owner == self.owners - 1:
                tile = split_again(tile)
            self.tiles[owner] = tile.astype(BF16)
        self.others(self.owners, lambda owner: self.to_owner(owner).start())

        @self.owned
        def _():
            self.arrived[self.block] = self.tiles[self.block]

    def gather(self):
        blocks = lax.axis_size(DP)

        @self.owned
        def _():
            self.others(blocks, lambda k: self.from_block(k).wait_recv())
            tile = sum_blocks(self.arrived)
            if self.halves:
                tile = jnp.where(self.block == self.owners - 1, split_again(tile), tile)
            self.done[self.block] = tile.astype(BF16)
            self.others(blocks, lambda k: self.tile_to(k).start())

    def result(self):
        self.others(self.owners, lambda k: self.tile_from(k).wait_recv())
        for k in range(self.owners):
            self.whole[self.here, :, k * 128 : (k + 1) * 128] = self.done[k]
        self.last = share_block(TENSOR, self.whole, self.sems[3])
        self.last.arrive()
        return across(self.whole, 0).astype(F32)

    def finish(self):
        self.first.finish()
        self.others(self.owners, lambda owner: self.to_owner(owner).wait_send())
        blocks = lax.axis_size(DP)
        self.owned(lambda: self.others(blocks, lambda k: self.tile_to(k).wait_send()))
        self.last.finish()


class Everyone:
    def __init__(self, buffer, sems):
        self.buffer, self.sems = buffer, sems
        self.tensor = lax.axis_size(TENSOR)
        self.total = lax.axis_size(DP) * self.tensor
        self.here = lax.axis_index(DP) * self.tensor + lax.axis_index(TENSOR)

    def copy(self, step):
        other = lax.rem(self.here + step, self.total)
        return pltpu.make_async_remote_copy(
            src_ref=self.buffer.at[self.here],
            dst_ref=self.buffer.at[self.here],
            send_sem=self.sems.at[0, step],
            recv_sem=self.sems.at[1, step],
            device_id={DP: other // self.tensor, TENSOR: lax.rem(other, self.tensor)},
            device_id_type=MESH,
        )

    def each(self, act):
        def one(step, carry):
            act(self.copy(step))
            return carry

        lax.fori_loop(1, self.total, one, 0)

    def start(self):
        self.each(lambda copy: copy.start())
        return self

    def arrive(self):
        self.each(lambda copy: copy.wait_recv())

    def finish(self):
        self.each(lambda copy: copy.wait_send())


def dot_nt(a, b):
    return lax.dot_general(a, b, (((1,), (1,)), ((), ())), preferred_element_type=F32)


def dot_nn(a, b):
    return jnp.dot(a, b, preferred_element_type=F32)


def root_of(v):
    return lax.rsqrt(jnp.mean(v * v, -1, keepdims=True) + NORM_EPS)


def low(v):
    return v.astype(BF16).astype(F32)


def gelu_value(x):
    slope = math.sqrt(2.0 / math.pi)
    return 0.5 * x * (1.0 + jnp.tanh(slope * (x + 0.044715 * (x * x * x))))


def gelu_slope(x):
    slope = math.sqrt(2.0 / math.pi)
    t = jnp.tanh(slope * (x + 0.044715 * (x * x * x)))
    return 0.5 * (1.0 + t) + 0.5 * x * (1.0 - t * t) * (slope * (1.0 + 3 * 0.044715 * x * x))


def lanes(shape):
    return lax.broadcasted_iota(jnp.int32, shape, len(shape) - 1)


def sublanes(shape):
    return lax.broadcasted_iota(jnp.int32, shape, len(shape) - 2)


def tensor_sum(total, buffer, sems):
    buffer[lax.axis_index(TENSOR)] = total.astype(BF16)
    move = share_block(TENSOR, buffer, sems)
    move.arrive()
    return sum_blocks(buffer), move


def norm_back_rows(v, g, upstream):
    root = root_of(v)
    scaled = g * upstream
    inner = jnp.sum(scaled * v, -1, keepdims=True)
    back = root * scaled - v * (root * root * root * inner / v.shape[-1])
    return back, jnp.sum(upstream * v * root, 0, keepdims=True)


def sum_blocks(ref):
    total = ref[0].astype(F32)
    for k in range(1, ref.shape[0]):
        total = total + ref[k].astype(F32)
    return total


def packed_rows(value):
    rows, wide = value.shape
    whole, half = wide // 128, rows // 2
    tail = value[:, whole * 128 :]
    parts = [value[:, t * 128 : (t + 1) * 128] for t in range(whole)]
    return jnp.concatenate(parts + [jnp.concatenate([tail[0:half], tail[half:]], 1)], 0)


def unpacked_rows(value, rows):
    whole = value.shape[0] // rows
    tail = value[whole * rows :]
    parts = [value[t * rows : (t + 1) * rows] for t in range(whole)]
    return jnp.concatenate(parts + [jnp.concatenate([tail[:, 0:64], tail[:, 64:]], 0)], 1)


def across(ref, axis):
    return jnp.concatenate([ref[k] for k in range(ref.shape[0])], axis)


def squared(value):
    return jnp.sum(value * value, keepdims=True)


def step_kernel(names, small, weights, experts, vocab_rows, starts, *refs):
    r = types.SimpleNamespace(**dict(zip(names, refs, strict=True)))
    block, here = lax.axis_index(DP), lax.axis_index(TENSOR)
    blocks, tensor = lax.axis_size(DP), lax.axis_size(TENSOR)
    rows = r.own_ids.shape[1]
    every = rows * blocks
    picks = r.own_offsets.shape[1]
    count = picks * blocks
    columns, width = r.proj_weight.shape[1:]
    features = columns * blocks
    heads = width // HD
    share = r.pages.shape[2]
    group = blocks // tensor
    scale = 1.0 / math.sqrt(HD)
    moves = []

    def all_sum(source, number):
        scratch = [getattr(r, f"sum_{k}_{number}") for k in range(5)]
        sems = [getattr(r, f"sum_sem_{k}_{number}") for k in range(4)]
        return keep(AllSum(source, scratch, sems, number == 2))

    def keep(move):
        moves.append(move)
        return move

    def load(name, sems, k):
        copy = pltpu.make_async_copy(getattr(r, name + OUTSIDE), getattr(r, name), sems.at[k])
        copy.start()
        return copy

    loads = [load(name, r.load_sems, k) for k, name in enumerate(small)]
    greeting = greet_everyone()
    held = [load(name, r.held_sems, k) for k, name in enumerate(weights)]
    proj_load, map_load, table_load, in_load, out_load = held[:5]
    for copy in loads:
        copy.wait()

    ids = r.own_ids[...].astype(F32)
    offset_row = jnp.concatenate(
        [r.own_offsets[...].astype(F32), jnp.zeros((1, rows - picks), F32)], 1
    )
    slot = lanes((rows, rows))
    loss_hot = (sublanes((rows, rows)).astype(F32) == offset_row) & (slot < picks)
    targets = r.own_targets[...]
    upper = targets // 256
    facts = jnp.concatenate(
        [
            upper.astype(F32),
            (targets - upper * 256).astype(F32),
            r.own_routes[...].astype(F32),
            jnp.zeros((4, rows), F32),
        ],
        0,
    )
    facts = dot_nn(facts.astype(BF16), loss_hot.astype(F32).astype(BF16))
    known = jnp.concatenate(
        [
            offset_row,
            facts[0:1] * 256.0 + facts[1:2],
            facts[2:4],
            ids,
            jnp.zeros((3, rows), F32),
        ],
        0,
    )
    r.known[block] = known
    own_router = r.own_router[...]
    own_small = jnp.concatenate(
        [own_router, jnp.zeros((4 - experts, columns), F32), r.own_gains[...], jnp.zeros((1, columns), F32)]
        if experts < 4
        else [own_router, r.own_gains[...], jnp.zeros((1, columns), F32)],
        0,
    )
    r.small[block] = jnp.concatenate([own_small, jnp.zeros((8, 128 - columns), F32)], 1)
    map_load.wait()
    r.maps[here, block] = packed_rows(r.map_weight[...].T).astype(BF16)
    proj_load.wait()
    own_proj = jnp.concatenate([r.proj_weight[s] for s in range(3)], 1)
    r.proj[block] = packed_rows(own_proj).astype(BF16)
    own_proj = own_proj.astype(BF16)
    pl.semaphore_wait(*greeting)
    to_known = keep(share_block(DP, r.known, r.sem_known))
    to_small = keep(share_block(DP, r.small, r.sem_small))
    to_maps = keep(Relay(r.maps, r.sem_map, r.sem_maps).start())
    to_proj = keep(PairGather(r.proj, r.sem_proj).start())

    table_load.wait()
    for k in range(blocks):
        stop = min(vocab_rows, (k + 1) * share)
        span = max(0, stop - k * share)
        if span > 0:
            r.pages[k, :, 0:span] = r.table_weight[:, k * share : stop].astype(BF16)
        if span < share:
            r.pages[k, :, span:share] = jnp.zeros((columns, share - span), BF16)
    r.table[block] = r.pages[block]

    def pages_move(steps):
        return keep(
            Move(DP, lambda target: r.pages.at[target], r.table, r.sem_pages, steps).start()
        )

    to_known.arrive()
    base = (here * vocab_rows).astype(F32)
    for k in range(blocks):
        r.id_row[:, k * rows : (k + 1) * rows] = r.known[k][4:5, :] - base
    chunk = group * rows
    id_high = jnp.floor(r.id_row[...] * (1.0 / STRIP))
    r.id_high[...] = id_high
    r.id_place[...] = r.id_row[...] - id_high * STRIP
    strips_of_page = share // STRIP
    for step in range(1, tensor + 1):
        target = lax.rem(here + step, tensor)
        at = pl.ds(pl.multiple_of(target * chunk, chunk), chunk)
        hot = sublanes((STRIP, chunk)).astype(F32) == r.id_place[:, at]
        hot = hot.astype(F32).astype(BF16)
        number = r.id_high[:, at]

        def look(k, total, hot=hot, number=number):
            strips = jnp.concatenate(
                [r.pages[k, :, n * STRIP : (n + 1) * STRIP] for n in range(strips_of_page)], 0
            )
            found = dot_nn(strips, hot)
            for n in range(strips_of_page):
                mine = number == (k * strips_of_page + n).astype(F32)
                total = total + jnp.where(mine, found[n * columns : (n + 1) * columns], 0.0)
            return total

        found = lax.fori_loop(0, blocks, look, jnp.zeros((columns, chunk), F32))
        for b in range(group):
            r.looked[target, b] = found[:, b * rows : (b + 1) * rows].astype(BF16)
        if step == tensor - 1:
            to_total = keep(
                Move(TENSOR, lambda target: r.looked.at[target], r.first, r.sem_first).start()
            )
    to_maps.pass_on()
    to_proj.forward()
    r.first[here] = r.looked[here]
    to_total.arrive()
    for b in range(group):
        r.streams[here, block, :, b * rows : (b + 1) * rows] = sum_blocks(r.first.at[:, b]).astype(
            BF16
        )
    to_streams = keep(Relay(r.streams, r.sem_stream, r.sem_streams).start())
    to_streams.pass_on()
    pages_now = [pages_move((4, 2, 6, 3))]
    to_small.arrive()
    gain_columns = [low(r.small[k].T[0:columns, 4:5]) for k in range(blocks)]
    small_rows = jnp.concatenate([r.small[k][:, 0:columns] for k in range(blocks)], 1)
    gains = low(small_rows)
    r.router[...] = jnp.concatenate(
        [
            jnp.where(sublanes(gains.shape) < experts, gains, 0.0),
            jnp.zeros((128 - gains.shape[0], features), F32),
        ],
        0,
    ).astype(BF16)
    r.gains[...] = gains
    r.id_low[...] = (
        (sublanes((STRIP, every)).astype(F32) == r.id_place[...]).astype(F32).astype(BF16).T
    )

    def column_of(field):
        table = jnp.concatenate(
            [r.known[k][field : field + 1, :] for k in range(blocks)]
            + ([jnp.zeros((8 - blocks, rows), F32)] if blocks < 8 else []),
            0,
        ).T
        return jnp.concatenate([table[0:picks, k : k + 1] for k in range(blocks)], 0)

    offsets, wanted, route_a, route_b = (
        column_of(field).astype(jnp.int32) for field in range(4)
    )
    positions = offsets + sublanes((count, 1)) // picks * rows
    period = 2 * every
    bucket_row = jnp.concatenate(
        [r.own_buckets[...].astype(F32), jnp.zeros((1, 1), F32)], 1
    )
    strips = [bucket_row[:, k * rows : (k + 1) * rows] for k in range(period // rows)]
    mirror = (lanes((rows, rows)) + sublanes((rows, rows)) == rows - 1).astype(F32).astype(BF16)
    strips = dot_nn(jnp.concatenate(strips, 0).astype(BF16), mirror)
    flipped = jnp.concatenate(
        [strips[k : k + 1, :] for k in reversed(range(period // rows))], 1
    )
    spread = jnp.broadcast_to(flipped, (rows, period))
    turned = pltpu.roll(spread, period - rows, 1, stride=1, stride_axis=0).astype(BF16)
    chosen = (lanes((count, rows)) == offsets).astype(F32).astype(BF16)
    r.shifted[...] = dot_nn(chosen, turned).astype(jnp.int32)
    for k in range(blocks):
        begin = rows * (blocks - 1 - k)
        r.bucket[k * picks : (k + 1) * picks, :] = r.shifted[
            k * picks : (k + 1) * picks, begin : begin + every
        ]
    bucket_count = r.position_bias.shape[1]

    def fill(k, carry):
        at = pl.ds(pl.multiple_of(k * picks, picks), picks)
        numbers = r.bucket[at, :]
        terms = [jnp.zeros(numbers.shape, F32)] * heads
        for b in range(bucket_count):
            same = numbers == b
            terms = [jnp.where(same, r.position_bias[h, b], terms[h]) for h in range(heads)]
        for h in range(heads):
            r.bias[h, at, :] = terms[h]
        return carry

    lax.fori_loop(0, blocks, fill, 0)

    def picture_at(place):
        inside = jnp.full(place.shape, -1, jnp.int32)
        for n in range(starts):
            begin = r.picture_start[0, n]
            inside = jnp.where((place >= begin) & (place < begin + PIECE), n, inside)
        return inside

    key_position = lanes((count, every))
    query_picture = picture_at(positions)
    allowed = (key_position <= positions) | (
        (picture_at(lanes((1, every))) == query_picture) & (query_picture >= 0)
    )
    to_streams.spread()
    to_proj.arrive()
    all_proj = jnp.concatenate([unpacked_rows(r.proj[k], columns) for k in range(blocks)], 0)
    key_proj, value_proj = (
        all_proj[:, k * width : (k + 1) * width].astype(F32).T.astype(BF16) for k in (1, 2)
    )
    gain_column = jnp.concatenate(gain_columns, 0)
    back_hot = (key_position == positions).astype(F32).astype(BF16)
    stream = jnp.zeros((count, features), F32)
    normed_loss = jnp.zeros((count, features), F32)
    to_streams.arrive()
    for k in range(tensor):
        part = slice(k * chunk, (k + 1) * chunk)
        low_part = across(r.streams.at[k], 0)
        wide_part = low_part.astype(F32)
        root = lax.rsqrt(jnp.mean(wide_part * wide_part, 0, keepdims=True) + NORM_EPS)
        r.roots[:, part] = root
        normed_in = (wide_part * root * gain_column).astype(BF16)
        r.keys[:, part] = dot_nn(key_proj, normed_in).astype(BF16)
        r.values[:, part] = dot_nn(value_proj, normed_in).astype(BF16)
        stream = stream + dot_nt(back_hot[:, part], low_part)
        normed_loss = normed_loss + dot_nt(back_hot[:, part], normed_in)
    query = dot_nn(normed_loss.astype(BF16), all_proj[:, 0:width]).astype(BF16)
    to_maps.spread()

    def head(value, h):
        return value[:, h * HD : (h + 1) * HD]

    def tall(ref, h):
        return ref[h * HD : (h + 1) * HD, :]

    for h in range(heads):
        raw = dot_nn(head(query, h), tall(r.keys, h)) * scale + r.bias[h]
        raw = jnp.where(allowed, raw, NEGATIVE)
        terms = jnp.exp(raw - jnp.max(raw, -1, keepdims=True))
        r.probs[h] = terms / jnp.sum(terms, -1, keepdims=True)
    attended = jnp.concatenate(
        [dot_nt(r.probs[h].astype(BF16), tall(r.values, h)).astype(BF16) for h in range(heads)],
        1,
    )
    r.heads[here] = attended
    to_heads = keep(share_block(TENSOR, r.heads, r.sem_heads))
    in_load.wait()
    out_load.wait()
    in_low, out_low = r.in_weight[...].astype(BF16), r.out_weight[...].astype(BF16)
    to_maps.arrive()
    to_heads.arrive()

    middle = stream
    for k in range(tensor):
        full = jnp.concatenate([unpacked_rows(r.maps[k, i], columns) for i in range(blocks)], 0)
        middle = middle + dot_nt(r.heads[k], full)
    r.middle[...] = middle
    gain_middle, gain_final = r.gains[5:6, :], r.gains[6:7, :]
    normed_mid = (middle * root_of(middle) * gain_middle).astype(BF16)
    inner = dot_nn(normed_mid, in_low)
    active = gelu_value(inner).astype(BF16)
    r.piece[...] = dot_nn(active, out_low).astype(BF16)
    mixing = all_sum(r.piece, 0)
    router_logits = dot_nt(normed_mid, r.router[...])
    lane = lanes(router_logits.shape)
    hot_a, hot_b = lane == route_a, lane == route_b
    logit_a = jnp.sum(jnp.where(hot_a, router_logits, 0.0), 1, keepdims=True)
    logit_b = jnp.sum(jnp.where(hot_b, router_logits, 0.0), 1, keepdims=True)
    logit_top = jnp.maximum(logit_a, logit_b)
    gate_a, gate_b = jnp.exp(logit_a - logit_top), jnp.exp(logit_b - logit_top)
    both = gate_a + gate_b
    r.gates[...] = jnp.where(hot_a, gate_a / both, 0.0) + jnp.where(hot_b, gate_b / both, 0.0)
    expert = block // (blocks // experts)
    r.gate[...] = jnp.sum(jnp.where(lane == expert, r.gates[...], 0.0), 1, keepdims=True)
    mixing.scatter(r.gate)
    pages_now.append(pages_move((5,)))
    mixing.gather()
    pages_now.append(pages_move((1, 7)))
    final = middle + mixing.result()
    out = (final * root_of(final) * gain_final).astype(BF16)
    for move in pages_now:
        move.arrive()

    table = across(r.table, 0)
    logits = dot_nn(out, table)
    slot = lanes(logits.shape) + block * share
    logits = jnp.where(slot < vocab_rows, logits, NEGATIVE)
    hit = slot == wanted - here * vocab_rows
    local_top = jnp.max(logits, -1, keepdims=True)
    local_stats = (
        local_top,
        jnp.sum(jnp.exp(logits - local_top), -1, keepdims=True),
        jnp.sum(jnp.where(hit & (slot < vocab_rows), logits, 0.0), -1, keepdims=True),
        jnp.sum(jnp.where(slot < vocab_rows, logits, 0.0), -1, keepdims=True),
    )
    packed = jnp.zeros((count, 128), F32)
    for k, column in enumerate(local_stats):
        packed = jnp.where(lane == k, column, packed)
    r.stats[block * tensor + here] = packed.T[0:4, :]
    to_stats = keep(Everyone(r.stats, r.sem_stats).start())
    weight = (query_picture < 0).astype(F32)
    weight_row = jnp.where(lane == 0, weight, 0.0).T[0:1, :]
    to_stats.arrive()
    peaks = r.stats[:, 0]
    peak = jnp.max(peaks, 0, keepdims=True)
    stats = (
        peak,
        jnp.sum(r.stats[:, 1] * jnp.exp(peaks - peak), 0, keepdims=True),
        jnp.sum(r.stats[:, 2], 0, keepdims=True),
        jnp.sum(r.stats[:, 3], 0, keepdims=True),
    )
    log_total = stats[0] + jnp.log(stats[1])
    per_row = (
        log_total
        - (1 - SMOOTH) * stats[2]
        - SMOOTH * stats[3] / VOCAB
        + ZLOSS * log_total * log_total
    )
    loss_sum = jnp.sum(weight_row * per_row, keepdims=True)
    loss_count = jnp.sum(weight_row, keepdims=True)
    total_column = jnp.where(sublanes((128, count)) == 0, log_total, 0.0).T[:, 0:1]
    d_logits = weight * (
        (1 + 2 * ZLOSS * total_column) * jnp.exp(logits - total_column)
        - jnp.where(hit, 1 - SMOOTH, 0.0)
        - SMOOTH / VOCAB
    )
    d_logits = jnp.where(slot < vocab_rows, d_logits, 0.0).astype(BF16)
    r.d_logits_parts = [r.d_logits.at[k] for k in range(r.d_logits.shape[0])]
    piece_rows = r.d_logits.shape[2]
    for k, part in enumerate(r.d_logits_parts):
        part[block] = d_logits[k * piece_rows : (k + 1) * piece_rows]
    logit_moves = [
        keep(PairGather(part, r.sem_logits.at[k])) for k, part in enumerate(r.d_logits_parts)
    ]
    r.sent[...] = dot_nt(d_logits, table).astype(BF16)
    summing = all_sum(r.sent, 1)
    summing.scatter()
    logit_moves[0].start()
    summing.gather()
    logit_moves[0].forward()
    logit_moves[1].start()
    upstream, grad_final = norm_back_rows(final, gain_final, summing.result())
    gate = r.gate[...]
    d_piece = (gate * upstream).astype(BF16)
    d_inner = (dot_nt(d_piece, out_low) * gelu_slope(inner)).astype(BF16)
    r.wide[:, 0:features] = dot_nt(d_inner, in_low).astype(BF16)
    gate_part = jnp.sum(upstream * r.piece[...].astype(F32), 1, keepdims=True)
    high = low(gate_part)
    r.wide[:, features:] = jnp.where(
        lane == expert, high, jnp.where(lane == expert + 64, gate_part - high, 0.0)
    ).astype(BF16)
    summing = all_sum(r.wide, 2)
    grad_out = dot_nn(active.T, d_piece)
    grad_in = dot_nn(normed_mid.T, d_inner)
    r.grad_out[...] = grad_out
    r.grad_in[...] = grad_in
    squares = squared(grad_out) + squared(grad_in)
    summing.scatter()
    logit_moves[1].forward()
    logit_moves[2].start()
    summing.gather()
    logit_moves[2].forward()
    logit_moves[3].start()
    total = summing.result()
    tail = total[:, features:]
    d_gates = tail + pltpu.roll(tail, 64, 1)
    named = hot_a | hot_b
    d_gates = jnp.where(named, d_gates, 0.0)
    mean = jnp.sum(r.gates[...] * d_gates, 1, keepdims=True)
    d_router = jnp.where(named, r.gates[...] * (d_gates - mean), 0.0).astype(BF16)
    d_normed_mid = total[:, 0:features] + dot_nn(d_router, r.router[...])
    d_from_mid, grad_middle = norm_back_rows(middle, gain_middle, d_normed_mid)
    d_attn = (upstream + d_from_mid).astype(BF16)
    stream_c = jnp.concatenate([r.streams[k, block] for k in range(tensor)], 1).astype(F32)
    roots = r.roots[...]
    gain_column = low(r.small[block].T[0:columns, 4:5])
    normed_c = (stream_c * roots * gain_column).astype(BF16)
    normed_loss = dot_nt(normed_c, back_hot).astype(BF16)
    query_wide = dot_nn(query.T, back_hot)

    own_map = jnp.concatenate(
        [unpacked_rows(r.maps[here, i], columns) for i in range(blocks)], 0
    )
    d_attended = dot_nn(d_attn, own_map).astype(BF16)
    d_query = []
    for h in range(heads):
        soft = r.probs[h]
        d_head = head(d_attended, h)
        d_probs = dot_nn(d_head, tall(r.values, h))
        d_scores = soft * (d_probs - jnp.sum(soft * d_probs, -1, keepdims=True))
        d_scores = d_scores.astype(BF16)
        r.bias[h] = d_scores.astype(F32)
        d_query.append((dot_nt(d_scores, tall(r.keys, h)) * scale).astype(BF16))
        r.d_keys[h * HD : (h + 1) * HD, :] = (
            dot_nn(head(query, h).T, d_scores) * scale
        ).astype(BF16)
        r.d_values[h * HD : (h + 1) * HD, :] = dot_nn(d_head.T, soft.astype(BF16)).astype(BF16)
    d_query = jnp.concatenate(d_query, 1)
    d_query_wide = dot_nn(d_query.T, back_hot).astype(BF16)
    d_columns = (
        dot_nn(own_proj[:, 0:width], d_query_wide)
        + dot_nn(own_proj[:, width : 2 * width], r.d_keys[...])
        + dot_nn(own_proj[:, 2 * width :], r.d_values[...])
    )
    inner_row = jnp.sum(
        d_query_wide.astype(F32) * query_wide
        + r.d_keys[...].astype(F32) * r.keys[...].astype(F32)
        + r.d_values[...].astype(F32) * r.values[...].astype(F32),
        0,
        keepdims=True,
    )
    inner_high = low(inner_row)
    extra = sublanes((16, every))
    r.part[0:columns, :] = d_columns.astype(BF16)
    r.part[columns:, :] = jnp.where(
        extra == 0, inner_high, jnp.where(extra == 1, inner_row - inner_high, 0.0)
    ).astype(BF16)
    to_part = keep(
        Move(
            TENSOR,
            lambda target: r.part.at[:, pl.ds(pl.multiple_of(target * chunk, chunk), chunk)],
            r.part_in,
            r.sem_part,
        ).start()
    )
    r.part_in[here] = r.part[:, pl.ds(pl.multiple_of(here * chunk, chunk), chunk)]
    grad_proj = (
        dot_nn(normed_loss, d_query),
        dot_nt(normed_c, r.d_keys[...]),
        dot_nt(normed_c, r.d_values[...]),
    )
    for s in range(3):
        r.grad_proj[s] = grad_proj[s]
        squares = squares + squared(grad_proj[s])
    to_part.arrive()
    r.part_all[here] = sum_blocks(r.part_in).astype(BF16)
    to_parts = keep(share_block(TENSOR, r.part_all, r.sem_part_all))
    r.bias_rows[...] = jnp.zeros(r.bias_rows.shape, F32)

    def collect(k, carry):
        at = pl.ds(pl.multiple_of(k * picks, picks), picks)
        numbers = r.bucket[at, :]
        parts = [r.bias[h, at, :] for h in range(heads)]
        for b in range(bucket_count):
            same = numbers == b
            for h in range(heads):
                kept = jnp.where(same, parts[h], 0.0)
                kept = kept[0:8] + kept[8:16]
                narrow = kept[:, 0:128]
                for c in range(1, every // 128):
                    narrow = narrow + kept[:, c * 128 : (c + 1) * 128]
                r.bias_rows[h, b] += narrow
        return carry

    lax.fori_loop(0, count // picks, collect, 0)
    grad_bias = jnp.sum(r.bias_rows[...], 2)
    r.grad_bias[...] = grad_bias
    grad_bias = jnp.sum(grad_bias, -1, keepdims=True)
    squares = squares + jnp.sum(grad_bias * grad_bias, keepdims=True)[0] / blocks
    pick_own = lanes((columns, features)) == sublanes((columns, features)) + block * columns
    pick_own = pick_own.astype(F32).astype(BF16)
    d_attn_t = dot_nt(pick_own, d_attn).astype(BF16)
    out_t = dot_nt(pick_own, out).astype(BF16)
    middle_t = dot_nt(pick_own, normed_mid).astype(BF16)
    grad_map = dot_nt(attended.T, d_attn_t)
    r.grad_map[...] = grad_map
    squares = squares + squared(grad_map)
    grad_router = dot_nt(d_router.T, middle_t)[0:8]
    residual = dot_nn(d_attn_t, back_hot)
    logit_moves[3].forward()
    gain_sum = jnp.concatenate(
        [grad_middle, grad_final, jnp.zeros((6, features), F32)], 0
    )
    gain_sum = pltpu.roll(gain_sum, lax.rem(features - block * columns, features), 1)
    to_parts.arrive()
    parts = across(r.part_all, 1).astype(F32)
    d_columns = parts[0:columns]
    inner_row = parts[columns : columns + 1] + parts[columns + 1 : columns + 2]
    grad_first = jnp.sum(d_columns * stream_c * roots, 1, keepdims=True)
    grad_first = jnp.broadcast_to(grad_first, (columns, 128)).T[0:1, :]
    small = jnp.concatenate(
        [
            grad_router[0:4],
            grad_first,
            gain_sum[0:2, 0:columns],
            jnp.zeros((1, columns), F32),
        ],
        0,
    )
    r.grad_small[:, 0:columns] = small
    r.grad_small[:, columns:] = jnp.zeros((8, 128 - columns), F32)
    squares = squares + squared(small) / tensor
    d_stream = (
        roots * gain_column * d_columns
        - stream_c * (roots * roots * inner_row / features)
        + residual
    )
    d_high = d_stream.astype(BF16)
    d_low = (d_stream - d_high.astype(F32)).astype(BF16)
    low_half = d_stream.astype(BF16)
    full = vocab_rows // STRIP
    ends = [(k, min(STRIP, vocab_rows - k * STRIP)) for k in range(full - full % 4, -(-vocab_rows // STRIP))]

    def strip_mask(number):
        return (r.id_high[...] == number).astype(F32).astype(BF16)

    def scatter_four(k, carry):
        masked = [low_half * strip_mask((k * 4 + n).astype(F32)) for n in range(4)]
        found = dot_nn(jnp.concatenate(masked, 0), r.id_low[...])
        begin = pl.multiple_of(k * 4 * STRIP, STRIP)
        for n in range(4):
            r.grad_table[:, pl.ds(begin + n * STRIP, STRIP)] = found[
                n * columns : (n + 1) * columns
            ]
        return carry

    lax.fori_loop(0, full // 4, scatter_four, 0)
    masked = jnp.concatenate([low_half * strip_mask(float(k)) for k, size in ends], 0)
    found = dot_nn(masked, r.id_low[...])
    for n, (k, size) in enumerate(ends):
        r.grad_table[:, k * STRIP : k * STRIP + size] = found[
            n * columns : (n + 1) * columns, 0:size
        ]
    for move in logit_moves:
        move.arrive()

    def page_strips(k, total):
        begin = pl.multiple_of(k * share, share)
        return total + add_page(k, pl.ds(begin, share))

    def add_page(k, where, size=share):
        page = jnp.concatenate([part[k] for part in r.d_logits_parts], 0)
        value = r.grad_table[:, where] + dot_nn(out_t, page)[:, 0:size]
        r.grad_table[:, where] = value
        return squared(value)

    whole = vocab_rows // share
    squares = squares + lax.fori_loop(0, whole, page_strips, jnp.zeros((1, 1), F32))
    if vocab_rows > whole * share:
        squares = squares + add_page(
            whole, slice(whole * share, vocab_rows), vocab_rows - whole * share
        )
    r.squares[block * tensor + here] = jnp.broadcast_to(squares, (1, 128))
    to_squares = keep(Everyone(r.squares, r.sem_squares).start())
    to_squares.arrive()
    norm = jnp.sqrt(sum_blocks(r.squares))
    r.norm[...] = norm[:, 0:1]
    r.clip[...] = (MAX_NORM / jnp.maximum(norm, MAX_NORM))[:, 0:1]
    r.loss_sum[...] = loss_sum
    r.loss_count[...] = loss_count
    for copy in held[5:]:
        copy.wait()
    for move in moves:
        move.finish()


def run_step(blocks, tensor, experts, small, held, scalars):
    rows = small["own_ids"].shape[1]
    every = rows * blocks
    picks = small["own_offsets"].shape[1]
    count = picks * blocks
    columns, width = held["proj_weight"].shape[1:]
    features = columns * blocks
    hidden = held["in_weight"].shape[1]
    vocab_rows = held["table_weight"].shape[1]
    heads, bucket_count = scalars["position_bias"].shape
    share = -(-vocab_rows // (blocks * STRIP)) * STRIP
    group = blocks // tensor
    chunk = group * rows
    wide = features + 128
    outputs = dict(
        grad_table=(columns, vocab_rows),
        grad_proj=(3, columns, width),
        grad_map=(width, columns),
        grad_small=(8, 128),
        grad_in=(features, hidden),
        grad_out=(hidden, features),
        grad_bias=(heads, bucket_count, 128),
        norm=(1, 1),
        clip=(1, 1),
        loss_sum=(1, 1),
        loss_count=(1, 1),
    )
    scratch = dict(
        known=((blocks, 8, rows), F32),
        small=((blocks, 8, 128), F32),
        proj=((blocks, columns * 3 * width // 128, 128), BF16),
        maps=((tensor, blocks, columns * width // 128, 128), BF16),
        pages=((blocks, columns, share), BF16),
        table=((blocks, columns, share), BF16),
        id_row=((1, every), F32),
        id_high=((1, every), F32),
        id_place=((1, every), F32),
        id_low=((every, STRIP), BF16),
        looked=((tensor, group, columns, rows), BF16),
        first=((tensor, group, columns, rows), BF16),
        router=((128, features), BF16),
        gains=((8, features), F32),
        roots=((1, every), F32),
        streams=((tensor, blocks, columns, chunk), BF16),
        shifted=((count, 2 * every), jnp.int32),
        bucket=((count, every), jnp.int32),
        bias=((heads, count, every), F32),
        keys=((width, every), BF16),
        values=((width, every), BF16),
        probs=((heads, count, every), F32),
        heads=((tensor, count, width), BF16),
        middle=((count, features), F32),
        piece=((count, features), BF16),
        gates=((count, 128), F32),
        gate=((count, 1), F32),
        stats=((blocks * tensor, 4, 128), F32),
        d_logits=((4, blocks, count // 4, share), BF16),
        sent=((count, features), BF16),
        wide=((count, wide), BF16),
        d_keys=((width, every), BF16),
        d_values=((width, every), BF16),
        part=((columns + 16, every), BF16),
        part_in=((tensor, columns + 16, chunk), BF16),
        part_all=((tensor, columns + 16, chunk), BF16),
        bias_rows=((heads, bucket_count, 8, 128), F32),
        squares=((blocks * tensor, 1, 128), F32),
    )
    scratch.update({name: (array.shape, array.dtype) for name, array in small.items()})
    outputs.update({name: array.shape for name, array in held.items()})
    dp, ten = (2, blocks), (2, tensor)
    sems = dict(
        load_sems=(len(small),),
        held_sems=(len(held),),
        sem_squares=(2, blocks * tensor),
        sem_stats=(2, blocks * tensor),
        sem_logits=(4, 2, blocks),
        sem_known=dp,
        sem_small=dp,
        sem_proj=dp,
        sem_map=dp,
        sem_pages=dp,
        sem_first=ten,
        sem_stream=dp,
        sem_streams=(2, 3, blocks),
        sem_maps=(2, 3, blocks),
        sem_heads=ten,
        sem_part=ten,
        sem_part_all=ten,
    )
    height = count // tensor
    for number, span in enumerate((features, features, wide)):
        shapes = (
            (tensor, height, span),
            (span // 128, height, 128),
            (blocks, height, 128),
            (span // 128, height, 128),
            (tensor, height, span),
        )
        scratch.update({f"sum_{k}_{number}": (shape, BF16) for k, shape in enumerate(shapes)})
        for k, shape in enumerate((ten, dp, dp, ten)):
            sems[f"sum_sem_{k}_{number}"] = shape
    copied = {**small, **held}
    names = tuple(name + OUTSIDE for name in copied) + tuple(scalars)
    names += tuple(outputs) + tuple(scratch) + tuple(sems)
    starts = scalars["picture_start"].shape[1]
    results = pl.pallas_call(
        functools.partial(
            step_kernel, names, tuple(small), tuple(held), experts, vocab_rows, starts
        ),
        out_shape=[
            jax.ShapeDtypeStruct(shape, F32) if shape == (1, 1) else pltpu.VMEM(shape, F32)
            for shape in outputs.values()
        ],
        in_specs=[pl.BlockSpec(memory_space=pltpu.HBM)] * len(copied)
        + [pl.BlockSpec(memory_space=pltpu.SMEM)] * len(scalars),
        out_specs=[WHOLE] * len(outputs),
        scratch_shapes=[pltpu.VMEM(*spec) for spec in scratch.values()]
        + [DMA(shape) for shape in sems.values()],
        compiler_params=pltpu.CompilerParams(
            collective_id=0, has_side_effects=True, vmem_limit_bytes=VMEM_BYTES
        ),
        name="training_step",
    )(*copied.values(), *scalars.values())
    return dict(zip(outputs, results))


def update_piece(weight, first, second, grad, rate, decay):
    first = BETA1 * first + (1 - BETA1) * grad
    second = BETA2 * second + (1 - BETA2) * (grad * grad)
    spread = second * lax.rsqrt(second) * math.sqrt(1 / (1 - BETA2**STEP)) + ADAM_EPS
    step = first / spread
    return weight * (1 - rate * decay) - (rate / (1 - BETA1**STEP)) * step, first, second


def update_kernel(jobs, clip, *refs):
    grads, refs = refs[: len(jobs)], refs[len(jobs) :]
    total = 3 * len(jobs)
    olds, outs, news, done = refs[:total], refs[total : 2 * total], refs[2 * total : -1], refs[-1]
    factor = clip[0, 0]
    copies = []
    for index, (height, rate, decay, begin, reduced) in enumerate(jobs):
        trio = slice(3 * index, 3 * index + 3)
        whole = news[3 * index].shape[0]
        for piece in range(0, whole, height):
            rows = slice(piece, piece + height)
            if reduced:
                change = jnp.sum(grads[index][...], -1)
            elif begin is not None:
                change = grads[index][begin : begin + whole, 0 : news[3 * index].shape[1]]
            else:
                change = grads[index][rows]
            values = update_piece(
                *(ref[rows] for ref in olds[trio]), factor * change, rate, decay
            )
            for which, value in enumerate(values):
                new, out = news[3 * index + which], outs[3 * index + which]
                new[rows] = value
                part = pl.ds(piece, height)
                copy = pltpu.make_async_copy(new.at[part], out.at[part], done.at[len(copies)])
                copy.start()
                copies.append(copy)
    for copy in copies:
        copy.wait()


def run_update(clip, jobs, grads, olds):
    shapes = [old.shape for old in olds]
    pieces = sum(3 * shapes[3 * k][0] // job[0] for k, job in enumerate(jobs))
    results = pl.pallas_call(
        functools.partial(update_kernel, jobs),
        out_shape=[jax.ShapeDtypeStruct(shape, F32) for shape in shapes],
        in_specs=[pl.BlockSpec(memory_space=pltpu.SMEM)] + [WHOLE] * (len(grads) + len(olds)),
        out_specs=[pl.BlockSpec(memory_space=pltpu.HBM)] * len(shapes),
        scratch_shapes=[pltpu.VMEM(shape, F32) for shape in shapes] + [DMA((pieces,))],
        compiler_params=pltpu.CompilerParams(vmem_limit_bytes=UPDATE_BYTES),
        name="update",
    )(clip, *grads, *olds)
    return [results[3 * k : 3 * k + 3] for k in range(len(jobs))]


def fast_local(
    token_ids,
    targets,
    loss_offsets,
    routes,
    picture_start,
    buckets,
    embedding,
    embedding_first,
    embedding_second,
    attn_proj,
    attn_proj_first,
    attn_proj_second,
    out_proj,
    out_proj_first,
    out_proj_second,
    router,
    router_first,
    router_second,
    expert_in,
    expert_in_first,
    expert_in_second,
    expert_out,
    expert_out_first,
    expert_out_second,
    norm_gains,
    norm_gains_first,
    norm_gains_second,
    position_bias,
    position_bias_first,
    position_bias_second,
):
    dp_count = lax.axis_size("dp")
    tensor_count = lax.axis_size("tensor")
    experts = router.shape[0]
    small = dict(
        own_ids=token_ids[None, :],
        own_targets=targets[None, :],
        own_offsets=loss_offsets[None, :],
        own_routes=routes.T,
        own_buckets=buckets[None, :],
        own_router=router,
        own_gains=norm_gains,
    )
    held = dict(
        proj_weight=attn_proj,
        map_weight=out_proj,
        table_weight=embedding.T,
        in_weight=expert_in,
        out_weight=expert_out,
        table_first=embedding_first.T,
        table_second=embedding_second.T,
        in_first=expert_in_first,
        in_second=expert_in_second,
        out_first=expert_out_first,
        out_second=expert_out_second,
        proj_first=attn_proj_first,
        proj_second=attn_proj_second,
        map_first=out_proj_first,
        map_second=out_proj_second,
    )
    scalars = dict(position_bias=position_bias, picture_start=picture_start)
    g = types.SimpleNamespace(**run_step(dp_count, tensor_count, experts, small, held, scalars))
    kinds = (
        (8, 0, None, False),
        (expert_in.shape[0] // 8, 4, None, False),
        (expert_out.shape[0] // 8, 5, None, False),
        (1, 1, None, False),
        (out_proj.shape[0], 2, None, False),
        (experts, 3, 0, False),
        (3, 6, 4, False),
        (position_bias.shape[0], 7, None, True),
    )
    jobs = tuple(
        (height, RATES[k], DECAYS[k], begin, reduced) for height, k, begin, reduced in kinds
    )
    grads = (g.grad_table, g.grad_in, g.grad_out, g.grad_proj, g.grad_map)
    grads += (g.grad_small, g.grad_small, g.grad_bias)
    olds = (g.table_weight, g.table_first, g.table_second, g.in_weight, g.in_first, g.in_second)
    olds += (g.out_weight, g.out_first, g.out_second, g.proj_weight, g.proj_first, g.proj_second)
    olds += (g.map_weight, g.map_first, g.map_second, router, router_first, router_second)
    olds += (norm_gains, norm_gains_first, norm_gains_second)
    olds += (position_bias, position_bias_first, position_bias_second)
    new = run_update(g.clip, jobs, grads, olds)
    results = [value.T for value in new[0]]
    for k in (3, 4, 5, 1, 2, 6, 7):
        results.extend(new[k])
    grad_norm, loss_sum, loss_count = (
        value.reshape(()) for value in (g.norm, g.loss_sum, g.loss_count)
    )
    return (*results, grad_norm, loss_sum, loss_count)


def local(
    token_ids,
    targets,
    loss_offsets,
    routes,
    picture_start,
    buckets,
    embedding,
    embedding_first,
    embedding_second,
    attn_proj,
    attn_proj_first,
    attn_proj_second,
    out_proj,
    out_proj_first,
    out_proj_second,
    router,
    router_first,
    router_second,
    expert_in,
    expert_in_first,
    expert_in_second,
    expert_out,
    expert_out_first,
    expert_out_second,
    norm_gains,
    norm_gains_first,
    norm_gains_second,
    position_bias,
    position_bias_first,
    position_bias_second,
):
    f32 = jnp.float32
    bf16 = jnp.bfloat16
    dp_count = lax.axis_size("dp")
    tensor_count = lax.axis_size("tensor")
    dp_place = lax.axis_index("dp")
    tensor_place = lax.axis_index("tensor")
    rows = token_ids.shape[0]
    every = rows * dp_count
    length = min(SEQ, every)
    seqs = every // length
    sub = rows // seqs
    scale = 1.0 / math.sqrt(HD)
    vocab_rows = embedding.shape[0]
    table, projection, output_map, router_full, gain_full = (
        lax.all_gather(embedding.astype(bf16), "dp", axis=1, tiled=True),
        lax.all_gather(attn_proj.astype(bf16), "dp", axis=1, tiled=True),
        lax.all_gather(out_proj.astype(bf16), "dp", axis=1, tiled=True),
        lax.all_gather(router.astype(bf16), "dp", axis=1, tiled=True),
        lax.all_gather(norm_gains.astype(bf16), "dp", axis=1, tiled=True),
    )
    gain = gain_full.astype(f32)
    features = table.shape[1]
    offset = token_ids - tensor_place * vocab_rows
    owned = (offset >= 0) & (offset < vocab_rows)
    offset = jnp.clip(offset, 0, vocab_rows - 1)
    looked = jnp.take(table, offset, axis=0).astype(f32)
    stream_in = tensor_total(jnp.where(owned[:, None], looked, 0.0))
    pos_here = dp_place * sub + jnp.arange(sub, dtype=jnp.int32)
    seq_positions = jnp.arange(length, dtype=jnp.int32)
    picture_all = jax.vmap(lambda starts: picture_of(seq_positions, starts, PIECE))(picture_start)
    picture_here = lax.dynamic_slice_in_dim(picture_all, dp_place * sub, sub, 1)
    bucket_ids = jnp.arange(position_bias.shape[1], dtype=jnp.int32)
    bucket_hot = (bucket_ids[:, None] == buckets[None, :]).astype(f32)
    relative = jnp.dot(position_bias, bucket_hot, precision=HIGH)
    normed_in = normed(stream_in, gain[0]).astype(bf16)
    fresh = jnp.einsum("td,sde->ste", normed_in, projection, preferred_element_type=f32).astype(
        bf16
    )
    width = fresh.shape[2]
    heads = width // HD
    keys_local = fresh[1].reshape(seqs, sub, width)
    values_local = fresh[2].reshape(seqs, sub, width)
    query_heads = fresh[0].reshape(seqs, sub, heads, HD)
    keys_all, values_all = (
        lax.all_gather(keys_local, "dp", axis=1, tiled=True),
        lax.all_gather(values_local, "dp", axis=1, tiled=True),
    )
    block = min(512, length)
    blocks = length // block
    block_ids = jnp.arange(blocks, dtype=jnp.int32)

    def pair_scores(q_heads, q_pos, q_pic, k_heads, k_pos, k_pic, bias):
        raw = (
            jnp.einsum("sqhd,skhd->shqk", q_heads, k_heads, preferred_element_type=f32) * scale
            + bias[None]
        )
        allowed = (k_pos[None, :] <= q_pos[:, None])[None] | (
            k_pic[:, None, :] == q_pic[:, :, None]
        ) & (q_pic[:, :, None] >= 0)
        return jnp.where(allowed[:, None], raw, NEGATIVE)

    def key_slice(source, start):
        return lax.dynamic_slice_in_dim(source, start, block, 1).reshape(seqs, block, heads, HD)

    def own_bias(start):
        return rel_window(relative, dp_place * sub, sub, start, block, length)

    def fwd_scores(index, key_source):
        start = index * block
        key_pos = start + jnp.arange(block, dtype=jnp.int32)
        return pair_scores(
            query_heads,
            pos_here,
            picture_here,
            key_slice(key_source, start),
            key_pos,
            lax.dynamic_slice_in_dim(picture_all, start, block, 1),
            own_bias(start),
        )

    def max_step(carry, index):
        top, total = carry
        s = fwd_scores(index, keys_all)
        new_top = jnp.maximum(top, jnp.max(s, -1))
        terms = jnp.where(s > 0.5 * NEGATIVE, jnp.exp(s - new_top[..., None]), 0.0)
        total = total * jnp.exp(top - new_top) + jnp.sum(terms, -1)
        return ((new_top, total), None)

    start_top = jnp.full((seqs, heads, sub), NEGATIVE, f32)
    (top, total), unused = lax.scan(
        max_step, (start_top, jnp.zeros((seqs, heads, sub), f32)), block_ids
    )
    log_total = top + jnp.log(total)

    def out_step(accum, index):
        s = fwd_scores(index, keys_all)
        probs = jnp.exp(s - log_total[..., None]).astype(bf16)
        value_heads = key_slice(values_all, index * block)
        return (
            accum + jnp.einsum("shqk,skhd->sqhd", probs, value_heads, preferred_element_type=f32),
            None,
        )

    attended, unused = lax.scan(out_step, jnp.zeros((seqs, sub, heads, HD), f32), block_ids)
    attended_low = attended.reshape(rows, width).astype(bf16)
    stream_mid = stream_in + tensor_total(
        jnp.dot(attended_low, output_map, preferred_element_type=f32)
    )
    normed_mid = normed(stream_mid, gain[1]).astype(bf16)
    router_logits = jnp.dot(normed_mid, router_full.T, preferred_element_type=f32)
    gates = jax.nn.softmax(jnp.take_along_axis(router_logits, routes, 1), -1)
    experts = router_full.shape[0]
    top_k = routes.shape[1]
    capacity = 2 * rows * top_k // experts
    flat = routes.reshape(-1)
    owner = jnp.arange(rows * top_k, dtype=jnp.int32) // top_k
    hits = (flat[:, None] == jnp.arange(experts, dtype=jnp.int32)[None, :]).astype(jnp.int32)
    slot = jnp.sum(jnp.cumsum(hits, 0) * hits, 1) - 1
    first_row = 2 * flat * capacity + slot

    def pack(values):
        buffer = jnp.zeros((experts, capacity, features), bf16).at[flat, slot].set(values)
        return jnp.repeat(buffer, 2, axis=0).reshape(2 * experts * capacity, features)

    def unpack(values):
        return values[first_row].astype(f32) + values[first_row + capacity].astype(f32)

    in_low = expert_in.astype(bf16)
    out_low = expert_out.astype(bf16)
    arrived = route_exchange(pack(normed_mid[owner]))
    inner = jnp.dot(arrived, in_low, preferred_element_type=f32)
    active = jax.nn.gelu(inner).astype(bf16)
    produced = jnp.dot(active, out_low, preferred_element_type=f32).astype(bf16)
    returned = unpack(route_exchange(produced))
    mixed = jnp.sum((gates.reshape(-1)[:, None] * returned).reshape(rows, top_k, features), 1)
    stream_out = stream_mid + tensor_total(mixed)
    normed_out = normed(stream_out, gain[2]).astype(bf16)
    picked = normed_out[loss_offsets]
    logits = jnp.dot(picked, table.T, preferred_element_type=f32)
    wanted = targets[loss_offsets] - tensor_place * vocab_rows
    hit = jnp.arange(vocab_rows, dtype=jnp.int32)[None, :] == wanted[:, None]
    local_top = jnp.max(logits, -1)
    stats = (
        local_top,
        jnp.sum(jnp.exp(logits - local_top[:, None]), -1),
        jnp.sum(jnp.where(hit, logits, 0.0), -1),
        jnp.sum(logits, -1),
    )
    peak, vocab_total, target_logit, logit_sum = merged(stats, "tensor", combine_stats)
    loss_total = peak + jnp.log(vocab_total)
    weight = (picture_here.reshape(rows)[loss_offsets] < 0).astype(f32)
    per_row = (
        loss_total
        - (1 - SMOOTH) * target_logit
        - SMOOTH * logit_sum / VOCAB
        + ZLOSS * loss_total * loss_total
    )
    loss_local = jnp.sum(weight * per_row)
    soft = jnp.exp(logits - loss_total[:, None])
    d_logits = (
        weight[:, None]
        * (
            (1 + 2 * ZLOSS * loss_total)[:, None] * soft
            - (1 - SMOOTH) * hit.astype(f32)
            - SMOOTH / VOCAB
        )
    ).astype(bf16)
    d_picked = jnp.dot(d_logits, table, preferred_element_type=f32)
    grad_table = jnp.dot(d_logits.T, picked, preferred_element_type=f32)
    d_normed_out = tensor_total(jnp.zeros((rows, features), f32).at[loss_offsets].add(d_picked))
    d_stream_out, grad_final = norm_back(stream_out, gain[2], d_normed_out)
    d_piece = (gates.reshape(-1)[:, None] * d_stream_out[owner]).astype(bf16)
    d_arrived = route_exchange(pack(d_piece))
    d_active = jnp.dot(d_arrived, out_low.T, preferred_element_type=f32)
    unused, gelu_pull = jax.vjp(jax.nn.gelu, inner)
    d_inner = gelu_pull(d_active)[0].astype(bf16)
    grad_out = jnp.dot(active.T, d_arrived, preferred_element_type=f32)
    grad_in = jnp.dot(arrived.T, d_inner, preferred_element_type=f32)
    sent_back = jnp.dot(d_inner, in_low.T, preferred_element_type=f32).astype(bf16)
    d_routes = unpack(route_exchange(sent_back))
    gate_part = jnp.sum(d_stream_out[owner] * returned, -1).reshape(rows, top_k)
    route_part = jnp.sum(d_routes.reshape(rows, top_k, features), 1)
    d_from_experts, d_gates = tensor_total((route_part, gate_part))
    d_chosen = gates * (d_gates - jnp.sum(gates * d_gates, -1, keepdims=True))
    expert_hot = (routes[..., None] == jnp.arange(experts, dtype=jnp.int32)).astype(f32)
    d_router_logits = jnp.sum(expert_hot * d_chosen[..., None], 1).astype(bf16)
    grad_router = jnp.dot(d_router_logits.T, normed_mid, preferred_element_type=f32)
    d_normed_mid = d_from_experts + jnp.dot(
        d_router_logits, router_full, preferred_element_type=f32
    )
    d_from_mid, grad_middle = norm_back(stream_mid, gain[1], d_normed_mid)
    d_stream_mid = d_stream_out + d_from_mid
    d_attn_low = d_stream_mid.astype(bf16)
    grad_output_map = jnp.dot(attended_low.T, d_attn_low, preferred_element_type=f32)
    d_attended = jnp.dot(d_attn_low, output_map.T, preferred_element_type=f32).astype(bf16)
    d_heads = d_attended.reshape(seqs, sub, heads, HD)
    delta = jnp.moveaxis(jnp.sum(d_heads.astype(f32) * attended, -1), 2, 1)
    key_source, value_source = (
        lax.all_gather(keys_local, "dp", axis=1, tiled=True),
        lax.all_gather(values_local, "dp", axis=1, tiled=True),
    )

    def score_grads(
        q_heads, q_pos, q_pic, k_heads, k_pos, k_pic, bias, totals, deltas, dq_heads, v_heads
    ):
        s = pair_scores(q_heads, q_pos, q_pic, k_heads, k_pos, k_pic, bias)
        probs = jnp.exp(s - totals[..., None])
        d_probs = jnp.einsum("sqhd,skhd->shqk", dq_heads, v_heads, preferred_element_type=f32)
        d_scores = (probs * (d_probs - deltas[..., None])).astype(bf16)
        return (probs, d_scores)

    def key_step(carry, index):
        d_query, d_rel = carry
        start = index * block
        key_pos = start + jnp.arange(block, dtype=jnp.int32)
        key_heads = key_slice(key_source, start)
        value_heads = key_slice(value_source, start)
        bias, bias_pull = jax.vjp(
            lambda table_rel: rel_window(table_rel, dp_place * sub, sub, start, block, length),
            relative,
        )
        probs, d_scores = score_grads(
            query_heads,
            pos_here,
            picture_here,
            key_heads,
            key_pos,
            lax.dynamic_slice_in_dim(picture_all, start, block, 1),
            bias,
            log_total,
            delta,
            d_heads,
            value_heads,
        )
        d_query = (
            d_query
            + jnp.einsum("shqk,skhd->sqhd", d_scores, key_heads, preferred_element_type=f32) * scale
        )
        d_rel = d_rel + bias_pull(jnp.sum(d_scores.astype(f32), 0))[0]
        d_key = (
            jnp.einsum("shqk,sqhd->skhd", d_scores, query_heads, preferred_element_type=f32) * scale
        )
        d_value = jnp.einsum(
            "shqk,sqhd->skhd", probs.astype(bf16), d_heads, preferred_element_type=f32
        )
        joined = jnp.concatenate(
            [d_key.reshape(seqs, block, width), d_value.reshape(seqs, block, width)], 2
        )
        return ((d_query, d_rel), joined)

    start_carry = (jnp.zeros((seqs, sub, heads, HD), f32), jnp.zeros(relative.shape, f32))
    (d_query, d_rel), key_terms = lax.scan(key_step, start_carry, block_ids)
    d_bias = jnp.dot(d_rel, bucket_hot.T, precision=HIGH)
    ordered = jnp.moveaxis(key_terms, 0, 1).reshape(seqs, length, 2 * width)
    key_grads = lax.psum_scatter(ordered, "dp", scatter_dimension=1, tiled=True).reshape(
        rows, 2 * width
    )
    d_fresh = jnp.stack(
        [d_query.reshape(rows, width), key_grads[:, :width], key_grads[:, width:]]
    ).astype(bf16)
    grad_proj = jnp.einsum("td,ste->sde", normed_in, d_fresh, preferred_element_type=f32)
    d_normed_in = tensor_total(
        jnp.einsum("ste,sde->td", d_fresh, projection, preferred_element_type=f32)
    )
    d_from_in, grad_first = norm_back(stream_in, gain[0], d_normed_in)
    d_stream_in = d_stream_mid + d_from_in
    grad_table = grad_table + jnp.zeros((vocab_rows, features), f32).at[offset].add(
        jnp.where(owned[:, None], d_stream_in, 0.0)
    )
    sum_table, sum_proj, sum_output, sum_router, sum_gains = (
        lax.psum_scatter(grad_table, "dp", scatter_dimension=1, tiled=True),
        lax.psum_scatter(grad_proj, "dp", scatter_dimension=1, tiled=True),
        lax.psum_scatter(grad_output_map, "dp", scatter_dimension=1, tiled=True),
        lax.psum_scatter(grad_router, "dp", scatter_dimension=1, tiled=True),
        lax.psum_scatter(
            jnp.stack([grad_first, grad_middle, grad_final]), "dp", scatter_dimension=1, tiled=True
        ),
    )
    sum_bias = lax.psum(d_bias, "dp")
    squares = (
        jnp.sum(sum_table * sum_table)
        + jnp.sum(sum_proj * sum_proj)
        + jnp.sum(sum_output * sum_output)
        + jnp.sum(grad_in * grad_in)
        + jnp.sum(grad_out * grad_out)
        + (jnp.sum(sum_router * sum_router) + jnp.sum(sum_gains * sum_gains)) / tensor_count
        + jnp.sum(sum_bias * sum_bias) / dp_count
    )
    total_squares, loss_sum, loss_count = lax.psum(
        (squares, loss_local / tensor_count, jnp.sum(weight) / tensor_count), ("dp", "tensor")
    )
    grad_norm = jnp.sqrt(total_squares)
    clip = MAX_NORM / jnp.maximum(grad_norm, MAX_NORM)
    params = (
        embedding,
        attn_proj,
        out_proj,
        router,
        expert_in,
        expert_out,
        norm_gains,
        position_bias,
    )
    firsts = (
        embedding_first,
        attn_proj_first,
        out_proj_first,
        router_first,
        expert_in_first,
        expert_out_first,
        norm_gains_first,
        position_bias_first,
    )
    seconds = (
        embedding_second,
        attn_proj_second,
        out_proj_second,
        router_second,
        expert_in_second,
        expert_out_second,
        norm_gains_second,
        position_bias_second,
    )
    grads = (sum_table, sum_proj, sum_output, sum_router, grad_in, grad_out, sum_gains, sum_bias)
    results = []
    for index in range(8):
        results.extend(
            adam_update(
                params[index],
                firsts[index],
                seconds[index],
                clip * grads[index],
                RATES[index],
                DECAYS[index],
            )
        )
    return (
        results[0],
        results[1],
        results[2],
        results[3],
        results[4],
        results[5],
        results[6],
        results[7],
        results[8],
        results[9],
        results[10],
        results[11],
        results[12],
        results[13],
        results[14],
        results[15],
        results[16],
        results[17],
        results[18],
        results[19],
        results[20],
        results[21],
        results[22],
        results[23],
        grad_norm,
        loss_sum,
        loss_count,
    )


def fits(dp_count, tensor_count, arrays):
    token_ids, loss_offsets, routes, picture_start = arrays[0], arrays[2], arrays[3], arrays[4]
    columns, router, gains = arrays[6].shape[1], arrays[15], arrays[24]
    rows, picks = token_ids.shape[0], loss_offsets.shape[0]
    return (
        rows == 128
        and rows * dp_count <= SEQ
        and picture_start.shape[0] == 1
        and picks == 16
        and picks * dp_count == 128
        and dp_count % 4 == 0
        and tensor_count == 4
        and dp_count % router.shape[0] == 0
        and dp_count % 2 == 0
        and dp_count <= 8
        and router.shape[0] <= 4
        and routes.shape[1] == 2
        and gains.shape[0] == 3
        and columns % 32 == 0
        and arrays[9].shape[2] % 128 == 64
        and columns <= 128
    )


def solution(mesh):
    in_specs = (
        P("dp"),
        P("dp"),
        P("dp"),
        P("dp", None),
        P(),
        P(),
        P("tensor", "dp"),
        P("tensor", "dp"),
        P("tensor", "dp"),
        P(None, "dp", "tensor"),
        P(None, "dp", "tensor"),
        P(None, "dp", "tensor"),
        P("tensor", "dp"),
        P("tensor", "dp"),
        P("tensor", "dp"),
        P(None, "dp"),
        P(None, "dp"),
        P(None, "dp"),
        P(None, ("dp", "tensor")),
        P(None, ("dp", "tensor")),
        P(None, ("dp", "tensor")),
        P(("dp", "tensor"), None),
        P(("dp", "tensor"), None),
        P(("dp", "tensor"), None),
        P(None, "dp"),
        P(None, "dp"),
        P(None, "dp"),
        P("tensor", None),
        P("tensor", None),
        P("tensor", None),
    )
    out_specs = (
        P("tensor", "dp"),
        P("tensor", "dp"),
        P("tensor", "dp"),
        P(None, "dp", "tensor"),
        P(None, "dp", "tensor"),
        P(None, "dp", "tensor"),
        P("tensor", "dp"),
        P("tensor", "dp"),
        P("tensor", "dp"),
        P(None, "dp"),
        P(None, "dp"),
        P(None, "dp"),
        P(None, ("dp", "tensor")),
        P(None, ("dp", "tensor")),
        P(None, ("dp", "tensor")),
        P(("dp", "tensor"), None),
        P(("dp", "tensor"), None),
        P(("dp", "tensor"), None),
        P(None, "dp"),
        P(None, "dp"),
        P(None, "dp"),
        P("tensor", None),
        P("tensor", None),
        P("tensor", None),
        P(),
        P(),
        P(),
    )

    def chosen(*arrays):
        sizes = lax.axis_size("dp"), lax.axis_size("tensor")
        return (fast_local if fits(*sizes, arrays) else local)(*arrays)

    return jax.shard_map(chosen, mesh=mesh, in_specs=in_specs, out_specs=out_specs, check_vma=False)
```

```python
import functools
import math
import types

import jax
import jax.numpy as jnp
from jax.experimental import pallas as pl
from jax.experimental.pallas import tpu as pltpu
from jax import lax
from jax.sharding import PartitionSpec as P

HD = 64
VOCAB = 32000
PIECE = 256
SEQ = 4096
STEP = 10


SMOOTH = 0.1
ZLOSS = 0.0001
NORM_EPS = 1e-06
MAX_NORM = 1.0
BETA1 = 0.9
BETA2 = 0.95
ADAM_EPS = 1e-08
RATES = (0.04, 0.04, 1.0, 0.03, 0.07, 0.035, 1.0, 0.7)
DECAYS = (0.1, 0.1, 0.1, 0.1, 0.1, 0.1, 0.0, 0.0)
NEGATIVE = -1e30
HIGH = lax.Precision.HIGHEST


def merged(shard, axis, combine):
    everything = jax.tree.map(lambda part: lax.all_gather(part, axis), shard)
    initial = jax.tree.map(lambda part: part[0], everything)

    def lap(k, so_far):
        return combine(so_far, jax.tree.map(lambda part: part[k], everything))

    return lax.fori_loop(1, lax.axis_size(axis), lap, initial)


def normed(v, g):
    return v * lax.rsqrt(jnp.mean(v * v, -1, keepdims=True) + NORM_EPS) * g


def norm_back(v, g, upstream):
    unused, pull = jax.vjp(normed, v, g)
    return pull(upstream)


def picture_of(positions, starts, width):
    inside = (positions[:, None] >= starts[None, :]) & (
        positions[:, None] < starts[None, :] + width
    )
    number = jnp.arange(starts.shape[0], dtype=jnp.int32) + 1
    return jnp.sum(inside.astype(jnp.int32) * number[None, :], 1) - 1


def rel_window(relative, query_start, query_count, key_start, key_count, length):
    centre = query_start - key_start + length - 1
    window = lax.dynamic_slice_in_dim(
        relative, centre - key_count + 1, query_count + key_count - 1, 1
    )
    span = query_count + key_count
    wrapped = jnp.concatenate(
        [
            jnp.flip(window[:, :key_count], 1),
            jnp.zeros((window.shape[0], 1), window.dtype),
            jnp.flip(window[:, key_count:], 1),
        ],
        1,
    )
    tiled = jnp.tile(wrapped, (1, query_count))[:, : query_count * (span - 1)]
    return tiled.reshape(window.shape[0], query_count, span - 1)[:, :, :key_count]


def tensor_total(value):
    return lax.psum(value, "tensor")


def route_exchange(value):
    return lax.all_to_all(value, "dp", split_axis=0, concat_axis=0, tiled=True)


def combine_stats(left, right):
    peak = jnp.maximum(left[0], right[0])
    total = left[1] * jnp.exp(left[0] - peak) + right[1] * jnp.exp(right[0] - peak)
    return (peak, total, left[2] + right[2], left[3] + right[3])


def adam_update(weight, first, second, grad, rate, decay):
    first = BETA1 * first + (1 - BETA1) * grad
    second = BETA2 * second + (1 - BETA2) * grad * grad
    fixed_first = first / (1 - BETA1**STEP)
    fixed_second = second / (1 - BETA2**STEP)
    weight = weight - rate * (fixed_first / (jnp.sqrt(fixed_second) + ADAM_EPS) + decay * weight)
    return (weight, first, second)


MESH = pl.DeviceIdType.MESH
DP = "dp"
OUTSIDE = "_hbm"
TENSOR = "tensor"
UPDATE_BYTES = 20 * 1024 * 1024
VMEM_BYTES = 33 * 1024 * 1024
WHOLE = pl.BlockSpec(memory_space=pltpu.VMEM)
DMA = pltpu.SemaphoreType.DMA
F32 = jnp.float32
BF16 = jnp.bfloat16
STRIP = 256


def greet_everyone():
    barrier = pltpu.get_barrier_semaphore()
    tensor = lax.axis_size(TENSOR)
    total = lax.axis_size(DP) * tensor
    here = lax.axis_index(DP) * tensor + lax.axis_index(TENSOR)

    def signal(step, carry):
        other = lax.rem(here + step, total)
        pl.semaphore_signal(
            barrier,
            inc=1,
            device_id={DP: other // tensor, TENSOR: lax.rem(other, tensor)},
            device_id_type=MESH,
        )
        return carry

    lax.fori_loop(1, total, signal, 0)
    return barrier, total - 1


class Move:
    def __init__(self, axis, source, dest, sems, steps=None):
        self.axis, self.count, self.here = axis, lax.axis_size(axis), lax.axis_index(axis)
        self.source, self.dest, self.sems = source, dest, sems
        self.steps = range(1, self.count) if steps is None else steps

    def copy(self, step):
        target = lax.rem(self.here + step, self.count)
        return pltpu.make_async_remote_copy(
            src_ref=self.source(target),
            dst_ref=self.dest.at[self.here],
            send_sem=self.sems.at[0, step],
            recv_sem=self.sems.at[1, step],
            device_id={self.axis: target},
            device_id_type=MESH,
        )

    def start(self):
        for step in self.steps:
            self.copy(step).start()
        return self

    def arrive(self):
        for step in self.steps:
            self.copy(step).wait_recv()

    def finish(self):
        for step in self.steps:
            self.copy(step).wait_send()


def scatter_rows(axis, source, dest, sems):
    height = dest.shape[1]
    return Move(
        axis,
        lambda target: source.at[pl.ds(pl.multiple_of(target * height, height), height)],
        dest,
        sems,
    ).start()


def share_block(axis, dest, sems):
    here = lax.axis_index(axis)
    return Move(axis, lambda target: dest.at[here], dest, sems).start()


class PairGather:
    def __init__(self, buffer, sems):
        self.buffer, self.sems = buffer, sems
        self.count, self.here = lax.axis_size(DP), lax.axis_index(DP)
        self.partner = self.here + 1 - 2 * lax.rem(self.here, 2)
        self.half = self.count // 2

    def copy(self, block, target, slot):
        return pltpu.make_async_remote_copy(
            src_ref=self.buffer.at[block],
            dst_ref=self.buffer.at[block],
            send_sem=self.sems.at[0, slot],
            recv_sem=self.sems.at[1, slot],
            device_id={DP: target},
            device_id_type=MESH,
        )

    def direct(self, step):
        return self.copy(self.here, lax.rem(self.here + 2 * step, self.count), step)

    def onward(self, step):
        block = lax.rem(self.here + self.count - 2 * step, self.count)
        return self.copy(block, self.partner, self.half + step)

    def start(self):
        for step in range(1, self.half):
            self.direct(step).start()
        self.onward(0).start()
        return self

    def forward_one(self, step):
        self.direct(step).wait_recv()
        self.onward(step).start()

    def forward(self):
        for step in range(1, self.half):
            self.forward_one(step)

    def arrive(self):
        for step in range(self.half):
            self.onward(step).wait_recv()

    def finish(self):
        for step in range(1, self.half):
            self.direct(step).wait_send()
        for step in range(self.half):
            self.onward(step).wait_send()


class Relay:
    def __init__(self, buffer, dp_sems, sems):
        self.buffer, self.sems = buffer, sems
        self.here = lax.axis_index(TENSOR)
        self.gather = PairGather(buffer.at[self.here], dp_sems)
        self.far = lax.rem(self.here + 2, 4)
        self.near = self.here + 1 - 2 * lax.rem(self.here, 2)
        self.blocks, self.block = lax.axis_size(DP), lax.axis_index(DP)
        self.half = self.blocks // 2
        partner = self.gather.partner
        own = [lax.rem(self.block + self.blocks - 2 * k, self.blocks) for k in range(self.half)]
        other = [lax.rem(partner + self.blocks - 2 * k, self.blocks) for k in range(self.half)]
        self.order = own + other

    def copy(self, kind, index):
        source = self.far if kind == 2 else self.here
        block = self.order[index]
        return pltpu.make_async_remote_copy(
            src_ref=self.buffer.at[source, block],
            dst_ref=self.buffer.at[source, block],
            send_sem=self.sems.at[0, kind, index],
            recv_sem=self.sems.at[1, kind, index],
            device_id={TENSOR: self.far if kind == 0 else self.near},
            device_id_type=MESH,
        )

    def send(self, index):
        self.copy(0, index).start()
        self.copy(1, index).start()

    def start(self):
        self.gather.start()
        self.send(0)
        return self

    def pass_on(self):
        for step in range(1, self.half):
            self.gather.forward_one(step)
            self.send(step)
        for step in range(self.half):
            self.gather.onward(step).wait_recv()
            self.send(self.half + step)

    def spread(self):
        for index in range(self.blocks):
            self.copy(0, index).wait_recv()
            self.copy(2, index).start()

    def arrive(self):
        for index in range(self.blocks):
            self.copy(1, index).wait_recv()
            self.copy(2, index).wait_recv()

    def finish(self):
        self.gather.finish()
        for index in range(self.blocks):
            for kind in range(3):
                self.copy(kind, index).wait_send()


def split_again(tile):
    value = tile + pltpu.roll(tile, 64, 1)
    high = value.astype(BF16).astype(F32)
    return jnp.where(lanes(tile.shape) < 64, high, value - high)


class AllSum:
    def __init__(self, source, scratch, sems, halves):
        self.source, self.sems, self.halves = source, sems, halves
        self.parts, self.tiles, self.arrived, self.done, self.whole = scratch
        self.here, self.block = lax.axis_index(TENSOR), lax.axis_index(DP)
        self.height = self.parts.shape[1]
        self.owners = self.tiles.shape[0]
        self.own = pl.ds(pl.multiple_of(self.here * self.height, self.height), self.height)
        self.first = scatter_rows(TENSOR, source, self.parts, sems[0])
        self.parts[self.here] = source[self.own, :]

    def owned(self, act):
        pl.when(self.block < self.owners)(act)

    def to_owner(self, owner):
        return pltpu.make_async_remote_copy(
            src_ref=self.tiles.at[owner],
            dst_ref=self.arrived.at[self.block],
            send_sem=self.sems[1].at[0, owner],
            recv_sem=self.sems[1].at[1, self.block],
            device_id={DP: owner},
            device_id_type=MESH,
        )

    def from_block(self, k):
        return pltpu.make_async_remote_copy(
            src_ref=self.tiles.at[0],
            dst_ref=self.arrived.at[k],
            send_sem=self.sems[1].at[0, 0],
            recv_sem=self.sems[1].at[1, k],
            device_id={DP: k},
            device_id_type=MESH,
        )

    def others(self, limit, act):
        for k in range(limit):
            pl.when(self.block != k)(lambda k=k: act(k))

    def tile_to(self, k):
        return pltpu.make_async_remote_copy(
            src_ref=self.done.at[self.block],
            dst_ref=self.done.at[self.block],
            send_sem=self.sems[2].at[0, k],
            recv_sem=self.sems[2].at[1, self.block],
            device_id={DP: k},
            device_id_type=MESH,
        )

    def tile_from(self, k):
        return pltpu.make_async_remote_copy(
            src_ref=self.done.at[k],
            dst_ref=self.done.at[k],
            send_sem=self.sems[2].at[0, k],
            recv_sem=self.sems[2].at[1, k],
            device_id={DP: k},
            device_id_type=MESH,
        )

    def scatter(self, factor=None):
        self.first.arrive()
        total = sum_blocks(self.parts)
        if factor is not None:
            total = total * factor[self.own, :]
        for owner in range(self.owners):
            tile = total[:, owner * 128 : (owner + 1) * 128]
            if self.halves and owner == self.owners - 1:
                tile = split_again(tile)
            self.tiles[owner] = tile.astype(BF16)
        self.others(self.owners, lambda owner: self.to_owner(owner).start())

        @self.owned
        def _():
            self.arrived[self.block] = self.tiles[self.block]

    def gather(self):
        blocks = lax.axis_size(DP)

        @self.owned
        def _():
            self.others(blocks, lambda k: self.from_block(k).wait_recv())
            tile = sum_blocks(self.arrived)
            if self.halves:
                tile = jnp.where(self.block == self.owners - 1, split_again(tile), tile)
            self.done[self.block] = tile.astype(BF16)
            self.others(blocks, lambda k: self.tile_to(k).start())

    def result(self):
        self.others(self.owners, lambda k: self.tile_from(k).wait_recv())
        for k in range(self.owners):
            self.whole[self.here, :, k * 128 : (k + 1) * 128] = self.done[k]
        self.last = share_block(TENSOR, self.whole, self.sems[3])
        self.last.arrive()
        return across(self.whole, 0).astype(F32)

    def finish(self):
        self.first.finish()
        self.others(self.owners, lambda owner: self.to_owner(owner).wait_send())
        blocks = lax.axis_size(DP)
        self.owned(lambda: self.others(blocks, lambda k: self.tile_to(k).wait_send()))
        self.last.finish()


class Everyone:
    def __init__(self, buffer, sems):
        self.buffer, self.sems = buffer, sems
        self.tensor = lax.axis_size(TENSOR)
        self.total = lax.axis_size(DP) * self.tensor
        self.here = lax.axis_index(DP) * self.tensor + lax.axis_index(TENSOR)

    def copy(self, step):
        other = lax.rem(self.here + step, self.total)
        return pltpu.make_async_remote_copy(
            src_ref=self.buffer.at[self.here],
            dst_ref=self.buffer.at[self.here],
            send_sem=self.sems.at[0, step],
            recv_sem=self.sems.at[1, step],
            device_id={DP: other // self.tensor, TENSOR: lax.rem(other, self.tensor)},
            device_id_type=MESH,
        )

    def each(self, act):
        def one(step, carry):
            act(self.copy(step))
            return carry

        lax.fori_loop(1, self.total, one, 0)

    def start(self):
        self.each(lambda copy: copy.start())
        return self

    def arrive(self):
        self.each(lambda copy: copy.wait_recv())

    def finish(self):
        self.each(lambda copy: copy.wait_send())


def dot_nt(a, b):
    return lax.dot_general(a, b, (((1,), (1,)), ((), ())), preferred_element_type=F32)


def dot_nn(a, b):
    return jnp.dot(a, b, preferred_element_type=F32)


def root_of(v):
    return lax.rsqrt(jnp.mean(v * v, -1, keepdims=True) + NORM_EPS)


def low(v):
    return v.astype(BF16).astype(F32)


def gelu_value(x):
    slope = math.sqrt(2.0 / math.pi)
    return 0.5 * x * (1.0 + jnp.tanh(slope * (x + 0.044715 * (x * x * x))))


def gelu_slope(x):
    slope = math.sqrt(2.0 / math.pi)
    t = jnp.tanh(slope * (x + 0.044715 * (x * x * x)))
    return 0.5 * (1.0 + t) + 0.5 * x * (1.0 - t * t) * (slope * (1.0 + 3 * 0.044715 * x * x))


def lanes(shape):
    return lax.broadcasted_iota(jnp.int32, shape, len(shape) - 1)


def sublanes(shape):
    return lax.broadcasted_iota(jnp.int32, shape, len(shape) - 2)


def tensor_sum(total, buffer, sems):
    buffer[lax.axis_index(TENSOR)] = total.astype(BF16)
    move = share_block(TENSOR, buffer, sems)
    move.arrive()
    return sum_blocks(buffer), move


def norm_back_rows(v, g, upstream):
    root = root_of(v)
    scaled = g * upstream
    inner = jnp.sum(scaled * v, -1, keepdims=True)
    back = root * scaled - v * (root * root * root * inner / v.shape[-1])
    return back, jnp.sum(upstream * v * root, 0, keepdims=True)


def sum_blocks(ref):
    total = ref[0].astype(F32)
    for k in range(1, ref.shape[0]):
        total = total + ref[k].astype(F32)
    return total


def packed_rows(value):
    rows, wide = value.shape
    whole, half = wide // 128, rows // 2
    tail = value[:, whole * 128 :]
    parts = [value[:, t * 128 : (t + 1) * 128] for t in range(whole)]
    return jnp.concatenate(parts + [jnp.concatenate([tail[0:half], tail[half:]], 1)], 0)


def unpacked_rows(value, rows):
    whole = value.shape[0] // rows
    tail = value[whole * rows :]
    parts = [value[t * rows : (t + 1) * rows] for t in range(whole)]
    return jnp.concatenate(parts + [jnp.concatenate([tail[:, 0:64], tail[:, 64:]], 0)], 1)


def across(ref, axis):
    return jnp.concatenate([ref[k] for k in range(ref.shape[0])], axis)


def squared(value):
    return jnp.sum(value * value, keepdims=True)


def step_kernel(names, small, weights, experts, vocab_rows, starts, *refs):
    r = types.SimpleNamespace(**dict(zip(names, refs, strict=True)))
    block, here = lax.axis_index(DP), lax.axis_index(TENSOR)
    blocks, tensor = lax.axis_size(DP), lax.axis_size(TENSOR)
    rows = r.own_ids.shape[1]
    every = rows * blocks
    picks = r.own_offsets.shape[1]
    count = picks * blocks
    columns, width = r.proj_weight.shape[1:]
    features = columns * blocks
    heads = width // HD
    share = r.pages.shape[2]
    group = blocks // tensor
    scale = 1.0 / math.sqrt(HD)
    moves = []

    def all_sum(source, number):
        scratch = [getattr(r, f"sum_{k}_{number}") for k in range(5)]
        sems = [getattr(r, f"sum_sem_{k}_{number}") for k in range(4)]
        return keep(AllSum(source, scratch, sems, number == 2))

    def keep(move):
        moves.append(move)
        return move

    def load(name, sems, k):
        copy = pltpu.make_async_copy(getattr(r, name + OUTSIDE), getattr(r, name), sems.at[k])
        copy.start()
        return copy

    loads = [load(name, r.load_sems, k) for k, name in enumerate(small)]
    greeting = greet_everyone()
    held = [load(name, r.held_sems, k) for k, name in enumerate(weights)]
    proj_load, map_load, table_load, in_load, out_load = held[:5]
    for copy in loads:
        copy.wait()

    ids = r.own_ids[...].astype(F32)
    offset_row = jnp.concatenate(
        [r.own_offsets[...].astype(F32), jnp.zeros((1, rows - picks), F32)], 1
    )
    slot = lanes((rows, rows))
    loss_hot = (sublanes((rows, rows)).astype(F32) == offset_row) & (slot < picks)
    targets = r.own_targets[...]
    upper = targets // 256
    facts = jnp.concatenate(
        [
            upper.astype(F32),
            (targets - upper * 256).astype(F32),
            r.own_routes[...].astype(F32),
            jnp.zeros((4, rows), F32),
        ],
        0,
    )
    facts = dot_nn(facts.astype(BF16), loss_hot.astype(F32).astype(BF16))
    known = jnp.concatenate(
        [
            offset_row,
            facts[0:1] * 256.0 + facts[1:2],
            facts[2:4],
            ids,
            jnp.zeros((3, rows), F32),
        ],
        0,
    )
    r.known[block] = known
    own_router = r.own_router[...]
    own_small = jnp.concatenate(
        [own_router, jnp.zeros((4 - experts, columns), F32), r.own_gains[...], jnp.zeros((1, columns), F32)]
        if experts < 4
        else [own_router, r.own_gains[...], jnp.zeros((1, columns), F32)],
        0,
    )
    r.small[block] = jnp.concatenate([own_small, jnp.zeros((8, 128 - columns), F32)], 1)
    map_load.wait()
    r.maps[here, block] = packed_rows(r.map_weight[...].T).astype(BF16)
    proj_load.wait()
    own_proj = jnp.concatenate([r.proj_weight[s] for s in range(3)], 1)
    r.proj[block] = packed_rows(own_proj).astype(BF16)
    own_proj = own_proj.astype(BF16)
    pl.semaphore_wait(*greeting)
    to_known = keep(share_block(DP, r.known, r.sem_known))
    to_small = keep(share_block(DP, r.small, r.sem_small))
    to_maps = keep(Relay(r.maps, r.sem_map, r.sem_maps).start())
    to_proj = keep(PairGather(r.proj, r.sem_proj).start())

    table_load.wait()
    for k in range(blocks):
        stop = min(vocab_rows, (k + 1) * share)
        span = max(0, stop - k * share)
        if span > 0:
            r.pages[k, :, 0:span] = r.table_weight[:, k * share : stop].astype(BF16)
        if span < share:
            r.pages[k, :, span:share] = jnp.zeros((columns, share - span), BF16)
    r.table[block] = r.pages[block]

    def pages_move(steps):
        return keep(
            Move(DP, lambda target: r.pages.at[target], r.table, r.sem_pages, steps).start()
        )

    to_known.arrive()
    base = (here * vocab_rows).astype(F32)
    for k in range(blocks):
        r.id_row[:, k * rows : (k + 1) * rows] = r.known[k][4:5, :] - base
    chunk = group * rows
    id_high = jnp.floor(r.id_row[...] * (1.0 / STRIP))
    r.id_high[...] = id_high
    r.id_place[...] = r.id_row[...] - id_high * STRIP
    strips_of_page = share // STRIP
    for step in range(1, tensor + 1):
        target = lax.rem(here + step, tensor)
        at = pl.ds(pl.multiple_of(target * chunk, chunk), chunk)
        hot = sublanes((STRIP, chunk)).astype(F32) == r.id_place[:, at]
        hot = hot.astype(F32).astype(BF16)
        number = r.id_high[:, at]

        def look(k, total, hot=hot, number=number):
            strips = jnp.concatenate(
                [r.pages[k, :, n * STRIP : (n + 1) * STRIP] for n in range(strips_of_page)], 0
            )
            found = dot_nn(strips, hot)
            for n in range(strips_of_page):
                mine = number == (k * strips_of_page + n).astype(F32)
                total = total + jnp.where(mine, found[n * columns : (n + 1) * columns], 0.0)
            return total

        found = lax.fori_loop(0, blocks, look, jnp.zeros((columns, chunk), F32))
        for b in range(group):
            r.looked[target, b] = found[:, b * rows : (b + 1) * rows].astype(BF16)
        if step == tensor - 1:
            to_total = keep(
                Move(TENSOR, lambda target: r.looked.at[target], r.first, r.sem_first).start()
            )
    to_maps.pass_on()
    to_proj.forward()
    r.first[here] = r.looked[here]
    to_total.arrive()
    for b in range(group):
        r.streams[here, block, :, b * rows : (b + 1) * rows] = sum_blocks(r.first.at[:, b]).astype(
            BF16
        )
    to_streams = keep(Relay(r.streams, r.sem_stream, r.sem_streams).start())
    to_streams.pass_on()
    pages_now = [pages_move((4, 2, 6, 3))]
    to_small.arrive()
    gain_columns = [low(r.small[k].T[0:columns, 4:5]) for k in range(blocks)]
    small_rows = jnp.concatenate([r.small[k][:, 0:columns] for k in range(blocks)], 1)
    gains = low(small_rows)
    r.router[...] = jnp.concatenate(
        [
            jnp.where(sublanes(gains.shape) < experts, gains, 0.0),
            jnp.zeros((128 - gains.shape[0], features), F32),
        ],
        0,
    ).astype(BF16)
    r.gains[...] = gains
    r.id_low[...] = (
        (sublanes((STRIP, every)).astype(F32) == r.id_place[...]).astype(F32).astype(BF16).T
    )

    def column_of(field):
        table = jnp.concatenate(
            [r.known[k][field : field + 1, :] for k in range(blocks)]
            + ([jnp.zeros((8 - blocks, rows), F32)] if blocks < 8 else []),
            0,
        ).T
        return jnp.concatenate([table[0:picks, k : k + 1] for k in range(blocks)], 0)

    offsets, wanted, route_a, route_b = (
        column_of(field).astype(jnp.int32) for field in range(4)
    )
    positions = offsets + sublanes((count, 1)) // picks * rows
    period = 2 * every
    bucket_row = jnp.concatenate(
        [r.own_buckets[...].astype(F32), jnp.zeros((1, 1), F32)], 1
    )
    strips = [bucket_row[:, k * rows : (k + 1) * rows] for k in range(period // rows)]
    mirror = (lanes((rows, rows)) + sublanes((rows, rows)) == rows - 1).astype(F32).astype(BF16)
    strips = dot_nn(jnp.concatenate(strips, 0).astype(BF16), mirror)
    flipped = jnp.concatenate(
        [strips[k : k + 1, :] for k in reversed(range(period // rows))], 1
    )
    spread = jnp.broadcast_to(flipped, (rows, period))
    turned = pltpu.roll(spread, period - rows, 1, stride=1, stride_axis=0).astype(BF16)
    chosen = (lanes((count, rows)) == offsets).astype(F32).astype(BF16)
    r.shifted[...] = dot_nn(chosen, turned).astype(jnp.int32)
    for k in range(blocks):
        begin = rows * (blocks - 1 - k)
        r.bucket[k * picks : (k + 1) * picks, :] = r.shifted[
            k * picks : (k + 1) * picks, begin : begin + every
        ]
    bucket_count = r.position_bias.shape[1]

    def fill(k, carry):
        at = pl.ds(pl.multiple_of(k * picks, picks), picks)
        numbers = r.bucket[at, :]
        terms = [jnp.zeros(numbers.shape, F32)] * heads
        for b in range(bucket_count):
            same = numbers == b
            terms = [jnp.where(same, r.position_bias[h, b], terms[h]) for h in range(heads)]
        for h in range(heads):
            r.bias[h, at, :] = terms[h]
        return carry

    lax.fori_loop(0, blocks, fill, 0)

    def picture_at(place):
        inside = jnp.full(place.shape, -1, jnp.int32)
        for n in range(starts):
            begin = r.picture_start[0, n]
            inside = jnp.where((place >= begin) & (place < begin + PIECE), n, inside)
        return inside

    key_position = lanes((count, every))
    query_picture = picture_at(positions)
    allowed = (key_position <= positions) | (
        (picture_at(lanes((1, every))) == query_picture) & (query_picture >= 0)
    )
    to_streams.spread()
    to_proj.arrive()
    all_proj = jnp.concatenate([unpacked_rows(r.proj[k], columns) for k in range(blocks)], 0)
    key_proj, value_proj = (
        all_proj[:, k * width : (k + 1) * width].astype(F32).T.astype(BF16) for k in (1, 2)
    )
    gain_column = jnp.concatenate(gain_columns, 0)
    back_hot = (key_position == positions).astype(F32).astype(BF16)
    stream = jnp.zeros((count, features), F32)
    normed_loss = jnp.zeros((count, features), F32)
    to_streams.arrive()
    for k in range(tensor):
        part = slice(k * chunk, (k + 1) * chunk)
        low_part = across(r.streams.at[k], 0)
        wide_part = low_part.astype(F32)
        root = lax.rsqrt(jnp.mean(wide_part * wide_part, 0, keepdims=True) + NORM_EPS)
        r.roots[:, part] = root
        normed_in = (wide_part * root * gain_column).astype(BF16)
        r.keys[:, part] = dot_nn(key_proj, normed_in).astype(BF16)
        r.values[:, part] = dot_nn(value_proj, normed_in).astype(BF16)
        stream = stream + dot_nt(back_hot[:, part], low_part)
        normed_loss = normed_loss + dot_nt(back_hot[:, part], normed_in)
    query = dot_nn(normed_loss.astype(BF16), all_proj[:, 0:width]).astype(BF16)
    to_maps.spread()

    def head(value, h):
        return value[:, h * HD : (h + 1) * HD]

    def tall(ref, h):
        return ref[h * HD : (h + 1) * HD, :]

    for h in range(heads):
        raw = dot_nn(head(query, h), tall(r.keys, h)) * scale + r.bias[h]
        raw = jnp.where(allowed, raw, NEGATIVE)
        terms = jnp.exp(raw - jnp.max(raw, -1, keepdims=True))
        r.probs[h] = terms / jnp.sum(terms, -1, keepdims=True)
    attended = jnp.concatenate(
        [dot_nt(r.probs[h].astype(BF16), tall(r.values, h)).astype(BF16) for h in range(heads)],
        1,
    )
    r.heads[here] = attended
    to_heads = keep(share_block(TENSOR, r.heads, r.sem_heads))
    in_load.wait()
    out_load.wait()
    in_low, out_low = r.in_weight[...].astype(BF16), r.out_weight[...].astype(BF16)
    to_maps.arrive()
    to_heads.arrive()

    middle = stream
    for k in range(tensor):
        full = jnp.concatenate([unpacked_rows(r.maps[k, i], columns) for i in range(blocks)], 0)
        middle = middle + dot_nt(r.heads[k], full)
    r.middle[...] = middle
    gain_middle, gain_final = r.gains[5:6, :], r.gains[6:7, :]
    normed_mid = (middle * root_of(middle) * gain_middle).astype(BF16)
    inner = dot_nn(normed_mid, in_low)
    active = gelu_value(inner).astype(BF16)
    r.piece[...] = dot_nn(active, out_low).astype(BF16)
    mixing = all_sum(r.piece, 0)
    router_logits = dot_nt(normed_mid, r.router[...])
    lane = lanes(router_logits.shape)
    hot_a, hot_b = lane == route_a, lane == route_b
    logit_a = jnp.sum(jnp.where(hot_a, router_logits, 0.0), 1, keepdims=True)
    logit_b = jnp.sum(jnp.where(hot_b, router_logits, 0.0), 1, keepdims=True)
    logit_top = jnp.maximum(logit_a, logit_b)
    gate_a, gate_b = jnp.exp(logit_a - logit_top), jnp.exp(logit_b - logit_top)
    both = gate_a + gate_b
    r.gates[...] = jnp.where(hot_a, gate_a / both, 0.0) + jnp.where(hot_b, gate_b / both, 0.0)
    expert = block // (blocks // experts)
    r.gate[...] = jnp.sum(jnp.where(lane == expert, r.gates[...], 0.0), 1, keepdims=True)
    mixing.scatter(r.gate)
    pages_now.append(pages_move((5,)))
    mixing.gather()
    pages_now.append(pages_move((1, 7)))
    final = middle + mixing.result()
    out = (final * root_of(final) * gain_final).astype(BF16)
    for move in pages_now:
        move.arrive()

    table = across(r.table, 0)
    logits = dot_nn(out, table)
    slot = lanes(logits.shape) + block * share
    logits = jnp.where(slot < vocab_rows, logits, NEGATIVE)
    hit = slot == wanted - here * vocab_rows
    local_top = jnp.max(logits, -1, keepdims=True)
    local_stats = (
        local_top,
        jnp.sum(jnp.exp(logits - local_top), -1, keepdims=True),
        jnp.sum(jnp.where(hit & (slot < vocab_rows), logits, 0.0), -1, keepdims=True),
        jnp.sum(jnp.where(slot < vocab_rows, logits, 0.0), -1, keepdims=True),
    )
    packed = jnp.zeros((count, 128), F32)
    for k, column in enumerate(local_stats):
        packed = jnp.where(lane == k, column, packed)
    r.stats[block * tensor + here] = packed.T[0:4, :]
    to_stats = keep(Everyone(r.stats, r.sem_stats).start())
    weight = (query_picture < 0).astype(F32)
    weight_row = jnp.where(lane == 0, weight, 0.0).T[0:1, :]
    to_stats.arrive()
    peaks = r.stats[:, 0]
    peak = jnp.max(peaks, 0, keepdims=True)
    stats = (
        peak,
        jnp.sum(r.stats[:, 1] * jnp.exp(peaks - peak), 0, keepdims=True),
        jnp.sum(r.stats[:, 2], 0, keepdims=True),
        jnp.sum(r.stats[:, 3], 0, keepdims=True),
    )
    log_total = stats[0] + jnp.log(stats[1])
    per_row = (
        log_total
        - (1 - SMOOTH) * stats[2]
        - SMOOTH * stats[3] / VOCAB
        + ZLOSS * log_total * log_total
    )
    loss_sum = jnp.sum(weight_row * per_row, keepdims=True)
    loss_count = jnp.sum(weight_row, keepdims=True)
    total_column = jnp.where(sublanes((128, count)) == 0, log_total, 0.0).T[:, 0:1]
    d_logits = weight * (
        (1 + 2 * ZLOSS * total_column) * jnp.exp(logits - total_column)
        - jnp.where(hit, 1 - SMOOTH, 0.0)
        - SMOOTH / VOCAB
    )
    d_logits = jnp.where(slot < vocab_rows, d_logits, 0.0).astype(BF16)
    r.d_logits_parts = [r.d_logits.at[k] for k in range(r.d_logits.shape[0])]
    piece_rows = r.d_logits.shape[2]
    for k, part in enumerate(r.d_logits_parts):
        part[block] = d_logits[k * piece_rows : (k + 1) * piece_rows]
    logit_moves = [
        keep(PairGather(part, r.sem_logits.at[k])) for k, part in enumerate(r.d_logits_parts)
    ]
    r.sent[...] = dot_nt(d_logits, table).astype(BF16)
    summing = all_sum(r.sent, 1)
    logit_moves[0].start()
    summing.scatter()
    summing.gather()
    logit_moves[0].forward()
    logit_moves[1].start()
    upstream, grad_final = norm_back_rows(final, gain_final, summing.result())
    gate = r.gate[...]
    logit_moves[2].start()
    d_piece = (gate * upstream).astype(BF16)
    d_inner = (dot_nt(d_piece, out_low) * gelu_slope(inner)).astype(BF16)
    r.wide[:, 0:features] = dot_nt(d_inner, in_low).astype(BF16)
    gate_part = jnp.sum(upstream * r.piece[...].astype(F32), 1, keepdims=True)
    high = low(gate_part)
    r.wide[:, features:] = jnp.where(
        lane == expert, high, jnp.where(lane == expert + 64, gate_part - high, 0.0)
    ).astype(BF16)
    summing = all_sum(r.wide, 2)
    logit_moves[1].forward()
    grad_out = dot_nn(active.T, d_piece)
    grad_in = dot_nn(normed_mid.T, d_inner)
    r.grad_out[...] = grad_out
    r.grad_in[...] = grad_in
    squares = squared(grad_out) + squared(grad_in)
    summing.scatter()
    logit_moves[2].forward()
    summing.gather()
    logit_moves[3].start()
    total = summing.result()
    tail = total[:, features:]
    d_gates = tail + pltpu.roll(tail, 64, 1)
    named = hot_a | hot_b
    d_gates = jnp.where(named, d_gates, 0.0)
    mean = jnp.sum(r.gates[...] * d_gates, 1, keepdims=True)
    d_router = jnp.where(named, r.gates[...] * (d_gates - mean), 0.0).astype(BF16)
    d_normed_mid = total[:, 0:features] + dot_nn(d_router, r.router[...])
    d_from_mid, grad_middle = norm_back_rows(middle, gain_middle, d_normed_mid)
    d_attn = (upstream + d_from_mid).astype(BF16)
    stream_c = jnp.concatenate([r.streams[k, block] for k in range(tensor)], 1).astype(F32)
    roots = r.roots[...]
    gain_column = low(r.small[block].T[0:columns, 4:5])
    normed_c = (stream_c * roots * gain_column).astype(BF16)
    normed_loss = dot_nt(normed_c, back_hot).astype(BF16)
    query_wide = dot_nn(query.T, back_hot)

    own_map = jnp.concatenate(
        [unpacked_rows(r.maps[here, i], columns) for i in range(blocks)], 0
    )
    d_attended = dot_nn(d_attn, own_map).astype(BF16)
    d_query = []
    for h in range(heads):
        soft = r.probs[h]
        d_head = head(d_attended, h)
        d_probs = dot_nn(d_head, tall(r.values, h))
        d_scores = soft * (d_probs - jnp.sum(soft * d_probs, -1, keepdims=True))
        d_scores = d_scores.astype(BF16)
        r.bias[h] = d_scores.astype(F32)
        d_query.append((dot_nt(d_scores, tall(r.keys, h)) * scale).astype(BF16))
        r.d_keys[h * HD : (h + 1) * HD, :] = (
            dot_nn(head(query, h).T, d_scores) * scale
        ).astype(BF16)
        r.d_values[h * HD : (h + 1) * HD, :] = dot_nn(d_head.T, soft.astype(BF16)).astype(BF16)
    d_query = jnp.concatenate(d_query, 1)
    d_query_wide = dot_nn(d_query.T, back_hot).astype(BF16)
    d_columns = (
        dot_nn(own_proj[:, 0:width], d_query_wide)
        + dot_nn(own_proj[:, width : 2 * width], r.d_keys[...])
        + dot_nn(own_proj[:, 2 * width :], r.d_values[...])
    )
    inner_row = jnp.sum(
        d_query_wide.astype(F32) * query_wide
        + r.d_keys[...].astype(F32) * r.keys[...].astype(F32)
        + r.d_values[...].astype(F32) * r.values[...].astype(F32),
        0,
        keepdims=True,
    )
    inner_high = low(inner_row)
    extra = sublanes((16, every))
    r.part[0:columns, :] = d_columns.astype(BF16)
    r.part[columns:, :] = jnp.where(
        extra == 0, inner_high, jnp.where(extra == 1, inner_row - inner_high, 0.0)
    ).astype(BF16)
    to_part = keep(
        Move(
            TENSOR,
            lambda target: r.part.at[:, pl.ds(pl.multiple_of(target * chunk, chunk), chunk)],
            r.part_in,
            r.sem_part,
        ).start()
    )
    r.part_in[here] = r.part[:, pl.ds(pl.multiple_of(here * chunk, chunk), chunk)]
    grad_proj = (
        dot_nn(normed_loss, d_query),
        dot_nt(normed_c, r.d_keys[...]),
        dot_nt(normed_c, r.d_values[...]),
    )
    for s in range(3):
        r.grad_proj[s] = grad_proj[s]
        squares = squares + squared(grad_proj[s])
    to_part.arrive()
    r.part_all[here] = sum_blocks(r.part_in).astype(BF16)
    to_parts = keep(share_block(TENSOR, r.part_all, r.sem_part_all))
    r.bias_rows[...] = jnp.zeros(r.bias_rows.shape, F32)

    def collect(k, carry):
        at = pl.ds(pl.multiple_of(k * picks, picks), picks)
        numbers = r.bucket[at, :]
        parts = [r.bias[h, at, :] for h in range(heads)]
        for b in range(bucket_count):
            same = numbers == b
            for h in range(heads):
                kept = jnp.where(same, parts[h], 0.0)
                kept = kept[0:8] + kept[8:16]
                narrow = kept[:, 0:128]
                for c in range(1, every // 128):
                    narrow = narrow + kept[:, c * 128 : (c + 1) * 128]
                r.bias_rows[h, b] += narrow
        return carry

    lax.fori_loop(0, count // picks, collect, 0)
    grad_bias = jnp.sum(r.bias_rows[...], 2)
    r.grad_bias[...] = grad_bias
    grad_bias = jnp.sum(grad_bias, -1, keepdims=True)
    squares = squares + jnp.sum(grad_bias * grad_bias, keepdims=True)[0] / blocks
    pick_own = lanes((columns, features)) == sublanes((columns, features)) + block * columns
    pick_own = pick_own.astype(F32).astype(BF16)
    d_attn_t = dot_nt(pick_own, d_attn).astype(BF16)
    out_t = dot_nt(pick_own, out).astype(BF16)
    middle_t = dot_nt(pick_own, normed_mid).astype(BF16)
    grad_map = dot_nt(attended.T, d_attn_t)
    r.grad_map[...] = grad_map
    squares = squares + squared(grad_map)
    grad_router = dot_nt(d_router.T, middle_t)[0:8]
    residual = dot_nn(d_attn_t, back_hot)
    logit_moves[3].forward()
    gain_sum = jnp.concatenate(
        [grad_middle, grad_final, jnp.zeros((6, features), F32)], 0
    )
    gain_sum = pltpu.roll(gain_sum, lax.rem(features - block * columns, features), 1)
    to_parts.arrive()
    parts = across(r.part_all, 1).astype(F32)
    d_columns = parts[0:columns]
    inner_row = parts[columns : columns + 1] + parts[columns + 1 : columns + 2]
    grad_first = jnp.sum(d_columns * stream_c * roots, 1, keepdims=True)
    grad_first = jnp.broadcast_to(grad_first, (columns, 128)).T[0:1, :]
    small = jnp.concatenate(
        [
            grad_router[0:4],
            grad_first,
            gain_sum[0:2, 0:columns],
            jnp.zeros((1, columns), F32),
        ],
        0,
    )
    r.grad_small[:, 0:columns] = small
    r.grad_small[:, columns:] = jnp.zeros((8, 128 - columns), F32)
    squares = squares + squared(small) / tensor
    d_stream = (
        roots * gain_column * d_columns
        - stream_c * (roots * roots * inner_row / features)
        + residual
    )
    d_high = d_stream.astype(BF16)
    d_low = (d_stream - d_high.astype(F32)).astype(BF16)
    low_half = d_stream.astype(BF16)
    full = vocab_rows // STRIP
    ends = [(k, min(STRIP, vocab_rows - k * STRIP)) for k in range(full - full % 4, -(-vocab_rows // STRIP))]

    def strip_mask(number):
        return (r.id_high[...] == number).astype(F32).astype(BF16)

    def scatter_four(k, carry):
        masked = [low_half * strip_mask((k * 4 + n).astype(F32)) for n in range(4)]
        found = dot_nn(jnp.concatenate(masked, 0), r.id_low[...])
        begin = pl.multiple_of(k * 4 * STRIP, STRIP)
        for n in range(4):
            r.grad_table[:, pl.ds(begin + n * STRIP, STRIP)] = found[
                n * columns : (n + 1) * columns
            ]
        return carry

    lax.fori_loop(0, full // 4, scatter_four, 0)
    masked = jnp.concatenate([low_half * strip_mask(float(k)) for k, size in ends], 0)
    found = dot_nn(masked, r.id_low[...])
    for n, (k, size) in enumerate(ends):
        r.grad_table[:, k * STRIP : k * STRIP + size] = found[
            n * columns : (n + 1) * columns, 0:size
        ]
    for move in logit_moves:
        move.arrive()

    def page_strips(k, total):
        begin = pl.multiple_of(k * share, share)
        return total + add_page(k, pl.ds(begin, share))

    def add_page(k, where, size=share):
        page = jnp.concatenate([part[k] for part in r.d_logits_parts], 0)
        value = r.grad_table[:, where] + dot_nn(out_t, page)[:, 0:size]
        r.grad_table[:, where] = value
        return squared(value)

    whole = vocab_rows // share
    squares = squares + lax.fori_loop(0, whole, page_strips, jnp.zeros((1, 1), F32))
    if vocab_rows > whole * share:
        squares = squares + add_page(
            whole, slice(whole * share, vocab_rows), vocab_rows - whole * share
        )
    r.squares[block * tensor + here] = jnp.broadcast_to(squares, (1, 128))
    to_squares = keep(Everyone(r.squares, r.sem_squares).start())
    to_squares.arrive()
    norm = jnp.sqrt(sum_blocks(r.squares))
    clip = MAX_NORM / jnp.maximum(norm, MAX_NORM)
    place = lanes(norm.shape)
    r.facts[...] = jnp.where(
        place == 0,
        clip,
        jnp.where(place == 1, norm, jnp.where(place == 2, loss_sum, loss_count)),
    )
    for copy in held[5:]:
        copy.wait()
    for move in moves:
        move.finish()


def run_step(blocks, tensor, experts, small, held, scalars):
    rows = small["own_ids"].shape[1]
    every = rows * blocks
    picks = small["own_offsets"].shape[1]
    count = picks * blocks
    columns, width = held["proj_weight"].shape[1:]
    features = columns * blocks
    hidden = held["in_weight"].shape[1]
    vocab_rows = held["table_weight"].shape[1]
    heads, bucket_count = scalars["position_bias"].shape
    share = -(-vocab_rows // (blocks * STRIP)) * STRIP
    group = blocks // tensor
    chunk = group * rows
    wide = features + 128
    outputs = dict(
        grad_table=(columns, vocab_rows),
        grad_proj=(3, columns, width),
        grad_map=(width, columns),
        grad_small=(8, 128),
        grad_in=(features, hidden),
        grad_out=(hidden, features),
        grad_bias=(heads, bucket_count, 128),
        facts=(1, 128),
    )
    scratch = dict(
        known=((blocks, 8, rows), F32),
        small=((blocks, 8, 128), F32),
        proj=((blocks, columns * 3 * width // 128, 128), BF16),
        maps=((tensor, blocks, columns * width // 128, 128), BF16),
        pages=((blocks, columns, share), BF16),
        table=((blocks, columns, share), BF16),
        id_row=((1, every), F32),
        id_high=((1, every), F32),
        id_place=((1, every), F32),
        id_low=((every, STRIP), BF16),
        looked=((tensor, group, columns, rows), BF16),
        first=((tensor, group, columns, rows), BF16),
        router=((128, features), BF16),
        gains=((8, features), F32),
        roots=((1, every), F32),
        streams=((tensor, blocks, columns, chunk), BF16),
        shifted=((count, 2 * every), jnp.int32),
        bucket=((count, every), jnp.int32),
        bias=((heads, count, every), F32),
        keys=((width, every), BF16),
        values=((width, every), BF16),
        probs=((heads, count, every), F32),
        heads=((tensor, count, width), BF16),
        middle=((count, features), F32),
        piece=((count, features), BF16),
        gates=((count, 128), F32),
        gate=((count, 1), F32),
        stats=((blocks * tensor, 4, 128), F32),
        d_logits=((4, blocks, count // 4, share), BF16),
        sent=((count, features), BF16),
        wide=((count, wide), BF16),
        d_keys=((width, every), BF16),
        d_values=((width, every), BF16),
        part=((columns + 16, every), BF16),
        part_in=((tensor, columns + 16, chunk), BF16),
        part_all=((tensor, columns + 16, chunk), BF16),
        bias_rows=((heads, bucket_count, 8, 128), F32),
        squares=((blocks * tensor, 1, 128), F32),
    )
    scratch.update({name: (array.shape, array.dtype) for name, array in small.items()})
    outputs.update({name: array.shape for name, array in held.items()})
    dp, ten = (2, blocks), (2, tensor)
    sems = dict(
        load_sems=(len(small),),
        held_sems=(len(held),),
        sem_squares=(2, blocks * tensor),
        sem_stats=(2, blocks * tensor),
        sem_logits=(4, 2, blocks),
        sem_known=dp,
        sem_small=dp,
        sem_proj=dp,
        sem_map=dp,
        sem_pages=dp,
        sem_first=ten,
        sem_stream=dp,
        sem_streams=(2, 3, blocks),
        sem_maps=(2, 3, blocks),
        sem_heads=ten,
        sem_part=ten,
        sem_part_all=ten,
    )
    height = count // tensor
    for number, span in enumerate((features, features, wide)):
        shapes = (
            (tensor, height, span),
            (span // 128, height, 128),
            (blocks, height, 128),
            (span // 128, height, 128),
            (tensor, height, span),
        )
        scratch.update({f"sum_{k}_{number}": (shape, BF16) for k, shape in enumerate(shapes)})
        for k, shape in enumerate((ten, dp, dp, ten)):
            sems[f"sum_sem_{k}_{number}"] = shape
    copied = {**small, **held}
    names = tuple(name + OUTSIDE for name in copied) + tuple(scalars)
    names += tuple(outputs) + tuple(scratch) + tuple(sems)
    starts = scalars["picture_start"].shape[1]
    results = pl.pallas_call(
        functools.partial(
            step_kernel, names, tuple(small), tuple(held), experts, vocab_rows, starts
        ),
        out_shape=[pltpu.VMEM(shape, F32) for shape in outputs.values()],
        in_specs=[pl.BlockSpec(memory_space=pltpu.HBM)] * len(copied)
        + [pl.BlockSpec(memory_space=pltpu.SMEM)] * len(scalars),
        out_specs=[WHOLE] * len(outputs),
        scratch_shapes=[pltpu.VMEM(*spec) for spec in scratch.values()]
        + [DMA(shape) for shape in sems.values()],
        compiler_params=pltpu.CompilerParams(
            collective_id=0, has_side_effects=True, vmem_limit_bytes=VMEM_BYTES
        ),
        name="training_step",
    )(*copied.values(), *scalars.values())
    return dict(zip(outputs, results))


def update_piece(weight, first, second, grad, rate, decay):
    first = BETA1 * first + (1 - BETA1) * grad
    second = BETA2 * second + (1 - BETA2) * (grad * grad)
    spread = second * lax.rsqrt(second) * math.sqrt(1 / (1 - BETA2**STEP)) + ADAM_EPS
    step = first / spread
    return weight * (1 - rate * decay) - (rate / (1 - BETA1**STEP)) * step, first, second


def spread_over(factor, change):
    return factor.reshape((1,) * change.ndim) * change


def update_kernel(jobs, facts, *refs):
    grads, refs = refs[: len(jobs)], refs[len(jobs) :]
    total = 3 * len(jobs)
    olds, outs, refs = refs[:total], refs[total : 2 * total], refs[2 * total :]
    scalars, news, done = refs[:3], refs[3:-1], refs[-1]
    for k, scalar in enumerate(scalars):
        scalar[...] = facts[:, k + 1 : k + 2]
    factor = facts[:, 0:1]
    copies = []
    for index, (height, rate, decay, begin, reduced) in enumerate(jobs):
        trio = slice(3 * index, 3 * index + 3)
        whole = news[3 * index].shape[0]
        for piece in range(0, whole, height):
            rows = slice(piece, piece + height)
            if reduced:
                change = jnp.sum(grads[index][...], -1)
            elif begin is not None:
                change = grads[index][begin : begin + whole, 0 : news[3 * index].shape[1]]
            else:
                change = grads[index][rows]
            values = update_piece(
                *(ref[rows] for ref in olds[trio]), spread_over(factor, change), rate, decay
            )
            for which, value in enumerate(values):
                new, out = news[3 * index + which], outs[3 * index + which]
                new[rows] = value
                part = pl.ds(piece, height)
                copy = pltpu.make_async_copy(new.at[part], out.at[part], done.at[len(copies)])
                copy.start()
                copies.append(copy)
    for copy in copies:
        copy.wait()


def run_update(facts, jobs, grads, olds):
    shapes = [old.shape for old in olds]
    pieces = sum(3 * shapes[3 * k][0] // job[0] for k, job in enumerate(jobs))
    results = pl.pallas_call(
        functools.partial(update_kernel, jobs),
        out_shape=[jax.ShapeDtypeStruct(shape, F32) for shape in shapes + [(1, 1)] * 3],
        in_specs=[WHOLE] * (1 + len(grads) + len(olds)),
        out_specs=[pl.BlockSpec(memory_space=pltpu.HBM)] * len(shapes) + [WHOLE] * 3,
        scratch_shapes=[pltpu.VMEM(shape, F32) for shape in shapes] + [DMA((pieces,))],
        compiler_params=pltpu.CompilerParams(vmem_limit_bytes=UPDATE_BYTES),
        name="update",
    )(facts, *grads, *olds)
    return [results[3 * k : 3 * k + 3] for k in range(len(jobs) + 1)]


def fast_local(
    token_ids,
    targets,
    loss_offsets,
    routes,
    picture_start,
    buckets,
    embedding,
    embedding_first,
    embedding_second,
    attn_proj,
    attn_proj_first,
    attn_proj_second,
    out_proj,
    out_proj_first,
    out_proj_second,
    router,
    router_first,
    router_second,
    expert_in,
    expert_in_first,
    expert_in_second,
    expert_out,
    expert_out_first,
    expert_out_second,
    norm_gains,
    norm_gains_first,
    norm_gains_second,
    position_bias,
    position_bias_first,
    position_bias_second,
):
    dp_count = lax.axis_size("dp")
    tensor_count = lax.axis_size("tensor")
    experts = router.shape[0]
    small = dict(
        own_ids=token_ids[None, :],
        own_targets=targets[None, :],
        own_offsets=loss_offsets[None, :],
        own_routes=routes.T,
        own_buckets=buckets[None, :],
        own_router=router,
        own_gains=norm_gains,
    )
    held = dict(
        proj_weight=attn_proj,
        map_weight=out_proj,
        table_weight=embedding.T,
        in_weight=expert_in,
        out_weight=expert_out,
        table_first=embedding_first.T,
        table_second=embedding_second.T,
        in_first=expert_in_first,
        in_second=expert_in_second,
        out_first=expert_out_first,
        out_second=expert_out_second,
        proj_first=attn_proj_first,
        proj_second=attn_proj_second,
        map_first=out_proj_first,
        map_second=out_proj_second,
    )
    scalars = dict(position_bias=position_bias, picture_start=picture_start)
    g = types.SimpleNamespace(**run_step(dp_count, tensor_count, experts, small, held, scalars))
    kinds = (
        (8, 0, None, False),
        (expert_in.shape[0] // 8, 4, None, False),
        (expert_out.shape[0] // 8, 5, None, False),
        (1, 1, None, False),
        (out_proj.shape[0], 2, None, False),
        (experts, 3, 0, False),
        (3, 6, 4, False),
        (position_bias.shape[0], 7, None, True),
    )
    jobs = tuple(
        (height, RATES[k], DECAYS[k], begin, reduced) for height, k, begin, reduced in kinds
    )
    grads = (g.grad_table, g.grad_in, g.grad_out, g.grad_proj, g.grad_map)
    grads += (g.grad_small, g.grad_small, g.grad_bias)
    olds = (g.table_weight, g.table_first, g.table_second, g.in_weight, g.in_first, g.in_second)
    olds += (g.out_weight, g.out_first, g.out_second, g.proj_weight, g.proj_first, g.proj_second)
    olds += (g.map_weight, g.map_first, g.map_second, router, router_first, router_second)
    olds += (norm_gains, norm_gains_first, norm_gains_second)
    olds += (position_bias, position_bias_first, position_bias_second)
    new = run_update(g.facts, jobs, grads, olds)
    results = [value.T for value in new[0]]
    for k in (3, 4, 5, 1, 2, 6, 7):
        results.extend(new[k])
    grad_norm, loss_sum, loss_count = (value.reshape(()) for value in new[-1])
    return (*results, grad_norm, loss_sum, loss_count)


def local(
    token_ids,
    targets,
    loss_offsets,
    routes,
    picture_start,
    buckets,
    embedding,
    embedding_first,
    embedding_second,
    attn_proj,
    attn_proj_first,
    attn_proj_second,
    out_proj,
    out_proj_first,
    out_proj_second,
    router,
    router_first,
    router_second,
    expert_in,
    expert_in_first,
    expert_in_second,
    expert_out,
    expert_out_first,
    expert_out_second,
    norm_gains,
    norm_gains_first,
    norm_gains_second,
    position_bias,
    position_bias_first,
    position_bias_second,
):
    f32 = jnp.float32
    bf16 = jnp.bfloat16
    dp_count = lax.axis_size("dp")
    tensor_count = lax.axis_size("tensor")
    dp_place = lax.axis_index("dp")
    tensor_place = lax.axis_index("tensor")
    rows = token_ids.shape[0]
    every = rows * dp_count
    length = min(SEQ, every)
    seqs = every // length
    sub = rows // seqs
    scale = 1.0 / math.sqrt(HD)
    vocab_rows = embedding.shape[0]
    table, projection, output_map, router_full, gain_full = (
        lax.all_gather(embedding.astype(bf16), "dp", axis=1, tiled=True),
        lax.all_gather(attn_proj.astype(bf16), "dp", axis=1, tiled=True),
        lax.all_gather(out_proj.astype(bf16), "dp", axis=1, tiled=True),
        lax.all_gather(router.astype(bf16), "dp", axis=1, tiled=True),
        lax.all_gather(norm_gains.astype(bf16), "dp", axis=1, tiled=True),
    )
    gain = gain_full.astype(f32)
    features = table.shape[1]
    offset = token_ids - tensor_place * vocab_rows
    owned = (offset >= 0) & (offset < vocab_rows)
    offset = jnp.clip(offset, 0, vocab_rows - 1)
    looked = jnp.take(table, offset, axis=0).astype(f32)
    stream_in = tensor_total(jnp.where(owned[:, None], looked, 0.0))
    pos_here = dp_place * sub + jnp.arange(sub, dtype=jnp.int32)
    seq_positions = jnp.arange(length, dtype=jnp.int32)
    picture_all = jax.vmap(lambda starts: picture_of(seq_positions, starts, PIECE))(picture_start)
    picture_here = lax.dynamic_slice_in_dim(picture_all, dp_place * sub, sub, 1)
    bucket_ids = jnp.arange(position_bias.shape[1], dtype=jnp.int32)
    bucket_hot = (bucket_ids[:, None] == buckets[None, :]).astype(f32)
    relative = jnp.dot(position_bias, bucket_hot, precision=HIGH)
    normed_in = normed(stream_in, gain[0]).astype(bf16)
    fresh = jnp.einsum("td,sde->ste", normed_in, projection, preferred_element_type=f32).astype(
        bf16
    )
    width = fresh.shape[2]
    heads = width // HD
    keys_local = fresh[1].reshape(seqs, sub, width)
    values_local = fresh[2].reshape(seqs, sub, width)
    query_heads = fresh[0].reshape(seqs, sub, heads, HD)
    keys_all, values_all = (
        lax.all_gather(keys_local, "dp", axis=1, tiled=True),
        lax.all_gather(values_local, "dp", axis=1, tiled=True),
    )
    block = min(512, length)
    blocks = length // block
    block_ids = jnp.arange(blocks, dtype=jnp.int32)

    def pair_scores(q_heads, q_pos, q_pic, k_heads, k_pos, k_pic, bias):
        raw = (
            jnp.einsum("sqhd,skhd->shqk", q_heads, k_heads, preferred_element_type=f32) * scale
            + bias[None]
        )
        allowed = (k_pos[None, :] <= q_pos[:, None])[None] | (
            k_pic[:, None, :] == q_pic[:, :, None]
        ) & (q_pic[:, :, None] >= 0)
        return jnp.where(allowed[:, None], raw, NEGATIVE)

    def key_slice(source, start):
        return lax.dynamic_slice_in_dim(source, start, block, 1).reshape(seqs, block, heads, HD)

    def own_bias(start):
        return rel_window(relative, dp_place * sub, sub, start, block, length)

    def fwd_scores(index, key_source):
        start = index * block
        key_pos = start + jnp.arange(block, dtype=jnp.int32)
        return pair_scores(
            query_heads,
            pos_here,
            picture_here,
            key_slice(key_source, start),
            key_pos,
            lax.dynamic_slice_in_dim(picture_all, start, block, 1),
            own_bias(start),
        )

    def max_step(carry, index):
        top, total = carry
        s = fwd_scores(index, keys_all)
        new_top = jnp.maximum(top, jnp.max(s, -1))
        terms = jnp.where(s > 0.5 * NEGATIVE, jnp.exp(s - new_top[..., None]), 0.0)
        total = total * jnp.exp(top - new_top) + jnp.sum(terms, -1)
        return ((new_top, total), None)

    start_top = jnp.full((seqs, heads, sub), NEGATIVE, f32)
    (top, total), unused = lax.scan(
        max_step, (start_top, jnp.zeros((seqs, heads, sub), f32)), block_ids
    )
    log_total = top + jnp.log(total)

    def out_step(accum, index):
        s = fwd_scores(index, keys_all)
        probs = jnp.exp(s - log_total[..., None]).astype(bf16)
        value_heads = key_slice(values_all, index * block)
        return (
            accum + jnp.einsum("shqk,skhd->sqhd", probs, value_heads, preferred_element_type=f32),
            None,
        )

    attended, unused = lax.scan(out_step, jnp.zeros((seqs, sub, heads, HD), f32), block_ids)
    attended_low = attended.reshape(rows, width).astype(bf16)
    stream_mid = stream_in + tensor_total(
        jnp.dot(attended_low, output_map, preferred_element_type=f32)
    )
    normed_mid = normed(stream_mid, gain[1]).astype(bf16)
    router_logits = jnp.dot(normed_mid, router_full.T, preferred_element_type=f32)
    gates = jax.nn.softmax(jnp.take_along_axis(router_logits, routes, 1), -1)
    experts = router_full.shape[0]
    top_k = routes.shape[1]
    capacity = 2 * rows * top_k // experts
    flat = routes.reshape(-1)
    owner = jnp.arange(rows * top_k, dtype=jnp.int32) // top_k
    hits = (flat[:, None] == jnp.arange(experts, dtype=jnp.int32)[None, :]).astype(jnp.int32)
    slot = jnp.sum(jnp.cumsum(hits, 0) * hits, 1) - 1
    first_row = 2 * flat * capacity + slot

    def pack(values):
        buffer = jnp.zeros((experts, capacity, features), bf16).at[flat, slot].set(values)
        return jnp.repeat(buffer, 2, axis=0).reshape(2 * experts * capacity, features)

    def unpack(values):
        return values[first_row].astype(f32) + values[first_row + capacity].astype(f32)

    in_low = expert_in.astype(bf16)
    out_low = expert_out.astype(bf16)
    arrived = route_exchange(pack(normed_mid[owner]))
    inner = jnp.dot(arrived, in_low, preferred_element_type=f32)
    active = jax.nn.gelu(inner).astype(bf16)
    produced = jnp.dot(active, out_low, preferred_element_type=f32).astype(bf16)
    returned = unpack(route_exchange(produced))
    mixed = jnp.sum((gates.reshape(-1)[:, None] * returned).reshape(rows, top_k, features), 1)
    stream_out = stream_mid + tensor_total(mixed)
    normed_out = normed(stream_out, gain[2]).astype(bf16)
    picked = normed_out[loss_offsets]
    logits = jnp.dot(picked, table.T, preferred_element_type=f32)
    wanted = targets[loss_offsets] - tensor_place * vocab_rows
    hit = jnp.arange(vocab_rows, dtype=jnp.int32)[None, :] == wanted[:, None]
    local_top = jnp.max(logits, -1)
    stats = (
        local_top,
        jnp.sum(jnp.exp(logits - local_top[:, None]), -1),
        jnp.sum(jnp.where(hit, logits, 0.0), -1),
        jnp.sum(logits, -1),
    )
    peak, vocab_total, target_logit, logit_sum = merged(stats, "tensor", combine_stats)
    loss_total = peak + jnp.log(vocab_total)
    weight = (picture_here.reshape(rows)[loss_offsets] < 0).astype(f32)
    per_row = (
        loss_total
        - (1 - SMOOTH) * target_logit
        - SMOOTH * logit_sum / VOCAB
        + ZLOSS * loss_total * loss_total
    )
    loss_local = jnp.sum(weight * per_row)
    soft = jnp.exp(logits - loss_total[:, None])
    d_logits = (
        weight[:, None]
        * (
            (1 + 2 * ZLOSS * loss_total)[:, None] * soft
            - (1 - SMOOTH) * hit.astype(f32)
            - SMOOTH / VOCAB
        )
    ).astype(bf16)
    d_picked = jnp.dot(d_logits, table, preferred_element_type=f32)
    grad_table = jnp.dot(d_logits.T, picked, preferred_element_type=f32)
    d_normed_out = tensor_total(jnp.zeros((rows, features), f32).at[loss_offsets].add(d_picked))
    d_stream_out, grad_final = norm_back(stream_out, gain[2], d_normed_out)
    d_piece = (gates.reshape(-1)[:, None] * d_stream_out[owner]).astype(bf16)
    d_arrived = route_exchange(pack(d_piece))
    d_active = jnp.dot(d_arrived, out_low.T, preferred_element_type=f32)
    unused, gelu_pull = jax.vjp(jax.nn.gelu, inner)
    d_inner = gelu_pull(d_active)[0].astype(bf16)
    grad_out = jnp.dot(active.T, d_arrived, preferred_element_type=f32)
    grad_in = jnp.dot(arrived.T, d_inner, preferred_element_type=f32)
    sent_back = jnp.dot(d_inner, in_low.T, preferred_element_type=f32).astype(bf16)
    d_routes = unpack(route_exchange(sent_back))
    gate_part = jnp.sum(d_stream_out[owner] * returned, -1).reshape(rows, top_k)
    route_part = jnp.sum(d_routes.reshape(rows, top_k, features), 1)
    d_from_experts, d_gates = tensor_total((route_part, gate_part))
    d_chosen = gates * (d_gates - jnp.sum(gates * d_gates, -1, keepdims=True))
    expert_hot = (routes[..., None] == jnp.arange(experts, dtype=jnp.int32)).astype(f32)
    d_router_logits = jnp.sum(expert_hot * d_chosen[..., None], 1).astype(bf16)
    grad_router = jnp.dot(d_router_logits.T, normed_mid, preferred_element_type=f32)
    d_normed_mid = d_from_experts + jnp.dot(
        d_router_logits, router_full, preferred_element_type=f32
    )
    d_from_mid, grad_middle = norm_back(stream_mid, gain[1], d_normed_mid)
    d_stream_mid = d_stream_out + d_from_mid
    d_attn_low = d_stream_mid.astype(bf16)
    grad_output_map = jnp.dot(attended_low.T, d_attn_low, preferred_element_type=f32)
    d_attended = jnp.dot(d_attn_low, output_map.T, preferred_element_type=f32).astype(bf16)
    d_heads = d_attended.reshape(seqs, sub, heads, HD)
    delta = jnp.moveaxis(jnp.sum(d_heads.astype(f32) * attended, -1), 2, 1)
    key_source, value_source = (
        lax.all_gather(keys_local, "dp", axis=1, tiled=True),
        lax.all_gather(values_local, "dp", axis=1, tiled=True),
    )

    def score_grads(
        q_heads, q_pos, q_pic, k_heads, k_pos, k_pic, bias, totals, deltas, dq_heads, v_heads
    ):
        s = pair_scores(q_heads, q_pos, q_pic, k_heads, k_pos, k_pic, bias)
        probs = jnp.exp(s - totals[..., None])
        d_probs = jnp.einsum("sqhd,skhd->shqk", dq_heads, v_heads, preferred_element_type=f32)
        d_scores = (probs * (d_probs - deltas[..., None])).astype(bf16)
        return (probs, d_scores)

    def key_step(carry, index):
        d_query, d_rel = carry
        start = index * block
        key_pos = start + jnp.arange(block, dtype=jnp.int32)
        key_heads = key_slice(key_source, start)
        value_heads = key_slice(value_source, start)
        bias, bias_pull = jax.vjp(
            lambda table_rel: rel_window(table_rel, dp_place * sub, sub, start, block, length),
            relative,
        )
        probs, d_scores = score_grads(
            query_heads,
            pos_here,
            picture_here,
            key_heads,
            key_pos,
            lax.dynamic_slice_in_dim(picture_all, start, block, 1),
            bias,
            log_total,
            delta,
            d_heads,
            value_heads,
        )
        d_query = (
            d_query
            + jnp.einsum("shqk,skhd->sqhd", d_scores, key_heads, preferred_element_type=f32) * scale
        )
        d_rel = d_rel + bias_pull(jnp.sum(d_scores.astype(f32), 0))[0]
        d_key = (
            jnp.einsum("shqk,sqhd->skhd", d_scores, query_heads, preferred_element_type=f32) * scale
        )
        d_value = jnp.einsum(
            "shqk,sqhd->skhd", probs.astype(bf16), d_heads, preferred_element_type=f32
        )
        joined = jnp.concatenate(
            [d_key.reshape(seqs, block, width), d_value.reshape(seqs, block, width)], 2
        )
        return ((d_query, d_rel), joined)

    start_carry = (jnp.zeros((seqs, sub, heads, HD), f32), jnp.zeros(relative.shape, f32))
    (d_query, d_rel), key_terms = lax.scan(key_step, start_carry, block_ids)
    d_bias = jnp.dot(d_rel, bucket_hot.T, precision=HIGH)
    ordered = jnp.moveaxis(key_terms, 0, 1).reshape(seqs, length, 2 * width)
    key_grads = lax.psum_scatter(ordered, "dp", scatter_dimension=1, tiled=True).reshape(
        rows, 2 * width
    )
    d_fresh = jnp.stack(
        [d_query.reshape(rows, width), key_grads[:, :width], key_grads[:, width:]]
    ).astype(bf16)
    grad_proj = jnp.einsum("td,ste->sde", normed_in, d_fresh, preferred_element_type=f32)
    d_normed_in = tensor_total(
        jnp.einsum("ste,sde->td", d_fresh, projection, preferred_element_type=f32)
    )
    d_from_in, grad_first = norm_back(stream_in, gain[0], d_normed_in)
    d_stream_in = d_stream_mid + d_from_in
    grad_table = grad_table + jnp.zeros((vocab_rows, features), f32).at[offset].add(
        jnp.where(owned[:, None], d_stream_in, 0.0)
    )
    sum_table, sum_proj, sum_output, sum_router, sum_gains = (
        lax.psum_scatter(grad_table, "dp", scatter_dimension=1, tiled=True),
        lax.psum_scatter(grad_proj, "dp", scatter_dimension=1, tiled=True),
        lax.psum_scatter(grad_output_map, "dp", scatter_dimension=1, tiled=True),
        lax.psum_scatter(grad_router, "dp", scatter_dimension=1, tiled=True),
        lax.psum_scatter(
            jnp.stack([grad_first, grad_middle, grad_final]), "dp", scatter_dimension=1, tiled=True
        ),
    )
    sum_bias = lax.psum(d_bias, "dp")
    squares = (
        jnp.sum(sum_table * sum_table)
        + jnp.sum(sum_proj * sum_proj)
        + jnp.sum(sum_output * sum_output)
        + jnp.sum(grad_in * grad_in)
        + jnp.sum(grad_out * grad_out)
        + (jnp.sum(sum_router * sum_router) + jnp.sum(sum_gains * sum_gains)) / tensor_count
        + jnp.sum(sum_bias * sum_bias) / dp_count
    )
    total_squares, loss_sum, loss_count = lax.psum(
        (squares, loss_local / tensor_count, jnp.sum(weight) / tensor_count), ("dp", "tensor")
    )
    grad_norm = jnp.sqrt(total_squares)
    clip = MAX_NORM / jnp.maximum(grad_norm, MAX_NORM)
    params = (
        embedding,
        attn_proj,
        out_proj,
        router,
        expert_in,
        expert_out,
        norm_gains,
        position_bias,
    )
    firsts = (
        embedding_first,
        attn_proj_first,
        out_proj_first,
        router_first,
        expert_in_first,
        expert_out_first,
        norm_gains_first,
        position_bias_first,
    )
    seconds = (
        embedding_second,
        attn_proj_second,
        out_proj_second,
        router_second,
        expert_in_second,
        expert_out_second,
        norm_gains_second,
        position_bias_second,
    )
    grads = (sum_table, sum_proj, sum_output, sum_router, grad_in, grad_out, sum_gains, sum_bias)
    results = []
    for index in range(8):
        results.extend(
            adam_update(
                params[index],
                firsts[index],
                seconds[index],
                clip * grads[index],
                RATES[index],
                DECAYS[index],
            )
        )
    return (
        results[0],
        results[1],
        results[2],
        results[3],
        results[4],
        results[5],
        results[6],
        results[7],
        results[8],
        results[9],
        results[10],
        results[11],
        results[12],
        results[13],
        results[14],
        results[15],
        results[16],
        results[17],
        results[18],
        results[19],
        results[20],
        results[21],
        results[22],
        results[23],
        grad_norm,
        loss_sum,
        loss_count,
    )


def fits(dp_count, tensor_count, arrays):
    token_ids, loss_offsets, routes, picture_start = arrays[0], arrays[2], arrays[3], arrays[4]
    columns, router, gains = arrays[6].shape[1], arrays[15], arrays[24]
    rows, picks = token_ids.shape[0], loss_offsets.shape[0]
    return (
        rows == 128
        and rows * dp_count <= SEQ
        and picture_start.shape[0] == 1
        and picks == 16
        and picks * dp_count == 128
        and dp_count % 4 == 0
        and tensor_count == 4
        and dp_count % router.shape[0] == 0
        and dp_count % 2 == 0
        and dp_count <= 8
        and router.shape[0] <= 4
        and routes.shape[1] == 2
        and gains.shape[0] == 3
        and columns % 32 == 0
        and arrays[9].shape[2] % 128 == 64
        and columns <= 128
    )


def solution(mesh):
    in_specs = (
        P("dp"),
        P("dp"),
        P("dp"),
        P("dp", None),
        P(),
        P(),
        P("tensor", "dp"),
        P("tensor", "dp"),
        P("tensor", "dp"),
        P(None, "dp", "tensor"),
        P(None, "dp", "tensor"),
        P(None, "dp", "tensor"),
        P("tensor", "dp"),
        P("tensor", "dp"),
        P("tensor", "dp"),
        P(None, "dp"),
        P(None, "dp"),
        P(None, "dp"),
        P(None, ("dp", "tensor")),
        P(None, ("dp", "tensor")),
        P(None, ("dp", "tensor")),
        P(("dp", "tensor"), None),
        P(("dp", "tensor"), None),
        P(("dp", "tensor"), None),
        P(None, "dp"),
        P(None, "dp"),
        P(None, "dp"),
        P("tensor", None),
        P("tensor", None),
        P("tensor", None),
    )
    out_specs = (
        P("tensor", "dp"),
        P("tensor", "dp"),
        P("tensor", "dp"),
        P(None, "dp", "tensor"),
        P(None, "dp", "tensor"),
        P(None, "dp", "tensor"),
        P("tensor", "dp"),
        P("tensor", "dp"),
        P("tensor", "dp"),
        P(None, "dp"),
        P(None, "dp"),
        P(None, "dp"),
        P(None, ("dp", "tensor")),
        P(None, ("dp", "tensor")),
        P(None, ("dp", "tensor")),
        P(("dp", "tensor"), None),
        P(("dp", "tensor"), None),
        P(("dp", "tensor"), None),
        P(None, "dp"),
        P(None, "dp"),
        P(None, "dp"),
        P("tensor", None),
        P("tensor", None),
        P("tensor", None),
        P(),
        P(),
        P(),
    )

    def chosen(*arrays):
        sizes = lax.axis_size("dp"), lax.axis_size("tensor")
        return (fast_local if fits(*sizes, arrays) else local)(*arrays)

    return jax.shard_map(chosen, mesh=mesh, in_specs=in_specs, out_specs=out_specs, check_vma=False)
```

```python
import functools
import math
import types

import jax
import jax.numpy as jnp
from jax.experimental import pallas as pl
from jax.experimental.pallas import tpu as pltpu
from jax import lax
from jax.sharding import PartitionSpec as P

HD = 64
VOCAB = 32000
PIECE = 256
SEQ = 4096
STEP = 10


SMOOTH = 0.1
ZLOSS = 0.0001
NORM_EPS = 1e-06
MAX_NORM = 1.0
BETA1 = 0.9
BETA2 = 0.95
ADAM_EPS = 1e-08
RATES = (0.04, 0.04, 1.0, 0.03, 0.07, 0.035, 1.0, 0.7)
DECAYS = (0.1, 0.1, 0.1, 0.1, 0.1, 0.1, 0.0, 0.0)
NEGATIVE = -1e30
HIGH = lax.Precision.HIGHEST


def merged(shard, axis, combine):
    everything = jax.tree.map(lambda part: lax.all_gather(part, axis), shard)
    initial = jax.tree.map(lambda part: part[0], everything)

    def lap(k, so_far):
        return combine(so_far, jax.tree.map(lambda part: part[k], everything))

    return lax.fori_loop(1, lax.axis_size(axis), lap, initial)


def normed(v, g):
    return v * lax.rsqrt(jnp.mean(v * v, -1, keepdims=True) + NORM_EPS) * g


def norm_back(v, g, upstream):
    unused, pull = jax.vjp(normed, v, g)
    return pull(upstream)


def picture_of(positions, starts, width):
    inside = (positions[:, None] >= starts[None, :]) & (
        positions[:, None] < starts[None, :] + width
    )
    number = jnp.arange(starts.shape[0], dtype=jnp.int32) + 1
    return jnp.sum(inside.astype(jnp.int32) * number[None, :], 1) - 1


def rel_window(relative, query_start, query_count, key_start, key_count, length):
    centre = query_start - key_start + length - 1
    window = lax.dynamic_slice_in_dim(
        relative, centre - key_count + 1, query_count + key_count - 1, 1
    )
    span = query_count + key_count
    wrapped = jnp.concatenate(
        [
            jnp.flip(window[:, :key_count], 1),
            jnp.zeros((window.shape[0], 1), window.dtype),
            jnp.flip(window[:, key_count:], 1),
        ],
        1,
    )
    tiled = jnp.tile(wrapped, (1, query_count))[:, : query_count * (span - 1)]
    return tiled.reshape(window.shape[0], query_count, span - 1)[:, :, :key_count]


def tensor_total(value):
    return lax.psum(value, "tensor")


def route_exchange(value):
    return lax.all_to_all(value, "dp", split_axis=0, concat_axis=0, tiled=True)


def combine_stats(left, right):
    peak = jnp.maximum(left[0], right[0])
    total = left[1] * jnp.exp(left[0] - peak) + right[1] * jnp.exp(right[0] - peak)
    return (peak, total, left[2] + right[2], left[3] + right[3])


def adam_update(weight, first, second, grad, rate, decay):
    first = BETA1 * first + (1 - BETA1) * grad
    second = BETA2 * second + (1 - BETA2) * grad * grad
    fixed_first = first / (1 - BETA1**STEP)
    fixed_second = second / (1 - BETA2**STEP)
    weight = weight - rate * (fixed_first / (jnp.sqrt(fixed_second) + ADAM_EPS) + decay * weight)
    return (weight, first, second)


MESH = pl.DeviceIdType.MESH
DP = "dp"
OUTSIDE = "_hbm"
TENSOR = "tensor"
UPDATE_BYTES = 20 * 1024 * 1024
VMEM_BYTES = 33 * 1024 * 1024
WHOLE = pl.BlockSpec(memory_space=pltpu.VMEM)
DMA = pltpu.SemaphoreType.DMA
F32 = jnp.float32
BF16 = jnp.bfloat16
STRIP = 256


def greet_everyone():
    barrier = pltpu.get_barrier_semaphore()
    tensor = lax.axis_size(TENSOR)
    total = lax.axis_size(DP) * tensor
    here = lax.axis_index(DP) * tensor + lax.axis_index(TENSOR)

    def signal(step, carry):
        other = lax.rem(here + step, total)
        pl.semaphore_signal(
            barrier,
            inc=1,
            device_id={DP: other // tensor, TENSOR: lax.rem(other, tensor)},
            device_id_type=MESH,
        )
        return carry

    lax.fori_loop(1, total, signal, 0)
    return barrier, total - 1


class Move:
    def __init__(self, axis, source, dest, sems, steps=None):
        self.axis, self.count, self.here = axis, lax.axis_size(axis), lax.axis_index(axis)
        self.source, self.dest, self.sems = source, dest, sems
        self.steps = range(1, self.count) if steps is None else steps

    def copy(self, step):
        target = lax.rem(self.here + step, self.count)
        return pltpu.make_async_remote_copy(
            src_ref=self.source(target),
            dst_ref=self.dest.at[self.here],
            send_sem=self.sems.at[0, step],
            recv_sem=self.sems.at[1, step],
            device_id={self.axis: target},
            device_id_type=MESH,
        )

    def start(self):
        for step in self.steps:
            self.copy(step).start()
        return self

    def arrive(self):
        for step in self.steps:
            self.copy(step).wait_recv()

    def finish(self):
        for step in self.steps:
            self.copy(step).wait_send()


def scatter_rows(axis, source, dest, sems):
    height = dest.shape[1]
    return Move(
        axis,
        lambda target: source.at[pl.ds(pl.multiple_of(target * height, height), height)],
        dest,
        sems,
    ).start()


def share_block(axis, dest, sems):
    here = lax.axis_index(axis)
    return Move(axis, lambda target: dest.at[here], dest, sems).start()


class PairGather:
    def __init__(self, buffer, sems):
        self.buffer, self.sems = buffer, sems
        self.count, self.here = lax.axis_size(DP), lax.axis_index(DP)
        self.partner = self.here + 1 - 2 * lax.rem(self.here, 2)
        self.half = self.count // 2

    def copy(self, block, target, slot):
        return pltpu.make_async_remote_copy(
            src_ref=self.buffer.at[block],
            dst_ref=self.buffer.at[block],
            send_sem=self.sems.at[0, slot],
            recv_sem=self.sems.at[1, slot],
            device_id={DP: target},
            device_id_type=MESH,
        )

    def direct(self, step):
        return self.copy(self.here, lax.rem(self.here + 2 * step, self.count), step)

    def onward(self, step):
        block = lax.rem(self.here + self.count - 2 * step, self.count)
        return self.copy(block, self.partner, self.half + step)

    def start(self):
        for step in range(1, self.half):
            self.direct(step).start()
        self.onward(0).start()
        return self

    def forward_one(self, step):
        self.direct(step).wait_recv()
        self.onward(step).start()

    def forward(self):
        for step in range(1, self.half):
            self.forward_one(step)

    def arrive(self):
        for step in range(self.half):
            self.onward(step).wait_recv()

    def finish(self):
        for step in range(1, self.half):
            self.direct(step).wait_send()
        for step in range(self.half):
            self.onward(step).wait_send()


class Relay:
    def __init__(self, buffer, dp_sems, sems):
        self.buffer, self.sems = buffer, sems
        self.here = lax.axis_index(TENSOR)
        self.gather = PairGather(buffer.at[self.here], dp_sems)
        self.far = lax.rem(self.here + 2, 4)
        self.near = self.here + 1 - 2 * lax.rem(self.here, 2)
        self.blocks, self.block = lax.axis_size(DP), lax.axis_index(DP)
        self.half = self.blocks // 2
        partner = self.gather.partner
        own = [lax.rem(self.block + self.blocks - 2 * k, self.blocks) for k in range(self.half)]
        other = [lax.rem(partner + self.blocks - 2 * k, self.blocks) for k in range(self.half)]
        self.order = own + other

    def copy(self, kind, index):
        source = self.far if kind == 2 else self.here
        block = self.order[index]
        return pltpu.make_async_remote_copy(
            src_ref=self.buffer.at[source, block],
            dst_ref=self.buffer.at[source, block],
            send_sem=self.sems.at[0, kind, index],
            recv_sem=self.sems.at[1, kind, index],
            device_id={TENSOR: self.far if kind == 0 else self.near},
            device_id_type=MESH,
        )

    def send(self, index):
        self.copy(0, index).start()
        self.copy(1, index).start()

    def start(self):
        self.gather.start()
        self.send(0)
        return self

    def pass_on(self):
        for step in range(1, self.half):
            self.gather.forward_one(step)
            self.send(step)
        for step in range(self.half):
            self.gather.onward(step).wait_recv()
            self.send(self.half + step)

    def spread(self):
        for index in range(self.blocks):
            self.copy(0, index).wait_recv()
            self.copy(2, index).start()

    def arrive(self):
        for index in range(self.blocks):
            self.copy(1, index).wait_recv()
            self.copy(2, index).wait_recv()

    def finish(self):
        self.gather.finish()
        for index in range(self.blocks):
            for kind in range(3):
                self.copy(kind, index).wait_send()


def split_again(tile):
    value = tile + pltpu.roll(tile, 64, 1)
    high = value.astype(BF16).astype(F32)
    return jnp.where(lanes(tile.shape) < 64, high, value - high)


class AllSum:
    def __init__(self, source, scratch, sems, halves):
        self.source, self.sems, self.halves = source, sems, halves
        self.parts, self.tiles, self.arrived, self.done, self.whole = scratch
        self.here, self.block = lax.axis_index(TENSOR), lax.axis_index(DP)
        self.height = self.parts.shape[1]
        self.owners = self.tiles.shape[0]
        self.own = pl.ds(pl.multiple_of(self.here * self.height, self.height), self.height)
        self.first = scatter_rows(TENSOR, source, self.parts, sems[0])
        self.parts[self.here] = source[self.own, :]

    def owned(self, act):
        pl.when(self.block < self.owners)(act)

    def to_owner(self, owner):
        return pltpu.make_async_remote_copy(
            src_ref=self.tiles.at[owner],
            dst_ref=self.arrived.at[self.block],
            send_sem=self.sems[1].at[0, owner],
            recv_sem=self.sems[1].at[1, self.block],
            device_id={DP: owner},
            device_id_type=MESH,
        )

    def from_block(self, k):
        return pltpu.make_async_remote_copy(
            src_ref=self.tiles.at[0],
            dst_ref=self.arrived.at[k],
            send_sem=self.sems[1].at[0, 0],
            recv_sem=self.sems[1].at[1, k],
            device_id={DP: k},
            device_id_type=MESH,
        )

    def others(self, limit, act):
        for k in range(limit):
            pl.when(self.block != k)(lambda k=k: act(k))

    def tile_to(self, k):
        return pltpu.make_async_remote_copy(
            src_ref=self.done.at[self.block],
            dst_ref=self.done.at[self.block],
            send_sem=self.sems[2].at[0, k],
            recv_sem=self.sems[2].at[1, self.block],
            device_id={DP: k},
            device_id_type=MESH,
        )

    def tile_from(self, k):
        return pltpu.make_async_remote_copy(
            src_ref=self.done.at[k],
            dst_ref=self.done.at[k],
            send_sem=self.sems[2].at[0, k],
            recv_sem=self.sems[2].at[1, k],
            device_id={DP: k},
            device_id_type=MESH,
        )

    def scatter(self, factor=None):
        self.first.arrive()
        total = sum_blocks(self.parts)
        if factor is not None:
            total = total * factor[self.own, :]
        for owner in range(self.owners):
            tile = total[:, owner * 128 : (owner + 1) * 128]
            if self.halves and owner == self.owners - 1:
                tile = split_again(tile)
            self.tiles[owner] = tile.astype(BF16)
        self.others(self.owners, lambda owner: self.to_owner(owner).start())

        @self.owned
        def _():
            self.arrived[self.block] = self.tiles[self.block]

    def gather(self):
        blocks = lax.axis_size(DP)

        @self.owned
        def _():
            self.others(blocks, lambda k: self.from_block(k).wait_recv())
            tile = sum_blocks(self.arrived)
            if self.halves:
                tile = jnp.where(self.block == self.owners - 1, split_again(tile), tile)
            self.done[self.block] = tile.astype(BF16)
            self.others(blocks, lambda k: self.tile_to(k).start())

    def result(self):
        self.others(self.owners, lambda k: self.tile_from(k).wait_recv())
        for k in range(self.owners):
            self.whole[self.here, :, k * 128 : (k + 1) * 128] = self.done[k]
        self.last = share_block(TENSOR, self.whole, self.sems[3])
        self.last.arrive()
        return across(self.whole, 0).astype(F32)

    def finish(self):
        self.first.finish()
        self.others(self.owners, lambda owner: self.to_owner(owner).wait_send())
        blocks = lax.axis_size(DP)
        self.owned(lambda: self.others(blocks, lambda k: self.tile_to(k).wait_send()))
        self.last.finish()


class Everyone:
    def __init__(self, buffer, sems):
        self.buffer, self.sems = buffer, sems
        self.tensor = lax.axis_size(TENSOR)
        self.total = lax.axis_size(DP) * self.tensor
        self.here = lax.axis_index(DP) * self.tensor + lax.axis_index(TENSOR)

    def copy(self, step):
        other = lax.rem(self.here + step, self.total)
        return pltpu.make_async_remote_copy(
            src_ref=self.buffer.at[self.here],
            dst_ref=self.buffer.at[self.here],
            send_sem=self.sems.at[0, step],
            recv_sem=self.sems.at[1, step],
            device_id={DP: other // self.tensor, TENSOR: lax.rem(other, self.tensor)},
            device_id_type=MESH,
        )

    def each(self, act):
        def one(step, carry):
            act(self.copy(step))
            return carry

        lax.fori_loop(1, self.total, one, 0)

    def start(self):
        self.each(lambda copy: copy.start())
        return self

    def arrive(self):
        self.each(lambda copy: copy.wait_recv())

    def finish(self):
        self.each(lambda copy: copy.wait_send())


def dot_nt(a, b):
    return lax.dot_general(a, b, (((1,), (1,)), ((), ())), preferred_element_type=F32)


def dot_nn(a, b):
    return jnp.dot(a, b, preferred_element_type=F32)


def root_of(v):
    return lax.rsqrt(jnp.mean(v * v, -1, keepdims=True) + NORM_EPS)


def low(v):
    return v.astype(BF16).astype(F32)


def gelu_value(x):
    slope = math.sqrt(2.0 / math.pi)
    return 0.5 * x * (1.0 + jnp.tanh(slope * (x + 0.044715 * (x * x * x))))


def gelu_slope(x):
    slope = math.sqrt(2.0 / math.pi)
    t = jnp.tanh(slope * (x + 0.044715 * (x * x * x)))
    return 0.5 * (1.0 + t) + 0.5 * x * (1.0 - t * t) * (slope * (1.0 + 3 * 0.044715 * x * x))


def lanes(shape):
    return lax.broadcasted_iota(jnp.int32, shape, len(shape) - 1)


def sublanes(shape):
    return lax.broadcasted_iota(jnp.int32, shape, len(shape) - 2)


def tensor_sum(total, buffer, sems):
    buffer[lax.axis_index(TENSOR)] = total.astype(BF16)
    move = share_block(TENSOR, buffer, sems)
    move.arrive()
    return sum_blocks(buffer), move


def norm_back_rows(v, g, upstream):
    root = root_of(v)
    scaled = g * upstream
    inner = jnp.sum(scaled * v, -1, keepdims=True)
    back = root * scaled - v * (root * root * root * inner / v.shape[-1])
    return back, jnp.sum(upstream * v * root, 0, keepdims=True)


def sum_blocks(ref):
    total = ref[0].astype(F32)
    for k in range(1, ref.shape[0]):
        total = total + ref[k].astype(F32)
    return total


def packed_rows(value):
    rows, wide = value.shape
    whole, half = wide // 128, rows // 2
    tail = value[:, whole * 128 :]
    parts = [value[:, t * 128 : (t + 1) * 128] for t in range(whole)]
    return jnp.concatenate(parts + [jnp.concatenate([tail[0:half], tail[half:]], 1)], 0)


def unpacked_rows(value, rows):
    whole = value.shape[0] // rows
    tail = value[whole * rows :]
    parts = [value[t * rows : (t + 1) * rows] for t in range(whole)]
    return jnp.concatenate(parts + [jnp.concatenate([tail[:, 0:64], tail[:, 64:]], 0)], 1)


def across(ref, axis):
    return jnp.concatenate([ref[k] for k in range(ref.shape[0])], axis)


def squared(value):
    return jnp.sum(value * value, keepdims=True)


def step_kernel(names, small, weights, experts, vocab_rows, starts, *refs):
    r = types.SimpleNamespace(**dict(zip(names, refs, strict=True)))
    block, here = lax.axis_index(DP), lax.axis_index(TENSOR)
    blocks, tensor = lax.axis_size(DP), lax.axis_size(TENSOR)
    rows = r.own_ids.shape[1]
    every = rows * blocks
    picks = r.own_offsets.shape[1]
    count = picks * blocks
    columns, width = r.proj_weight.shape[1:]
    features = columns * blocks
    heads = width // HD
    share = r.pages.shape[2]
    group = blocks // tensor
    scale = 1.0 / math.sqrt(HD)
    moves = []

    def all_sum(source, number):
        scratch = [getattr(r, f"sum_{k}_{number}") for k in range(5)]
        sems = [getattr(r, f"sum_sem_{k}_{number}") for k in range(4)]
        return keep(AllSum(source, scratch, sems, number == 2))

    def keep(move):
        moves.append(move)
        return move

    def load(name, sems, k):
        copy = pltpu.make_async_copy(getattr(r, name + OUTSIDE), getattr(r, name), sems.at[k])
        copy.start()
        return copy

    loads = [load(name, r.load_sems, k) for k, name in enumerate(small)]
    greeting = greet_everyone()
    held = [load(name, r.held_sems, k) for k, name in enumerate(weights)]
    proj_load, map_load, table_load, in_load, out_load = held[:5]
    for copy in loads:
        copy.wait()

    ids = r.own_ids[...].astype(F32)
    offset_row = jnp.concatenate(
        [r.own_offsets[...].astype(F32), jnp.zeros((1, rows - picks), F32)], 1
    )
    slot = lanes((rows, rows))
    loss_hot = (sublanes((rows, rows)).astype(F32) == offset_row) & (slot < picks)
    targets = r.own_targets[...]
    upper = targets // 256
    facts = jnp.concatenate(
        [
            upper.astype(F32),
            (targets - upper * 256).astype(F32),
            r.own_routes[...].astype(F32),
            jnp.zeros((4, rows), F32),
        ],
        0,
    )
    facts = dot_nn(facts.astype(BF16), loss_hot.astype(F32).astype(BF16))
    known = jnp.concatenate(
        [
            offset_row,
            facts[0:1] * 256.0 + facts[1:2],
            facts[2:4],
            ids,
            jnp.zeros((3, rows), F32),
        ],
        0,
    )
    r.known[block] = known
    own_router = r.own_router[...]
    own_small = jnp.concatenate(
        [own_router, jnp.zeros((4 - experts, columns), F32), r.own_gains[...], jnp.zeros((1, columns), F32)]
        if experts < 4
        else [own_router, r.own_gains[...], jnp.zeros((1, columns), F32)],
        0,
    )
    r.small[block] = jnp.concatenate([own_small, jnp.zeros((8, 128 - columns), F32)], 1)
    map_load.wait()
    r.maps[here, block] = packed_rows(r.map_weight[...].T).astype(BF16)
    proj_load.wait()
    own_proj = jnp.concatenate([r.proj_weight[s] for s in range(3)], 1)
    r.proj[block] = packed_rows(own_proj).astype(BF16)
    own_proj = own_proj.astype(BF16)
    pl.semaphore_wait(*greeting)
    to_known = keep(share_block(DP, r.known, r.sem_known))
    to_small = keep(share_block(DP, r.small, r.sem_small))
    to_maps = keep(Relay(r.maps, r.sem_map, r.sem_maps).start())
    to_proj = keep(PairGather(r.proj, r.sem_proj).start())

    table_load.wait()
    for k in range(blocks):
        stop = min(vocab_rows, (k + 1) * share)
        span = max(0, stop - k * share)
        if span > 0:
            r.pages[k, :, 0:span] = r.table_weight[:, k * share : stop].astype(BF16)
        if span < share:
            r.pages[k, :, span:share] = jnp.zeros((columns, share - span), BF16)
    r.table[block] = r.pages[block]

    def pages_move(steps):
        return keep(
            Move(DP, lambda target: r.pages.at[target], r.table, r.sem_pages, steps).start()
        )

    to_known.arrive()
    base = (here * vocab_rows).astype(F32)
    for k in range(blocks):
        r.id_row[:, k * rows : (k + 1) * rows] = r.known[k][4:5, :] - base
    chunk = group * rows
    id_high = jnp.floor(r.id_row[...] * (1.0 / STRIP))
    r.id_high[...] = id_high
    r.id_place[...] = r.id_row[...] - id_high * STRIP
    strips_of_page = share // STRIP
    for step in range(1, tensor + 1):
        target = lax.rem(here + step, tensor)
        at = pl.ds(pl.multiple_of(target * chunk, chunk), chunk)
        hot = sublanes((STRIP, chunk)).astype(F32) == r.id_place[:, at]
        hot = hot.astype(F32).astype(BF16)
        number = r.id_high[:, at]

        def look(k, total, hot=hot, number=number):
            strips = jnp.concatenate(
                [r.pages[k, :, n * STRIP : (n + 1) * STRIP] for n in range(strips_of_page)], 0
            )
            found = dot_nn(strips, hot)
            for n in range(strips_of_page):
                mine = number == (k * strips_of_page + n).astype(F32)
                total = total + jnp.where(mine, found[n * columns : (n + 1) * columns], 0.0)
            return total

        found = lax.fori_loop(0, blocks, look, jnp.zeros((columns, chunk), F32))
        for b in range(group):
            r.looked[target, b] = found[:, b * rows : (b + 1) * rows].astype(BF16)
        if step == tensor - 1:
            to_total = keep(
                Move(TENSOR, lambda target: r.looked.at[target], r.first, r.sem_first).start()
            )
    to_maps.pass_on()
    to_proj.forward()
    r.first[here] = r.looked[here]
    to_total.arrive()
    for b in range(group):
        r.streams[here, block, :, b * rows : (b + 1) * rows] = sum_blocks(r.first.at[:, b]).astype(
            BF16
        )
    to_streams = keep(Relay(r.streams, r.sem_stream, r.sem_streams).start())
    to_streams.pass_on()
    pages_now = [pages_move((4, 2, 6, 3))]
    to_small.arrive()
    gain_columns = [low(r.small[k].T[0:columns, 4:5]) for k in range(blocks)]
    small_rows = jnp.concatenate([r.small[k][:, 0:columns] for k in range(blocks)], 1)
    gains = low(small_rows)
    r.router[...] = jnp.concatenate(
        [
            jnp.where(sublanes(gains.shape) < experts, gains, 0.0),
            jnp.zeros((128 - gains.shape[0], features), F32),
        ],
        0,
    ).astype(BF16)
    r.gains[...] = gains
    r.id_low[...] = (
        (sublanes((STRIP, every)).astype(F32) == r.id_place[...]).astype(F32).astype(BF16).T
    )

    def column_of(field):
        table = jnp.concatenate(
            [r.known[k][field : field + 1, :] for k in range(blocks)]
            + ([jnp.zeros((8 - blocks, rows), F32)] if blocks < 8 else []),
            0,
        ).T
        return jnp.concatenate([table[0:picks, k : k + 1] for k in range(blocks)], 0)

    offsets, wanted, route_a, route_b = (
        column_of(field).astype(jnp.int32) for field in range(4)
    )
    positions = offsets + sublanes((count, 1)) // picks * rows
    period = 2 * every
    bucket_row = jnp.concatenate(
        [r.own_buckets[...].astype(F32), jnp.zeros((1, 1), F32)], 1
    )
    strips = [bucket_row[:, k * rows : (k + 1) * rows] for k in range(period // rows)]
    mirror = (lanes((rows, rows)) + sublanes((rows, rows)) == rows - 1).astype(F32).astype(BF16)
    strips = dot_nn(jnp.concatenate(strips, 0).astype(BF16), mirror)
    flipped = jnp.concatenate(
        [strips[k : k + 1, :] for k in reversed(range(period // rows))], 1
    )
    spread = jnp.broadcast_to(flipped, (rows, period))
    turned = pltpu.roll(spread, period - rows, 1, stride=1, stride_axis=0).astype(BF16)
    chosen = (lanes((count, rows)) == offsets).astype(F32).astype(BF16)
    r.shifted[...] = dot_nn(chosen, turned).astype(jnp.int32)
    for k in range(blocks):
        begin = rows * (blocks - 1 - k)
        r.bucket[k * picks : (k + 1) * picks, :] = r.shifted[
            k * picks : (k + 1) * picks, begin : begin + every
        ]
    bucket_count = r.position_bias.shape[1]

    def fill(k, carry):
        at = pl.ds(pl.multiple_of(k * picks, picks), picks)
        numbers = r.bucket[at, :]
        terms = [jnp.zeros(numbers.shape, F32)] * heads
        for b in range(bucket_count):
            same = numbers == b
            terms = [jnp.where(same, r.position_bias[h, b], terms[h]) for h in range(heads)]
        for h in range(heads):
            r.bias[h, at, :] = terms[h]
        return carry

    lax.fori_loop(0, blocks, fill, 0)

    def picture_at(place):
        inside = jnp.full(place.shape, -1, jnp.int32)
        for n in range(starts):
            begin = r.picture_start[0, n]
            inside = jnp.where((place >= begin) & (place < begin + PIECE), n, inside)
        return inside

    key_position = lanes((count, every))
    query_picture = picture_at(positions)
    allowed = (key_position <= positions) | (
        (picture_at(lanes((1, every))) == query_picture) & (query_picture >= 0)
    )
    to_streams.spread()
    to_proj.arrive()
    all_proj = jnp.concatenate([unpacked_rows(r.proj[k], columns) for k in range(blocks)], 0)
    key_proj, value_proj = (
        all_proj[:, k * width : (k + 1) * width].astype(F32).T.astype(BF16) for k in (1, 2)
    )
    gain_column = jnp.concatenate(gain_columns, 0)
    back_hot = (key_position == positions).astype(F32).astype(BF16)
    stream = jnp.zeros((count, features), F32)
    normed_loss = jnp.zeros((count, features), F32)
    to_streams.arrive()
    for k in range(tensor):
        part = slice(k * chunk, (k + 1) * chunk)
        low_part = across(r.streams.at[k], 0)
        wide_part = low_part.astype(F32)
        root = lax.rsqrt(jnp.mean(wide_part * wide_part, 0, keepdims=True) + NORM_EPS)
        r.roots[:, part] = root
        normed_in = (wide_part * root * gain_column).astype(BF16)
        r.keys[:, part] = dot_nn(key_proj, normed_in).astype(BF16)
        r.values[:, part] = dot_nn(value_proj, normed_in).astype(BF16)
        stream = stream + dot_nt(back_hot[:, part], low_part)
        normed_loss = normed_loss + dot_nt(back_hot[:, part], normed_in)
    query = dot_nn(normed_loss.astype(BF16), all_proj[:, 0:width]).astype(BF16)
    to_maps.spread()

    def head(value, h):
        return value[:, h * HD : (h + 1) * HD]

    def tall(ref, h):
        return ref[h * HD : (h + 1) * HD, :]

    for h in range(heads):
        raw = dot_nn(head(query, h), tall(r.keys, h)) * scale + r.bias[h]
        raw = jnp.where(allowed, raw, NEGATIVE)
        terms = jnp.exp(raw - jnp.max(raw, -1, keepdims=True))
        r.probs[h] = terms / jnp.sum(terms, -1, keepdims=True)
    attended = jnp.concatenate(
        [dot_nt(r.probs[h].astype(BF16), tall(r.values, h)).astype(BF16) for h in range(heads)],
        1,
    )
    r.heads[here] = attended
    to_heads = keep(share_block(TENSOR, r.heads, r.sem_heads))
    in_load.wait()
    out_load.wait()
    in_low, out_low = r.in_weight[...].astype(BF16), r.out_weight[...].astype(BF16)
    to_maps.arrive()
    to_heads.arrive()

    middle = stream
    for k in range(tensor):
        full = jnp.concatenate([unpacked_rows(r.maps[k, i], columns) for i in range(blocks)], 0)
        middle = middle + dot_nt(r.heads[k], full)
    r.middle[...] = middle
    gain_middle, gain_final = r.gains[5:6, :], r.gains[6:7, :]
    normed_mid = (middle * root_of(middle) * gain_middle).astype(BF16)
    inner = dot_nn(normed_mid, in_low)
    active = gelu_value(inner).astype(BF16)
    r.piece[...] = dot_nn(active, out_low).astype(BF16)
    mixing = all_sum(r.piece, 0)
    router_logits = dot_nt(normed_mid, r.router[...])
    lane = lanes(router_logits.shape)
    hot_a, hot_b = lane == route_a, lane == route_b
    logit_a = jnp.sum(jnp.where(hot_a, router_logits, 0.0), 1, keepdims=True)
    logit_b = jnp.sum(jnp.where(hot_b, router_logits, 0.0), 1, keepdims=True)
    logit_top = jnp.maximum(logit_a, logit_b)
    gate_a, gate_b = jnp.exp(logit_a - logit_top), jnp.exp(logit_b - logit_top)
    both = gate_a + gate_b
    r.gates[...] = jnp.where(hot_a, gate_a / both, 0.0) + jnp.where(hot_b, gate_b / both, 0.0)
    expert = block // (blocks // experts)
    r.gate[...] = jnp.sum(jnp.where(lane == expert, r.gates[...], 0.0), 1, keepdims=True)
    mixing.scatter(r.gate)
    pages_now.append(pages_move((5,)))
    mixing.gather()
    pages_now.append(pages_move((1, 7)))
    final = middle + mixing.result()
    out = (final * root_of(final) * gain_final).astype(BF16)
    for move in pages_now:
        move.arrive()

    table = across(r.table, 0)
    logits = dot_nn(out, table)
    slot = lanes(logits.shape) + block * share
    logits = jnp.where(slot < vocab_rows, logits, NEGATIVE)
    hit = slot == wanted - here * vocab_rows
    local_top = jnp.max(logits, -1, keepdims=True)
    local_stats = (
        local_top,
        jnp.sum(jnp.exp(logits - local_top), -1, keepdims=True),
        jnp.sum(jnp.where(hit & (slot < vocab_rows), logits, 0.0), -1, keepdims=True),
        jnp.sum(jnp.where(slot < vocab_rows, logits, 0.0), -1, keepdims=True),
    )
    packed = jnp.zeros((count, 128), F32)
    for k, column in enumerate(local_stats):
        packed = jnp.where(lane == k, column, packed)
    r.stats[block * tensor + here] = packed.T[0:4, :]
    to_stats = keep(Everyone(r.stats, r.sem_stats).start())
    weight = (query_picture < 0).astype(F32)
    weight_row = jnp.where(lane == 0, weight, 0.0).T[0:1, :]
    to_stats.arrive()
    peaks = r.stats[:, 0]
    peak = jnp.max(peaks, 0, keepdims=True)
    stats = (
        peak,
        jnp.sum(r.stats[:, 1] * jnp.exp(peaks - peak), 0, keepdims=True),
        jnp.sum(r.stats[:, 2], 0, keepdims=True),
        jnp.sum(r.stats[:, 3], 0, keepdims=True),
    )
    log_total = stats[0] + jnp.log(stats[1])
    per_row = (
        log_total
        - (1 - SMOOTH) * stats[2]
        - SMOOTH * stats[3] / VOCAB
        + ZLOSS * log_total * log_total
    )
    loss_sum = jnp.sum(weight_row * per_row, keepdims=True)
    loss_count = jnp.sum(weight_row, keepdims=True)
    total_column = jnp.where(sublanes((128, count)) == 0, log_total, 0.0).T[:, 0:1]
    d_logits = weight * (
        (1 + 2 * ZLOSS * total_column) * jnp.exp(logits - total_column)
        - jnp.where(hit, 1 - SMOOTH, 0.0)
        - SMOOTH / VOCAB
    )
    d_logits = jnp.where(slot < vocab_rows, d_logits, 0.0).astype(BF16)
    r.d_logits_parts = [r.d_logits.at[k] for k in range(r.d_logits.shape[0])]
    piece_rows = r.d_logits.shape[2]
    for k, part in enumerate(r.d_logits_parts):
        part[block] = d_logits[k * piece_rows : (k + 1) * piece_rows]
    logit_moves = [
        keep(PairGather(part, r.sem_logits.at[k])) for k, part in enumerate(r.d_logits_parts)
    ]
    r.sent[...] = dot_nt(d_logits, table).astype(BF16)
    summing = all_sum(r.sent, 1)
    logit_moves[0].start()
    summing.scatter()
    summing.gather()
    logit_moves[0].forward()
    logit_moves[1].start()
    upstream, grad_final = norm_back_rows(final, gain_final, summing.result())
    gate = r.gate[...]
    logit_moves[2].start()
    d_piece = (gate * upstream).astype(BF16)
    d_inner = (dot_nt(d_piece, out_low) * gelu_slope(inner)).astype(BF16)
    r.wide[:, 0:features] = dot_nt(d_inner, in_low).astype(BF16)
    gate_part = jnp.sum(upstream * r.piece[...].astype(F32), 1, keepdims=True)
    high = low(gate_part)
    r.wide[:, features:] = jnp.where(
        lane == expert, high, jnp.where(lane == expert + 64, gate_part - high, 0.0)
    ).astype(BF16)
    summing = all_sum(r.wide, 2)
    logit_moves[1].forward()
    grad_out = dot_nn(active.T, d_piece)
    grad_in = dot_nn(normed_mid.T, d_inner)
    r.grad_out[...] = grad_out
    r.grad_in[...] = grad_in
    squares = squared(grad_out) + squared(grad_in)
    summing.scatter()
    logit_moves[2].forward()
    summing.gather()
    logit_moves[3].start()
    total = summing.result()
    tail = total[:, features:]
    d_gates = tail + pltpu.roll(tail, 64, 1)
    named = hot_a | hot_b
    d_gates = jnp.where(named, d_gates, 0.0)
    mean = jnp.sum(r.gates[...] * d_gates, 1, keepdims=True)
    d_router = jnp.where(named, r.gates[...] * (d_gates - mean), 0.0).astype(BF16)
    d_normed_mid = total[:, 0:features] + dot_nn(d_router, r.router[...])
    d_from_mid, grad_middle = norm_back_rows(middle, gain_middle, d_normed_mid)
    d_attn = (upstream + d_from_mid).astype(BF16)
    stream_c = jnp.concatenate([r.streams[k, block] for k in range(tensor)], 1).astype(F32)
    roots = r.roots[...]
    gain_column = low(r.small[block].T[0:columns, 4:5])
    normed_c = (stream_c * roots * gain_column).astype(BF16)
    normed_loss = dot_nt(normed_c, back_hot).astype(BF16)
    query_wide = dot_nn(query.T, back_hot)

    own_map = jnp.concatenate(
        [unpacked_rows(r.maps[here, i], columns) for i in range(blocks)], 0
    )
    d_attended = dot_nn(d_attn, own_map).astype(BF16)
    d_query = []
    for h in range(heads):
        soft = r.probs[h]
        d_head = head(d_attended, h)
        d_probs = dot_nn(d_head, tall(r.values, h))
        d_scores = soft * (d_probs - jnp.sum(soft * d_probs, -1, keepdims=True))
        d_scores = d_scores.astype(BF16)
        r.bias[h] = d_scores.astype(F32)
        d_query.append((dot_nt(d_scores, tall(r.keys, h)) * scale).astype(BF16))
        r.d_keys[h * HD : (h + 1) * HD, :] = (
            dot_nn(head(query, h).T, d_scores) * scale
        ).astype(BF16)
        r.d_values[h * HD : (h + 1) * HD, :] = dot_nn(d_head.T, soft.astype(BF16)).astype(BF16)
    d_query = jnp.concatenate(d_query, 1)
    d_query_wide = dot_nn(d_query.T, back_hot).astype(BF16)
    d_columns = (
        dot_nn(own_proj[:, 0:width], d_query_wide)
        + dot_nn(own_proj[:, width : 2 * width], r.d_keys[...])
        + dot_nn(own_proj[:, 2 * width :], r.d_values[...])
    )
    inner_row = jnp.sum(
        d_query_wide.astype(F32) * query_wide
        + r.d_keys[...].astype(F32) * r.keys[...].astype(F32)
        + r.d_values[...].astype(F32) * r.values[...].astype(F32),
        0,
        keepdims=True,
    )
    inner_high = low(inner_row)
    extra = sublanes((16, every))
    r.part[0:columns, :] = d_columns.astype(BF16)
    r.part[columns:, :] = jnp.where(
        extra == 0, inner_high, jnp.where(extra == 1, inner_row - inner_high, 0.0)
    ).astype(BF16)
    to_part = keep(
        Move(
            TENSOR,
            lambda target: r.part.at[:, pl.ds(pl.multiple_of(target * chunk, chunk), chunk)],
            r.part_in,
            r.sem_part,
        ).start()
    )
    r.part_in[here] = r.part[:, pl.ds(pl.multiple_of(here * chunk, chunk), chunk)]
    grad_proj = (
        dot_nn(normed_loss, d_query),
        dot_nt(normed_c, r.d_keys[...]),
        dot_nt(normed_c, r.d_values[...]),
    )
    for s in range(3):
        r.grad_proj[s] = grad_proj[s]
        squares = squares + squared(grad_proj[s])
    to_part.arrive()
    r.part_all[here] = sum_blocks(r.part_in).astype(BF16)
    to_parts = keep(share_block(TENSOR, r.part_all, r.sem_part_all))
    r.bias_rows[...] = jnp.zeros(r.bias_rows.shape, F32)

    def collect(k, carry):
        at = pl.ds(pl.multiple_of(k * picks, picks), picks)
        numbers = r.bucket[at, :]
        parts = [r.bias[h, at, :] for h in range(heads)]
        for b in range(bucket_count):
            same = numbers == b
            for h in range(heads):
                kept = jnp.where(same, parts[h], 0.0)
                kept = kept[0:8] + kept[8:16]
                narrow = kept[:, 0:128]
                for c in range(1, every // 128):
                    narrow = narrow + kept[:, c * 128 : (c + 1) * 128]
                r.bias_rows[h, b] += narrow
        return carry

    lax.fori_loop(0, count // picks, collect, 0)
    grad_bias = jnp.sum(r.bias_rows[...], 2)
    r.grad_bias[...] = grad_bias
    grad_bias = jnp.sum(grad_bias, -1, keepdims=True)
    squares = squares + jnp.sum(grad_bias * grad_bias, keepdims=True)[0] / blocks
    pick_own = lanes((columns, features)) == sublanes((columns, features)) + block * columns
    pick_own = pick_own.astype(F32).astype(BF16)
    d_attn_t = dot_nt(pick_own, d_attn).astype(BF16)
    out_t = dot_nt(pick_own, out).astype(BF16)
    middle_t = dot_nt(pick_own, normed_mid).astype(BF16)
    grad_map = dot_nt(attended.T, d_attn_t)
    r.grad_map[...] = grad_map
    squares = squares + squared(grad_map)
    grad_router = dot_nt(d_router.T, middle_t)[0:8]
    residual = dot_nn(d_attn_t, back_hot)
    logit_moves[3].forward()
    gain_sum = jnp.concatenate(
        [grad_middle, grad_final, jnp.zeros((6, features), F32)], 0
    )
    gain_sum = pltpu.roll(gain_sum, lax.rem(features - block * columns, features), 1)
    for move in logit_moves[:-1]:
        move.arrive()
    late_rows = r.d_logits_parts[-1].shape[1]
    out_early, out_late = out_t[:, 0 : count - late_rows], out_t[:, count - late_rows :]
    whole = vocab_rows // share

    def first_page(k, where, size):
        page = jnp.concatenate([part[k] for part in r.d_logits_parts[:-1]], 0)
        r.grad_table[:, where] = dot_nn(out_early, page)[:, 0:size]

    def first_pages(k, carry):
        first_page(k, pl.ds(pl.multiple_of(k * share, share), share), share)
        return carry

    lax.fori_loop(0, whole, first_pages, 0)
    if vocab_rows > whole * share:
        first_page(whole, slice(whole * share, vocab_rows), vocab_rows - whole * share)
    to_parts.arrive()
    parts = across(r.part_all, 1).astype(F32)
    d_columns = parts[0:columns]
    inner_row = parts[columns : columns + 1] + parts[columns + 1 : columns + 2]
    grad_first = jnp.sum(d_columns * stream_c * roots, 1, keepdims=True)
    grad_first = jnp.broadcast_to(grad_first, (columns, 128)).T[0:1, :]
    small = jnp.concatenate(
        [
            grad_router[0:4],
            grad_first,
            gain_sum[0:2, 0:columns],
            jnp.zeros((1, columns), F32),
        ],
        0,
    )
    r.grad_small[:, 0:columns] = small
    r.grad_small[:, columns:] = jnp.zeros((8, 128 - columns), F32)
    squares = squares + squared(small) / tensor
    d_stream = (
        roots * gain_column * d_columns
        - stream_c * (roots * roots * inner_row / features)
        + residual
    )
    d_high = d_stream.astype(BF16)
    d_low = (d_stream - d_high.astype(F32)).astype(BF16)
    low_half = d_stream.astype(BF16)
    full = vocab_rows // STRIP
    ends = [(k, min(STRIP, vocab_rows - k * STRIP)) for k in range(full - full % 4, -(-vocab_rows // STRIP))]

    def strip_mask(number):
        return (r.id_high[...] == number).astype(F32).astype(BF16)

    def scatter_four(k, carry):
        masked = [low_half * strip_mask((k * 4 + n).astype(F32)) for n in range(4)]
        found = dot_nn(jnp.concatenate(masked, 0), r.id_low[...])
        begin = pl.multiple_of(k * 4 * STRIP, STRIP)
        for n in range(4):
            r.grad_table[:, pl.ds(begin + n * STRIP, STRIP)] += found[
                n * columns : (n + 1) * columns
            ]
        return carry

    lax.fori_loop(0, full // 4, scatter_four, 0)
    masked = jnp.concatenate([low_half * strip_mask(float(k)) for k, size in ends], 0)
    found = dot_nn(masked, r.id_low[...])
    for n, (k, size) in enumerate(ends):
        r.grad_table[:, k * STRIP : k * STRIP + size] += found[
            n * columns : (n + 1) * columns, 0:size
        ]
    logit_moves[-1].arrive()

    def page_strips(k, total):
        begin = pl.multiple_of(k * share, share)
        return total + add_page(k, pl.ds(begin, share))

    def add_page(k, where, size=share):
        page = r.d_logits_parts[-1][k]
        value = r.grad_table[:, where] + dot_nn(out_late, page)[:, 0:size]
        r.grad_table[:, where] = value
        return squared(value)

    squares = squares + lax.fori_loop(0, whole, page_strips, jnp.zeros((1, 1), F32))
    if vocab_rows > whole * share:
        squares = squares + add_page(
            whole, slice(whole * share, vocab_rows), vocab_rows - whole * share
        )
    r.squares[block * tensor + here] = jnp.broadcast_to(squares, (1, 128))
    to_squares = keep(Everyone(r.squares, r.sem_squares).start())
    to_squares.arrive()
    norm = jnp.sqrt(sum_blocks(r.squares))
    clip = MAX_NORM / jnp.maximum(norm, MAX_NORM)
    place = lanes(norm.shape)
    r.facts[...] = jnp.where(
        place == 0,
        clip,
        jnp.where(place == 1, norm, jnp.where(place == 2, loss_sum, loss_count)),
    )
    for copy in held[5:]:
        copy.wait()
    for move in moves:
        move.finish()


def run_step(blocks, tensor, experts, small, held, scalars):
    rows = small["own_ids"].shape[1]
    every = rows * blocks
    picks = small["own_offsets"].shape[1]
    count = picks * blocks
    columns, width = held["proj_weight"].shape[1:]
    features = columns * blocks
    hidden = held["in_weight"].shape[1]
    vocab_rows = held["table_weight"].shape[1]
    heads, bucket_count = scalars["position_bias"].shape
    share = -(-vocab_rows // (blocks * STRIP)) * STRIP
    group = blocks // tensor
    chunk = group * rows
    wide = features + 128
    outputs = dict(
        grad_table=(columns, vocab_rows),
        grad_proj=(3, columns, width),
        grad_map=(width, columns),
        grad_small=(8, 128),
        grad_in=(features, hidden),
        grad_out=(hidden, features),
        grad_bias=(heads, bucket_count, 128),
        facts=(1, 128),
    )
    scratch = dict(
        known=((blocks, 8, rows), F32),
        small=((blocks, 8, 128), F32),
        proj=((blocks, columns * 3 * width // 128, 128), BF16),
        maps=((tensor, blocks, columns * width // 128, 128), BF16),
        pages=((blocks, columns, share), BF16),
        table=((blocks, columns, share), BF16),
        id_row=((1, every), F32),
        id_high=((1, every), F32),
        id_place=((1, every), F32),
        id_low=((every, STRIP), BF16),
        looked=((tensor, group, columns, rows), BF16),
        first=((tensor, group, columns, rows), BF16),
        router=((128, features), BF16),
        gains=((8, features), F32),
        roots=((1, every), F32),
        streams=((tensor, blocks, columns, chunk), BF16),
        shifted=((count, 2 * every), jnp.int32),
        bucket=((count, every), jnp.int32),
        bias=((heads, count, every), F32),
        keys=((width, every), BF16),
        values=((width, every), BF16),
        probs=((heads, count, every), F32),
        heads=((tensor, count, width), BF16),
        middle=((count, features), F32),
        piece=((count, features), BF16),
        gates=((count, 128), F32),
        gate=((count, 1), F32),
        stats=((blocks * tensor, 4, 128), F32),
        d_logits=((4, blocks, count // 4, share), BF16),
        sent=((count, features), BF16),
        wide=((count, wide), BF16),
        d_keys=((width, every), BF16),
        d_values=((width, every), BF16),
        part=((columns + 16, every), BF16),
        part_in=((tensor, columns + 16, chunk), BF16),
        part_all=((tensor, columns + 16, chunk), BF16),
        bias_rows=((heads, bucket_count, 8, 128), F32),
        squares=((blocks * tensor, 1, 128), F32),
    )
    scratch.update({name: (array.shape, array.dtype) for name, array in small.items()})
    outputs.update({name: array.shape for name, array in held.items()})
    dp, ten = (2, blocks), (2, tensor)
    sems = dict(
        load_sems=(len(small),),
        held_sems=(len(held),),
        sem_squares=(2, blocks * tensor),
        sem_stats=(2, blocks * tensor),
        sem_logits=(4, 2, blocks),
        sem_known=dp,
        sem_small=dp,
        sem_proj=dp,
        sem_map=dp,
        sem_pages=dp,
        sem_first=ten,
        sem_stream=dp,
        sem_streams=(2, 3, blocks),
        sem_maps=(2, 3, blocks),
        sem_heads=ten,
        sem_part=ten,
        sem_part_all=ten,
    )
    height = count // tensor
    for number, span in enumerate((features, features, wide)):
        shapes = (
            (tensor, height, span),
            (span // 128, height, 128),
            (blocks, height, 128),
            (span // 128, height, 128),
            (tensor, height, span),
        )
        scratch.update({f"sum_{k}_{number}": (shape, BF16) for k, shape in enumerate(shapes)})
        for k, shape in enumerate((ten, dp, dp, ten)):
            sems[f"sum_sem_{k}_{number}"] = shape
    copied = {**small, **held}
    names = tuple(name + OUTSIDE for name in copied) + tuple(scalars)
    names += tuple(outputs) + tuple(scratch) + tuple(sems)
    starts = scalars["picture_start"].shape[1]
    results = pl.pallas_call(
        functools.partial(
            step_kernel, names, tuple(small), tuple(held), experts, vocab_rows, starts
        ),
        out_shape=[pltpu.VMEM(shape, F32) for shape in outputs.values()],
        in_specs=[pl.BlockSpec(memory_space=pltpu.HBM)] * len(copied)
        + [pl.BlockSpec(memory_space=pltpu.SMEM)] * len(scalars),
        out_specs=[WHOLE] * len(outputs),
        scratch_shapes=[pltpu.VMEM(*spec) for spec in scratch.values()]
        + [DMA(shape) for shape in sems.values()],
        compiler_params=pltpu.CompilerParams(
            collective_id=0, has_side_effects=True, vmem_limit_bytes=VMEM_BYTES
        ),
        name="training_step",
    )(*copied.values(), *scalars.values())
    return dict(zip(outputs, results))


def update_piece(weight, first, second, grad, rate, decay):
    first = BETA1 * first + (1 - BETA1) * grad
    second = BETA2 * second + (1 - BETA2) * (grad * grad)
    spread = second * lax.rsqrt(second) * math.sqrt(1 / (1 - BETA2**STEP)) + ADAM_EPS
    step = first / spread
    return weight * (1 - rate * decay) - (rate / (1 - BETA1**STEP)) * step, first, second


def spread_over(factor, change):
    return factor.reshape((1,) * change.ndim) * change


def update_kernel(jobs, facts, *refs):
    grads, refs = refs[: len(jobs)], refs[len(jobs) :]
    total = 3 * len(jobs)
    olds, outs, refs = refs[:total], refs[total : 2 * total], refs[2 * total :]
    scalars, news, done = refs[:3], refs[3:-1], refs[-1]
    for k, scalar in enumerate(scalars):
        scalar[...] = facts[:, k + 1 : k + 2]
    factor = facts[:, 0:1]
    copies = []
    for index, (height, rate, decay, begin, reduced) in enumerate(jobs):
        trio = slice(3 * index, 3 * index + 3)
        whole = news[3 * index].shape[0]
        for piece in range(0, whole, height):
            rows = slice(piece, piece + height)
            if reduced:
                change = jnp.sum(grads[index][...], -1)
            elif begin is not None:
                change = grads[index][begin : begin + whole, 0 : news[3 * index].shape[1]]
            else:
                change = grads[index][rows]
            values = update_piece(
                *(ref[rows] for ref in olds[trio]), spread_over(factor, change), rate, decay
            )
            for which, value in enumerate(values):
                new, out = news[3 * index + which], outs[3 * index + which]
                new[rows] = value
                part = pl.ds(piece, height)
                copy = pltpu.make_async_copy(new.at[part], out.at[part], done.at[len(copies)])
                copy.start()
                copies.append(copy)
    for copy in copies:
        copy.wait()


def run_update(facts, jobs, grads, olds):
    shapes = [old.shape for old in olds]
    pieces = sum(3 * shapes[3 * k][0] // job[0] for k, job in enumerate(jobs))
    results = pl.pallas_call(
        functools.partial(update_kernel, jobs),
        out_shape=[jax.ShapeDtypeStruct(shape, F32) for shape in shapes + [(1, 1)] * 3],
        in_specs=[WHOLE] * (1 + len(grads) + len(olds)),
        out_specs=[pl.BlockSpec(memory_space=pltpu.HBM)] * len(shapes) + [WHOLE] * 3,
        scratch_shapes=[pltpu.VMEM(shape, F32) for shape in shapes] + [DMA((pieces,))],
        compiler_params=pltpu.CompilerParams(vmem_limit_bytes=UPDATE_BYTES),
        name="update",
    )(facts, *grads, *olds)
    return [results[3 * k : 3 * k + 3] for k in range(len(jobs) + 1)]


def fast_local(
    token_ids,
    targets,
    loss_offsets,
    routes,
    picture_start,
    buckets,
    embedding,
    embedding_first,
    embedding_second,
    attn_proj,
    attn_proj_first,
    attn_proj_second,
    out_proj,
    out_proj_first,
    out_proj_second,
    router,
    router_first,
    router_second,
    expert_in,
    expert_in_first,
    expert_in_second,
    expert_out,
    expert_out_first,
    expert_out_second,
    norm_gains,
    norm_gains_first,
    norm_gains_second,
    position_bias,
    position_bias_first,
    position_bias_second,
):
    dp_count = lax.axis_size("dp")
    tensor_count = lax.axis_size("tensor")
    experts = router.shape[0]
    small = dict(
        own_ids=token_ids[None, :],
        own_targets=targets[None, :],
        own_offsets=loss_offsets[None, :],
        own_routes=routes.T,
        own_buckets=buckets[None, :],
        own_router=router,
        own_gains=norm_gains,
    )
    held = dict(
        proj_weight=attn_proj,
        map_weight=out_proj,
        table_weight=embedding.T,
        in_weight=expert_in,
        out_weight=expert_out,
        table_first=embedding_first.T,
        table_second=embedding_second.T,
        in_first=expert_in_first,
        in_second=expert_in_second,
        out_first=expert_out_first,
        out_second=expert_out_second,
        proj_first=attn_proj_first,
        proj_second=attn_proj_second,
        map_first=out_proj_first,
        map_second=out_proj_second,
    )
    scalars = dict(position_bias=position_bias, picture_start=picture_start)
    g = types.SimpleNamespace(**run_step(dp_count, tensor_count, experts, small, held, scalars))
    kinds = (
        (8, 0, None, False),
        (expert_in.shape[0] // 8, 4, None, False),
        (expert_out.shape[0] // 8, 5, None, False),
        (1, 1, None, False),
        (out_proj.shape[0], 2, None, False),
        (experts, 3, 0, False),
        (3, 6, 4, False),
        (position_bias.shape[0], 7, None, True),
    )
    jobs = tuple(
        (height, RATES[k], DECAYS[k], begin, reduced) for height, k, begin, reduced in kinds
    )
    grads = (g.grad_table, g.grad_in, g.grad_out, g.grad_proj, g.grad_map)
    grads += (g.grad_small, g.grad_small, g.grad_bias)
    olds = (g.table_weight, g.table_first, g.table_second, g.in_weight, g.in_first, g.in_second)
    olds += (g.out_weight, g.out_first, g.out_second, g.proj_weight, g.proj_first, g.proj_second)
    olds += (g.map_weight, g.map_first, g.map_second, router, router_first, router_second)
    olds += (norm_gains, norm_gains_first, norm_gains_second)
    olds += (position_bias, position_bias_first, position_bias_second)
    new = run_update(g.facts, jobs, grads, olds)
    results = [value.T for value in new[0]]
    for k in (3, 4, 5, 1, 2, 6, 7):
        results.extend(new[k])
    grad_norm, loss_sum, loss_count = (value.reshape(()) for value in new[-1])
    return (*results, grad_norm, loss_sum, loss_count)


def local(
    token_ids,
    targets,
    loss_offsets,
    routes,
    picture_start,
    buckets,
    embedding,
    embedding_first,
    embedding_second,
    attn_proj,
    attn_proj_first,
    attn_proj_second,
    out_proj,
    out_proj_first,
    out_proj_second,
    router,
    router_first,
    router_second,
    expert_in,
    expert_in_first,
    expert_in_second,
    expert_out,
    expert_out_first,
    expert_out_second,
    norm_gains,
    norm_gains_first,
    norm_gains_second,
    position_bias,
    position_bias_first,
    position_bias_second,
):
    f32 = jnp.float32
    bf16 = jnp.bfloat16
    dp_count = lax.axis_size("dp")
    tensor_count = lax.axis_size("tensor")
    dp_place = lax.axis_index("dp")
    tensor_place = lax.axis_index("tensor")
    rows = token_ids.shape[0]
    every = rows * dp_count
    length = min(SEQ, every)
    seqs = every // length
    sub = rows // seqs
    scale = 1.0 / math.sqrt(HD)
    vocab_rows = embedding.shape[0]
    table, projection, output_map, router_full, gain_full = (
        lax.all_gather(embedding.astype(bf16), "dp", axis=1, tiled=True),
        lax.all_gather(attn_proj.astype(bf16), "dp", axis=1, tiled=True),
        lax.all_gather(out_proj.astype(bf16), "dp", axis=1, tiled=True),
        lax.all_gather(router.astype(bf16), "dp", axis=1, tiled=True),
        lax.all_gather(norm_gains.astype(bf16), "dp", axis=1, tiled=True),
    )
    gain = gain_full.astype(f32)
    features = table.shape[1]
    offset = token_ids - tensor_place * vocab_rows
    owned = (offset >= 0) & (offset < vocab_rows)
    offset = jnp.clip(offset, 0, vocab_rows - 1)
    looked = jnp.take(table, offset, axis=0).astype(f32)
    stream_in = tensor_total(jnp.where(owned[:, None], looked, 0.0))
    pos_here = dp_place * sub + jnp.arange(sub, dtype=jnp.int32)
    seq_positions = jnp.arange(length, dtype=jnp.int32)
    picture_all = jax.vmap(lambda starts: picture_of(seq_positions, starts, PIECE))(picture_start)
    picture_here = lax.dynamic_slice_in_dim(picture_all, dp_place * sub, sub, 1)
    bucket_ids = jnp.arange(position_bias.shape[1], dtype=jnp.int32)
    bucket_hot = (bucket_ids[:, None] == buckets[None, :]).astype(f32)
    relative = jnp.dot(position_bias, bucket_hot, precision=HIGH)
    normed_in = normed(stream_in, gain[0]).astype(bf16)
    fresh = jnp.einsum("td,sde->ste", normed_in, projection, preferred_element_type=f32).astype(
        bf16
    )
    width = fresh.shape[2]
    heads = width // HD
    keys_local = fresh[1].reshape(seqs, sub, width)
    values_local = fresh[2].reshape(seqs, sub, width)
    query_heads = fresh[0].reshape(seqs, sub, heads, HD)
    keys_all, values_all = (
        lax.all_gather(keys_local, "dp", axis=1, tiled=True),
        lax.all_gather(values_local, "dp", axis=1, tiled=True),
    )
    block = min(512, length)
    blocks = length // block
    block_ids = jnp.arange(blocks, dtype=jnp.int32)

    def pair_scores(q_heads, q_pos, q_pic, k_heads, k_pos, k_pic, bias):
        raw = (
            jnp.einsum("sqhd,skhd->shqk", q_heads, k_heads, preferred_element_type=f32) * scale
            + bias[None]
        )
        allowed = (k_pos[None, :] <= q_pos[:, None])[None] | (
            k_pic[:, None, :] == q_pic[:, :, None]
        ) & (q_pic[:, :, None] >= 0)
        return jnp.where(allowed[:, None], raw, NEGATIVE)

    def key_slice(source, start):
        return lax.dynamic_slice_in_dim(source, start, block, 1).reshape(seqs, block, heads, HD)

    def own_bias(start):
        return rel_window(relative, dp_place * sub, sub, start, block, length)

    def fwd_scores(index, key_source):
        start = index * block
        key_pos = start + jnp.arange(block, dtype=jnp.int32)
        return pair_scores(
            query_heads,
            pos_here,
            picture_here,
            key_slice(key_source, start),
            key_pos,
            lax.dynamic_slice_in_dim(picture_all, start, block, 1),
            own_bias(start),
        )

    def max_step(carry, index):
        top, total = carry
        s = fwd_scores(index, keys_all)
        new_top = jnp.maximum(top, jnp.max(s, -1))
        terms = jnp.where(s > 0.5 * NEGATIVE, jnp.exp(s - new_top[..., None]), 0.0)
        total = total * jnp.exp(top - new_top) + jnp.sum(terms, -1)
        return ((new_top, total), None)

    start_top = jnp.full((seqs, heads, sub), NEGATIVE, f32)
    (top, total), unused = lax.scan(
        max_step, (start_top, jnp.zeros((seqs, heads, sub), f32)), block_ids
    )
    log_total = top + jnp.log(total)

    def out_step(accum, index):
        s = fwd_scores(index, keys_all)
        probs = jnp.exp(s - log_total[..., None]).astype(bf16)
        value_heads = key_slice(values_all, index * block)
        return (
            accum + jnp.einsum("shqk,skhd->sqhd", probs, value_heads, preferred_element_type=f32),
            None,
        )

    attended, unused = lax.scan(out_step, jnp.zeros((seqs, sub, heads, HD), f32), block_ids)
    attended_low = attended.reshape(rows, width).astype(bf16)
    stream_mid = stream_in + tensor_total(
        jnp.dot(attended_low, output_map, preferred_element_type=f32)
    )
    normed_mid = normed(stream_mid, gain[1]).astype(bf16)
    router_logits = jnp.dot(normed_mid, router_full.T, preferred_element_type=f32)
    gates = jax.nn.softmax(jnp.take_along_axis(router_logits, routes, 1), -1)
    experts = router_full.shape[0]
    top_k = routes.shape[1]
    capacity = 2 * rows * top_k // experts
    flat = routes.reshape(-1)
    owner = jnp.arange(rows * top_k, dtype=jnp.int32) // top_k
    hits = (flat[:, None] == jnp.arange(experts, dtype=jnp.int32)[None, :]).astype(jnp.int32)
    slot = jnp.sum(jnp.cumsum(hits, 0) * hits, 1) - 1
    first_row = 2 * flat * capacity + slot

    def pack(values):
        buffer = jnp.zeros((experts, capacity, features), bf16).at[flat, slot].set(values)
        return jnp.repeat(buffer, 2, axis=0).reshape(2 * experts * capacity, features)

    def unpack(values):
        return values[first_row].astype(f32) + values[first_row + capacity].astype(f32)

    in_low = expert_in.astype(bf16)
    out_low = expert_out.astype(bf16)
    arrived = route_exchange(pack(normed_mid[owner]))
    inner = jnp.dot(arrived, in_low, preferred_element_type=f32)
    active = jax.nn.gelu(inner).astype(bf16)
    produced = jnp.dot(active, out_low, preferred_element_type=f32).astype(bf16)
    returned = unpack(route_exchange(produced))
    mixed = jnp.sum((gates.reshape(-1)[:, None] * returned).reshape(rows, top_k, features), 1)
    stream_out = stream_mid + tensor_total(mixed)
    normed_out = normed(stream_out, gain[2]).astype(bf16)
    picked = normed_out[loss_offsets]
    logits = jnp.dot(picked, table.T, preferred_element_type=f32)
    wanted = targets[loss_offsets] - tensor_place * vocab_rows
    hit = jnp.arange(vocab_rows, dtype=jnp.int32)[None, :] == wanted[:, None]
    local_top = jnp.max(logits, -1)
    stats = (
        local_top,
        jnp.sum(jnp.exp(logits - local_top[:, None]), -1),
        jnp.sum(jnp.where(hit, logits, 0.0), -1),
        jnp.sum(logits, -1),
    )
    peak, vocab_total, target_logit, logit_sum = merged(stats, "tensor", combine_stats)
    loss_total = peak + jnp.log(vocab_total)
    weight = (picture_here.reshape(rows)[loss_offsets] < 0).astype(f32)
    per_row = (
        loss_total
        - (1 - SMOOTH) * target_logit
        - SMOOTH * logit_sum / VOCAB
        + ZLOSS * loss_total * loss_total
    )
    loss_local = jnp.sum(weight * per_row)
    soft = jnp.exp(logits - loss_total[:, None])
    d_logits = (
        weight[:, None]
        * (
            (1 + 2 * ZLOSS * loss_total)[:, None] * soft
            - (1 - SMOOTH) * hit.astype(f32)
            - SMOOTH / VOCAB
        )
    ).astype(bf16)
    d_picked = jnp.dot(d_logits, table, preferred_element_type=f32)
    grad_table = jnp.dot(d_logits.T, picked, preferred_element_type=f32)
    d_normed_out = tensor_total(jnp.zeros((rows, features), f32).at[loss_offsets].add(d_picked))
    d_stream_out, grad_final = norm_back(stream_out, gain[2], d_normed_out)
    d_piece = (gates.reshape(-1)[:, None] * d_stream_out[owner]).astype(bf16)
    d_arrived = route_exchange(pack(d_piece))
    d_active = jnp.dot(d_arrived, out_low.T, preferred_element_type=f32)
    unused, gelu_pull = jax.vjp(jax.nn.gelu, inner)
    d_inner = gelu_pull(d_active)[0].astype(bf16)
    grad_out = jnp.dot(active.T, d_arrived, preferred_element_type=f32)
    grad_in = jnp.dot(arrived.T, d_inner, preferred_element_type=f32)
    sent_back = jnp.dot(d_inner, in_low.T, preferred_element_type=f32).astype(bf16)
    d_routes = unpack(route_exchange(sent_back))
    gate_part = jnp.sum(d_stream_out[owner] * returned, -1).reshape(rows, top_k)
    route_part = jnp.sum(d_routes.reshape(rows, top_k, features), 1)
    d_from_experts, d_gates = tensor_total((route_part, gate_part))
    d_chosen = gates * (d_gates - jnp.sum(gates * d_gates, -1, keepdims=True))
    expert_hot = (routes[..., None] == jnp.arange(experts, dtype=jnp.int32)).astype(f32)
    d_router_logits = jnp.sum(expert_hot * d_chosen[..., None], 1).astype(bf16)
    grad_router = jnp.dot(d_router_logits.T, normed_mid, preferred_element_type=f32)
    d_normed_mid = d_from_experts + jnp.dot(
        d_router_logits, router_full, preferred_element_type=f32
    )
    d_from_mid, grad_middle = norm_back(stream_mid, gain[1], d_normed_mid)
    d_stream_mid = d_stream_out + d_from_mid
    d_attn_low = d_stream_mid.astype(bf16)
    grad_output_map = jnp.dot(attended_low.T, d_attn_low, preferred_element_type=f32)
    d_attended = jnp.dot(d_attn_low, output_map.T, preferred_element_type=f32).astype(bf16)
    d_heads = d_attended.reshape(seqs, sub, heads, HD)
    delta = jnp.moveaxis(jnp.sum(d_heads.astype(f32) * attended, -1), 2, 1)
    key_source, value_source = (
        lax.all_gather(keys_local, "dp", axis=1, tiled=True),
        lax.all_gather(values_local, "dp", axis=1, tiled=True),
    )

    def score_grads(
        q_heads, q_pos, q_pic, k_heads, k_pos, k_pic, bias, totals, deltas, dq_heads, v_heads
    ):
        s = pair_scores(q_heads, q_pos, q_pic, k_heads, k_pos, k_pic, bias)
        probs = jnp.exp(s - totals[..., None])
        d_probs = jnp.einsum("sqhd,skhd->shqk", dq_heads, v_heads, preferred_element_type=f32)
        d_scores = (probs * (d_probs - deltas[..., None])).astype(bf16)
        return (probs, d_scores)

    def key_step(carry, index):
        d_query, d_rel = carry
        start = index * block
        key_pos = start + jnp.arange(block, dtype=jnp.int32)
        key_heads = key_slice(key_source, start)
        value_heads = key_slice(value_source, start)
        bias, bias_pull = jax.vjp(
            lambda table_rel: rel_window(table_rel, dp_place * sub, sub, start, block, length),
            relative,
        )
        probs, d_scores = score_grads(
            query_heads,
            pos_here,
            picture_here,
            key_heads,
            key_pos,
            lax.dynamic_slice_in_dim(picture_all, start, block, 1),
            bias,
            log_total,
            delta,
            d_heads,
            value_heads,
        )
        d_query = (
            d_query
            + jnp.einsum("shqk,skhd->sqhd", d_scores, key_heads, preferred_element_type=f32) * scale
        )
        d_rel = d_rel + bias_pull(jnp.sum(d_scores.astype(f32), 0))[0]
        d_key = (
            jnp.einsum("shqk,sqhd->skhd", d_scores, query_heads, preferred_element_type=f32) * scale
        )
        d_value = jnp.einsum(
            "shqk,sqhd->skhd", probs.astype(bf16), d_heads, preferred_element_type=f32
        )
        joined = jnp.concatenate(
            [d_key.reshape(seqs, block, width), d_value.reshape(seqs, block, width)], 2
        )
        return ((d_query, d_rel), joined)

    start_carry = (jnp.zeros((seqs, sub, heads, HD), f32), jnp.zeros(relative.shape, f32))
    (d_query, d_rel), key_terms = lax.scan(key_step, start_carry, block_ids)
    d_bias = jnp.dot(d_rel, bucket_hot.T, precision=HIGH)
    ordered = jnp.moveaxis(key_terms, 0, 1).reshape(seqs, length, 2 * width)
    key_grads = lax.psum_scatter(ordered, "dp", scatter_dimension=1, tiled=True).reshape(
        rows, 2 * width
    )
    d_fresh = jnp.stack(
        [d_query.reshape(rows, width), key_grads[:, :width], key_grads[:, width:]]
    ).astype(bf16)
    grad_proj = jnp.einsum("td,ste->sde", normed_in, d_fresh, preferred_element_type=f32)
    d_normed_in = tensor_total(
        jnp.einsum("ste,sde->td", d_fresh, projection, preferred_element_type=f32)
    )
    d_from_in, grad_first = norm_back(stream_in, gain[0], d_normed_in)
    d_stream_in = d_stream_mid + d_from_in
    grad_table = grad_table + jnp.zeros((vocab_rows, features), f32).at[offset].add(
        jnp.where(owned[:, None], d_stream_in, 0.0)
    )
    sum_table, sum_proj, sum_output, sum_router, sum_gains = (
        lax.psum_scatter(grad_table, "dp", scatter_dimension=1, tiled=True),
        lax.psum_scatter(grad_proj, "dp", scatter_dimension=1, tiled=True),
        lax.psum_scatter(grad_output_map, "dp", scatter_dimension=1, tiled=True),
        lax.psum_scatter(grad_router, "dp", scatter_dimension=1, tiled=True),
        lax.psum_scatter(
            jnp.stack([grad_first, grad_middle, grad_final]), "dp", scatter_dimension=1, tiled=True
        ),
    )
    sum_bias = lax.psum(d_bias, "dp")
    squares = (
        jnp.sum(sum_table * sum_table)
        + jnp.sum(sum_proj * sum_proj)
        + jnp.sum(sum_output * sum_output)
        + jnp.sum(grad_in * grad_in)
        + jnp.sum(grad_out * grad_out)
        + (jnp.sum(sum_router * sum_router) + jnp.sum(sum_gains * sum_gains)) / tensor_count
        + jnp.sum(sum_bias * sum_bias) / dp_count
    )
    total_squares, loss_sum, loss_count = lax.psum(
        (squares, loss_local / tensor_count, jnp.sum(weight) / tensor_count), ("dp", "tensor")
    )
    grad_norm = jnp.sqrt(total_squares)
    clip = MAX_NORM / jnp.maximum(grad_norm, MAX_NORM)
    params = (
        embedding,
        attn_proj,
        out_proj,
        router,
        expert_in,
        expert_out,
        norm_gains,
        position_bias,
    )
    firsts = (
        embedding_first,
        attn_proj_first,
        out_proj_first,
        router_first,
        expert_in_first,
        expert_out_first,
        norm_gains_first,
        position_bias_first,
    )
    seconds = (
        embedding_second,
        attn_proj_second,
        out_proj_second,
        router_second,
        expert_in_second,
        expert_out_second,
        norm_gains_second,
        position_bias_second,
    )
    grads = (sum_table, sum_proj, sum_output, sum_router, grad_in, grad_out, sum_gains, sum_bias)
    results = []
    for index in range(8):
        results.extend(
            adam_update(
                params[index],
                firsts[index],
                seconds[index],
                clip * grads[index],
                RATES[index],
                DECAYS[index],
            )
        )
    return (
        results[0],
        results[1],
        results[2],
        results[3],
        results[4],
        results[5],
        results[6],
        results[7],
        results[8],
        results[9],
        results[10],
        results[11],
        results[12],
        results[13],
        results[14],
        results[15],
        results[16],
        results[17],
        results[18],
        results[19],
        results[20],
        results[21],
        results[22],
        results[23],
        grad_norm,
        loss_sum,
        loss_count,
    )


def fits(dp_count, tensor_count, arrays):
    token_ids, loss_offsets, routes, picture_start = arrays[0], arrays[2], arrays[3], arrays[4]
    columns, router, gains = arrays[6].shape[1], arrays[15], arrays[24]
    rows, picks = token_ids.shape[0], loss_offsets.shape[0]
    return (
        rows == 128
        and rows * dp_count <= SEQ
        and picture_start.shape[0] == 1
        and picks == 16
        and picks * dp_count == 128
        and dp_count % 4 == 0
        and tensor_count == 4
        and dp_count % router.shape[0] == 0
        and dp_count % 2 == 0
        and dp_count <= 8
        and router.shape[0] <= 4
        and routes.shape[1] == 2
        and gains.shape[0] == 3
        and columns % 32 == 0
        and arrays[9].shape[2] % 128 == 64
        and columns <= 128
    )


def solution(mesh):
    in_specs = (
        P("dp"),
        P("dp"),
        P("dp"),
        P("dp", None),
        P(),
        P(),
        P("tensor", "dp"),
        P("tensor", "dp"),
        P("tensor", "dp"),
        P(None, "dp", "tensor"),
        P(None, "dp", "tensor"),
        P(None, "dp", "tensor"),
        P("tensor", "dp"),
        P("tensor", "dp"),
        P("tensor", "dp"),
        P(None, "dp"),
        P(None, "dp"),
        P(None, "dp"),
        P(None, ("dp", "tensor")),
        P(None, ("dp", "tensor")),
        P(None, ("dp", "tensor")),
        P(("dp", "tensor"), None),
        P(("dp", "tensor"), None),
        P(("dp", "tensor"), None),
        P(None, "dp"),
        P(None, "dp"),
        P(None, "dp"),
        P("tensor", None),
        P("tensor", None),
        P("tensor", None),
    )
    out_specs = (
        P("tensor", "dp"),
        P("tensor", "dp"),
        P("tensor", "dp"),
        P(None, "dp", "tensor"),
        P(None, "dp", "tensor"),
        P(None, "dp", "tensor"),
        P("tensor", "dp"),
        P("tensor", "dp"),
        P("tensor", "dp"),
        P(None, "dp"),
        P(None, "dp"),
        P(None, "dp"),
        P(None, ("dp", "tensor")),
        P(None, ("dp", "tensor")),
        P(None, ("dp", "tensor")),
        P(("dp", "tensor"), None),
        P(("dp", "tensor"), None),
        P(("dp", "tensor"), None),
        P(None, "dp"),
        P(None, "dp"),
        P(None, "dp"),
        P("tensor", None),
        P("tensor", None),
        P("tensor", None),
        P(),
        P(),
        P(),
    )

    def chosen(*arrays):
        sizes = lax.axis_size("dp"), lax.axis_size("tensor")
        return (fast_local if fits(*sizes, arrays) else local)(*arrays)

    return jax.shard_map(chosen, mesh=mesh, in_specs=in_specs, out_specs=out_specs, check_vma=False)
```
